32 devices in a mesh: gz: 2 (over x), row: 8 (over z, core), col: 2 (over y).
Axes of the slice: x: 2, y: 2, z: 4, core: 2. Of those that a mesh axis runs over, the one named last changes fastest.
Arguments:
- volume: bfloat16 [32, 512, 512], P('gz', 'row', 'col'), may hold values from -7 to 7
Outputs:
- tensor: float32 [6, 8, 128, 128], P(None, 'gz', 'row', 'col')
The draws below stay inside these ranges and needn't reach their ends.
All inputs are finite; a program needn't handle non-finite values.
Results may differ from the reference program's by a relative error of at most 0.0028.
Values may be sent and summed in bfloat16 or wider, within the bound.
No kernel may reach another device: no remote copies, remote signals or barrier semaphores. Data moves between devices by JAX's collectives and lax.ppermute only.
A program may use at most 128 MiB of HBM per device.

```python
import math
import jax
import jax.numpy as jnp
from jax import lax

CX = 256
R = 3
R2 = 8
NZ = 32
NY = 512
NX = 512
N_COL = 2


def draw_volume(key, part):
    key = jax.random.fold_in(key, 11)
    key_family, key_azimuth, key_height, key_number, key_phase, key_noise = jax.random.split(key, 6)
    z_regions = NZ // 16
    y_regions = NY // 32
    x_regions = NX // 32
    region_shape = (z_regions, 1, y_regions, 1, x_regions, 1)
    family = jax.random.randint(key_family, region_shape, 0, 4)
    aligned = (family == 0).astype(jnp.float32)
    diagonal_low = (family == 1).astype(jnp.float32)
    diagonal_high = (family == 2).astype(jnp.float32)
    oblique = (family == 3).astype(jnp.float32)
    azimuth = jax.random.uniform(key_azimuth, region_shape, jnp.float32, -math.pi, math.pi)
    height = jax.random.uniform(key_height, region_shape, jnp.float32, -1.0, 1.0)
    radial = jnp.sqrt(jnp.maximum(1.0 - height * height, 0.0))
    number = jax.random.uniform(key_number, region_shape, jnp.float32, 0.5, 1.2)
    phases = jax.random.uniform(key_phase, region_shape, jnp.float32, -math.pi, math.pi)
    quarter = math.pi / 4.0
    halfway = math.pi / 2.0
    wave_z = quarter * diagonal_low + halfway * diagonal_high + oblique * number * height
    wave_y = quarter * diagonal_low + halfway * diagonal_high + oblique * number * radial * jnp.sin(azimuth)
    wave_x = halfway * aligned + quarter * diagonal_low + halfway * diagonal_high + oblique * number * radial * jnp.cos(azimuth)
    strength = 1.5 * aligned + 1.8 * diagonal_low + 5.5 * diagonal_high + 1.5 * oblique
    z_coord = jnp.arange(NZ).astype(jnp.float32).reshape(z_regions, 16, 1, 1, 1, 1)
    y_coord = jnp.arange(NY).astype(jnp.float32).reshape(1, 1, y_regions, 32, 1, 1)
    x_coord = jnp.arange(NX).astype(jnp.float32).reshape(1, 1, 1, 1, x_regions, 32)
    angles = wave_z * z_coord + wave_y * y_coord + wave_x * x_coord + phases
    full_shape = (z_regions, 16, y_regions, 32, x_regions, 32)
    noises = 0.3 * jnp.clip(jax.random.normal(key_noise, full_shape, jnp.float32), -3.0, 3.0)
    field_values = strength * jnp.cos(angles) + noises
    return field_values.reshape(NZ, NY, NX).astype(jnp.bfloat16)


def setup_inputs(seed: int = 0) -> dict:
    key_of = jax.random.split(jax.random.key(seed), 2)
    return {
        "volume": draw_volume(jax.random.fold_in(key_of[1], 71), 0),
    }


pair_table = ((0, 0), (1, 1), (2, 2), (0, 1), (0, 2), (1, 2))


def gauss_taps(radius):
    offsets = jnp.arange(-radius, radius + 1).astype(jnp.float32)
    spread = radius / 3.0
    smooth = jnp.exp(-offsets * offsets / (2.0 * spread * spread))
    smooth = smooth / jnp.sum(smooth)
    slopes = offsets * smooth
    slopes = slopes / jnp.sum(offsets * slopes)
    return smooth.astype(jnp.bfloat16), slopes.astype(jnp.bfloat16)


def pad_along(source, along_dim, radius):
    widths = [(0, 0)] * source.ndim
    widths[along_dim] = (radius, radius)
    return jnp.pad(source, widths)


def correlate(source, tap_values, along_dim, radius, stride, with_pad):
    padded = pad_along(source, along_dim, radius) if with_pad else source
    length = padded.shape[along_dim] - 2 * radius
    weights = tap_values.astype(jnp.float32)
    summed = jnp.zeros(lax.slice_in_dim(padded, 0, length, stride=stride, axis=along_dim).shape, jnp.float32)
    for offset in range(2 * radius + 1):
        shifted = lax.slice_in_dim(padded, offset, offset + length, stride=stride, axis=along_dim)
        summed = summed + weights[offset] * shifted.astype(jnp.float32)
    return summed


def reference(volume):
    smooth_d, slope_d = gauss_taps(R)
    smooth_i, unused = gauss_taps(R2)
    margin = R + R2
    padded = pad_along(volume, 2, margin)

    def one_strip(strip_index):
        start_col = strip_index * CX
        strip_cells = lax.dynamic_slice_in_dim(padded, start_col, CX + 2 * margin, 2)
        z_smooth = correlate(strip_cells, smooth_d, 0, R, 1, True).astype(jnp.bfloat16)
        z_slope = correlate(strip_cells, slope_d, 0, R, 1, True).astype(jnp.bfloat16)
        plane_gg = correlate(z_smooth, smooth_d, 1, R, 1, True).astype(jnp.bfloat16)
        plane_dg = correlate(z_smooth, slope_d, 1, R, 1, True).astype(jnp.bfloat16)
        plane_gd = correlate(z_slope, smooth_d, 1, R, 1, True).astype(jnp.bfloat16)
        grad_x = correlate(plane_gg, slope_d, 2, R, 1, False)
        grad_y = correlate(plane_dg, smooth_d, 2, R, 1, False)
        grad_z = correlate(plane_gd, smooth_d, 2, R, 1, False)
        gradients = [grad_x.astype(jnp.bfloat16), grad_y.astype(jnp.bfloat16), grad_z.astype(jnp.bfloat16)]
        columns = jnp.arange(CX + 2 * R2).astype(jnp.int32) + start_col - R2
        inside = ((columns >= 0) & (columns < NX)).astype(jnp.float32)
        outputs = []
        for first_pair, second_pair in pair_table:
            product = gradients[first_pair].astype(jnp.float32) * gradients[second_pair].astype(jnp.float32)
            product = (product * inside).astype(jnp.bfloat16)
            smooth_x = correlate(product, smooth_i, 2, R2, 4, False).astype(jnp.bfloat16)
            smooth_y = correlate(smooth_x, smooth_i, 1, R2, 4, True).astype(jnp.bfloat16)
            outputs.append(correlate(smooth_y, smooth_i, 0, R2, 4, True))
        return jnp.stack(outputs)

    strips = lax.map(one_strip, jnp.arange(N_COL, dtype=jnp.int32))
    return jnp.transpose(strips, (1, 2, 3, 0, 4)).reshape(6, NZ // 4, NY // 4, NX // 4)
```

```python
import jax
import jax.numpy as jnp
import ml_dtypes
import numpy as np
from jax import lax
from jax.experimental import pallas as pl
from jax.experimental.pallas import tpu as pltpu
from jax.sharding import PartitionSpec as P

R = 3
R2 = 8
HALO = 16
NEED = R + R2
NT = (((1,), (1,)), ((), ()))
F32 = jnp.float32
BF16 = jnp.bfloat16

pair_table = ((0, 0), (1, 1), (2, 2), (0, 1), (0, 2), (1, 2))


def gauss_taps(radius):
    offsets = np.arange(-radius, radius + 1).astype(np.float32)
    spread = np.float32(radius / 3.0)
    smooth = np.exp(-offsets * offsets / (np.float32(2.0) * spread * spread))
    smooth = smooth / np.sum(smooth)
    slopes = offsets * smooth
    slopes = slopes / np.sum(offsets * slopes)
    as_f32 = lambda t: t.astype(ml_dtypes.bfloat16).astype(np.float32)
    return as_f32(smooth), as_f32(slopes)


SMOOTH_D, SLOPE_D = gauss_taps(R)
SMOOTH_I, _ = gauss_taps(R2)


def band(taps, sources, targets):
    radius = len(taps) // 2
    gap = np.asarray(sources)[:, None] - np.asarray(targets)[None, :]
    return np.where(np.abs(gap) <= radius, taps[np.clip(gap + radius, 0, 2 * radius)], 0.0)


def weight_table(depth, rows, cols):
    ext = rows + 2 * HALO
    grad_rows = rows + 16
    far = 10**6
    y_in = np.arange(ext) - HALO
    y_out = np.arange(grad_rows) - R2
    smooth_y = band(SMOOTH_D, y_in, y_out).T
    slope_y = band(SLOPE_D, y_in, y_out).T
    zero = np.zeros_like(smooth_y)
    wy = np.block([[smooth_y, zero], [slope_y, zero], [zero, smooth_y]])
    x_all = np.arange(cols)
    slot_in = np.full(32, far)
    slot_in[0:8] = cols + np.arange(8)
    slot_in[8:14] = np.arange(6)
    slot_in[14:20] = cols - 6 + np.arange(6)
    slot_in[21:32] = np.arange(-11, 0)
    slot_out = np.full(32, -far)
    slot_out[0:11] = np.arange(-8, 3)
    slot_out[11:19] = cols - 3 + np.arange(8)
    eye8 = np.eye(8)
    inner = np.where((x_all >= R) & (x_all < cols - R), x_all, far)
    quarter = cols // 4
    coarse_edge = np.full(8, 3 * far)
    coarse_edge[0:5] = [0, 1, 2, quarter - 2, quarter - 1]
    xs_edge = band(SMOOTH_I, slot_out, 4 * coarse_edge)
    ys = band(SMOOTH_I, y_out, 4 * np.arange(rows // 4)).T
    own = np.zeros((32, cols))
    for slot in range(8, 20):
        own[slot, slot_in[slot]] = 1.0
    right = (x_all[None, :] == cols - HALO + np.arange(HALO)[:, None]).astype(np.float32)
    left = (x_all[None, :] == np.arange(HALO)[:, None]).astype(np.float32)
    zq = 4 * (np.arange(depth // 4 + 4) - 2)
    zs = band(SMOOTH_I, np.arange(depth), zq)
    place = np.zeros((8, 128))
    for j in range(5):
        place[j, coarse_edge[j]] = 1.0
    g = np.einsum("zq,jx->zjqx", zs, place).reshape(depth * 8, len(zq) * 128)
    parts = {
        "wy": wy,
        "wy_slope": smooth_y,
        "wxd": band(SLOPE_D, x_all, x_all),
        "wxs": band(SMOOTH_D, x_all, x_all),
        "bdd": np.kron(eye8, band(SLOPE_D, slot_in, slot_out)),
        "bds": np.kron(eye8, band(SMOOTH_D, slot_in, slot_out)),
        "ysm": np.kron(np.eye(3), ys),
        "xsm": band(SMOOTH_I, inner, 4 * np.arange(quarter)),
        "bdx": np.kron(eye8, xs_edge),
        "sel_right": right,
        "sel_left": left,
        "sel_own": own,
        "g0": g[:, 0:256],
        "g1": g[:, 256:512],
        "g2": g[:, 512:768],
        "g3": g[:, 768:1024],
    }
    place_of, blocks, at = {}, [], 0
    for name, part in parts.items():
        height = -(-part.shape[0] // 16) * 16
        block = np.zeros((height, 256), np.float32)
        block[: part.shape[0], : part.shape[1]] = part
        place_of[name] = (at, part.shape[0], part.shape[1])
        blocks.append(block)
        at += height
    return np.concatenate(blocks).astype(ml_dtypes.bfloat16), place_of, zs


def z_filter(v, count):
    for z in range(count):
        w = v[z : z + 7]
        smooth = w[3] * float(SMOOTH_D[3])
        slope = None
        for s in (1, 2, 3):
            smooth = smooth + (w[3 + s] + w[3 - s]) * float(SMOOTH_D[3 + s])
            term = (w[3 + s] - w[3 - s]) * float(SLOPE_D[3 + s])
            slope = term if slope is None else slope + term
        yield z, smooth.astype(BF16), slope.astype(BF16)


def getter(place_of, w):
    def get(name, width=None):
        at, height, own_width = place_of[name]
        return w[at : at + height, 0 : (width or own_width)]

    return get


def spread_rows(first, transposed):
    shape = (16 * HALO, 16 * NEED) if transposed else (16 * NEED, 16 * HALO)
    packed = lax.broadcasted_iota(jnp.int32, shape, 1 if transposed else 0)
    full = lax.broadcasted_iota(jnp.int32, shape, 0 if transposed else 1)
    z = lax.shift_right_logical(packed * 373, 12)
    return jnp.where(full == packed + z * (HALO - NEED) + first, 1.0, 0.0).astype(BF16)


def load_kernel(n_row, vol, s1, s2, zmsg):
    depth, rows, cols = vol.shape
    odd = lax.rem(lax.axis_index("row"), 2) == 1
    base = jnp.where(lax.axis_index("gz") == 0, depth - R, 0)
    top = vol[:, 0:HALO, :].reshape(depth * HALO, cols)
    bottom = vol[:, rows - HALO : rows, :].reshape(depth * HALO, cols)
    to_before = jnp.dot(spread_rows(0, False), top, preferred_element_type=F32).astype(BF16)
    to_after = jnp.dot(
        spread_rows(HALO - NEED, False), bottom, preferred_element_type=F32
    ).astype(BF16)
    s1[...] = jnp.where(odd, to_before, to_after)
    s2[...] = jnp.where(odd, to_after, to_before)
    zmsg[...] = vol[pl.ds(base, R)]


def stage_kernel(vol, w, vol_out, w_out, sems):
    copies = [
        pltpu.make_async_copy(vol, vol_out, sems.at[0]),
        pltpu.make_async_copy(w, w_out, sems.at[1]),
    ]
    for copy in copies:
        copy.start()
    for copy in copies:
        copy.wait()


def pack_kernel(place_of, n_row, n_col, vol, r1, r2, w, *refs):
    n_side = 1 if n_col == 2 else 2
    yud, zcorner, strips = refs[0:3]
    xmsgs, zxmsgs = refs[3 : 3 + n_side], refs[3 + n_side : 3 + 2 * n_side]
    ext = refs[3 + 2 * n_side]
    depth, rows, cols = vol.shape
    gz, row = lax.axis_index("gz"), lax.axis_index("row")
    odd = lax.rem(row, 2) == 1
    base = jnp.where(gz == 0, depth - R, 0)
    none = jnp.zeros((), BF16)
    got1, got2 = r1[...], r2[...]
    from_before = jnp.where(odd, got1, jnp.where(row == 0, none, got2))
    from_after = jnp.where(odd, jnp.where(row == n_row - 1, none, got2), got1)
    above = jnp.dot(
        spread_rows(HALO - NEED, True), from_before, preferred_element_type=F32
    ).astype(BF16).reshape(depth, HALO, cols)
    below = jnp.dot(
        spread_rows(0, True), from_after, preferred_element_type=F32
    ).astype(BF16).reshape(depth, HALO, cols)
    yud[:, 0:HALO, :] = above
    yud[:, HALO:, :] = below
    zcorner[...] = yud[pl.ds(base, R)]
    ext[:, 0:HALO, :] = above
    ext[:, HALO : HALO + rows, :] = vol[...]
    ext[:, HALO + rows : 2 * HALO + rows, :] = below
    ext[:, 2 * HALO + rows :, :] = jnp.zeros((depth, 128 - rows - 2 * HALO, cols), BF16)
    get = getter(place_of, w)
    if n_col == 2:
        col = lax.axis_index("col")
        at_r, at_l = place_of["sel_right"][0], place_of["sel_left"][0]
        at = pl.multiple_of(jnp.where(col == 0, at_r, at_l), 16)
        selects = [get("sel_own"), w[pl.ds(at, HALO), :]]
    else:
        selects = [get("sel_own"), get("sel_right"), get("sel_left")]
    select = jnp.concatenate(selects, axis=0)
    for z in range(depth):
        picked = lax.dot_general(select, ext[z], NT, preferred_element_type=F32).astype(BF16)
        strips[z] = picked[0:32]
        for side in range(n_side):
            xmsgs[side][z] = picked[32 + 16 * side : 48 + 16 * side]
    for side in range(n_side):
        zxmsgs[side][...] = xmsgs[side][pl.ds(base, R)]


def row_mask(get, n_row, rows, gr, quarter_rows):
    row = lax.axis_index("row")
    lane = lax.broadcasted_iota(jnp.int32, (3 * quarter_rows, 3 * gr), 1)
    y_out = lax.rem(lane, gr) - R2
    outside = ((row == 0) & (y_out < 0)) | ((row == n_row - 1) & (y_out >= rows))
    return jnp.where(outside, 0.0, get("ysm").astype(F32)).astype(BF16)


def layers_to_sums(get, ysm, load, count, shape, u_ref, zf, planes, prod, sm):
    rows, cols = shape
    ext = rows + 2 * HALO
    gr = rows + 16
    n_rows = 6 * (rows // 4)
    half_rows = n_rows // 2
    for tile in range(cols // 128):
        lanes = slice(tile * 128, tile * 128 + 128)
        for at in range(0, ext, 16):
            for z, smooth, slope in z_filter(load(at, lanes), count):
                zf[z, at : at + 16, lanes] = smooth
                zf[z, ext + at : ext + at + 16, lanes] = slope
    wy = get("wy")
    for z in range(count):
        out = jnp.dot(wy, zf[z], preferred_element_type=F32).astype(BF16)
        planes[0, z] = out[0:gr]
        planes[1, z] = out[gr : 2 * gr]
        planes[2, z] = out[2 * gr :]
    group = 4 if count % 4 == 0 else count
    for at in range(0, count, group):
        grads = []
        for f, name in enumerate(("wxd", "wxs", "wxs")):
            part = planes[f, at : at + group].reshape(group * gr, cols)
            out = jnp.dot(part, get(name), preferred_element_type=F32)
            grads.append(out.astype(BF16).reshape(group, gr, cols))
        for c, (a, b) in enumerate(pair_table):
            prod[at : at + group, c * gr : (c + 1) * gr] = grads[a] * grads[b]
    for z in range(count):
        for half in range(2):
            part = prod[z, half * 3 * gr : (half + 1) * 3 * gr]
            out = jnp.dot(ysm, part, preferred_element_type=F32)
            sm[z, half * half_rows : (half + 1) * half_rows] = out.astype(BF16)
    out = jnp.dot(
        sm[...].reshape(count * n_rows, cols), get("xsm"), preferred_element_type=F32
    )
    u_ref[...] = out.reshape(count, n_rows, cols // 4)


def block_loader(vol, yud, rows):
    def layer(z, at, lanes):
        if at < HALO:
            return yud[z, at : at + 16, lanes].astype(F32)
        if at < HALO + rows:
            return vol[z, at - HALO : at - HALO + 16, lanes].astype(F32)
        return yud[z, at - rows : at - rows + 16, lanes].astype(F32)

    return layer


FIRST = 8
EDGE = R
LAST = 5


def first_kernel(place_of, n_row, vol, yud, w, u_ref, *scratch):
    depth, rows, cols = vol.shape
    get = getter(place_of, w)
    ysm = row_mask(get, n_row, rows, rows + 16, rows // 4)
    base = jnp.where(lax.axis_index("gz") == 0, depth - EDGE - FIRST - R, 0)
    layer = block_loader(vol, yud, rows)
    load = lambda at, lanes: [layer(base + k, at, lanes) for k in range(FIRST + 2 * R)]
    layers_to_sums(get, ysm, load, FIRST, (rows, cols), u_ref, *scratch)


def strip_sums(place_of, n_col, ysm, w, layers, shape, hs, hd, pstrip):
    rows, cols = shape
    gr = rows + 16
    quarter_rows = rows // 4
    get = getter(place_of, w)
    col = lax.axis_index("col")
    for z, smooth, slope in z_filter(layers, 8):
        hs[32 * z : 32 * z + 32] = smooth
        hd[32 * z : 32 * z + 32] = slope
    at = place_of["wy"][0]
    wy_strip = w[at : at + 2 * gr, 0:128]
    p01 = lax.dot_general(wy_strip, hs[...], NT, preferred_element_type=F32).astype(BF16)
    wy_slope = get("wy_slope", 128)
    p2 = lax.dot_general(wy_slope, hd[...], NT, preferred_element_type=F32).astype(BF16)
    slot = lax.rem(lax.broadcasted_iota(jnp.int32, (3 * quarter_rows, 256), 1), 32)
    outside_x = ((col == 0) & (slot < 8)) | ((col == n_col - 1) & (slot >= 14))
    g0 = jnp.dot(p01[0:gr], get("bdd"), preferred_element_type=F32).astype(BF16)
    g1 = jnp.dot(p01[gr:], get("bds"), preferred_element_type=F32).astype(BF16)
    g2 = jnp.dot(p2, get("bds"), preferred_element_type=F32).astype(BF16)
    grads = [g0, g1, g2]
    for c, (a, b) in enumerate(pair_table):
        pstrip[c * gr : (c + 1) * gr] = grads[a] * grads[b]
    halves = []
    for half in range(2):
        rows_of = slice(half * 3 * gr, (half + 1) * 3 * gr)
        out = jnp.dot(ysm, pstrip[rows_of], preferred_element_type=F32)
        halves.append(jnp.where(outside_x, 0.0, out).astype(BF16))
    smoothed = jnp.concatenate(halves, axis=0)
    return jnp.dot(smoothed, get("bdx"), preferred_element_type=F32)


def split(array):
    high = array.astype(BF16)
    return high, (array - high.astype(F32)).astype(BF16)


def strip_joiner(n_col, strips_shape):
    slots = lax.broadcasted_iota(jnp.int32, strips_shape, 0)
    col = lax.axis_index("col")
    if n_col == 2:
        keep = ((slots < 8) & (col == 0)) | ((slots >= 21) & (col == 1))
        sides = lambda refs, z: (refs[0][z], refs[0][z])
    else:
        keep = (slots < 8) | (slots >= 21)
        sides = lambda refs, z: (refs[1][z], refs[0][z])

    def join(own_part, refs, z):
        both = jnp.concatenate([part.astype(F32) for part in sides(refs, z)], axis=0)
        return jnp.where(keep, both, own_part)

    return join


def edge_kernel(place_of, zs, n_row, n_col, vol, yud, zown, zcorner, strips, xh, zxh, u1, w,
                u_ref, us_ref, send_ref, zext, hs, hd, pstrip, *scratch):
    depth, rows, cols = vol.shape
    ext = rows + 2 * HALO
    quarter_rows, quarter = rows // 4, cols // 4
    n_zq = zs.shape[1]
    get = getter(place_of, w)
    low = lax.axis_index("gz") == 0
    ysm = row_mask(get, n_row, rows, rows + 16, quarter_rows)

    zext[:, 0:HALO] = zcorner[:, 0:HALO]
    zext[:, HALO : HALO + rows] = zown[...]
    zext[:, HALO + rows : ext] = zcorner[:, HALO:]
    zext[:, ext:] = jnp.zeros((R, 128 - ext, cols), BF16)

    join = strip_joiner(n_col, (32, 128))
    halo = lax.dot_general(
        get("sel_own"), zext[...].reshape(R * 128, cols), NT, preferred_element_type=F32
    )
    halo = [join(halo[:, 128 * k : 128 * k + 128], zxh, k) for k in range(R)]
    own = lambda z: join(strips[z].astype(F32), xh, z)
    layers = [jnp.where(low, own(depth - 11 + k), halo[k]) for k in range(R)]
    layers += [own(jnp.where(low, depth - 11, -R) + k) for k in range(R, 11)]
    layers += [jnp.where(low, halo[k - 11], own(k - R)) for k in range(11, 14)]
    u_strip = strip_sums(place_of, n_col, ysm, w, layers, (rows, cols), hs, hd, pstrip)
    us_ref[...] = u_strip
    g_last = place_of["g%d" % (n_zq // 2 - 1)][0] + 64
    at = pl.multiple_of(jnp.where(low, g_last, place_of["g0"][0]), 16)
    g = w[pl.ds(at, 64), :]
    strip_send = sum(jnp.dot(part, g, preferred_element_type=F32) for part in split(u_strip))

    layer = block_loader(vol, yud, rows)
    start = jnp.where(low, depth - R, 0)
    outer = jnp.where(low, depth - 2 * R, R)

    def load(at, lanes):
        beyond = [zext[k, at : at + 16, lanes].astype(F32) for k in range(R)]
        inner = [layer(outer + k, at, lanes) for k in range(R)]
        middle = [layer(start + k, at, lanes) for k in range(R)]
        before = [jnp.where(low, inner[k], beyond[k]) for k in range(R)]
        after = [jnp.where(low, beyond[k], inner[k]) for k in range(R)]
        return before + middle + after

    layers_to_sums(get, ysm, load, EDGE, (rows, cols), u_ref, *scratch)

    sends = []
    for k in range(2):
        total = strip_send[:, 128 * k : 128 * k + quarter]
        for i in range(FIRST + EDGE):
            from_low = depth - EDGE - FIRST + i
            from_high = EDGE + i if i < FIRST else i - FIRST
            a = float(zs[from_low, n_zq - 2 + k])
            b = float(zs[from_high, k])
            if a == 0.0 and b == 0.0:
                continue
            u = u1[i] if i < FIRST else u_ref[i - FIRST]
            total = total + u * jnp.where(low, a, b)
        sends.append(total)
    send_ref[...] = jnp.concatenate(sends, axis=1).astype(BF16)


def last_kernel(place_of, zs, n_row, n_col, vol, yud, strips, xh, u1, u2, us, w,
                own_ref, u3, hs, hd, pstrip, *scratch):
    depth, rows, cols = vol.shape
    quarter_rows, quarter = rows // 4, cols // 4
    get = getter(place_of, w)
    low = lax.axis_index("gz") == 0
    ysm = row_mask(get, n_row, rows, rows + 16, quarter_rows)
    join = strip_joiner(n_col, (32, 128))
    own = lambda z: join(strips[z].astype(F32), xh, z)
    strip_layers = [jnp.where(low, 0.0, own(depth - 11 + k)) for k in range(R)]
    strip_layers += [own(jnp.where(low, -R, depth - 11) + k) for k in range(R, 11)]
    strip_layers += [jnp.where(low, own(k - R), 0.0) for k in range(11, 14)]
    other = strip_sums(place_of, n_col, ysm, w, strip_layers, (rows, cols), hs, hd, pstrip)
    both = jnp.where(
        low,
        jnp.concatenate([other, us[...]], axis=1),
        jnp.concatenate([us[...], other], axis=1),
    )
    parts = split(both)
    v = []
    for name in ("g1", "g2"):
        out = sum(jnp.dot(part, get(name), preferred_element_type=F32) for part in parts)
        v += [out[:, 0:quarter], out[:, 128 : 128 + quarter]]
    layer = block_loader(vol, yud, rows)
    base = jnp.where(low, -R, depth - LAST - R)
    before_on = jnp.where(low, 0.0, 1.0)
    after_on = jnp.where(low, 1.0, 0.0)

    def load(at, lanes):
        out = []
        for k in range(LAST + 2 * R):
            block = layer(jnp.clip(base + k, 0, depth - 1), at, lanes)
            if k < R:
                block = block * before_on
            elif k >= LAST + R:
                block = block * after_on
            out.append(block)
        return out

    layers_to_sums(get, ysm, load, LAST, (rows, cols), u3, *scratch)
    for q in range(depth // 4):
        total = v[q]
        for i in range(depth):
            if i < FIRST:
                u, from_low, from_high = u1[i], depth - EDGE - FIRST + i, EDGE + i
            elif i < FIRST + EDGE:
                k = i - FIRST
                u, from_low, from_high = u2[k], depth - EDGE + k, k
            else:
                k = i - FIRST - EDGE
                u, from_low, from_high = u3[k], k, depth - LAST + k
            a, b = float(zs[from_low, q + 2]), float(zs[from_high, q + 2])
            if a == 0.0 and b == 0.0:
                continue
            total = total + u * jnp.where(low, a, b)
        own_ref[:, q] = total.reshape(6, quarter_rows, quarter)


def add_kernel(own, got, out):
    n_q, quarter = own.shape[1], own.shape[3]
    low = lax.axis_index("gz") == 0
    parts = [
        got[:, k * quarter : (k + 1) * quarter].astype(F32).reshape(own.shape[0], -1, quarter)
        for k in range(2)
    ]
    for q in range(n_q):
        total = own[:, q]
        if q < 2:
            total = total + parts[q] * jnp.where(low, 0.0, 1.0)
        if q >= n_q - 2:
            total = total + parts[q - n_q + 2] * jnp.where(low, 1.0, 0.0)
        out[:, q] = total


def call(body, outs, operands, scratch, name, in_hbm=False, flops=0):
    vmem = pl.BlockSpec(memory_space=pltpu.VMEM)
    source = pl.BlockSpec(memory_space=pltpu.HBM) if in_hbm else vmem
    moved = sum(o.size * o.dtype.itemsize for o in list(outs) + list(operands))
    return pl.pallas_call(
        body,
        out_shape=list(outs),
        in_specs=[source] * len(operands),
        out_specs=[vmem] * len(outs),
        scratch_shapes=scratch,
        compiler_params=pltpu.CompilerParams(vmem_limit_bytes=24 * 2**20),
        cost_estimate=pl.CostEstimate(flops=flops, bytes_accessed=moved, transcendentals=0),
        name=name,
    )(*operands)


def per_device(volume):
    depth, rows, cols = volume.shape
    n_row, n_col = lax.axis_size("row"), lax.axis_size("col")
    table, place_of, zs = weight_table(depth, rows, cols)
    ext = rows + 2 * HALO
    gr = rows + 16
    quarter_rows, quarter = rows // 4, cols // 4
    n_rows = 6 * quarter_rows
    sds = jax.ShapeDtypeStruct
    dma = pltpu.SemaphoreType.DMA

    def scratch_for(count):
        return [
            pltpu.VMEM((count, 2 * ext, cols), BF16),
            pltpu.VMEM((3, count, gr, cols), BF16),
            pltpu.VMEM((count, 6 * gr, cols), BF16),
            pltpu.VMEM((count, n_rows, cols), BF16),
        ]

    layer_flops = 2 * cols * (3 * gr * 2 * ext + 3 * gr * cols + n_rows * 3 * gr + n_rows * quarter)

    s1, s2, zmsg = call(
        lambda *refs: load_kernel(n_row, *refs),
        [sds((depth * NEED, cols), BF16)] * 2 + [sds((R, rows, cols), BF16)],
        [volume], [], "load",
    )
    inner = [(i, i + 1) for i in range(1, n_row - 1, 2)]
    inner = inner + [(j, i) for i, j in inner] + [(0, 0), (n_row - 1, n_row - 1)]
    r2 = lax.ppermute(s2, "row", inner)
    r1 = lax.ppermute(s1, "row", [(i, i ^ 1) for i in range(n_row)])
    swap = [(0, 1), (1, 0)]
    zown = lax.ppermute(zmsg, "gz", swap)
    vol, w = call(
        stage_kernel,
        [sds(volume.shape, BF16), sds(table.shape, BF16)],
        [volume, jnp.asarray(table)], [dma((2,))], "stage", in_hbm=True,
    )

    n_side = 1 if n_col == 2 else 2
    packed = call(
        lambda *refs: pack_kernel(place_of, n_row, n_col, *refs),
        [sds((depth, 2 * HALO, cols), BF16), sds((R, 2 * HALO, cols), BF16)]
        + [sds((depth, 32, 128), BF16)]
        + [sds((depth, HALO, 128), BF16)] * n_side
        + [sds((R, HALO, 128), BF16)] * n_side,
        [vol, r1, r2, w], [pltpu.VMEM((depth, 128, cols), BF16)], "pack",
    )
    yud, zcmsg, strips = packed[0:3]
    xmsgs, zxmsgs = packed[3 : 3 + n_side], packed[3 + n_side :]
    zcorner = lax.ppermute(zcmsg, "gz", swap)
    if n_col == 2:
        xh = [lax.ppermute(xmsgs[0], "col", swap)]
        zxh = [lax.ppermute(zxmsgs[0], ("gz", "col"), [(i, 3 - i) for i in range(4)])]
    else:
        xh, zxh = [], []
        for side, step in enumerate((1, -1)):
            line = [(i, i + step) for i in range(n_col) if 0 <= i + step < n_col]
            both = [
                (z * n_col + i, (1 - z) * n_col + j) for z in range(2) for i, j in line
            ]
            xh.append(lax.ppermute(xmsgs[side], "col", line))
            zxh.append(lax.ppermute(zxmsgs[side], ("gz", "col"), both))

    (u1,) = call(
        lambda *refs: first_kernel(place_of, n_row, *refs),
        [sds((FIRST, n_rows, quarter), F32)],
        [vol, yud, w], scratch_for(FIRST), "first", flops=FIRST * layer_flops,
    )

    def edge_body(*refs):
        x_refs = refs[5 : 5 + n_side]
        zx_refs = refs[5 + n_side : 5 + 2 * n_side]
        edge_kernel(
            place_of, zs, n_row, n_col, *refs[0:5], x_refs, zx_refs, *refs[5 + 2 * n_side :]
        )

    strip_scratch = [
        pltpu.VMEM((8 * 32, 128), BF16),
        pltpu.VMEM((8 * 32, 128), BF16),
        pltpu.VMEM((6 * gr, 8 * 32), BF16),
    ]
    u2, us, send = call(
        edge_body,
        [
            sds((EDGE, n_rows, quarter), F32),
            sds((n_rows, 64), F32),
            sds((n_rows, 2 * quarter), BF16),
        ],
        [vol, yud, zown, zcorner, strips] + xh + zxh + [u1, w],
        [pltpu.VMEM((R, 128, cols), BF16)] + strip_scratch + scratch_for(EDGE),
        "edge", flops=2 * EDGE * layer_flops,
    )
    got = lax.ppermute(send, "gz", swap)

    def last_body(*refs):
        last_kernel(
            place_of, zs, n_row, n_col, *refs[0:3], refs[3 : 3 + n_side], *refs[3 + n_side :]
        )

    (own,) = call(
        last_body,
        [sds((6, depth // 4, quarter_rows, quarter), F32)],
        [vol, yud, strips] + xh + [u1, u2, us, w],
        [pltpu.VMEM((LAST, n_rows, quarter), F32)] + strip_scratch + scratch_for(LAST),
        "last", flops=LAST * layer_flops,
    )
    (out,) = call(add_kernel, [sds(own.shape, F32)], [own, got], [], "add")
    return out


def solution(mesh):
    return jax.shard_map(
        per_device,
        mesh=mesh,
        in_specs=(P("gz", "row", "col"),),
        out_specs=P(None, "gz", "row", "col"),
        check_vma=False,
    )
```

```python
import jax
import jax.numpy as jnp
import ml_dtypes
import numpy as np
from jax import lax
from jax.experimental import pallas as pl
from jax.experimental.pallas import tpu as pltpu
from jax.sharding import PartitionSpec as P

R = 3
R2 = 8
HALO = 16
NEED = R + R2
EXTRA = 12
SLOTS = 32
NT = (((1,), (1,)), ((), ()))
F32 = jnp.float32
BF16 = jnp.bfloat16

pair_table = ((0, 0), (1, 1), (2, 2), (0, 1), (0, 2), (1, 2))


def gauss_taps(radius):
    offsets = np.arange(-radius, radius + 1).astype(np.float32)
    spread = np.float32(radius / 3.0)
    smooth = np.exp(-offsets * offsets / (np.float32(2.0) * spread * spread))
    smooth = smooth / np.sum(smooth)
    slopes = offsets * smooth
    slopes = slopes / np.sum(offsets * slopes)
    as_f32 = lambda t: t.astype(ml_dtypes.bfloat16).astype(np.float32)
    return as_f32(smooth), as_f32(slopes)


SMOOTH_D, SLOPE_D = gauss_taps(R)
SMOOTH_I, _ = gauss_taps(R2)


def band(taps, sources, targets):
    radius = len(taps) // 2
    gap = np.asarray(sources)[:, None] - np.asarray(targets)[None, :]
    return np.where(np.abs(gap) <= radius, taps[np.clip(gap + radius, 0, 2 * radius)], 0.0)


def weight_table(depth, rows, cols):
    ext = rows + 2 * HALO
    grad_rows = rows + 16
    far = 10**6
    y_in = np.arange(ext) - HALO
    y_out = np.arange(grad_rows) - R2
    smooth_y = band(SMOOTH_D, y_in, y_out).T
    slope_y = band(SLOPE_D, y_in, y_out).T
    zero = np.zeros_like(smooth_y)
    wy = np.block([[smooth_y, zero], [slope_y, zero], [zero, smooth_y]])
    order = np.concatenate([np.arange(rows), np.arange(HALO) - HALO, rows + np.arange(HALO)]) + HALO
    x_all = np.arange(cols)
    slot_in = np.full(SLOTS, far)
    slot_in[0:8] = cols + np.arange(8)
    slot_in[8:14] = np.arange(6)
    slot_in[14:20] = cols - 6 + np.arange(6)
    slot_in[21:32] = np.arange(-11, 0)
    slot_out = np.full(SLOTS, -far)
    slot_out[0:11] = np.arange(-8, 3)
    slot_out[11:19] = cols - 3 + np.arange(8)
    eye8 = np.eye(8)
    inner = np.where((x_all >= R) & (x_all < cols - R), x_all, far)
    quarter = cols // 4
    coarse_edge = np.full(8, 3 * far)
    coarse_edge[0:5] = [0, 1, 2, quarter - 2, quarter - 1]
    xs_edge = band(SMOOTH_I, slot_out, 4 * coarse_edge)
    ys = band(SMOOTH_I, y_out, 4 * np.arange(rows // 4)).T
    zs = band(SMOOTH_I, np.arange(depth), 4 * (np.arange(depth // 4 + 4) - 2))
    place = np.zeros((8, 128))
    for j in range(5):
        place[j, coarse_edge[j]] = 1.0
    own_z = 4 * np.arange(depth // 4)
    g = [
        np.einsum("zq,jx->zjqx", band(SMOOTH_I, np.arange(depth + 8) + first, own_z), place)
        for first in (0, -8)
    ]
    g = [t.reshape((depth + 8) * 8, len(own_z) * 128) for t in g]
    packed = np.arange(depth * NEED)
    above = np.zeros((depth * HALO, depth * NEED))
    above[packed + packed // NEED * (HALO - NEED) + HALO - NEED, packed] = 1.0
    below = np.zeros((depth * HALO, depth * NEED))
    below[packed + packed // NEED * (HALO - NEED), packed] = 1.0
    used = 2 * R + 13
    packed = np.arange(R * used)
    corner = np.zeros((64, R * 2 * HALO))
    corner[packed, packed + packed // used * (2 * HALO - used) + HALO - NEED] = 1.0
    parts = {
        "above": above,
        "below": below,
        "corner": corner,
        "corner_back": corner.T,
        "wy": wy,
        "wy_strip": np.concatenate([smooth_y, slope_y])[:, order],
        "wy_strip_slope": smooth_y[:, order],
        "wxd": band(SLOPE_D, x_all, x_all),
        "wxs": band(SMOOTH_D, x_all, x_all),
        "bdd": np.kron(eye8, band(SLOPE_D, slot_in, slot_out)),
        "bds": np.kron(eye8, band(SMOOTH_D, slot_in, slot_out)),
        "ysm": np.kron(np.eye(3), ys),
        "xsm": band(SMOOTH_I, inner, 4 * np.arange(quarter)),
        "bdx": np.kron(eye8, xs_edge),
        "g_low0": g[0][:, 0:256],
        "g_low1": g[0][:, 256:512],
        "g_high0": g[1][:, 0:256],
        "g_high1": g[1][:, 256:512],
    }
    place_of, blocks, at = {}, [], 0
    for name, part in parts.items():
        height = -(-part.shape[0] // 16) * 16
        block = np.zeros((height, 256), np.float32)
        block[: part.shape[0], : part.shape[1]] = part
        place_of[name] = (at, part.shape[0], part.shape[1])
        blocks.append(block)
        at += height
    return np.concatenate(blocks).astype(ml_dtypes.bfloat16), place_of, zs


def z_filter(v, count):
    for z in range(count):
        w = v[z : z + 7]
        smooth = w[3] * float(SMOOTH_D[3])
        slope = None
        for s in (1, 2, 3):
            smooth = smooth + (w[3 + s] + w[3 - s]) * float(SMOOTH_D[3 + s])
            term = (w[3 + s] - w[3 - s]) * float(SLOPE_D[3 + s])
            slope = term if slope is None else slope + term
        yield z, smooth.astype(BF16), slope.astype(BF16)


def getter(place_of, w):
    def get(name, width=None):
        at, height, own_width = place_of[name]
        return w[at : at + height, 0 : (width or own_width)]

    return get


def row_mask(get, n_row, rows, gr, quarter_rows):
    row = lax.axis_index("row")
    lane = lax.broadcasted_iota(jnp.int32, (3 * quarter_rows, 3 * gr), 1)
    y_out = lax.rem(lane, gr) - R2
    outside = ((row == 0) & (y_out < 0)) | ((row == n_row - 1) & (y_out >= rows))
    return jnp.where(outside, 0.0, get("ysm").astype(F32)).astype(BF16)


def layers_to_sums(get, ysm, load, count, shape, u_ref, zf, planes, prod, sm):
    rows, cols = shape
    ext = rows + 2 * HALO
    gr = rows + 16
    n_rows = 6 * (rows // 4)
    half_rows = n_rows // 2
    for tile in range(cols // 128):
        lanes = slice(tile * 128, tile * 128 + 128)
        for at in range(0, ext, 16):
            for z, smooth, slope in z_filter(load(at, lanes), count):
                zf[z, at : at + 16, lanes] = smooth
                zf[z, ext + at : ext + at + 16, lanes] = slope
    wy = get("wy")
    for z in range(count):
        out = jnp.dot(wy, zf[z], preferred_element_type=F32).astype(BF16)
        planes[0, z] = out[0:gr]
        planes[1, z] = out[gr : 2 * gr]
        planes[2, z] = out[2 * gr :]
    sides = []
    for first, n, name in ((0, 1, "wxd"), (1, 2, "wxs")):
        part = planes[first : first + n].reshape(n * count * gr, cols)
        out = jnp.dot(part, get(name), preferred_element_type=F32)
        sides.append(out.astype(BF16).reshape(n, count, gr, cols))
    grads = [sides[0][0], sides[1][0], sides[1][1]]
    for c, (a, b) in enumerate(pair_table):
        prod[:, c * gr : (c + 1) * gr] = grads[a] * grads[b]
    for z in range(count):
        for half in range(2):
            part = prod[z, half * 3 * gr : (half + 1) * 3 * gr]
            out = jnp.dot(ysm, part, preferred_element_type=F32)
            sm[z, half * half_rows : (half + 1) * half_rows] = out.astype(BF16)
    out = jnp.dot(
        sm[...].reshape(count * n_rows, cols), get("xsm"), preferred_element_type=F32
    )
    u_ref[...] = out.reshape(count, n_rows, cols // 4)


def block_loader(vol, yud, rows):
    def layer(z, at, lanes):
        if at < HALO:
            return yud[z, at : at + 16, lanes].astype(F32)
        if at < HALO + rows:
            return vol[z, at - HALO : at - HALO + 16, lanes].astype(F32)
        return yud[z, at - rows : at - rows + 16, lanes].astype(F32)

    return layer


def spread_rows(first):
    shape = (16 * NEED, 16 * HALO)
    packed = lax.broadcasted_iota(jnp.int32, shape, 0)
    full = lax.broadcasted_iota(jnp.int32, shape, 1)
    z = lax.shift_right_logical(packed * 373, 12)
    return jnp.where(full == packed + z * (HALO - NEED) + first, 1.0, 0.0).astype(BF16)


def load_kernel(vol, s1, s2):
    depth, rows, cols = vol.shape
    odd = lax.rem(lax.axis_index("row"), 2) == 1
    top = vol[:, 0:HALO, :].reshape(depth * HALO, cols)
    bottom = vol[:, rows - HALO : rows, :].reshape(depth * HALO, cols)
    to_before = jnp.dot(spread_rows(0), top, preferred_element_type=F32).astype(BF16)
    to_after = jnp.dot(
        spread_rows(HALO - NEED), bottom, preferred_element_type=F32
    ).astype(BF16)
    s1[...] = jnp.where(odd, to_before, to_after)
    s2[...] = jnp.where(odd, to_after, to_before)


def column_select(n_col, cols):
    n_side = 1 if n_col == 2 else 2
    shape = (SLOTS + 16 * n_side, cols)
    row = lax.broadcasted_iota(jnp.int32, shape, 0)
    lane = lax.broadcasted_iota(jnp.int32, shape, 1)
    picked = ((row >= 8) & (row < 14) & (lane == row - 8)) | (
        (row >= 14) & (row < 20) & (lane == row - 20 + cols)
    )
    for side in range(n_side):
        if n_col == 2:
            first = jnp.where(lax.axis_index("col") == 0, cols - HALO, 0)
        else:
            first = (cols - HALO, 0)[side]
        at = row - SLOTS - 16 * side
        picked = picked | ((at >= 0) & (at < 16) & (lane == at + first))
    return jnp.where(picked, 1.0, 0.0).astype(BF16)


def pick_columns(select, source):
    picked = lax.dot_general(select, source, NT, preferred_element_type=F32)
    messages = [picked[at : at + 16].astype(BF16) for at in range(SLOTS, picked.shape[0], 16)]
    return picked[0:SLOTS].astype(BF16), picked[8:24].astype(BF16), messages


def halve(chunk, at, value):
    n = value.shape[0]
    chunk[at : at + n] = value[:, 0:128]
    chunk[at + n : at + 2 * n] = value[:, 128:256]


def joined_halves(chunk, at, n):
    return jnp.concatenate([chunk[at : at + n], chunk[at + n : at + 2 * n]], axis=1)


def edges_kernel(n_col, vol, own, zmsg, *refs):
    depth, rows, cols = vol.shape
    gz = lax.axis_index("gz")
    select = column_select(n_col, cols)
    for b in range(depth // 2):
        source = vol[2 * b : 2 * b + 2].reshape(2 * rows, cols)
        slots, middle, messages = pick_columns(select, source)
        own[b] = slots
        for ref, message in zip(refs, [middle] + messages):
            ref[b] = message
    base = jnp.where(gz == 0, depth - R, 0)
    halve(zmsg, 0, vol[pl.ds(base, R)].reshape(R * rows, cols))
    first = jnp.where(gz == 0, (depth - EXTRA) // 2, 0)
    n = EXTRA // 2
    zmsg[2 * R * rows :] = refs[0][pl.ds(first, n)].reshape(n * 16, 128)


def pack_kernel(place_of, n_col, r1, r2, w, *refs):
    n_side = 1 if n_col == 2 else 2
    xown, (yud, halo, zcorner) = refs[:n_side], refs[n_side : n_side + 3]
    xmsgs, zxmsgs = refs[n_side + 3 : 2 * n_side + 3], refs[2 * n_side + 3 : 3 * n_side + 3]
    middles = refs[3 * n_side + 3]
    depth, cols = yud.shape[0], yud.shape[2]
    gz = lax.axis_index("gz")
    odd = lax.rem(lax.axis_index("row"), 2) == 1
    get = getter(place_of, w)
    got1, got2 = r1[...], r2[...]
    for at, name, part in (
        (0, "above", jnp.where(odd, got1, got2)),
        (HALO, "below", jnp.where(odd, got2, got1)),
    ):
        out = jnp.dot(get(name), part, preferred_element_type=F32).astype(BF16)
        yud[:, at : at + HALO, :] = out.reshape(depth, HALO, cols)
    select = column_select(n_col, cols)
    pairs, quads = depth // 2, depth // 4
    for b in range(quads):
        source = yud[4 * b : 4 * b + 4].reshape(4 * 2 * HALO, cols)
        slots, middle, messages = pick_columns(select, source)
        halo[b] = slots
        middles[b] = middle
        for ref, message in zip(xmsgs, messages):
            ref[pairs + b] = message
    for ref, part in zip(xmsgs, xown):
        ref[0:pairs] = part[...]
    base = jnp.where(gz == 0, depth - R, 0)
    edge = yud[pl.ds(base, R)].reshape(R * 2 * HALO, cols)
    halve(zcorner, 0, jnp.dot(get("corner"), edge, preferred_element_type=F32).astype(BF16))
    n2, n4 = EXTRA // 2, EXTRA // 4
    first2 = jnp.where(gz == 0, pairs - n2, 0)
    first4 = jnp.where(gz == 0, quads - n4, 0)
    zcorner[128:] = middles[pl.ds(first4, n4)].reshape(n4 * 16, 128)
    for ref, message in zip(zxmsgs, xmsgs):
        ref[0:n2] = message[pl.ds(first2, n2)]
        ref[n2:] = message[pl.ds(pairs + first4, n4)]


FIRST = 5
EDGE = R
LAST = 8


def first_kernel(place_of, n_row, vol, yud, w, u_ref, *scratch):
    depth, rows, cols = vol.shape
    get = getter(place_of, w)
    ysm = row_mask(get, n_row, rows, rows + 16, rows // 4)
    base = jnp.where(lax.axis_index("gz") == 0, depth - EDGE - FIRST - R, 0)
    layer = block_loader(vol, yud, rows)
    load = lambda at, lanes: [layer(base + k, at, lanes) for k in range(FIRST + 2 * R)]
    layers_to_sums(get, ysm, load, FIRST, (rows, cols), u_ref, *scratch)


def near_kernel(place_of, zs, n_row, vol, yud, zown, zcorner, u1, w, u_ref, send_ref, zext, *scratch):
    depth, rows, cols = vol.shape
    n_zq = zs.shape[1]
    get = getter(place_of, w)
    low = lax.axis_index("gz") == 0
    ysm = row_mask(get, n_row, rows, rows + 16, rows // 4)
    corner = jnp.dot(
        get("corner_back"), joined_halves(zcorner, 0, 64), preferred_element_type=F32
    ).astype(BF16).reshape(R, 2 * HALO, cols)
    zext[:, 0:HALO] = corner[:, 0:HALO]
    zext[:, HALO : HALO + rows] = joined_halves(zown, 0, R * rows).reshape(R, rows, cols)
    zext[:, HALO + rows :] = corner[:, HALO:]
    layer = block_loader(vol, yud, rows)
    start = jnp.where(low, depth - R, 0)
    outer = jnp.where(low, depth - 2 * R, R)

    def load(at, lanes):
        beyond = [zext[k, at : at + 16, lanes].astype(F32) for k in range(R)]
        inner = [layer(outer + k, at, lanes) for k in range(R)]
        middle = [layer(start + k, at, lanes) for k in range(R)]
        before = [jnp.where(low, inner[k], beyond[k]) for k in range(R)]
        after = [jnp.where(low, beyond[k], inner[k]) for k in range(R)]
        return before + middle + after

    layers_to_sums(get, ysm, load, EDGE, (rows, cols), u_ref, *scratch)
    sends = []
    for k in range(2):
        total = None
        for i in range(FIRST + EDGE):
            from_low = depth - EDGE - FIRST + i
            from_high = EDGE + i if i < FIRST else i - FIRST
            a = float(zs[from_low, n_zq - 2 + k])
            b = float(zs[from_high, k])
            if a == 0.0 and b == 0.0:
                continue
            term = (u1[i] if i < FIRST else u_ref[i - FIRST]) * jnp.where(low, a, b)
            total = term if total is None else total + term
        sends.append(total)
    send_ref[...] = jnp.concatenate(sends, axis=1).astype(BF16)


def last_layers(place_of, get, ysm, vol, yud, u_ref, *scratch):
    depth, rows, cols = vol.shape
    low = lax.axis_index("gz") == 0
    layer = block_loader(vol, yud, rows)
    base = jnp.where(low, -R, depth - LAST - R)
    before_on = jnp.where(low, 0.0, 1.0)
    after_on = jnp.where(low, 1.0, 0.0)

    def load(at, lanes):
        out = []
        for k in range(LAST + 2 * R):
            block = layer(jnp.clip(base + k, 0, depth - 1), at, lanes)
            if k < R:
                block = block * before_on
            elif k >= LAST + R:
                block = block * after_on
            out.append(block)
        return out

    layers_to_sums(get, ysm, load, LAST, (rows, cols), u_ref, *scratch)


def last_kernel(place_of, zs, n_row, n_col, vol, yud, own, halo, zown, zcorner, u1, u2, w,
                xs, zxs, own_ref, hs, hd, pstrip, u3, *scratch):
    depth, rows, cols = vol.shape
    gr = rows + 16
    quarter_rows, quarter = rows // 4, cols // 4
    get = getter(place_of, w)
    gz, col = lax.axis_index("gz"), lax.axis_index("col")
    low = gz == 0
    ysm = row_mask(get, n_row, rows, gr, quarter_rows)
    last_layers(place_of, get, ysm, vol, yud, u3, *scratch)
    slots = lax.broadcasted_iota(jnp.int32, (SLOTS, 128), 0)
    if n_col == 2:
        keep = ((slots < 8) & (col == 0)) | ((slots >= 21) & (col == 1))
    else:
        keep = (slots < 8) | (slots >= 21)

    def join(part, messages, b):
        sides = [messages[-1][b].astype(F32), messages[0][b].astype(F32)]
        return jnp.where(keep, jnp.concatenate(sides, axis=0), part)

    def from_middle(ref, at, b):
        rim = jnp.zeros((8, 128), F32)
        middle = ref[at + 16 * b : at + 16 * (b + 1)].astype(F32)
        return jnp.concatenate([rim, middle, rim], axis=0)

    lanes = lax.broadcasted_iota(jnp.int32, (SLOTS, 128), 1)

    def layers_of(pairs, quads):
        out = []
        for z in range(2 * len(pairs)):
            left, right = pairs[z // 2], quads[z // 4]
            if z % 2:
                left = pltpu.roll(left, 64, 1)
            turn = (rows - 32 * (z % 4)) % 128
            if turn:
                right = pltpu.roll(right, turn, 1)
            out.append(jnp.where(lanes < rows, left, right))
        return out

    n2, n4 = EXTRA // 2, EXTRA // 4
    own_layers = layers_of(
        [join(own[b].astype(F32), xs, b) for b in range(depth // 2)],
        [join(halo[b].astype(F32), xs, depth // 2 + b) for b in range(depth // 4)],
    )
    at = 2 * R * rows
    beyond = layers_of(
        [join(from_middle(zown, at, b), zxs, b) for b in range(n2)],
        [join(from_middle(zcorner, 128, b), zxs, n2 + b) for b in range(n4)],
    )
    count = depth + 8
    zero = [jnp.zeros((SLOTS, 128), F32)] * R
    at_low = zero + own_layers + beyond[0:11]
    at_high = beyond[1:12] + own_layers + zero
    layers = [jnp.where(low, a, b) for a, b in zip(at_low, at_high)]
    for z, smooth, slope in z_filter(layers, count):
        hs[SLOTS * z : SLOTS * (z + 1)] = smooth
        hd[SLOTS * z : SLOTS * (z + 1)] = slope
    p01 = lax.dot_general(
        get("wy_strip", 128), hs[...], NT, preferred_element_type=F32
    ).astype(BF16)
    p2 = lax.dot_general(
        get("wy_strip_slope", 128), hd[...], NT, preferred_element_type=F32
    ).astype(BF16)
    n = count // 8
    groups = [slice(256 * c, 256 * (c + 1)) for c in range(n)]
    stacks = [
        jnp.concatenate([p[:, g] for g in groups], axis=0) for p in (p01[0:gr], p01[gr:], p2)
    ]
    grads = [
        jnp.dot(stack, get(name), preferred_element_type=F32).astype(BF16).reshape(n, gr, 256)
        for stack, name in zip(stacks, ("bdd", "bds", "bds"))
    ]
    for c, (a, b) in enumerate(pair_table):
        pstrip[:, c * gr : (c + 1) * gr] = grads[a] * grads[b]
    slot = lax.rem(lax.broadcasted_iota(jnp.int32, (3 * quarter_rows, 256), 1), SLOTS)
    outside_x = ((col == 0) & (slot < 8)) | ((col == n_col - 1) & (slot >= 14))
    smoothed = []
    for c in range(n):
        for half in range(2):
            part = pstrip[c, half * 3 * gr : (half + 1) * 3 * gr]
            out = jnp.dot(ysm, part, preferred_element_type=F32)
            smoothed.append(jnp.where(outside_x, 0.0, out).astype(BF16))
    u = jnp.dot(jnp.concatenate(smoothed, axis=0), get("bdx"), preferred_element_type=F32)
    n_rows = 6 * quarter_rows
    u = u.astype(BF16)
    sums = []
    for name in ("0", "1"):
        at = jnp.where(low, place_of["g_low" + name][0], place_of["g_high" + name][0])
        total = None
        for c in range(n):
            g = w[pl.ds(pl.multiple_of(at + 64 * c, 16), 64), :]
            term = jnp.dot(u[n_rows * c : n_rows * (c + 1)], g, preferred_element_type=F32)
            total = term if total is None else total + term
        sums += [total[:, 0:quarter], total[:, 128 : 128 + quarter]]
    for q in range(depth // 4):
        total = sums[q]
        for i in range(depth):
            if i < FIRST:
                u, from_low, from_high = u1[i], depth - EDGE - FIRST + i, EDGE + i
            elif i < FIRST + EDGE:
                k = i - FIRST
                u, from_low, from_high = u2[k], depth - EDGE + k, k
            else:
                k = i - FIRST - EDGE
                u, from_low, from_high = u3[k], k, depth - LAST + k
            a, b = float(zs[from_low, q + 2]), float(zs[from_high, q + 2])
            if a == 0.0 and b == 0.0:
                continue
            total = total + u * jnp.where(low, a, b)
        own_ref[:, q] = total.reshape(6, quarter_rows, quarter)


def add_kernel(own, got, out):
    n_q, quarter = own.shape[1], own.shape[3]
    low = lax.axis_index("gz") == 0
    parts = [
        got[:, k * quarter : (k + 1) * quarter].astype(F32).reshape(own.shape[0], -1, quarter)
        for k in range(2)
    ]
    for q in range(n_q):
        total = own[:, q]
        if q < 2:
            total = total + parts[q] * jnp.where(low, 0.0, 1.0)
        if q >= n_q - 2:
            total = total + parts[q - n_q + 2] * jnp.where(low, 1.0, 0.0)
        out[:, q] = total


def call(body, outs, operands, scratch, name, flops=0):
    vmem = pl.BlockSpec(memory_space=pltpu.VMEM)
    moved = sum(o.size * o.dtype.itemsize for o in list(outs) + list(operands))
    return pl.pallas_call(
        body,
        out_shape=list(outs),
        in_specs=[vmem] * len(operands),
        out_specs=[vmem] * len(outs),
        scratch_shapes=scratch,
        compiler_params=pltpu.CompilerParams(vmem_limit_bytes=24 * 2**20),
        cost_estimate=pl.CostEstimate(flops=flops, bytes_accessed=moved, transcendentals=0),
        name=name,
    )(*operands)


def per_device(volume):
    depth, rows, cols = volume.shape
    n_row, n_col = lax.axis_size("row"), lax.axis_size("col")
    table, place_of, zs = weight_table(depth, rows, cols)
    ext = rows + 2 * HALO
    gr = rows + 16
    quarter_rows, quarter = rows // 4, cols // 4
    n_rows = 6 * quarter_rows
    n_side = 1 if n_col == 2 else 2
    pairs, quads = depth // 2, depth // 4
    n2, n4 = EXTRA // 2, EXTRA // 4
    sds = jax.ShapeDtypeStruct
    bf16 = lambda *shape: sds(shape, BF16)

    def scratch_for(count):
        return [
            pltpu.VMEM((count, 2 * ext, cols), BF16),
            pltpu.VMEM((3, count, gr, cols), BF16),
            pltpu.VMEM((count, 6 * gr, cols), BF16),
            pltpu.VMEM((count, n_rows, cols), BF16),
        ]

    layer_flops = 2 * cols * (3 * gr * 2 * ext + 3 * gr * cols + n_rows * 3 * gr + n_rows * quarter)

    s1, s2 = call(load_kernel, [bf16(depth * NEED, cols)] * 2, [volume], [], "load")
    inner = [(i, i + 1) for i in range(1, n_row - 1, 2)]
    inner = inner + [(j, i) for i, j in inner]
    r2 = lax.ppermute(s2, "row", inner)
    r1 = lax.ppermute(s1, "row", [(i, i ^ 1) for i in range(n_row)])
    vol, w = volume, jnp.asarray(table)
    own, zmsg, _, *xown = call(
        lambda *refs: edges_kernel(n_col, *refs),
        [bf16(pairs, SLOTS, 128), bf16(2 * R * rows + n2 * 16, 128)]
        + [bf16(pairs, HALO, 128)] * (n_side + 1),
        [volume], [], "edges",
    )
    swap = [(0, 1), (1, 0)]
    zown = lax.ppermute(zmsg, "gz", swap)

    yud, halo, zcmsg, *messages = call(
        lambda *refs: pack_kernel(place_of, n_col, *refs),
        [bf16(depth, 2 * HALO, cols), bf16(quads, SLOTS, 128), bf16(128 + n4 * 16, 128)]
        + [bf16(pairs + quads, HALO, 128)] * n_side
        + [bf16(n2 + n4, HALO, 128)] * n_side,
        [r1, r2, w] + xown, [pltpu.VMEM((quads, 16, 128), BF16)], "pack",
    )
    zcorner = lax.ppermute(zcmsg, "gz", swap)
    xs, zxs = [], []
    for side in range(n_side):
        step = 1 - 2 * side
        line = swap if n_col == 2 else [
            (i, i + step) for i in range(n_col) if 0 <= i + step < n_col
        ]
        both = [(z * n_col + i, (1 - z) * n_col + j) for z in range(2) for i, j in line]
        xs.append(lax.ppermute(messages[side], "col", line))
        zxs.append(lax.ppermute(messages[n_side + side], ("gz", "col"), both))

    (u1,) = call(
        lambda *refs: first_kernel(place_of, n_row, *refs),
        [sds((FIRST, n_rows, quarter), F32)],
        [vol, yud, w], scratch_for(FIRST), "first", flops=FIRST * layer_flops,
    )
    u2, send = call(
        lambda *refs: near_kernel(place_of, zs, n_row, *refs),
        [sds((EDGE, n_rows, quarter), F32), bf16(n_rows, 2 * quarter)],
        [vol, yud, zown, zcorner, u1, w],
        [pltpu.VMEM((R, ext, cols), BF16)] + scratch_for(EDGE),
        "near", flops=EDGE * layer_flops,
    )
    sums = lax.ppermute(send, "gz", swap)

    def last_body(*refs):
        head, x_refs, zx_refs = refs[0:9], refs[9 : 9 + n_side], refs[9 + n_side : 9 + 2 * n_side]
        last_kernel(
            place_of, zs, n_row, n_col, *head, x_refs, zx_refs, *refs[9 + 2 * n_side :]
        )

    count = depth + 8
    (result,) = call(
        last_body,
        [sds((6, depth // 4, quarter_rows, quarter), F32)],
        [vol, yud, own, halo, zown, zcorner, u1, u2, w] + xs + zxs,
        [
            pltpu.VMEM((count * SLOTS, 128), BF16),
            pltpu.VMEM((count * SLOTS, 128), BF16),
            pltpu.VMEM((count // 8, 6 * gr, 256), BF16),
            pltpu.VMEM((LAST, n_rows, quarter), F32),
        ]
        + scratch_for(LAST),
        "last", flops=(LAST + 3) * layer_flops,
    )
    (out,) = call(add_kernel, [sds(result.shape, F32)], [result, sums], [], "add")
    return out


def solution(mesh):
    return jax.shard_map(
        per_device,
        mesh=mesh,
        in_specs=(P("gz", "row", "col"),),
        out_specs=P(None, "gz", "row", "col"),
        check_vma=False,
    )
```

```python
import jax
import jax.numpy as jnp
import ml_dtypes
import numpy as np
from jax import lax
from jax.experimental import pallas as pl
from jax.experimental.pallas import tpu as pltpu
from jax.sharding import PartitionSpec as P

R = 3
R2 = 8
HALO = 16
NEED = R + R2
EXTRA = 12
SLOTS = 32
NT = (((1,), (1,)), ((), ()))
F32 = jnp.float32
BF16 = jnp.bfloat16

pair_table = ((0, 0), (1, 1), (2, 2), (0, 1), (0, 2), (1, 2))


def gauss_taps(radius):
    offsets = np.arange(-radius, radius + 1).astype(np.float32)
    spread = np.float32(radius / 3.0)
    smooth = np.exp(-offsets * offsets / (np.float32(2.0) * spread * spread))
    smooth = smooth / np.sum(smooth)
    slopes = offsets * smooth
    slopes = slopes / np.sum(offsets * slopes)
    as_f32 = lambda t: t.astype(ml_dtypes.bfloat16).astype(np.float32)
    return as_f32(smooth), as_f32(slopes)


SMOOTH_D, SLOPE_D = gauss_taps(R)
SMOOTH_I, _ = gauss_taps(R2)


def band(taps, sources, targets):
    radius = len(taps) // 2
    gap = np.asarray(sources)[:, None] - np.asarray(targets)[None, :]
    return np.where(np.abs(gap) <= radius, taps[np.clip(gap + radius, 0, 2 * radius)], 0.0)


def weight_table(depth, rows, cols):
    ext = rows + 2 * HALO
    grad_rows = rows + 16
    far = 10**6
    y_in = np.arange(ext) - HALO
    y_out = np.arange(grad_rows) - R2
    smooth_y = band(SMOOTH_D, y_in, y_out).T
    slope_y = band(SLOPE_D, y_in, y_out).T
    zero = np.zeros_like(smooth_y)
    wy = np.block([[smooth_y, zero], [slope_y, zero], [zero, smooth_y]])
    order = np.concatenate([np.arange(rows), np.arange(HALO) - HALO, rows + np.arange(HALO)]) + HALO
    x_all = np.arange(cols)
    slot_in = np.full(SLOTS, far)
    slot_in[0:8] = cols + np.arange(8)
    slot_in[8:14] = np.arange(6)
    slot_in[14:20] = cols - 6 + np.arange(6)
    slot_in[21:32] = np.arange(-11, 0)
    slot_out = np.full(SLOTS, -far)
    slot_out[0:11] = np.arange(-8, 3)
    slot_out[11:19] = cols - 3 + np.arange(8)
    eye8 = np.eye(8)
    inner = np.where((x_all >= R) & (x_all < cols - R), x_all, far)
    quarter = cols // 4
    coarse_edge = np.full(8, 3 * far)
    coarse_edge[0:5] = [0, 1, 2, quarter - 2, quarter - 1]
    xs_edge = band(SMOOTH_I, slot_out, 4 * coarse_edge)
    ys = band(SMOOTH_I, y_out, 4 * np.arange(rows // 4)).T
    zs = band(SMOOTH_I, np.arange(depth), 4 * (np.arange(depth // 4 + 4) - 2))
    place = np.zeros((8, 128))
    for j in range(5):
        place[j, coarse_edge[j]] = 1.0
    own_z = 4 * np.arange(depth // 4)
    g = [
        np.einsum("zq,jx->zjqx", band(SMOOTH_I, np.arange(depth + 8) + first, own_z), place)
        for first in (0, -8)
    ]
    g = [t.reshape((depth + 8) * 8, len(own_z) * 128) for t in g]
    packed = np.arange(depth * NEED)
    above = np.zeros((depth * HALO, depth * NEED))
    above[packed + packed // NEED * (HALO - NEED) + HALO - NEED, packed] = 1.0
    below = np.zeros((depth * HALO, depth * NEED))
    below[packed + packed // NEED * (HALO - NEED), packed] = 1.0
    used = 2 * R + 13
    packed = np.arange(R * used)
    corner = np.zeros((64, R * 2 * HALO))
    corner[packed, packed + packed // used * (2 * HALO - used) + HALO - NEED] = 1.0
    parts = {
        "above": above,
        "below": below,
        "corner": corner,
        "corner_back": corner.T,
        "wy": wy,
        "wy_strip": np.concatenate([smooth_y, slope_y])[:, order],
        "wy_strip_slope": smooth_y[:, order],
        "wxd": band(SLOPE_D, x_all, x_all),
        "wxs": band(SMOOTH_D, x_all, x_all),
        "bdd": np.kron(eye8, band(SLOPE_D, slot_in, slot_out)),
        "bds": np.kron(eye8, band(SMOOTH_D, slot_in, slot_out)),
        "ysm": np.kron(np.eye(3), ys),
        "xsm": band(SMOOTH_I, inner, 4 * np.arange(quarter)),
        "bdx": np.kron(eye8, xs_edge),
        "g_low0": g[0][:, 0:256],
        "g_low1": g[0][:, 256:512],
        "g_high0": g[1][:, 0:256],
        "g_high1": g[1][:, 256:512],
    }
    place_of, blocks, at = {}, [], 0
    for name, part in parts.items():
        height = -(-part.shape[0] // 16) * 16
        block = np.zeros((height, 256), np.float32)
        block[: part.shape[0], : part.shape[1]] = part
        place_of[name] = (at, part.shape[0], part.shape[1])
        blocks.append(block)
        at += height
    return np.concatenate(blocks).astype(ml_dtypes.bfloat16), place_of, zs


def z_filter(v, count):
    for z in range(count):
        w = v[z : z + 7]
        smooth = w[3] * float(SMOOTH_D[3])
        slope = None
        for s in (1, 2, 3):
            smooth = smooth + (w[3 + s] + w[3 - s]) * float(SMOOTH_D[3 + s])
            term = (w[3 + s] - w[3 - s]) * float(SLOPE_D[3 + s])
            slope = term if slope is None else slope + term
        yield z, smooth.astype(BF16), slope.astype(BF16)


def getter(place_of, w):
    def get(name, width=None):
        at, height, own_width = place_of[name]
        return w[at : at + height, 0 : (width or own_width)]

    return get


def row_mask(get, n_row, rows, gr, quarter_rows):
    row = lax.axis_index("row")
    lane = lax.broadcasted_iota(jnp.int32, (3 * quarter_rows, 3 * gr), 1)
    y_out = lax.rem(lane, gr) - R2
    outside = ((row == 0) & (y_out < 0)) | ((row == n_row - 1) & (y_out >= rows))
    return jnp.where(outside, 0.0, get("ysm").astype(F32)).astype(BF16)


def layers_to_sums(get, ysm, load, count, shape, u_ref, zf, planes, prod, sm):
    rows, cols = shape
    ext = rows + 2 * HALO
    gr = rows + 16
    n_rows = 6 * (rows // 4)
    half_rows = n_rows // 2
    for tile in range(cols // 128):
        lanes = slice(tile * 128, tile * 128 + 128)
        for at in range(0, ext, 16):
            for z, smooth, slope in z_filter(load(at, lanes), count):
                zf[z, at : at + 16, lanes] = smooth
                zf[z, ext + at : ext + at + 16, lanes] = slope
    wy = get("wy")
    for z in range(count):
        out = jnp.dot(wy, zf[z], preferred_element_type=F32).astype(BF16)
        planes[0, z] = out[0:gr]
        planes[1, z] = out[gr : 2 * gr]
        planes[2, z] = out[2 * gr :]
    group = 4 if count % 4 == 0 else count
    for at in range(0, count, group):
        grads = []
        for f, name in enumerate(("wxd", "wxs", "wxs")):
            part = planes[f, at : at + group].reshape(group * gr, cols)
            out = jnp.dot(part, get(name), preferred_element_type=F32)
            grads.append(out.astype(BF16).reshape(group, gr, cols))
        for c, (a, b) in enumerate(pair_table):
            prod[at : at + group, c * gr : (c + 1) * gr] = grads[a] * grads[b]
    for z in range(count):
        for half in range(2):
            part = prod[z, half * 3 * gr : (half + 1) * 3 * gr]
            out = jnp.dot(ysm, part, preferred_element_type=F32)
            sm[z, half * half_rows : (half + 1) * half_rows] = out.astype(BF16)
    out = jnp.dot(
        sm[...].reshape(count * n_rows, cols), get("xsm"), preferred_element_type=F32
    )
    u_ref[...] = out.reshape(count, n_rows, cols // 4)


def block_loader(vol, yud, rows):
    def layer(z, at, lanes):
        if at < HALO:
            return yud[z, at : at + 16, lanes].astype(F32)
        if at < HALO + rows:
            return vol[z, at - HALO : at - HALO + 16, lanes].astype(F32)
        return yud[z, at - rows : at - rows + 16, lanes].astype(F32)

    return layer


def spread_rows(first):
    shape = (16 * NEED, 16 * HALO)
    packed = lax.broadcasted_iota(jnp.int32, shape, 0)
    full = lax.broadcasted_iota(jnp.int32, shape, 1)
    z = lax.shift_right_logical(packed * 373, 12)
    return jnp.where(full == packed + z * (HALO - NEED) + first, 1.0, 0.0).astype(BF16)


def load_kernel(vol, s1, s2, vol_out, top, bottom, sems):
    depth, rows, cols = vol.shape
    odd = lax.rem(lax.axis_index("row"), 2) == 1
    copies = [
        pltpu.make_async_copy(vol.at[:, 0:HALO, :], top, sems.at[0]),
        pltpu.make_async_copy(vol.at[:, rows - HALO : rows, :], bottom, sems.at[1]),
        pltpu.make_async_copy(vol, vol_out, sems.at[2]),
    ]
    for copy in copies:
        copy.start()
    first_rows, last_rows = spread_rows(0), spread_rows(HALO - NEED)
    copies[0].wait()
    copies[1].wait()
    to_before = jnp.dot(
        first_rows, top[...].reshape(depth * HALO, cols), preferred_element_type=F32
    ).astype(BF16)
    to_after = jnp.dot(
        last_rows, bottom[...].reshape(depth * HALO, cols), preferred_element_type=F32
    ).astype(BF16)
    s1[...] = jnp.where(odd, to_before, to_after)
    s2[...] = jnp.where(odd, to_after, to_before)
    copies[2].wait()


def column_select(n_col, cols):
    n_side = 1 if n_col == 2 else 2
    shape = (SLOTS + 16 * n_side, cols)
    row = lax.broadcasted_iota(jnp.int32, shape, 0)
    lane = lax.broadcasted_iota(jnp.int32, shape, 1)
    picked = ((row >= 8) & (row < 14) & (lane == row - 8)) | (
        (row >= 14) & (row < 20) & (lane == row - 20 + cols)
    )
    for side in range(n_side):
        if n_col == 2:
            first = jnp.where(lax.axis_index("col") == 0, cols - HALO, 0)
        else:
            first = (cols - HALO, 0)[side]
        at = row - SLOTS - 16 * side
        picked = picked | ((at >= 0) & (at < 16) & (lane == at + first))
    return jnp.where(picked, 1.0, 0.0).astype(BF16)


def pick_columns(select, source):
    picked = lax.dot_general(select, source, NT, preferred_element_type=F32)
    messages = [picked[at : at + 16].astype(BF16) for at in range(SLOTS, picked.shape[0], 16)]
    return picked[0:SLOTS].astype(BF16), picked[8:24].astype(BF16), messages


def halve(chunk, at, value):
    n = value.shape[0]
    chunk[at : at + n] = value[:, 0:128]
    chunk[at + n : at + 2 * n] = value[:, 128:256]


def joined_halves(chunk, at, n):
    return jnp.concatenate([chunk[at : at + n], chunk[at + n : at + 2 * n]], axis=1)


def edges_kernel(n_col, vol, own, zmsg, *refs):
    depth, rows, cols = vol.shape
    gz = lax.axis_index("gz")
    refs, middles = refs[:-1], refs[-1]
    select = column_select(n_col, cols)
    for b in range(depth // 2):
        source = vol[2 * b : 2 * b + 2].reshape(2 * rows, cols)
        slots, middle, messages = pick_columns(select, source)
        own[b], middles[b] = slots, middle
        for ref, message in zip(refs, messages):
            ref[b] = message
    base = jnp.where(gz == 0, depth - R, 0)
    halve(zmsg, 0, vol[pl.ds(base, R)].reshape(R * rows, cols))
    first = jnp.where(gz == 0, (depth - EXTRA) // 2, 0)
    n = EXTRA // 2
    zmsg[2 * R * rows :] = middles[pl.ds(first, n)].reshape(n * 16, 128)


def pack_kernel(place_of, n_col, r1, r2, w, *refs):
    n_side = 1 if n_col == 2 else 2
    xown, (yud, halo, zcorner) = refs[:n_side], refs[n_side : n_side + 3]
    xmsgs, zxmsgs = refs[n_side + 3 : 2 * n_side + 3], refs[2 * n_side + 3 : 3 * n_side + 3]
    middles = refs[3 * n_side + 3]
    depth, cols = yud.shape[0], yud.shape[2]
    gz = lax.axis_index("gz")
    odd = lax.rem(lax.axis_index("row"), 2) == 1
    get = getter(place_of, w)
    got1, got2 = r1[...], r2[...]
    for at, name, part in (
        (0, "above", jnp.where(odd, got1, got2)),
        (HALO, "below", jnp.where(odd, got2, got1)),
    ):
        out = jnp.dot(get(name), part, preferred_element_type=F32).astype(BF16)
        yud[:, at : at + HALO, :] = out.reshape(depth, HALO, cols)
    select = column_select(n_col, cols)
    pairs, quads = depth // 2, depth // 4
    for b in range(quads):
        source = yud[4 * b : 4 * b + 4].reshape(4 * 2 * HALO, cols)
        slots, middle, messages = pick_columns(select, source)
        halo[b] = slots
        middles[b] = middle
        for ref, message in zip(xmsgs, messages):
            ref[pairs + b] = message
    for ref, part in zip(xmsgs, xown):
        ref[0:pairs] = part[...]
    base = jnp.where(gz == 0, depth - R, 0)
    edge = yud[pl.ds(base, R)].reshape(R * 2 * HALO, cols)
    halve(zcorner, 0, jnp.dot(get("corner"), edge, preferred_element_type=F32).astype(BF16))
    n2, n4 = EXTRA // 2, EXTRA // 4
    first2 = jnp.where(gz == 0, pairs - n2, 0)
    first4 = jnp.where(gz == 0, quads - n4, 0)
    zcorner[128:] = middles[pl.ds(first4, n4)].reshape(n4 * 16, 128)
    for ref, message in zip(zxmsgs, xmsgs):
        ref[0:n2] = message[pl.ds(first2, n2)]
        ref[n2:] = message[pl.ds(pairs + first4, n4)]


def stage_kernel(w, w_out):
    pass


FIRST = 5
EDGE = R
LAST = 8


def first_kernel(place_of, n_row, vol, yud, w, u_ref, *scratch):
    depth, rows, cols = vol.shape
    get = getter(place_of, w)
    ysm = row_mask(get, n_row, rows, rows + 16, rows // 4)
    base = jnp.where(lax.axis_index("gz") == 0, depth - EDGE - FIRST - R, 0)
    layer = block_loader(vol, yud, rows)
    load = lambda at, lanes: [layer(base + k, at, lanes) for k in range(FIRST + 2 * R)]
    layers_to_sums(get, ysm, load, FIRST, (rows, cols), u_ref, *scratch)


def near_kernel(place_of, zs, n_row, vol, yud, zown, zcorner, u1, w, u_ref, send_ref, zext, *scratch):
    depth, rows, cols = vol.shape
    n_zq = zs.shape[1]
    get = getter(place_of, w)
    low = lax.axis_index("gz") == 0
    ysm = row_mask(get, n_row, rows, rows + 16, rows // 4)
    corner = jnp.dot(
        get("corner_back"), joined_halves(zcorner, 0, 64), preferred_element_type=F32
    ).astype(BF16).reshape(R, 2 * HALO, cols)
    zext[:, 0:HALO] = corner[:, 0:HALO]
    zext[:, HALO : HALO + rows] = joined_halves(zown, 0, R * rows).reshape(R, rows, cols)
    zext[:, HALO + rows :] = corner[:, HALO:]
    layer = block_loader(vol, yud, rows)
    start = jnp.where(low, depth - R, 0)
    outer = jnp.where(low, depth - 2 * R, R)

    def load(at, lanes):
        beyond = [zext[k, at : at + 16, lanes].astype(F32) for k in range(R)]
        inner = [layer(outer + k, at, lanes) for k in range(R)]
        middle = [layer(start + k, at, lanes) for k in range(R)]
        before = [jnp.where(low, inner[k], beyond[k]) for k in range(R)]
        after = [jnp.where(low, beyond[k], inner[k]) for k in range(R)]
        return before + middle + after

    layers_to_sums(get, ysm, load, EDGE, (rows, cols), u_ref, *scratch)
    sends = []
    for k in range(2):
        total = None
        for i in range(FIRST + EDGE):
            from_low = depth - EDGE - FIRST + i
            from_high = EDGE + i if i < FIRST else i - FIRST
            a = float(zs[from_low, n_zq - 2 + k])
            b = float(zs[from_high, k])
            if a == 0.0 and b == 0.0:
                continue
            term = (u1[i] if i < FIRST else u_ref[i - FIRST]) * jnp.where(low, a, b)
            total = term if total is None else total + term
        sends.append(total)
    send_ref[...] = jnp.concatenate(sends, axis=1).astype(BF16)


def last_layers(place_of, get, ysm, vol, yud, u_ref, *scratch):
    depth, rows, cols = vol.shape
    low = lax.axis_index("gz") == 0
    layer = block_loader(vol, yud, rows)
    base = jnp.where(low, -R, depth - LAST - R)
    before_on = jnp.where(low, 0.0, 1.0)
    after_on = jnp.where(low, 1.0, 0.0)

    def load(at, lanes):
        out = []
        for k in range(LAST + 2 * R):
            block = layer(jnp.clip(base + k, 0, depth - 1), at, lanes)
            if k < R:
                block = block * before_on
            elif k >= LAST + R:
                block = block * after_on
            out.append(block)
        return out

    layers_to_sums(get, ysm, load, LAST, (rows, cols), u_ref, *scratch)


def last_kernel(place_of, zs, n_row, n_col, vol, yud, own, halo, zown, zcorner, u1, u2, w,
                xs, zxs, own_ref, hs, hd, pstrip, u3, *scratch):
    depth, rows, cols = vol.shape
    gr = rows + 16
    quarter_rows, quarter = rows // 4, cols // 4
    get = getter(place_of, w)
    gz, col = lax.axis_index("gz"), lax.axis_index("col")
    low = gz == 0
    ysm = row_mask(get, n_row, rows, gr, quarter_rows)
    last_layers(place_of, get, ysm, vol, yud, u3, *scratch)
    slots = lax.broadcasted_iota(jnp.int32, (SLOTS, 128), 0)
    if n_col == 2:
        keep = ((slots < 8) & (col == 0)) | ((slots >= 21) & (col == 1))
    else:
        keep = (slots < 8) | (slots >= 21)

    def join(part, messages, b):
        sides = [messages[-1][b].astype(F32), messages[0][b].astype(F32)]
        return jnp.where(keep, jnp.concatenate(sides, axis=0), part)

    def from_middle(ref, at, b):
        rim = jnp.zeros((8, 128), F32)
        middle = ref[at + 16 * b : at + 16 * (b + 1)].astype(F32)
        return jnp.concatenate([rim, middle, rim], axis=0)

    lanes = lax.broadcasted_iota(jnp.int32, (SLOTS, 128), 1)

    def layers_of(pairs, quads):
        out = []
        for z in range(2 * len(pairs)):
            left, right = pairs[z // 2], quads[z // 4]
            if z % 2:
                left = pltpu.roll(left, 64, 1)
            turn = (rows - 32 * (z % 4)) % 128
            if turn:
                right = pltpu.roll(right, turn, 1)
            out.append(jnp.where(lanes < rows, left, right))
        return out

    n2, n4 = EXTRA // 2, EXTRA // 4
    own_layers = layers_of(
        [join(own[b].astype(F32), xs, b) for b in range(depth // 2)],
        [join(halo[b].astype(F32), xs, depth // 2 + b) for b in range(depth // 4)],
    )
    at = 2 * R * rows
    beyond = layers_of(
        [join(from_middle(zown, at, b), zxs, b) for b in range(n2)],
        [join(from_middle(zcorner, 128, b), zxs, n2 + b) for b in range(n4)],
    )
    count = depth + 8
    zero = [jnp.zeros((SLOTS, 128), F32)] * R
    at_low = zero + own_layers + beyond[0:11]
    at_high = beyond[1:12] + own_layers + zero
    layers = [jnp.where(low, a, b) for a, b in zip(at_low, at_high)]
    for z, smooth, slope in z_filter(layers, count):
        hs[SLOTS * z : SLOTS * (z + 1)] = smooth
        hd[SLOTS * z : SLOTS * (z + 1)] = slope
    p01 = lax.dot_general(
        get("wy_strip", 128), hs[...], NT, preferred_element_type=F32
    ).astype(BF16)
    p2 = lax.dot_general(
        get("wy_strip_slope", 128), hd[...], NT, preferred_element_type=F32
    ).astype(BF16)
    n = count // 8
    groups = [slice(256 * c, 256 * (c + 1)) for c in range(n)]
    stacks = [
        jnp.concatenate([p[:, g] for g in groups], axis=0) for p in (p01[0:gr], p01[gr:], p2)
    ]
    grads = [
        jnp.dot(stack, get(name), preferred_element_type=F32).astype(BF16).reshape(n, gr, 256)
        for stack, name in zip(stacks, ("bdd", "bds", "bds"))
    ]
    for c, (a, b) in enumerate(pair_table):
        pstrip[:, c * gr : (c + 1) * gr] = grads[a] * grads[b]
    slot = lax.rem(lax.broadcasted_iota(jnp.int32, (3 * quarter_rows, 256), 1), SLOTS)
    outside_x = ((col == 0) & (slot < 8)) | ((col == n_col - 1) & (slot >= 14))
    smoothed = []
    for c in range(n):
        for half in range(2):
            part = pstrip[c, half * 3 * gr : (half + 1) * 3 * gr]
            out = jnp.dot(ysm, part, preferred_element_type=F32)
            smoothed.append(jnp.where(outside_x, 0.0, out).astype(BF16))
    u = jnp.dot(jnp.concatenate(smoothed, axis=0), get("bdx"), preferred_element_type=F32)
    n_rows = 6 * quarter_rows
    u = u.astype(BF16)
    sums = []
    for name in ("0", "1"):
        at = jnp.where(low, place_of["g_low" + name][0], place_of["g_high" + name][0])
        total = None
        for c in range(n):
            g = w[pl.ds(pl.multiple_of(at + 64 * c, 16), 64), :]
            term = jnp.dot(u[n_rows * c : n_rows * (c + 1)], g, preferred_element_type=F32)
            total = term if total is None else total + term
        sums += [total[:, 0:quarter], total[:, 128 : 128 + quarter]]
    for q in range(depth // 4):
        total = sums[q]
        for i in range(depth):
            if i < FIRST:
                u, from_low, from_high = u1[i], depth - EDGE - FIRST + i, EDGE + i
            elif i < FIRST + EDGE:
                k = i - FIRST
                u, from_low, from_high = u2[k], depth - EDGE + k, k
            else:
                k = i - FIRST - EDGE
                u, from_low, from_high = u3[k], k, depth - LAST + k
            a, b = float(zs[from_low, q + 2]), float(zs[from_high, q + 2])
            if a == 0.0 and b == 0.0:
                continue
            total = total + u * jnp.where(low, a, b)
        own_ref[:, q] = total.reshape(6, quarter_rows, quarter)


def add_kernel(own, got, out):
    n_q, quarter = own.shape[1], own.shape[3]
    low = lax.axis_index("gz") == 0
    parts = [
        got[:, k * quarter : (k + 1) * quarter].astype(F32).reshape(own.shape[0], -1, quarter)
        for k in range(2)
    ]
    for q in range(n_q):
        total = own[:, q]
        if q < 2:
            total = total + parts[q] * jnp.where(low, 0.0, 1.0)
        if q >= n_q - 2:
            total = total + parts[q - n_q + 2] * jnp.where(low, 1.0, 0.0)
        out[:, q] = total


def call(body, outs, operands, scratch, name, flops=0, aliases=None, n_hbm=0):
    vmem = pl.BlockSpec(memory_space=pltpu.VMEM)
    hbm = pl.BlockSpec(memory_space=pltpu.HBM)
    operands = [
        pltpu.with_memory_space_constraint(o, pltpu.HBM) if i < n_hbm else o
        for i, o in enumerate(operands)
    ]
    moved = sum(o.size * o.dtype.itemsize for o in list(outs) + list(operands))
    return pl.pallas_call(
        body,
        out_shape=list(outs),
        in_specs=[hbm] * n_hbm + [vmem] * (len(operands) - n_hbm),
        out_specs=[vmem] * len(outs),
        scratch_shapes=scratch,
        input_output_aliases=aliases or {},
        compiler_params=pltpu.CompilerParams(vmem_limit_bytes=24 * 2**20),
        cost_estimate=pl.CostEstimate(flops=flops, bytes_accessed=moved, transcendentals=0),
        name=name,
    )(*operands)


def per_device(volume):
    depth, rows, cols = volume.shape
    n_row, n_col = lax.axis_size("row"), lax.axis_size("col")
    table, place_of, zs = weight_table(depth, rows, cols)
    ext = rows + 2 * HALO
    gr = rows + 16
    quarter_rows, quarter = rows // 4, cols // 4
    n_rows = 6 * quarter_rows
    n_side = 1 if n_col == 2 else 2
    pairs, quads = depth // 2, depth // 4
    n2, n4 = EXTRA // 2, EXTRA // 4
    sds = jax.ShapeDtypeStruct
    bf16 = lambda *shape: sds(shape, BF16)

    def scratch_for(count):
        return [
            pltpu.VMEM((count, 2 * ext, cols), BF16),
            pltpu.VMEM((3, count, gr, cols), BF16),
            pltpu.VMEM((count, 6 * gr, cols), BF16),
            pltpu.VMEM((count, n_rows, cols), BF16),
        ]

    layer_flops = 2 * cols * (3 * gr * 2 * ext + 3 * gr * cols + n_rows * 3 * gr + n_rows * quarter)

    dma = pltpu.SemaphoreType.DMA
    s1, s2, vol = call(
        load_kernel,
        [bf16(depth * NEED, cols)] * 2 + [bf16(depth, rows, cols)],
        [volume], [pltpu.VMEM((depth, HALO, cols), BF16)] * 2 + [dma((3,))], "load", n_hbm=1,
    )
    inner = [(i, i + 1) for i in range(1, n_row - 1, 2)]
    inner = inner + [(j, i) for i, j in inner]
    r2 = lax.ppermute(s2, "row", inner)
    r1 = lax.ppermute(s1, "row", [(i, i ^ 1) for i in range(n_row)])
    (w,) = call(
        stage_kernel, [bf16(*table.shape)], [jnp.asarray(table)], [], "stage", aliases={0: 0}
    )
    own, zmsg, *xown = call(
        lambda *refs: edges_kernel(n_col, *refs),
        [bf16(pairs, SLOTS, 128), bf16(2 * R * rows + n2 * 16, 128)]
        + [bf16(pairs, HALO, 128)] * n_side,
        [vol], [pltpu.VMEM((pairs, 16, 128), BF16)], "edges",
    )
    swap = [(0, 1), (1, 0)]
    zown = lax.ppermute(zmsg, "gz", swap)

    yud, halo, zcmsg, *messages = call(
        lambda *refs: pack_kernel(place_of, n_col, *refs),
        [bf16(depth, 2 * HALO, cols), bf16(quads, SLOTS, 128), bf16(128 + n4 * 16, 128)]
        + [bf16(pairs + quads, HALO, 128)] * n_side
        + [bf16(n2 + n4, HALO, 128)] * n_side,
        [r1, r2, w] + xown, [pltpu.VMEM((quads, 16, 128), BF16)], "pack",
    )
    zcorner = lax.ppermute(zcmsg, "gz", swap)
    xs, zxs = [], []
    for side in range(n_side):
        step = 1 - 2 * side
        line = swap if n_col == 2 else [
            (i, i + step) for i in range(n_col) if 0 <= i + step < n_col
        ]
        both = [(z * n_col + i, (1 - z) * n_col + j) for z in range(2) for i, j in line]
        xs.append(lax.ppermute(messages[side], "col", line))
        zxs.append(lax.ppermute(messages[n_side + side], ("gz", "col"), both))

    (u1,) = call(
        lambda *refs: first_kernel(place_of, n_row, *refs),
        [sds((FIRST, n_rows, quarter), F32)],
        [vol, yud, w], scratch_for(FIRST), "first", flops=FIRST * layer_flops,
    )
    u2, send = call(
        lambda *refs: near_kernel(place_of, zs, n_row, *refs),
        [sds((EDGE, n_rows, quarter), F32), bf16(n_rows, 2 * quarter)],
        [vol, yud, zown, zcorner, u1, w],
        [pltpu.VMEM((R, ext, cols), BF16)] + scratch_for(EDGE),
        "near", flops=EDGE * layer_flops,
    )
    sums = lax.ppermute(send, "gz", swap)

    def last_body(*refs):
        head, x_refs, zx_refs = refs[0:9], refs[9 : 9 + n_side], refs[9 + n_side : 9 + 2 * n_side]
        last_kernel(
            place_of, zs, n_row, n_col, *head, x_refs, zx_refs, *refs[9 + 2 * n_side :]
        )

    count = depth + 8
    (result,) = call(
        last_body,
        [sds((6, depth // 4, quarter_rows, quarter), F32)],
        [vol, yud, own, halo, zown, zcorner, u1, u2, w] + xs + zxs,
        [
            pltpu.VMEM((count * SLOTS, 128), BF16),
            pltpu.VMEM((count * SLOTS, 128), BF16),
            pltpu.VMEM((count // 8, 6 * gr, 256), BF16),
            pltpu.VMEM((LAST, n_rows, quarter), F32),
        ]
        + scratch_for(LAST),
        "last", flops=(LAST + 3) * layer_flops,
    )
    (out,) = call(add_kernel, [sds(result.shape, F32)], [result, sums], [], "add")
    return out


def solution(mesh):
    return jax.shard_map(
        per_device,
        mesh=mesh,
        in_specs=(P("gz", "row", "col"),),
        out_specs=P(None, "gz", "row", "col"),
        check_vma=False,
    )
```

```python
import jax
import jax.numpy as jnp
import ml_dtypes
import numpy as np
from jax import lax
from jax.experimental import pallas as pl
from jax.experimental.pallas import tpu as pltpu
from jax.sharding import PartitionSpec as P

R = 3
R2 = 8
HALO = 16
NEED = R + R2
EXTRA = 12
SLOTS = 32
NT = (((1,), (1,)), ((), ()))
F32 = jnp.float32
BF16 = jnp.bfloat16

pair_table = ((0, 0), (1, 1), (2, 2), (0, 1), (0, 2), (1, 2))


def gauss_taps(radius):
    offsets = np.arange(-radius, radius + 1).astype(np.float32)
    spread = np.float32(radius / 3.0)
    smooth = np.exp(-offsets * offsets / (np.float32(2.0) * spread * spread))
    smooth = smooth / np.sum(smooth)
    slopes = offsets * smooth
    slopes = slopes / np.sum(offsets * slopes)
    as_f32 = lambda t: t.astype(ml_dtypes.bfloat16).astype(np.float32)
    return as_f32(smooth), as_f32(slopes)


SMOOTH_D, SLOPE_D = gauss_taps(R)
SMOOTH_I, _ = gauss_taps(R2)


def band(taps, sources, targets):
    radius = len(taps) // 2
    gap = np.asarray(sources)[:, None] - np.asarray(targets)[None, :]
    return np.where(np.abs(gap) <= radius, taps[np.clip(gap + radius, 0, 2 * radius)], 0.0)


def weight_table(depth, rows, cols):
    ext = rows + 2 * HALO
    grad_rows = rows + 16
    far = 10**6
    y_in = np.arange(ext) - HALO
    y_out = np.arange(grad_rows) - R2
    smooth_y = band(SMOOTH_D, y_in, y_out).T
    slope_y = band(SLOPE_D, y_in, y_out).T
    zero = np.zeros_like(smooth_y)
    wy = np.block([[smooth_y, zero], [slope_y, zero], [zero, smooth_y]])
    order = np.concatenate([np.arange(rows), np.arange(HALO) - HALO, rows + np.arange(HALO)]) + HALO
    x_all = np.arange(cols)
    slot_in = np.full(SLOTS, far)
    slot_in[0:8] = cols + np.arange(8)
    slot_in[8:14] = np.arange(6)
    slot_in[14:20] = cols - 6 + np.arange(6)
    slot_in[21:32] = np.arange(-11, 0)
    slot_out = np.full(SLOTS, -far)
    slot_out[0:11] = np.arange(-8, 3)
    slot_out[11:19] = cols - 3 + np.arange(8)
    eye8 = np.eye(8)
    inner = np.where((x_all >= R) & (x_all < cols - R), x_all, far)
    quarter = cols // 4
    coarse_edge = np.full(8, 3 * far)
    coarse_edge[0:5] = [0, 1, 2, quarter - 2, quarter - 1]
    xs_edge = band(SMOOTH_I, slot_out, 4 * coarse_edge)
    ys = band(SMOOTH_I, y_out, 4 * np.arange(rows // 4)).T
    zs = band(SMOOTH_I, np.arange(depth), 4 * (np.arange(depth // 4 + 4) - 2))
    place = np.zeros((8, 128))
    for j in range(5):
        place[j, coarse_edge[j]] = 1.0
    own_z = 4 * np.arange(depth // 4)
    g = [
        np.einsum("zq,jx->zjqx", band(SMOOTH_I, np.arange(depth + 8) + first, own_z), place)
        for first in (0, -8)
    ]
    g = [t.reshape((depth + 8) * 8, len(own_z) * 128) for t in g]
    packed = np.arange(depth * NEED)
    above = np.zeros((depth * HALO, depth * NEED))
    above[packed + packed // NEED * (HALO - NEED) + HALO - NEED, packed] = 1.0
    below = np.zeros((depth * HALO, depth * NEED))
    below[packed + packed // NEED * (HALO - NEED), packed] = 1.0
    used = 2 * R + 13
    packed = np.arange(R * used)
    corner = np.zeros((64, R * 2 * HALO))
    corner[packed, packed + packed // used * (2 * HALO - used) + HALO - NEED] = 1.0
    parts = {
        "above": above,
        "below": below,
        "corner": corner,
        "corner_back": corner.T,
        "wy": wy,
        "wy_strip": np.concatenate([smooth_y, slope_y])[:, order],
        "wy_strip_slope": smooth_y[:, order],
        "wxd": band(SLOPE_D, x_all, x_all),
        "wxs": band(SMOOTH_D, x_all, x_all),
        "bdd": np.kron(eye8, band(SLOPE_D, slot_in, slot_out)),
        "bds": np.kron(eye8, band(SMOOTH_D, slot_in, slot_out)),
        "ysm": np.kron(np.eye(3), ys),
        "xsm": band(SMOOTH_I, inner, 4 * np.arange(quarter)),
        "bdx": np.kron(eye8, xs_edge),
        "g_low0": g[0][:, 0:256],
        "g_low1": g[0][:, 256:512],
        "g_high0": g[1][:, 0:256],
        "g_high1": g[1][:, 256:512],
    }
    place_of, blocks, at = {}, [], 0
    for name, part in parts.items():
        height = -(-part.shape[0] // 16) * 16
        block = np.zeros((height, 256), np.float32)
        block[: part.shape[0], : part.shape[1]] = part
        place_of[name] = (at, part.shape[0], part.shape[1])
        blocks.append(block)
        at += height
    return np.concatenate(blocks).astype(ml_dtypes.bfloat16), place_of, zs


def z_filter(v, count):
    for z in range(count):
        w = v[z : z + 7]
        smooth = w[3] * float(SMOOTH_D[3])
        slope = None
        for s in (1, 2, 3):
            smooth = smooth + (w[3 + s] + w[3 - s]) * float(SMOOTH_D[3 + s])
            term = (w[3 + s] - w[3 - s]) * float(SLOPE_D[3 + s])
            slope = term if slope is None else slope + term
        yield z, smooth, slope


def getter(place_of, w):
    def get(name, width=None):
        at, height, own_width = place_of[name]
        return w[at : at + height, 0 : (width or own_width)]

    return get


def row_mask(get, n_row, rows, gr, quarter_rows):
    row = lax.axis_index("row")
    lane = lax.broadcasted_iota(jnp.int32, (3 * quarter_rows, 3 * gr), 1)
    y_out = lax.rem(lane, gr) - R2
    outside = ((row == 0) & (y_out < 0)) | ((row == n_row - 1) & (y_out >= rows))
    return jnp.where(outside, 0.0, get("ysm").astype(F32)).astype(BF16)


def layers_to_sums(get, ysm, load, count, shape, u_ref, zf, planes, prod, sm):
    rows, cols = shape
    ext = rows + 2 * HALO
    gr = rows + 16
    n_rows = 6 * (rows // 4)
    half_rows = n_rows // 2
    rest = jnp.zeros((8, 128), F32)
    for tile in range(cols // 128):
        lanes = slice(tile * 128, tile * 128 + 128)
        for at in range(0, ext, 16):
            blocks = load(at, lanes)
            if at == rows + HALO:
                blocks = [block[0:8] for block in blocks]
            for z, smooth, slope in z_filter(blocks, count):
                if at == rows + HALO:
                    smooth = jnp.concatenate([smooth, rest], axis=0)
                    slope = jnp.concatenate([slope, rest], axis=0)
                zf[z, at : at + 16, lanes] = smooth.astype(BF16)
                zf[z, ext + at : ext + at + 16, lanes] = slope.astype(BF16)
    wy = get("wy")
    for z in range(count):
        out = jnp.dot(wy, zf[z], preferred_element_type=F32).astype(BF16)
        planes[0, z] = out[0:gr]
        planes[1, z] = out[gr : 2 * gr]
        planes[2, z] = out[2 * gr :]
    group = 4 if count % 4 == 0 else count
    for at in range(0, count, group):
        grads = []
        for f, name in enumerate(("wxd", "wxs", "wxs")):
            part = planes[f, at : at + group].reshape(group * gr, cols)
            out = jnp.dot(part, get(name), preferred_element_type=F32)
            grads.append(out.astype(BF16).reshape(group, gr, cols))
        for c, (a, b) in enumerate(pair_table):
            prod[at : at + group, c * gr : (c + 1) * gr] = grads[a] * grads[b]
    for z in range(count):
        for half in range(2):
            part = prod[z, half * 3 * gr : (half + 1) * 3 * gr]
            out = jnp.dot(ysm, part, preferred_element_type=F32)
            sm[z, half * half_rows : (half + 1) * half_rows] = out.astype(BF16)
    out = jnp.dot(
        sm[...].reshape(count * n_rows, cols), get("xsm"), preferred_element_type=F32
    )
    u_ref[...] = out.reshape(count, n_rows, cols // 4)


def block_loader(vol, yud, rows):
    def layer(z, at, lanes):
        if at < HALO:
            return yud[z, at : at + 16, lanes].astype(F32)
        if at < HALO + rows:
            return vol[z, at - HALO : at - HALO + 16, lanes].astype(F32)
        return yud[z, at - rows : at - rows + 16, lanes].astype(F32)

    return layer


def spread_rows(first):
    shape = (16 * NEED, 16 * HALO)
    packed = lax.broadcasted_iota(jnp.int32, shape, 0)
    full = lax.broadcasted_iota(jnp.int32, shape, 1)
    z = lax.shift_right_logical(packed * 373, 12)
    return jnp.where(full == packed + z * (HALO - NEED) + first, 1.0, 0.0).astype(BF16)


def load_kernel(vol, s1, s2, vol_out, top, bottom, sems):
    depth, rows, cols = vol.shape
    odd = lax.rem(lax.axis_index("row"), 2) == 1
    copies = [
        pltpu.make_async_copy(vol.at[:, 0:HALO, :], top, sems.at[0]),
        pltpu.make_async_copy(vol.at[:, rows - HALO : rows, :], bottom, sems.at[1]),
        pltpu.make_async_copy(vol, vol_out, sems.at[2]),
    ]
    for copy in copies:
        copy.start()
    first_rows, last_rows = spread_rows(0), spread_rows(HALO - NEED)
    copies[0].wait()
    copies[1].wait()
    to_before = jnp.dot(
        first_rows, top[...].reshape(depth * HALO, cols), preferred_element_type=F32
    ).astype(BF16)
    to_after = jnp.dot(
        last_rows, bottom[...].reshape(depth * HALO, cols), preferred_element_type=F32
    ).astype(BF16)
    s1[...] = jnp.where(odd, to_before, to_after)
    s2[...] = jnp.where(odd, to_after, to_before)
    copies[2].wait()


def column_select(n_col, cols):
    n_side = 1 if n_col == 2 else 2
    shape = (SLOTS + 16 * n_side, cols)
    row = lax.broadcasted_iota(jnp.int32, shape, 0)
    lane = lax.broadcasted_iota(jnp.int32, shape, 1)
    picked = ((row >= 8) & (row < 14) & (lane == row - 8)) | (
        (row >= 14) & (row < 20) & (lane == row - 20 + cols)
    )
    for side in range(n_side):
        if n_col == 2:
            first = jnp.where(lax.axis_index("col") == 0, cols - HALO, 0)
        else:
            first = (cols - HALO, 0)[side]
        at = row - SLOTS - 16 * side
        picked = picked | ((at >= 0) & (at < 16) & (lane == at + first))
    return jnp.where(picked, 1.0, 0.0).astype(BF16)


def pick_columns(select, source):
    picked = lax.dot_general(select, source, NT, preferred_element_type=F32)
    messages = [picked[at : at + 16].astype(BF16) for at in range(SLOTS, picked.shape[0], 16)]
    return picked[0:SLOTS].astype(BF16), picked[8:24].astype(BF16), messages


def halve(chunk, at, value):
    n = value.shape[0]
    chunk[at : at + n] = value[:, 0:128]
    chunk[at + n : at + 2 * n] = value[:, 128:256]


def joined_halves(chunk, at, n):
    return jnp.concatenate([chunk[at : at + n], chunk[at + n : at + 2 * n]], axis=1)


def edges_kernel(n_col, vol, own, zmsg, *refs):
    depth, rows, cols = vol.shape
    gz = lax.axis_index("gz")
    refs, middles = refs[:-1], refs[-1]
    select = column_select(n_col, cols)
    for b in range(depth // 2):
        source = vol[2 * b : 2 * b + 2].reshape(2 * rows, cols)
        slots, middle, messages = pick_columns(select, source)
        own[b], middles[b] = slots, middle
        for ref, message in zip(refs, messages):
            ref[b] = message
    base = jnp.where(gz == 0, depth - R, 0)
    halve(zmsg, 0, vol[pl.ds(base, R)].reshape(R * rows, cols))
    first = jnp.where(gz == 0, (depth - EXTRA) // 2, 0)
    n = EXTRA // 2
    zmsg[2 * R * rows :] = middles[pl.ds(first, n)].reshape(n * 16, 128)


def pack_kernel(place_of, n_col, r1, r2, w, *refs):
    n_side = 1 if n_col == 2 else 2
    xown, (yud, halo, zcorner) = refs[:n_side], refs[n_side : n_side + 3]
    xmsgs, zxmsgs = refs[n_side + 3 : 2 * n_side + 3], refs[2 * n_side + 3 : 3 * n_side + 3]
    middles = refs[3 * n_side + 3]
    depth, cols = yud.shape[0], yud.shape[2]
    gz = lax.axis_index("gz")
    odd = lax.rem(lax.axis_index("row"), 2) == 1
    get = getter(place_of, w)
    got1, got2 = r1[...], r2[...]
    for at, name, part in (
        (0, "above", jnp.where(odd, got1, got2)),
        (HALO, "below", jnp.where(odd, got2, got1)),
    ):
        out = jnp.dot(get(name), part, preferred_element_type=F32).astype(BF16)
        yud[:, at : at + HALO, :] = out.reshape(depth, HALO, cols)
    select = column_select(n_col, cols)
    pairs, quads = depth // 2, depth // 4
    for b in range(quads):
        source = yud[4 * b : 4 * b + 4].reshape(4 * 2 * HALO, cols)
        slots, middle, messages = pick_columns(select, source)
        halo[b] = slots
        middles[b] = middle
        for ref, message in zip(xmsgs, messages):
            ref[pairs + b] = message
    for ref, part in zip(xmsgs, xown):
        ref[0:pairs] = part[...]
    base = jnp.where(gz == 0, depth - R, 0)
    edge = yud[pl.ds(base, R)].reshape(R * 2 * HALO, cols)
    halve(zcorner, 0, jnp.dot(get("corner"), edge, preferred_element_type=F32).astype(BF16))
    n2, n4 = EXTRA // 2, EXTRA // 4
    first2 = jnp.where(gz == 0, pairs - n2, 0)
    first4 = jnp.where(gz == 0, quads - n4, 0)
    zcorner[128:] = middles[pl.ds(first4, n4)].reshape(n4 * 16, 128)
    for ref, message in zip(zxmsgs, xmsgs):
        ref[0:n2] = message[pl.ds(first2, n2)]
        ref[n2:] = message[pl.ds(pairs + first4, n4)]


def stage_kernel(w, w_out):
    pass


FIRST = 7
EDGE = R
LAST = 6


def first_kernel(place_of, n_row, vol, yud, w, u_ref, *scratch):
    depth, rows, cols = vol.shape
    get = getter(place_of, w)
    ysm = row_mask(get, n_row, rows, rows + 16, rows // 4)
    base = jnp.where(lax.axis_index("gz") == 0, depth - EDGE - FIRST - R, 0)
    layer = block_loader(vol, yud, rows)
    load = lambda at, lanes: [layer(base + k, at, lanes) for k in range(FIRST + 2 * R)]
    layers_to_sums(get, ysm, load, FIRST, (rows, cols), u_ref, *scratch)


def near_kernel(place_of, zs, n_row, vol, yud, zown, zcorner, u1, w, u_ref, send_ref, zext, *scratch):
    depth, rows, cols = vol.shape
    n_zq = zs.shape[1]
    get = getter(place_of, w)
    low = lax.axis_index("gz") == 0
    ysm = row_mask(get, n_row, rows, rows + 16, rows // 4)
    corner = jnp.dot(
        get("corner_back"), joined_halves(zcorner, 0, 64), preferred_element_type=F32
    ).astype(BF16).reshape(R, 2 * HALO, cols)
    zext[:, 0:HALO] = corner[:, 0:HALO]
    zext[:, HALO : HALO + rows] = joined_halves(zown, 0, R * rows).reshape(R, rows, cols)
    zext[:, HALO + rows :] = corner[:, HALO:]
    layer = block_loader(vol, yud, rows)
    start = jnp.where(low, depth - R, 0)
    outer = jnp.where(low, depth - 2 * R, R)

    def load(at, lanes):
        beyond = [zext[k, at : at + 16, lanes].astype(F32) for k in range(R)]
        inner = [layer(outer + k, at, lanes) for k in range(R)]
        middle = [layer(start + k, at, lanes) for k in range(R)]
        before = [jnp.where(low, inner[k], beyond[k]) for k in range(R)]
        after = [jnp.where(low, beyond[k], inner[k]) for k in range(R)]
        return before + middle + after

    layers_to_sums(get, ysm, load, EDGE, (rows, cols), u_ref, *scratch)
    sends = []
    for k in range(2):
        total = None
        for i in range(FIRST + EDGE):
            from_low = depth - EDGE - FIRST + i
            from_high = EDGE + i if i < FIRST else i - FIRST
            a = float(zs[from_low, n_zq - 2 + k])
            b = float(zs[from_high, k])
            if a == 0.0 and b == 0.0:
                continue
            term = (u1[i] if i < FIRST else u_ref[i - FIRST]) * jnp.where(low, a, b)
            total = term if total is None else total + term
        sends.append(total)
    send_ref[...] = jnp.concatenate(sends, axis=1).astype(BF16)


def last_layers(place_of, get, ysm, vol, yud, u_ref, *scratch):
    depth, rows, cols = vol.shape
    low = lax.axis_index("gz") == 0
    layer = block_loader(vol, yud, rows)
    base = jnp.where(low, -R, depth - LAST - R)
    before_on = jnp.where(low, 0.0, 1.0)
    after_on = jnp.where(low, 1.0, 0.0)

    def load(at, lanes):
        out = []
        for k in range(LAST + 2 * R):
            block = layer(jnp.clip(base + k, 0, depth - 1), at, lanes)
            if k < R:
                block = block * before_on
            elif k >= LAST + R:
                block = block * after_on
            out.append(block)
        return out

    layers_to_sums(get, ysm, load, LAST, (rows, cols), u_ref, *scratch)


def last_kernel(place_of, zs, n_row, n_col, vol, yud, own, halo, zown, zcorner, u1, u2, w,
                xs, zxs, own_ref, hs, hd, pstrip, u3, *scratch):
    depth, rows, cols = vol.shape
    gr = rows + 16
    quarter_rows, quarter = rows // 4, cols // 4
    get = getter(place_of, w)
    gz, col = lax.axis_index("gz"), lax.axis_index("col")
    low = gz == 0
    ysm = row_mask(get, n_row, rows, gr, quarter_rows)
    last_layers(place_of, get, ysm, vol, yud, u3, *scratch)
    slots = lax.broadcasted_iota(jnp.int32, (SLOTS, 128), 0)
    if n_col == 2:
        keep = ((slots < 8) & (col == 0)) | ((slots >= 21) & (col == 1))
    else:
        keep = (slots < 8) | (slots >= 21)

    def join(part, messages, b):
        sides = [messages[-1][b].astype(F32), messages[0][b].astype(F32)]
        return jnp.where(keep, jnp.concatenate(sides, axis=0), part)

    def from_middle(ref, at, b):
        rim = jnp.zeros((8, 128), F32)
        middle = ref[at + 16 * b : at + 16 * (b + 1)].astype(F32)
        return jnp.concatenate([rim, middle, rim], axis=0)

    lanes = lax.broadcasted_iota(jnp.int32, (SLOTS, 128), 1)

    def layers_of(pairs, quads):
        out = []
        for z in range(2 * len(pairs)):
            left, right = pairs[z // 2], quads[z // 4]
            if z % 2:
                left = pltpu.roll(left, 64, 1)
            turn = (rows - 32 * (z % 4)) % 128
            if turn:
                right = pltpu.roll(right, turn, 1)
            out.append(jnp.where(lanes < rows, left, right))
        return out

    n2, n4 = EXTRA // 2, EXTRA // 4
    own_layers = layers_of(
        [join(own[b].astype(F32), xs, b) for b in range(depth // 2)],
        [join(halo[b].astype(F32), xs, depth // 2 + b) for b in range(depth // 4)],
    )
    at = 2 * R * rows
    beyond = layers_of(
        [join(from_middle(zown, at, b), zxs, b) for b in range(n2)],
        [join(from_middle(zcorner, 128, b), zxs, n2 + b) for b in range(n4)],
    )
    count = depth + 8
    zero = [jnp.zeros((SLOTS, 128), F32)] * R
    at_low = zero + own_layers + beyond[0:11]
    at_high = beyond[1:12] + own_layers + zero
    layers = [jnp.where(low, a, b) for a, b in zip(at_low, at_high)]
    for z, smooth, slope in z_filter(layers, count):
        hs[SLOTS * z : SLOTS * (z + 1)] = smooth.astype(BF16)
        hd[SLOTS * z : SLOTS * (z + 1)] = slope.astype(BF16)
    p01 = lax.dot_general(
        get("wy_strip", 128), hs[...], NT, preferred_element_type=F32
    ).astype(BF16)
    p2 = lax.dot_general(
        get("wy_strip_slope", 128), hd[...], NT, preferred_element_type=F32
    ).astype(BF16)
    n = count // 8
    groups = [slice(256 * c, 256 * (c + 1)) for c in range(n)]
    stacks = [
        jnp.concatenate([p[:, g] for g in groups], axis=0) for p in (p01[0:gr], p01[gr:], p2)
    ]
    grads = [
        jnp.dot(stack, get(name), preferred_element_type=F32).astype(BF16).reshape(n, gr, 256)
        for stack, name in zip(stacks, ("bdd", "bds", "bds"))
    ]
    for c, (a, b) in enumerate(pair_table):
        pstrip[:, c * gr : (c + 1) * gr] = grads[a] * grads[b]
    slot = lax.rem(lax.broadcasted_iota(jnp.int32, (3 * quarter_rows, 256), 1), SLOTS)
    outside_x = ((col == 0) & (slot < 8)) | ((col == n_col - 1) & (slot >= 14))
    smoothed = []
    for c in range(n):
        for half in range(2):
            part = pstrip[c, half * 3 * gr : (half + 1) * 3 * gr]
            out = jnp.dot(ysm, part, preferred_element_type=F32)
            smoothed.append(jnp.where(outside_x, 0.0, out).astype(BF16))
    u = jnp.dot(jnp.concatenate(smoothed, axis=0), get("bdx"), preferred_element_type=F32)
    n_rows = 6 * quarter_rows
    u = u.astype(BF16)
    sums = []
    for name in ("0", "1"):
        at = jnp.where(low, place_of["g_low" + name][0], place_of["g_high" + name][0])
        total = None
        for c in range(n):
            g = w[pl.ds(pl.multiple_of(at + 64 * c, 16), 64), :]
            term = jnp.dot(u[n_rows * c : n_rows * (c + 1)], g, preferred_element_type=F32)
            total = term if total is None else total + term
        sums += [total[:, 0:quarter], total[:, 128 : 128 + quarter]]
    for q in range(depth // 4):
        total = sums[q]
        for i in range(depth):
            if i < FIRST:
                u, from_low, from_high = u1[i], depth - EDGE - FIRST + i, EDGE + i
            elif i < FIRST + EDGE:
                k = i - FIRST
                u, from_low, from_high = u2[k], depth - EDGE + k, k
            else:
                k = i - FIRST - EDGE
                u, from_low, from_high = u3[k], k, depth - LAST + k
            a, b = float(zs[from_low, q + 2]), float(zs[from_high, q + 2])
            if a == 0.0 and b == 0.0:
                continue
            total = total + u * jnp.where(low, a, b)
        own_ref[:, q] = total.reshape(6, quarter_rows, quarter)


def add_kernel(own, got, out):
    n_q, quarter = own.shape[1], own.shape[3]
    low = lax.axis_index("gz") == 0
    parts = [
        got[:, k * quarter : (k + 1) * quarter].astype(F32).reshape(own.shape[0], -1, quarter)
        for k in range(2)
    ]
    for q in range(n_q):
        total = own[:, q]
        if q < 2:
            total = total + parts[q] * jnp.where(low, 0.0, 1.0)
        if q >= n_q - 2:
            total = total + parts[q - n_q + 2] * jnp.where(low, 1.0, 0.0)
        out[:, q] = total


def call(body, outs, operands, scratch, name, flops=0, aliases=None, n_hbm=0):
    vmem = pl.BlockSpec(memory_space=pltpu.VMEM)
    hbm = pl.BlockSpec(memory_space=pltpu.HBM)
    operands = [
        pltpu.with_memory_space_constraint(o, pltpu.HBM) if i < n_hbm else o
        for i, o in enumerate(operands)
    ]
    moved = sum(o.size * o.dtype.itemsize for o in list(outs) + list(operands))
    return pl.pallas_call(
        body,
        out_shape=list(outs),
        in_specs=[hbm] * n_hbm + [vmem] * (len(operands) - n_hbm),
        out_specs=[vmem] * len(outs),
        scratch_shapes=scratch,
        input_output_aliases=aliases or {},
        compiler_params=pltpu.CompilerParams(vmem_limit_bytes=24 * 2**20),
        cost_estimate=pl.CostEstimate(flops=flops, bytes_accessed=moved, transcendentals=0),
        name=name,
    )(*operands)


def per_device(volume):
    depth, rows, cols = volume.shape
    n_row, n_col = lax.axis_size("row"), lax.axis_size("col")
    table, place_of, zs = weight_table(depth, rows, cols)
    ext = rows + 2 * HALO
    gr = rows + 16
    quarter_rows, quarter = rows // 4, cols // 4
    n_rows = 6 * quarter_rows
    n_side = 1 if n_col == 2 else 2
    pairs, quads = depth // 2, depth // 4
    n2, n4 = EXTRA // 2, EXTRA // 4
    sds = jax.ShapeDtypeStruct
    bf16 = lambda *shape: sds(shape, BF16)

    def scratch_for(count):
        return [
            pltpu.VMEM((count, 2 * ext, cols), BF16),
            pltpu.VMEM((3, count, gr, cols), BF16),
            pltpu.VMEM((count, 6 * gr, cols), BF16),
            pltpu.VMEM((count, n_rows, cols), BF16),
        ]

    layer_flops = 2 * cols * (3 * gr * 2 * ext + 3 * gr * cols + n_rows * 3 * gr + n_rows * quarter)

    dma = pltpu.SemaphoreType.DMA
    s1, s2, vol = call(
        load_kernel,
        [bf16(depth * NEED, cols)] * 2 + [bf16(depth, rows, cols)],
        [volume], [pltpu.VMEM((depth, HALO, cols), BF16)] * 2 + [dma((3,))], "load", n_hbm=1,
    )
    inner = [(i, i + 1) for i in range(1, n_row - 1, 2)]
    inner = inner + [(j, i) for i, j in inner]
    r2 = lax.ppermute(s2, "row", inner)
    r1 = lax.ppermute(s1, "row", [(i, i ^ 1) for i in range(n_row)])
    (w,) = call(
        stage_kernel, [bf16(*table.shape)], [jnp.asarray(table)], [], "stage", aliases={0: 0}
    )
    own, zmsg, *xown = call(
        lambda *refs: edges_kernel(n_col, *refs),
        [bf16(pairs, SLOTS, 128), bf16(2 * R * rows + n2 * 16, 128)]
        + [bf16(pairs, HALO, 128)] * n_side,
        [vol], [pltpu.VMEM((pairs, 16, 128), BF16)], "edges",
    )
    swap = [(0, 1), (1, 0)]
    zown = lax.ppermute(zmsg, "gz", swap)

    yud, halo, zcmsg, *messages = call(
        lambda *refs: pack_kernel(place_of, n_col, *refs),
        [bf16(depth, 2 * HALO, cols), bf16(quads, SLOTS, 128), bf16(128 + n4 * 16, 128)]
        + [bf16(pairs + quads, HALO, 128)] * n_side
        + [bf16(n2 + n4, HALO, 128)] * n_side,
        [r1, r2, w] + xown, [pltpu.VMEM((quads, 16, 128), BF16)], "pack",
    )
    zcorner = lax.ppermute(zcmsg, "gz", swap)
    xs, zxs = [], []
    for side in range(n_side):
        step = 1 - 2 * side
        line = swap if n_col == 2 else [
            (i, i + step) for i in range(n_col) if 0 <= i + step < n_col
        ]
        both = [(z * n_col + i, (1 - z) * n_col + j) for z in range(2) for i, j in line]
        xs.append(lax.ppermute(messages[side], "col", line))
        zxs.append(lax.ppermute(messages[n_side + side], ("gz", "col"), both))

    (u1,) = call(
        lambda *refs: first_kernel(place_of, n_row, *refs),
        [sds((FIRST, n_rows, quarter), F32)],
        [vol, yud, w], scratch_for(FIRST), "first", flops=FIRST * layer_flops,
    )
    u2, send = call(
        lambda *refs: near_kernel(place_of, zs, n_row, *refs),
        [sds((EDGE, n_rows, quarter), F32), bf16(n_rows, 2 * quarter)],
        [vol, yud, zown, zcorner, u1, w],
        [pltpu.VMEM((R, ext, cols), BF16)] + scratch_for(EDGE),
        "near", flops=EDGE * layer_flops,
    )
    sums = lax.ppermute(send, "gz", swap)

    def last_body(*refs):
        head, x_refs, zx_refs = refs[0:9], refs[9 : 9 + n_side], refs[9 + n_side : 9 + 2 * n_side]
        last_kernel(
            place_of, zs, n_row, n_col, *head, x_refs, zx_refs, *refs[9 + 2 * n_side :]
        )

    count = depth + 8
    (result,) = call(
        last_body,
        [sds((6, depth // 4, quarter_rows, quarter), F32)],
        [vol, yud, own, halo, zown, zcorner, u1, u2, w] + xs + zxs,
        [
            pltpu.VMEM((count * SLOTS, 128), BF16),
            pltpu.VMEM((count * SLOTS, 128), BF16),
            pltpu.VMEM((count // 8, 6 * gr, 256), BF16),
            pltpu.VMEM((LAST, n_rows, quarter), F32),
        ]
        + scratch_for(LAST),
        "last", flops=(LAST + 3) * layer_flops,
    )
    (out,) = call(add_kernel, [sds(result.shape, F32)], [result, sums], [], "add")
    return out


def solution(mesh):
    return jax.shard_map(
        per_device,
        mesh=mesh,
        in_specs=(P("gz", "row", "col"),),
        out_specs=P(None, "gz", "row", "col"),
        check_vma=False,
    )
```

```python
import jax
import jax.numpy as jnp
import ml_dtypes
import numpy as np
from jax import lax
from jax.experimental import pallas as pl
from jax.experimental.pallas import tpu as pltpu
from jax.sharding import PartitionSpec as P

R = 3
R2 = 8
HALO = 16
NEED = R + R2
EXTRA = 12
SLOTS = 32
NT = (((1,), (1,)), ((), ()))
F32 = jnp.float32
BF16 = jnp.bfloat16

pair_table = ((0, 0), (1, 1), (2, 2), (0, 1), (0, 2), (1, 2))


def gauss_taps(radius):
    offsets = np.arange(-radius, radius + 1).astype(np.float32)
    spread = np.float32(radius / 3.0)
    smooth = np.exp(-offsets * offsets / (np.float32(2.0) * spread * spread))
    smooth = smooth / np.sum(smooth)
    slopes = offsets * smooth
    slopes = slopes / np.sum(offsets * slopes)
    as_f32 = lambda t: t.astype(ml_dtypes.bfloat16).astype(np.float32)
    return as_f32(smooth), as_f32(slopes)


SMOOTH_D, SLOPE_D = gauss_taps(R)
SMOOTH_I, _ = gauss_taps(R2)


def band(taps, sources, targets):
    radius = len(taps) // 2
    gap = np.asarray(sources)[:, None] - np.asarray(targets)[None, :]
    return np.where(np.abs(gap) <= radius, taps[np.clip(gap + radius, 0, 2 * radius)], 0.0)


def weight_table(depth, rows, cols):
    ext = rows + 2 * HALO
    grad_rows = rows + 16
    far = 10**6
    y_in = np.arange(ext) - HALO
    y_out = np.arange(grad_rows) - R2
    smooth_y = band(SMOOTH_D, y_in, y_out).T
    slope_y = band(SLOPE_D, y_in, y_out).T
    zero = np.zeros_like(smooth_y)
    wy = np.block([[smooth_y, zero], [slope_y, zero], [zero, smooth_y]])
    order = np.concatenate([np.arange(rows), np.arange(HALO) - HALO, rows + np.arange(HALO)]) + HALO
    x_all = np.arange(cols)
    slot_in = np.full(SLOTS, far)
    slot_in[0:8] = cols + np.arange(8)
    slot_in[8:14] = np.arange(6)
    slot_in[14:20] = cols - 6 + np.arange(6)
    slot_in[21:32] = np.arange(-11, 0)
    slot_out = np.full(SLOTS, -far)
    slot_out[0:11] = np.arange(-8, 3)
    slot_out[11:19] = cols - 3 + np.arange(8)
    eye8 = np.eye(8)
    inner = np.where((x_all >= R) & (x_all < cols - R), x_all, far)
    quarter = cols // 4
    coarse_edge = np.full(8, 3 * far)
    coarse_edge[0:5] = [0, 1, 2, quarter - 2, quarter - 1]
    xs_edge = band(SMOOTH_I, slot_out, 4 * coarse_edge)
    ys = band(SMOOTH_I, y_out, 4 * np.arange(rows // 4)).T
    zs = band(SMOOTH_I, np.arange(depth), 4 * (np.arange(depth // 4 + 4) - 2))
    place = np.zeros((8, 128))
    for j in range(5):
        place[j, coarse_edge[j]] = 1.0
    own_z = 4 * np.arange(depth // 4)
    g = [
        np.einsum("zq,jx->zjqx", band(SMOOTH_I, np.arange(depth + 8) + first, own_z), place)
        for first in (0, -8)
    ]
    g = [t.reshape((depth + 8) * 8, len(own_z) * 128) for t in g]
    packed = np.arange(depth * NEED)
    above = np.zeros((depth * HALO, depth * NEED))
    above[packed + packed // NEED * (HALO - NEED) + HALO - NEED, packed] = 1.0
    below = np.zeros((depth * HALO, depth * NEED))
    below[packed + packed // NEED * (HALO - NEED), packed] = 1.0
    used = 2 * R + 13
    packed = np.arange(R * used)
    corner = np.zeros((64, R * 2 * HALO))
    corner[packed, packed + packed // used * (2 * HALO - used) + HALO - NEED] = 1.0
    parts = {
        "above": above,
        "below": below,
        "corner": corner,
        "corner_back": corner.T,
        "wy": wy,
        "wy_strip": np.concatenate([smooth_y, slope_y])[:, order],
        "wy_strip_slope": smooth_y[:, order],
        "wxd": band(SLOPE_D, x_all, x_all),
        "wxs": band(SMOOTH_D, x_all, x_all),
        "bdd": np.kron(eye8, band(SLOPE_D, slot_in, slot_out)),
        "bds": np.kron(eye8, band(SMOOTH_D, slot_in, slot_out)),
        "ysm": np.kron(np.eye(3), ys),
        "xsm": band(SMOOTH_I, inner, 4 * np.arange(quarter)),
        "bdx": np.kron(eye8, xs_edge),
        "g_low0": g[0][:, 0:256],
        "g_low1": g[0][:, 256:512],
        "g_high0": g[1][:, 0:256],
        "g_high1": g[1][:, 256:512],
    }
    place_of, blocks, at = {}, [], 0
    for name, part in parts.items():
        height = -(-part.shape[0] // 16) * 16
        block = np.zeros((height, 256), np.float32)
        block[: part.shape[0], : part.shape[1]] = part
        place_of[name] = (at, part.shape[0], part.shape[1])
        blocks.append(block)
        at += height
    return np.concatenate(blocks).astype(ml_dtypes.bfloat16), place_of, zs


def z_filter(v, count):
    for z in range(count):
        w = v[z : z + 7]
        smooth = w[3] * float(SMOOTH_D[3])
        slope = None
        for s in (1, 2, 3):
            smooth = smooth + (w[3 + s] + w[3 - s]) * float(SMOOTH_D[3 + s])
            term = (w[3 + s] - w[3 - s]) * float(SLOPE_D[3 + s])
            slope = term if slope is None else slope + term
        yield z, smooth, slope


def getter(place_of, w):
    def get(name, width=None):
        at, height, own_width = place_of[name]
        return w[at : at + height, 0 : (width or own_width)]

    return get


def row_mask(get, n_row, rows, gr, quarter_rows):
    row = lax.axis_index("row")
    lane = lax.broadcasted_iota(jnp.int32, (3 * quarter_rows, 3 * gr), 1)
    y_out = lax.rem(lane, gr) - R2
    outside = ((row == 0) & (y_out < 0)) | ((row == n_row - 1) & (y_out >= rows))
    return jnp.where(outside, 0.0, get("ysm").astype(F32)).astype(BF16)


def layers_to_sums(get, ysm, load, count, shape, u_ref, zf, planes, prod, sm):
    rows, cols = shape
    ext = rows + 2 * HALO
    gr = rows + 16
    n_rows = 6 * (rows // 4)
    half_rows = n_rows // 2
    rest = jnp.zeros((8, 128), F32)
    for tile in range(cols // 128):
        lanes = slice(tile * 128, tile * 128 + 128)
        for at in range(0, ext, 16):
            blocks = load(at, lanes)
            if at == rows + HALO:
                blocks = [block[0:8] for block in blocks]
            for z, smooth, slope in z_filter(blocks, count):
                if at == rows + HALO:
                    smooth = jnp.concatenate([smooth, rest], axis=0)
                    slope = jnp.concatenate([slope, rest], axis=0)
                zf[z, at : at + 16, lanes] = smooth.astype(BF16)
                zf[z, ext + at : ext + at + 16, lanes] = slope.astype(BF16)
    wy = get("wy")
    for z in range(count):
        out = jnp.dot(wy, zf[z], preferred_element_type=F32).astype(BF16)
        planes[0, z] = out[0:gr]
        planes[1, z] = out[gr : 2 * gr]
        planes[2, z] = out[2 * gr :]
    for at in range(0, count, GROUP):
        n = min(GROUP, count - at)
        grads = []
        for f, name in enumerate(("wxd", "wxs", "wxs")):
            part = planes[f, at : at + n].reshape(n * gr, cols)
            out = jnp.dot(part, get(name), preferred_element_type=F32)
            grads.append(out.astype(BF16).reshape(n, gr, cols))
        for c, (a, b) in enumerate(pair_table):
            prod[at : at + n, c * gr : (c + 1) * gr] = grads[a] * grads[b]
    for z in range(count):
        for half in range(2):
            part = prod[z, half * 3 * gr : (half + 1) * 3 * gr]
            out = jnp.dot(ysm, part, preferred_element_type=F32)
            sm[z, half * half_rows : (half + 1) * half_rows] = out.astype(BF16)
    out = jnp.dot(
        sm[...].reshape(count * n_rows, cols), get("xsm"), preferred_element_type=F32
    )
    u_ref[...] = out.reshape(count, n_rows, cols // 4)


def block_loader(vol, yud, rows):
    def layer(z, at, lanes):
        if at < HALO:
            return yud[z, at : at + 16, lanes].astype(F32)
        if at < HALO + rows:
            return vol[z, at - HALO : at - HALO + 16, lanes].astype(F32)
        return yud[z, at - rows : at - rows + 16, lanes].astype(F32)

    return layer


def spread_rows(first):
    shape = (16 * NEED, 16 * HALO)
    packed = lax.broadcasted_iota(jnp.int32, shape, 0)
    full = lax.broadcasted_iota(jnp.int32, shape, 1)
    z = lax.shift_right_logical(packed * 373, 12)
    return jnp.where(full == packed + z * (HALO - NEED) + first, 1.0, 0.0).astype(BF16)


def load_kernel(vol, s1, s2, vol_out, top, bottom, sems):
    depth, rows, cols = vol.shape
    odd = lax.rem(lax.axis_index("row"), 2) == 1
    copies = [
        pltpu.make_async_copy(vol.at[:, 0:HALO, :], top, sems.at[0]),
        pltpu.make_async_copy(vol.at[:, rows - HALO : rows, :], bottom, sems.at[1]),
        pltpu.make_async_copy(vol, vol_out, sems.at[2]),
    ]
    for copy in copies:
        copy.start()
    first_rows, last_rows = spread_rows(0), spread_rows(HALO - NEED)
    copies[0].wait()
    copies[1].wait()
    to_before = jnp.dot(
        first_rows, top[...].reshape(depth * HALO, cols), preferred_element_type=F32
    ).astype(BF16)
    to_after = jnp.dot(
        last_rows, bottom[...].reshape(depth * HALO, cols), preferred_element_type=F32
    ).astype(BF16)
    s1[...] = jnp.where(odd, to_before, to_after)
    s2[...] = jnp.where(odd, to_after, to_before)
    copies[2].wait()


def column_select(n_col, cols):
    n_side = 1 if n_col == 2 else 2
    shape = (SLOTS + 16 * n_side, cols)
    row = lax.broadcasted_iota(jnp.int32, shape, 0)
    lane = lax.broadcasted_iota(jnp.int32, shape, 1)
    picked = ((row >= 8) & (row < 14) & (lane == row - 8)) | (
        (row >= 14) & (row < 20) & (lane == row - 20 + cols)
    )
    for side in range(n_side):
        if n_col == 2:
            first = jnp.where(lax.axis_index("col") == 0, cols - HALO, 0)
        else:
            first = (cols - HALO, 0)[side]
        at = row - SLOTS - 16 * side
        picked = picked | ((at >= 0) & (at < 16) & (lane == at + first))
    return jnp.where(picked, 1.0, 0.0).astype(BF16)


def pick_columns(select, source):
    picked = lax.dot_general(select, source, NT, preferred_element_type=F32)
    messages = [picked[at : at + 16].astype(BF16) for at in range(SLOTS, picked.shape[0], 16)]
    return picked[0:SLOTS].astype(BF16), picked[8:24].astype(BF16), messages


def halve(chunk, at, value):
    n = value.shape[0]
    chunk[at : at + n] = value[:, 0:128]
    chunk[at + n : at + 2 * n] = value[:, 128:256]


def joined_halves(chunk, at, n):
    return jnp.concatenate([chunk[at : at + n], chunk[at + n : at + 2 * n]], axis=1)


def edges_kernel(n_col, vol, own, zmsg, *refs):
    depth, rows, cols = vol.shape
    gz = lax.axis_index("gz")
    refs, middles = refs[:-1], refs[-1]
    select = column_select(n_col, cols)
    for b in range(depth // 2):
        source = vol[2 * b : 2 * b + 2].reshape(2 * rows, cols)
        slots, middle, messages = pick_columns(select, source)
        own[b], middles[b] = slots, middle
        for ref, message in zip(refs, messages):
            ref[b] = message
    base = jnp.where(gz == 0, depth - R, 0)
    halve(zmsg, 0, vol[pl.ds(base, R)].reshape(R * rows, cols))
    first = jnp.where(gz == 0, (depth - EXTRA) // 2, 0)
    n = EXTRA // 2
    zmsg[2 * R * rows :] = middles[pl.ds(first, n)].reshape(n * 16, 128)


def pack_kernel(place_of, n_col, r1, r2, w, *refs):
    n_side = 1 if n_col == 2 else 2
    xown, (yud, halo, zcorner) = refs[:n_side], refs[n_side : n_side + 3]
    xmsgs, zxmsgs = refs[n_side + 3 : 2 * n_side + 3], refs[2 * n_side + 3 : 3 * n_side + 3]
    middles = refs[3 * n_side + 3]
    depth, cols = yud.shape[0], yud.shape[2]
    gz = lax.axis_index("gz")
    odd = lax.rem(lax.axis_index("row"), 2) == 1
    get = getter(place_of, w)
    got1, got2 = r1[...], r2[...]
    for at, name, part in (
        (0, "above", jnp.where(odd, got1, got2)),
        (HALO, "below", jnp.where(odd, got2, got1)),
    ):
        out = jnp.dot(get(name), part, preferred_element_type=F32).astype(BF16)
        yud[:, at : at + HALO, :] = out.reshape(depth, HALO, cols)
    select = column_select(n_col, cols)
    pairs, quads = depth // 2, depth // 4
    for b in range(quads):
        source = yud[4 * b : 4 * b + 4].reshape(4 * 2 * HALO, cols)
        slots, middle, messages = pick_columns(select, source)
        halo[b] = slots
        middles[b] = middle
        for ref, message in zip(xmsgs, messages):
            ref[pairs + b] = message
    for ref, part in zip(xmsgs, xown):
        ref[0:pairs] = part[...]
    base = jnp.where(gz == 0, depth - R, 0)
    edge = yud[pl.ds(base, R)].reshape(R * 2 * HALO, cols)
    halve(zcorner, 0, jnp.dot(get("corner"), edge, preferred_element_type=F32).astype(BF16))
    n2, n4 = EXTRA // 2, EXTRA // 4
    first2 = jnp.where(gz == 0, pairs - n2, 0)
    first4 = jnp.where(gz == 0, quads - n4, 0)
    zcorner[128:] = middles[pl.ds(first4, n4)].reshape(n4 * 16, 128)
    for ref, message in zip(zxmsgs, xmsgs):
        ref[0:n2] = message[pl.ds(first2, n2)]
        ref[n2:] = message[pl.ds(pairs + first4, n4)]


def stage_kernel(w, w_out):
    pass


FIRST = 6
GROUP = 2
EDGE = R
LAST = 7


def first_kernel(place_of, n_row, vol, yud, w, u_ref, *scratch):
    depth, rows, cols = vol.shape
    get = getter(place_of, w)
    ysm = row_mask(get, n_row, rows, rows + 16, rows // 4)
    base = jnp.where(lax.axis_index("gz") == 0, depth - EDGE - FIRST - R, 0)
    layer = block_loader(vol, yud, rows)
    load = lambda at, lanes: [layer(base + k, at, lanes) for k in range(FIRST + 2 * R)]
    layers_to_sums(get, ysm, load, FIRST, (rows, cols), u_ref, *scratch)


def near_kernel(place_of, zs, n_row, vol, yud, zown, zcorner, u1, w, u_ref, send_ref, zext, *scratch):
    depth, rows, cols = vol.shape
    n_zq = zs.shape[1]
    get = getter(place_of, w)
    low = lax.axis_index("gz") == 0
    ysm = row_mask(get, n_row, rows, rows + 16, rows // 4)
    corner = jnp.dot(
        get("corner_back"), joined_halves(zcorner, 0, 64), preferred_element_type=F32
    ).astype(BF16).reshape(R, 2 * HALO, cols)
    zext[:, 0:HALO] = corner[:, 0:HALO]
    zext[:, HALO : HALO + rows] = joined_halves(zown, 0, R * rows).reshape(R, rows, cols)
    zext[:, HALO + rows :] = corner[:, HALO:]
    layer = block_loader(vol, yud, rows)
    start = jnp.where(low, depth - R, 0)
    outer = jnp.where(low, depth - 2 * R, R)

    def load(at, lanes):
        beyond = [zext[k, at : at + 16, lanes].astype(F32) for k in range(R)]
        inner = [layer(outer + k, at, lanes) for k in range(R)]
        middle = [layer(start + k, at, lanes) for k in range(R)]
        before = [jnp.where(low, inner[k], beyond[k]) for k in range(R)]
        after = [jnp.where(low, beyond[k], inner[k]) for k in range(R)]
        return before + middle + after

    layers_to_sums(get, ysm, load, EDGE, (rows, cols), u_ref, *scratch)
    sends = []
    for k in range(2):
        total = None
        for i in range(FIRST + EDGE):
            from_low = depth - EDGE - FIRST + i
            from_high = EDGE + i if i < FIRST else i - FIRST
            a = float(zs[from_low, n_zq - 2 + k])
            b = float(zs[from_high, k])
            if a == 0.0 and b == 0.0:
                continue
            term = (u1[i] if i < FIRST else u_ref[i - FIRST]) * jnp.where(low, a, b)
            total = term if total is None else total + term
        sends.append(total)
    send_ref[...] = jnp.concatenate(sends, axis=1).astype(BF16)


def last_layers(place_of, get, ysm, vol, yud, u_ref, *scratch):
    depth, rows, cols = vol.shape
    low = lax.axis_index("gz") == 0
    layer = block_loader(vol, yud, rows)
    base = jnp.where(low, -R, depth - LAST - R)
    before_on = jnp.where(low, 0.0, 1.0)
    after_on = jnp.where(low, 1.0, 0.0)

    def load(at, lanes):
        out = []
        for k in range(LAST + 2 * R):
            block = layer(jnp.clip(base + k, 0, depth - 1), at, lanes)
            if k < R:
                block = block * before_on
            elif k >= LAST + R:
                block = block * after_on
            out.append(block)
        return out

    layers_to_sums(get, ysm, load, LAST, (rows, cols), u_ref, *scratch)


def last_kernel(place_of, zs, n_row, n_col, vol, yud, own, halo, zown, zcorner, u1, u2, w,
                xs, zxs, own_ref, hs, hd, pstrip, u3, *scratch):
    depth, rows, cols = vol.shape
    gr = rows + 16
    quarter_rows, quarter = rows // 4, cols // 4
    get = getter(place_of, w)
    gz, col = lax.axis_index("gz"), lax.axis_index("col")
    low = gz == 0
    ysm = row_mask(get, n_row, rows, gr, quarter_rows)
    last_layers(place_of, get, ysm, vol, yud, u3, *scratch)
    slots = lax.broadcasted_iota(jnp.int32, (SLOTS, 128), 0)
    if n_col == 2:
        keep = ((slots < 8) & (col == 0)) | ((slots >= 21) & (col == 1))
    else:
        keep = (slots < 8) | (slots >= 21)

    def join(part, messages, b):
        sides = [messages[-1][b].astype(F32), messages[0][b].astype(F32)]
        return jnp.where(keep, jnp.concatenate(sides, axis=0), part)

    def from_middle(ref, at, b):
        rim = jnp.zeros((8, 128), F32)
        middle = ref[at + 16 * b : at + 16 * (b + 1)].astype(F32)
        return jnp.concatenate([rim, middle, rim], axis=0)

    lanes = lax.broadcasted_iota(jnp.int32, (SLOTS, 128), 1)

    def layers_of(pairs, quads):
        out = []
        for z in range(2 * len(pairs)):
            left, right = pairs[z // 2], quads[z // 4]
            if z % 2:
                left = pltpu.roll(left, 64, 1)
            turn = (rows - 32 * (z % 4)) % 128
            if turn:
                right = pltpu.roll(right, turn, 1)
            out.append(jnp.where(lanes < rows, left, right))
        return out

    n2, n4 = EXTRA // 2, EXTRA // 4
    own_layers = layers_of(
        [join(own[b].astype(F32), xs, b) for b in range(depth // 2)],
        [join(halo[b].astype(F32), xs, depth // 2 + b) for b in range(depth // 4)],
    )
    at = 2 * R * rows
    beyond = layers_of(
        [join(from_middle(zown, at, b), zxs, b) for b in range(n2)],
        [join(from_middle(zcorner, 128, b), zxs, n2 + b) for b in range(n4)],
    )
    count = depth + 8
    zero = [jnp.zeros((SLOTS, 128), F32)] * R
    at_low = zero + own_layers + beyond[0:11]
    at_high = beyond[1:12] + own_layers + zero
    layers = [jnp.where(low, a, b) for a, b in zip(at_low, at_high)]
    for z, smooth, slope in z_filter(layers, count):
        hs[SLOTS * z : SLOTS * (z + 1)] = smooth.astype(BF16)
        hd[SLOTS * z : SLOTS * (z + 1)] = slope.astype(BF16)
    p01 = lax.dot_general(
        get("wy_strip", 128), hs[...], NT, preferred_element_type=F32
    ).astype(BF16)
    p2 = lax.dot_general(
        get("wy_strip_slope", 128), hd[...], NT, preferred_element_type=F32
    ).astype(BF16)
    n = count // 8
    groups = [slice(256 * c, 256 * (c + 1)) for c in range(n)]
    stacks = [
        jnp.concatenate([p[:, g] for g in groups], axis=0) for p in (p01[0:gr], p01[gr:], p2)
    ]
    grads = [
        jnp.dot(stack, get(name), preferred_element_type=F32).astype(BF16).reshape(n, gr, 256)
        for stack, name in zip(stacks, ("bdd", "bds", "bds"))
    ]
    for c, (a, b) in enumerate(pair_table):
        pstrip[:, c * gr : (c + 1) * gr] = grads[a] * grads[b]
    slot = lax.rem(lax.broadcasted_iota(jnp.int32, (3 * quarter_rows, 256), 1), SLOTS)
    outside_x = ((col == 0) & (slot < 8)) | ((col == n_col - 1) & (slot >= 14))
    smoothed = []
    for c in range(n):
        for half in range(2):
            part = pstrip[c, half * 3 * gr : (half + 1) * 3 * gr]
            out = jnp.dot(ysm, part, preferred_element_type=F32)
            smoothed.append(jnp.where(outside_x, 0.0, out).astype(BF16))
    u = jnp.dot(jnp.concatenate(smoothed, axis=0), get("bdx"), preferred_element_type=F32)
    n_rows = 6 * quarter_rows
    u = u.astype(BF16)
    sums = []
    for name in ("0", "1"):
        at = jnp.where(low, place_of["g_low" + name][0], place_of["g_high" + name][0])
        total = None
        for c in range(n):
            g = w[pl.ds(pl.multiple_of(at + 64 * c, 16), 64), :]
            term = jnp.dot(u[n_rows * c : n_rows * (c + 1)], g, preferred_element_type=F32)
            total = term if total is None else total + term
        sums += [total[:, 0:quarter], total[:, 128 : 128 + quarter]]
    for q in range(depth // 4):
        total = sums[q]
        for i in range(depth):
            if i < FIRST:
                u, from_low, from_high = u1[i], depth - EDGE - FIRST + i, EDGE + i
            elif i < FIRST + EDGE:
                k = i - FIRST
                u, from_low, from_high = u2[k], depth - EDGE + k, k
            else:
                k = i - FIRST - EDGE
                u, from_low, from_high = u3[k], k, depth - LAST + k
            a, b = float(zs[from_low, q + 2]), float(zs[from_high, q + 2])
            if a == 0.0 and b == 0.0:
                continue
            total = total + u * jnp.where(low, a, b)
        own_ref[:, q] = total.reshape(6, quarter_rows, quarter)


def add_kernel(own, got, out):
    n_q, quarter = own.shape[1], own.shape[3]
    low = lax.axis_index("gz") == 0
    parts = [
        got[:, k * quarter : (k + 1) * quarter].astype(F32).reshape(own.shape[0], -1, quarter)
        for k in range(2)
    ]
    for q in range(n_q):
        total = own[:, q]
        if q < 2:
            total = total + parts[q] * jnp.where(low, 0.0, 1.0)
        if q >= n_q - 2:
            total = total + parts[q - n_q + 2] * jnp.where(low, 1.0, 0.0)
        out[:, q] = total


def call(body, outs, operands, scratch, name, flops=0, aliases=None, n_hbm=0):
    vmem = pl.BlockSpec(memory_space=pltpu.VMEM)
    hbm = pl.BlockSpec(memory_space=pltpu.HBM)
    operands = [
        pltpu.with_memory_space_constraint(o, pltpu.HBM) if i < n_hbm else o
        for i, o in enumerate(operands)
    ]
    moved = sum(o.size * o.dtype.itemsize for o in list(outs) + list(operands))
    return pl.pallas_call(
        body,
        out_shape=list(outs),
        in_specs=[hbm] * n_hbm + [vmem] * (len(operands) - n_hbm),
        out_specs=[vmem] * len(outs),
        scratch_shapes=scratch,
        input_output_aliases=aliases or {},
        compiler_params=pltpu.CompilerParams(vmem_limit_bytes=24 * 2**20),
        cost_estimate=pl.CostEstimate(flops=flops, bytes_accessed=moved, transcendentals=0),
        name=name,
    )(*operands)


def per_device(volume):
    depth, rows, cols = volume.shape
    n_row, n_col = lax.axis_size("row"), lax.axis_size("col")
    table, place_of, zs = weight_table(depth, rows, cols)
    ext = rows + 2 * HALO
    gr = rows + 16
    quarter_rows, quarter = rows // 4, cols // 4
    n_rows = 6 * quarter_rows
    n_side = 1 if n_col == 2 else 2
    pairs, quads = depth // 2, depth // 4
    n2, n4 = EXTRA // 2, EXTRA // 4
    sds = jax.ShapeDtypeStruct
    bf16 = lambda *shape: sds(shape, BF16)

    def scratch_for(count):
        return [
            pltpu.VMEM((count, 2 * ext, cols), BF16),
            pltpu.VMEM((3, count, gr, cols), BF16),
            pltpu.VMEM((count, 6 * gr, cols), BF16),
            pltpu.VMEM((count, n_rows, cols), BF16),
        ]

    layer_flops = 2 * cols * (3 * gr * 2 * ext + 3 * gr * cols + n_rows * 3 * gr + n_rows * quarter)

    dma = pltpu.SemaphoreType.DMA
    s1, s2, vol = call(
        load_kernel,
        [bf16(depth * NEED, cols)] * 2 + [bf16(depth, rows, cols)],
        [volume], [pltpu.VMEM((depth, HALO, cols), BF16)] * 2 + [dma((3,))], "load", n_hbm=1,
    )
    inner = [(i, i + 1) for i in range(1, n_row - 1, 2)]
    inner = inner + [(j, i) for i, j in inner]
    r2 = lax.ppermute(s2, "row", inner)
    r1 = lax.ppermute(s1, "row", [(i, i ^ 1) for i in range(n_row)])
    (w,) = call(
        stage_kernel, [bf16(*table.shape)], [jnp.asarray(table)], [], "stage", aliases={0: 0}
    )
    own, zmsg, *xown = call(
        lambda *refs: edges_kernel(n_col, *refs),
        [bf16(pairs, SLOTS, 128), bf16(2 * R * rows + n2 * 16, 128)]
        + [bf16(pairs, HALO, 128)] * n_side,
        [vol], [pltpu.VMEM((pairs, 16, 128), BF16)], "edges",
    )
    swap = [(0, 1), (1, 0)]
    zown = lax.ppermute(zmsg, "gz", swap)

    yud, halo, zcmsg, *messages = call(
        lambda *refs: pack_kernel(place_of, n_col, *refs),
        [bf16(depth, 2 * HALO, cols), bf16(quads, SLOTS, 128), bf16(128 + n4 * 16, 128)]
        + [bf16(pairs + quads, HALO, 128)] * n_side
        + [bf16(n2 + n4, HALO, 128)] * n_side,
        [r1, r2, w] + xown, [pltpu.VMEM((quads, 16, 128), BF16)], "pack",
    )
    zcorner = lax.ppermute(zcmsg, "gz", swap)
    xs, zxs = [], []
    for side in range(n_side):
        step = 1 - 2 * side
        line = swap if n_col == 2 else [
            (i, i + step) for i in range(n_col) if 0 <= i + step < n_col
        ]
        both = [(z * n_col + i, (1 - z) * n_col + j) for z in range(2) for i, j in line]
        xs.append(lax.ppermute(messages[side], "col", line))
        zxs.append(lax.ppermute(messages[n_side + side], ("gz", "col"), both))

    (u1,) = call(
        lambda *refs: first_kernel(place_of, n_row, *refs),
        [sds((FIRST, n_rows, quarter), F32)],
        [vol, yud, w], scratch_for(FIRST), "first", flops=FIRST * layer_flops,
    )
    u2, send = call(
        lambda *refs: near_kernel(place_of, zs, n_row, *refs),
        [sds((EDGE, n_rows, quarter), F32), bf16(n_rows, 2 * quarter)],
        [vol, yud, zown, zcorner, u1, w],
        [pltpu.VMEM((R, ext, cols), BF16)] + scratch_for(EDGE),
        "near", flops=EDGE * layer_flops,
    )
    sums = lax.ppermute(send, "gz", swap)

    def last_body(*refs):
        head, x_refs, zx_refs = refs[0:9], refs[9 : 9 + n_side], refs[9 + n_side : 9 + 2 * n_side]
        last_kernel(
            place_of, zs, n_row, n_col, *head, x_refs, zx_refs, *refs[9 + 2 * n_side :]
        )

    count = depth + 8
    (result,) = call(
        last_body,
        [sds((6, depth // 4, quarter_rows, quarter), F32)],
        [vol, yud, own, halo, zown, zcorner, u1, u2, w] + xs + zxs,
        [
            pltpu.VMEM((count * SLOTS, 128), BF16),
            pltpu.VMEM((count * SLOTS, 128), BF16),
            pltpu.VMEM((count // 8, 6 * gr, 256), BF16),
            pltpu.VMEM((LAST, n_rows, quarter), F32),
        ]
        + scratch_for(LAST),
        "last", flops=(LAST + 3) * layer_flops,
    )
    (out,) = call(add_kernel, [sds(result.shape, F32)], [result, sums], [], "add")
    return out


def solution(mesh):
    return jax.shard_map(
        per_device,
        mesh=mesh,
        in_specs=(P("gz", "row", "col"),),
        out_specs=P(None, "gz", "row", "col"),
        check_vma=False,
    )
```

```python
import jax
import jax.numpy as jnp
import ml_dtypes
import numpy as np
from jax import lax
from jax.experimental import pallas as pl
from jax.experimental.pallas import tpu as pltpu
from jax.sharding import PartitionSpec as P

R = 3
R2 = 8
HALO = 16
NEED = R + R2
EXTRA = 12
SLOTS = 32
NT = (((1,), (1,)), ((), ()))
F32 = jnp.float32
BF16 = jnp.bfloat16

pair_table = ((0, 0), (1, 1), (2, 2), (0, 1), (0, 2), (1, 2))


def gauss_taps(radius):
    offsets = np.arange(-radius, radius + 1).astype(np.float32)
    spread = np.float32(radius / 3.0)
    smooth = np.exp(-offsets * offsets / (np.float32(2.0) * spread * spread))
    smooth = smooth / np.sum(smooth)
    slopes = offsets * smooth
    slopes = slopes / np.sum(offsets * slopes)
    as_f32 = lambda t: t.astype(ml_dtypes.bfloat16).astype(np.float32)
    return as_f32(smooth), as_f32(slopes)


SMOOTH_D, SLOPE_D = gauss_taps(R)
SMOOTH_I, _ = gauss_taps(R2)


def band(taps, sources, targets):
    radius = len(taps) // 2
    gap = np.asarray(sources)[:, None] - np.asarray(targets)[None, :]
    return np.where(np.abs(gap) <= radius, taps[np.clip(gap + radius, 0, 2 * radius)], 0.0)


def weight_table(depth, rows, cols):
    ext = rows + 2 * HALO
    grad_rows = rows + 16
    far = 10**6
    y_in = np.arange(ext) - HALO
    y_out = np.arange(grad_rows) - R2
    smooth_y = band(SMOOTH_D, y_in, y_out).T
    slope_y = band(SLOPE_D, y_in, y_out).T
    zero = np.zeros_like(smooth_y)
    wy = np.block([[smooth_y, zero], [slope_y, zero], [zero, smooth_y]])
    order = np.concatenate([np.arange(rows), np.arange(HALO) - HALO, rows + np.arange(HALO)]) + HALO
    x_all = np.arange(cols)
    slot_in = np.full(SLOTS, far)
    slot_in[0:8] = cols + np.arange(8)
    slot_in[8:14] = np.arange(6)
    slot_in[14:20] = cols - 6 + np.arange(6)
    slot_in[21:32] = np.arange(-11, 0)
    slot_out = np.full(SLOTS, -far)
    slot_out[0:11] = np.arange(-8, 3)
    slot_out[11:19] = cols - 3 + np.arange(8)
    eye8 = np.eye(8)
    inner = np.where((x_all >= R) & (x_all < cols - R), x_all, far)
    quarter = cols // 4
    coarse_edge = np.full(8, 3 * far)
    coarse_edge[0:5] = [0, 1, 2, quarter - 2, quarter - 1]
    xs_edge = band(SMOOTH_I, slot_out, 4 * coarse_edge)
    ys = band(SMOOTH_I, y_out, 4 * np.arange(rows // 4)).T
    zs = band(SMOOTH_I, np.arange(depth), 4 * (np.arange(depth // 4 + 4) - 2))
    place = np.zeros((8, 128))
    for j in range(5):
        place[j, coarse_edge[j]] = 1.0
    own_z = 4 * np.arange(depth // 4)
    g = [
        np.einsum("zq,jx->zjqx", band(SMOOTH_I, np.arange(depth + 8) + first, own_z), place)
        for first in (0, -8)
    ]
    g = [t.reshape((depth + 8) * 8, len(own_z) * 128) for t in g]
    packed = np.arange(depth * NEED)
    above = np.zeros((depth * HALO, depth * NEED))
    above[packed + packed // NEED * (HALO - NEED) + HALO - NEED, packed] = 1.0
    below = np.zeros((depth * HALO, depth * NEED))
    below[packed + packed // NEED * (HALO - NEED), packed] = 1.0
    used = 2 * R + 13
    packed = np.arange(R * used)
    corner = np.zeros((64, R * 2 * HALO))
    corner[packed, packed + packed // used * (2 * HALO - used) + HALO - NEED] = 1.0
    parts = {
        "above": above,
        "below": below,
        "corner": corner,
        "corner_back": corner.T,
        "wy": wy,
        "wy_strip": np.concatenate([smooth_y, slope_y])[:, order],
        "wy_strip_slope": smooth_y[:, order],
        "wxd": band(SLOPE_D, x_all, x_all),
        "wxs": band(SMOOTH_D, x_all, x_all),
        "bdd": np.kron(eye8, band(SLOPE_D, slot_in, slot_out)),
        "bds": np.kron(eye8, band(SMOOTH_D, slot_in, slot_out)),
        "ysm": np.kron(np.eye(3), ys),
        "xsm": band(SMOOTH_I, inner, 4 * np.arange(quarter)),
        "bdx": np.kron(eye8, xs_edge),
        "g_low0": g[0][:, 0:256],
        "g_low1": g[0][:, 256:512],
        "g_high0": g[1][:, 0:256],
        "g_high1": g[1][:, 256:512],
    }
    place_of, blocks, at = {}, [], 0
    for name, part in parts.items():
        height = -(-part.shape[0] // 16) * 16
        block = np.zeros((height, 256), np.float32)
        block[: part.shape[0], : part.shape[1]] = part
        place_of[name] = (at, part.shape[0], part.shape[1])
        blocks.append(block)
        at += height
    return np.concatenate(blocks).astype(ml_dtypes.bfloat16), place_of, zs


def z_filter(v, count):
    for z in range(count):
        w = v[z : z + 7]
        smooth = w[3] * float(SMOOTH_D[3])
        slope = None
        for s in (1, 2, 3):
            smooth = smooth + (w[3 + s] + w[3 - s]) * float(SMOOTH_D[3 + s])
            term = (w[3 + s] - w[3 - s]) * float(SLOPE_D[3 + s])
            slope = term if slope is None else slope + term
        yield z, smooth, slope


def getter(place_of, w):
    def get(name, width=None):
        at, height, own_width = place_of[name]
        return w[at : at + height, 0 : (width or own_width)]

    return get


def row_mask(get, n_row, rows, gr, quarter_rows):
    row = lax.axis_index("row")
    lane = lax.broadcasted_iota(jnp.int32, (3 * quarter_rows, 3 * gr), 1)
    y_out = lax.rem(lane, gr) - R2
    outside = ((row == 0) & (y_out < 0)) | ((row == n_row - 1) & (y_out >= rows))
    return jnp.where(outside, 0.0, get("ysm").astype(F32)).astype(BF16)


def layers_to_sums(get, ysm, load, count, shape, u_ref, zf, planes, prod, sm):
    rows, cols = shape
    ext = rows + 2 * HALO
    gr = rows + 16
    n_rows = 6 * (rows // 4)
    half_rows = n_rows // 2
    rest = jnp.zeros((8, 128), F32)
    wy = get("wy")

    def z_filters(first, n):
        for tile in range(cols // 128):
            lanes = slice(tile * 128, tile * 128 + 128)
            for at in range(0, ext, 16):
                blocks = load(at, lanes, first, first + n + 2 * R)
                if at == rows + HALO:
                    blocks = [block[0:8] for block in blocks]
                for z, smooth, slope in z_filter(blocks, n):
                    if at == rows + HALO:
                        smooth = jnp.concatenate([smooth, rest], axis=0)
                        slope = jnp.concatenate([slope, rest], axis=0)
                    zf[first + z, at : at + 16, lanes] = smooth.astype(BF16)
                    zf[first + z, ext + at : ext + at + 16, lanes] = slope.astype(BF16)

    def y_filters(first, n):
        for z in range(first, first + n):
            out = jnp.dot(wy, zf[z], preferred_element_type=F32).astype(BF16)
            planes[0, z] = out[0:gr]
            planes[1, z] = out[gr : 2 * gr]
            planes[2, z] = out[2 * gr :]

    def x_filters(first, n):
        grads = []
        for f, name in enumerate(("wxd", "wxs", "wxs")):
            part = planes[f, first : first + n].reshape(n * gr, cols)
            out = jnp.dot(part, get(name), preferred_element_type=F32)
            grads.append(out.astype(BF16).reshape(n, gr, cols))
        for c, (a, b) in enumerate(pair_table):
            prod[first : first + n, c * gr : (c + 1) * gr] = grads[a] * grads[b]

    def y_smoothing(first, n):
        for z in range(first, first + n):
            for half in range(2):
                part = prod[z, half * 3 * gr : (half + 1) * 3 * gr]
                out = jnp.dot(ysm, part, preferred_element_type=F32)
                sm[z, half * half_rows : (half + 1) * half_rows] = out.astype(BF16)

    n_group = -(-count // GROUP)
    ends = [count * i // n_group for i in range(n_group + 1)]
    stages = (z_filters, y_filters, x_filters, y_smoothing)
    for step in range(n_group + len(stages) - 1):
        for k, stage in enumerate(stages):
            i = step - k
            if 0 <= i < n_group:
                stage(ends[i], ends[i + 1] - ends[i])
    out = jnp.dot(
        sm[...].reshape(count * n_rows, cols), get("xsm"), preferred_element_type=F32
    )
    u_ref[...] = out.reshape(count, n_rows, cols // 4)


def block_loader(vol, yud, rows):
    def layer(z, at, lanes):
        if at < HALO:
            return yud[z, at : at + 16, lanes].astype(F32)
        if at < HALO + rows:
            return vol[z, at - HALO : at - HALO + 16, lanes].astype(F32)
        return yud[z, at - rows : at - rows + 16, lanes].astype(F32)

    return layer


def spread_rows(first):
    shape = (16 * NEED, 16 * HALO)
    packed = lax.broadcasted_iota(jnp.int32, shape, 0)
    full = lax.broadcasted_iota(jnp.int32, shape, 1)
    z = lax.shift_right_logical(packed * 373, 12)
    return jnp.where(full == packed + z * (HALO - NEED) + first, 1.0, 0.0).astype(BF16)


def load_kernel(vol, s1, s2, vol_out, sems):
    depth, rows, cols = vol.shape
    odd = lax.rem(lax.axis_index("row"), 2) == 1
    parts = (slice(0, HALO), slice(rows - HALO, rows), slice(HALO, rows - HALO))
    copies = [
        pltpu.make_async_copy(vol.at[:, part, :], vol_out.at[:, part, :], sems.at[i])
        for i, part in enumerate(parts)
    ]
    for copy in copies:
        copy.start()
    first_rows, last_rows = spread_rows(0), spread_rows(HALO - NEED)
    copies[0].wait()
    copies[1].wait()
    to_before = jnp.dot(
        first_rows, vol_out[:, 0:HALO].reshape(depth * HALO, cols), preferred_element_type=F32
    ).astype(BF16)
    to_after = jnp.dot(
        last_rows, vol_out[:, rows - HALO :].reshape(depth * HALO, cols), preferred_element_type=F32
    ).astype(BF16)
    s1[...] = jnp.where(odd, to_before, to_after)
    s2[...] = jnp.where(odd, to_after, to_before)
    copies[2].wait()


def column_select(n_col, cols):
    n_side = 1 if n_col == 2 else 2
    shape = (SLOTS + 16 * n_side, cols)
    row = lax.broadcasted_iota(jnp.int32, shape, 0)
    lane = lax.broadcasted_iota(jnp.int32, shape, 1)
    picked = ((row >= 8) & (row < 14) & (lane == row - 8)) | (
        (row >= 14) & (row < 20) & (lane == row - 20 + cols)
    )
    for side in range(n_side):
        if n_col == 2:
            first = jnp.where(lax.axis_index("col") == 0, cols - HALO, 0)
        else:
            first = (cols - HALO, 0)[side]
        at = row - SLOTS - 16 * side
        picked = picked | ((at >= 0) & (at < 16) & (lane == at + first))
    return jnp.where(picked, 1.0, 0.0).astype(BF16)


def pick_columns(select, source):
    picked = lax.dot_general(select, source, NT, preferred_element_type=F32)
    messages = [picked[at : at + 16].astype(BF16) for at in range(SLOTS, picked.shape[0], 16)]
    return picked[0:SLOTS].astype(BF16), picked[8:24].astype(BF16), messages


def halve(chunk, at, value):
    n = value.shape[0]
    chunk[at : at + n] = value[:, 0:128]
    chunk[at + n : at + 2 * n] = value[:, 128:256]


def joined_halves(chunk, at, n):
    return jnp.concatenate([chunk[at : at + n], chunk[at + n : at + 2 * n]], axis=1)


def edges_kernel(n_col, vol, own, zmsg, *refs):
    depth, rows, cols = vol.shape
    gz = lax.axis_index("gz")
    refs, middles = refs[:-1], refs[-1]
    select = column_select(n_col, cols)
    for b in range(depth // 2):
        source = vol[2 * b : 2 * b + 2].reshape(2 * rows, cols)
        slots, middle, messages = pick_columns(select, source)
        own[b], middles[b] = slots, middle
        for ref, message in zip(refs, messages):
            ref[b] = message
    base = jnp.where(gz == 0, depth - R, 0)
    halve(zmsg, 0, vol[pl.ds(base, R)].reshape(R * rows, cols))
    first = jnp.where(gz == 0, (depth - EXTRA) // 2, 0)
    n = EXTRA // 2
    zmsg[2 * R * rows :] = middles[pl.ds(first, n)].reshape(n * 16, 128)


def pack_kernel(place_of, n_col, r1, r2, w, *refs):
    n_side = 1 if n_col == 2 else 2
    xown, (yud, halo, zcorner) = refs[:n_side], refs[n_side : n_side + 3]
    xmsgs, zxmsgs = refs[n_side + 3 : 2 * n_side + 3], refs[2 * n_side + 3 : 3 * n_side + 3]
    middles = refs[3 * n_side + 3]
    depth, cols = yud.shape[0], yud.shape[2]
    gz = lax.axis_index("gz")
    odd = lax.rem(lax.axis_index("row"), 2) == 1
    get = getter(place_of, w)
    got1, got2 = r1[...], r2[...]
    for at, name, part in (
        (0, "above", jnp.where(odd, got1, got2)),
        (HALO, "below", jnp.where(odd, got2, got1)),
    ):
        out = jnp.dot(get(name), part, preferred_element_type=F32).astype(BF16)
        yud[:, at : at + HALO, :] = out.reshape(depth, HALO, cols)
    select = column_select(n_col, cols)
    pairs, quads = depth // 2, depth // 4
    for b in range(quads):
        source = yud[4 * b : 4 * b + 4].reshape(4 * 2 * HALO, cols)
        slots, middle, messages = pick_columns(select, source)
        halo[b] = slots
        middles[b] = middle
        for ref, message in zip(xmsgs, messages):
            ref[pairs + b] = message
    for ref, part in zip(xmsgs, xown):
        ref[0:pairs] = part[...]
    base = jnp.where(gz == 0, depth - R, 0)
    edge = yud[pl.ds(base, R)].reshape(R * 2 * HALO, cols)
    halve(zcorner, 0, jnp.dot(get("corner"), edge, preferred_element_type=F32).astype(BF16))
    n2, n4 = EXTRA // 2, EXTRA // 4
    first2 = jnp.where(gz == 0, pairs - n2, 0)
    first4 = jnp.where(gz == 0, quads - n4, 0)
    zcorner[128:] = middles[pl.ds(first4, n4)].reshape(n4 * 16, 128)
    for ref, message in zip(zxmsgs, xmsgs):
        ref[0:n2] = message[pl.ds(first2, n2)]
        ref[n2:] = message[pl.ds(pairs + first4, n4)]


def stage_kernel(w, w_out):
    pass


FIRST = 7
GROUP = 3
EDGE = R
LAST = 6


def first_kernel(place_of, n_row, vol, yud, w, u_ref, *scratch):
    depth, rows, cols = vol.shape
    get = getter(place_of, w)
    ysm = row_mask(get, n_row, rows, rows + 16, rows // 4)
    base = jnp.where(lax.axis_index("gz") == 0, depth - EDGE - FIRST - R, 0)
    layer = block_loader(vol, yud, rows)
    load = lambda at, lanes, lo, hi: [layer(base + k, at, lanes) for k in range(lo, hi)]
    layers_to_sums(get, ysm, load, FIRST, (rows, cols), u_ref, *scratch)


def near_kernel(place_of, zs, n_row, vol, yud, zown, zcorner, u1, w, u_ref, send_ref, zext, *scratch):
    depth, rows, cols = vol.shape
    n_zq = zs.shape[1]
    get = getter(place_of, w)
    low = lax.axis_index("gz") == 0
    ysm = row_mask(get, n_row, rows, rows + 16, rows // 4)
    corner = jnp.dot(
        get("corner_back"), joined_halves(zcorner, 0, 64), preferred_element_type=F32
    ).astype(BF16).reshape(R, 2 * HALO, cols)
    zext[:, 0:HALO] = corner[:, 0:HALO]
    zext[:, HALO : HALO + rows] = joined_halves(zown, 0, R * rows).reshape(R, rows, cols)
    zext[:, HALO + rows :] = corner[:, HALO:]
    layer = block_loader(vol, yud, rows)
    start = jnp.where(low, depth - R, 0)
    outer = jnp.where(low, depth - 2 * R, R)

    def load(at, lanes, lo, hi):
        out = []
        for k in range(lo, hi):
            if R <= k < 2 * R:
                out.append(layer(start + k - R, at, lanes))
                continue
            i = k % R
            inner = layer(outer + i, at, lanes)
            beyond = zext[i, at : at + 16, lanes].astype(F32)
            first, second = (inner, beyond) if k < R else (beyond, inner)
            out.append(jnp.where(low, first, second))
        return out

    layers_to_sums(get, ysm, load, EDGE, (rows, cols), u_ref, *scratch)
    sends = []
    for k in range(2):
        total = None
        for i in range(FIRST + EDGE):
            from_low = depth - EDGE - FIRST + i
            from_high = EDGE + i if i < FIRST else i - FIRST
            a = float(zs[from_low, n_zq - 2 + k])
            b = float(zs[from_high, k])
            if a == 0.0 and b == 0.0:
                continue
            term = (u1[i] if i < FIRST else u_ref[i - FIRST]) * jnp.where(low, a, b)
            total = term if total is None else total + term
        sends.append(total)
    send_ref[...] = jnp.concatenate(sends, axis=1).astype(BF16)


def last_layers(place_of, get, ysm, vol, yud, u_ref, *scratch):
    depth, rows, cols = vol.shape
    low = lax.axis_index("gz") == 0
    layer = block_loader(vol, yud, rows)
    base = jnp.where(low, -R, depth - LAST - R)
    before_on = jnp.where(low, 0.0, 1.0)
    after_on = jnp.where(low, 1.0, 0.0)

    def load(at, lanes, lo, hi):
        out = []
        for k in range(lo, hi):
            block = layer(jnp.clip(base + k, 0, depth - 1), at, lanes)
            if k < R:
                block = block * before_on
            elif k >= LAST + R:
                block = block * after_on
            out.append(block)
        return out

    layers_to_sums(get, ysm, load, LAST, (rows, cols), u_ref, *scratch)


def last_kernel(place_of, zs, n_row, n_col, vol, yud, own, halo, zown, zcorner, u1, u2, w,
                xs, zxs, own_ref, hs, hd, pstrip, u3, *scratch):
    depth, rows, cols = vol.shape
    gr = rows + 16
    quarter_rows, quarter = rows // 4, cols // 4
    get = getter(place_of, w)
    gz, col = lax.axis_index("gz"), lax.axis_index("col")
    low = gz == 0
    ysm = row_mask(get, n_row, rows, gr, quarter_rows)
    last_layers(place_of, get, ysm, vol, yud, u3, *scratch)
    slots = lax.broadcasted_iota(jnp.int32, (SLOTS, 128), 0)
    if n_col == 2:
        keep = ((slots < 8) & (col == 0)) | ((slots >= 21) & (col == 1))
    else:
        keep = (slots < 8) | (slots >= 21)

    def join(part, messages, b):
        sides = [messages[-1][b].astype(F32), messages[0][b].astype(F32)]
        return jnp.where(keep, jnp.concatenate(sides, axis=0), part)

    def from_middle(ref, at, b):
        rim = jnp.zeros((8, 128), F32)
        middle = ref[at + 16 * b : at + 16 * (b + 1)].astype(F32)
        return jnp.concatenate([rim, middle, rim], axis=0)

    lanes = lax.broadcasted_iota(jnp.int32, (SLOTS, 128), 1)

    def layers_of(pairs, quads):
        out = []
        for z in range(2 * len(pairs)):
            left, right = pairs[z // 2], quads[z // 4]
            if z % 2:
                left = pltpu.roll(left, 64, 1)
            turn = (rows - 32 * (z % 4)) % 128
            if turn:
                right = pltpu.roll(right, turn, 1)
            out.append(jnp.where(lanes < rows, left, right))
        return out

    n2, n4 = EXTRA // 2, EXTRA // 4
    own_layers = layers_of(
        [join(own[b].astype(F32), xs, b) for b in range(depth // 2)],
        [join(halo[b].astype(F32), xs, depth // 2 + b) for b in range(depth // 4)],
    )
    at = 2 * R * rows
    beyond = layers_of(
        [join(from_middle(zown, at, b), zxs, b) for b in range(n2)],
        [join(from_middle(zcorner, 128, b), zxs, n2 + b) for b in range(n4)],
    )
    count = depth + 8
    zero = [jnp.zeros((SLOTS, 128), F32)] * R
    at_low = zero + own_layers + beyond[0:11]
    at_high = beyond[1:12] + own_layers + zero
    layers = [jnp.where(low, a, b) for a, b in zip(at_low, at_high)]
    for z, smooth, slope in z_filter(layers, count):
        hs[SLOTS * z : SLOTS * (z + 1)] = smooth.astype(BF16)
        hd[SLOTS * z : SLOTS * (z + 1)] = slope.astype(BF16)
    p01 = lax.dot_general(
        get("wy_strip", 128), hs[...], NT, preferred_element_type=F32
    ).astype(BF16)
    p2 = lax.dot_general(
        get("wy_strip_slope", 128), hd[...], NT, preferred_element_type=F32
    ).astype(BF16)
    n = count // 8
    groups = [slice(256 * c, 256 * (c + 1)) for c in range(n)]
    stacks = [
        jnp.concatenate([p[:, g] for g in groups], axis=0) for p in (p01[0:gr], p01[gr:], p2)
    ]
    grads = [
        jnp.dot(stack, get(name), preferred_element_type=F32).astype(BF16).reshape(n, gr, 256)
        for stack, name in zip(stacks, ("bdd", "bds", "bds"))
    ]
    for c, (a, b) in enumerate(pair_table):
        pstrip[:, c * gr : (c + 1) * gr] = grads[a] * grads[b]
    slot = lax.rem(lax.broadcasted_iota(jnp.int32, (3 * quarter_rows, 256), 1), SLOTS)
    outside_x = ((col == 0) & (slot < 8)) | ((col == n_col - 1) & (slot >= 14))
    smoothed = []
    for c in range(n):
        for half in range(2):
            part = pstrip[c, half * 3 * gr : (half + 1) * 3 * gr]
            out = jnp.dot(ysm, part, preferred_element_type=F32)
            smoothed.append(jnp.where(outside_x, 0.0, out).astype(BF16))
    u = jnp.dot(jnp.concatenate(smoothed, axis=0), get("bdx"), preferred_element_type=F32)
    n_rows = 6 * quarter_rows
    u = u.astype(BF16)
    sums = []
    for name in ("0", "1"):
        at = jnp.where(low, place_of["g_low" + name][0], place_of["g_high" + name][0])
        total = None
        for c in range(n):
            g = w[pl.ds(pl.multiple_of(at + 64 * c, 16), 64), :]
            term = jnp.dot(u[n_rows * c : n_rows * (c + 1)], g, preferred_element_type=F32)
            total = term if total is None else total + term
        sums += [total[:, 0:quarter], total[:, 128 : 128 + quarter]]
    for q in range(depth // 4):
        total = sums[q]
        for i in range(depth):
            if i < FIRST:
                u, from_low, from_high = u1[i], depth - EDGE - FIRST + i, EDGE + i
            elif i < FIRST + EDGE:
                k = i - FIRST
                u, from_low, from_high = u2[k], depth - EDGE + k, k
            else:
                k = i - FIRST - EDGE
                u, from_low, from_high = u3[k], k, depth - LAST + k
            a, b = float(zs[from_low, q + 2]), float(zs[from_high, q + 2])
            if a == 0.0 and b == 0.0:
                continue
            total = total + u * jnp.where(low, a, b)
        own_ref[:, q] = total.reshape(6, quarter_rows, quarter)


def add_kernel(own, got, out):
    n_q, quarter = own.shape[1], own.shape[3]
    low = lax.axis_index("gz") == 0
    parts = [
        got[:, k * quarter : (k + 1) * quarter].astype(F32).reshape(own.shape[0], -1, quarter)
        for k in range(2)
    ]
    for q in range(n_q):
        total = own[:, q]
        if q < 2:
            total = total + parts[q] * jnp.where(low, 0.0, 1.0)
        if q >= n_q - 2:
            total = total + parts[q - n_q + 2] * jnp.where(low, 1.0, 0.0)
        out[:, q] = total


def call(body, outs, operands, scratch, name, flops=0, aliases=None, n_hbm=0):
    vmem = pl.BlockSpec(memory_space=pltpu.VMEM)
    hbm = pl.BlockSpec(memory_space=pltpu.HBM)
    operands = [
        pltpu.with_memory_space_constraint(o, pltpu.HBM) if i < n_hbm else o
        for i, o in enumerate(operands)
    ]
    moved = sum(o.size * o.dtype.itemsize for o in list(outs) + list(operands))
    return pl.pallas_call(
        body,
        out_shape=list(outs),
        in_specs=[hbm] * n_hbm + [vmem] * (len(operands) - n_hbm),
        out_specs=[vmem] * len(outs),
        scratch_shapes=scratch,
        input_output_aliases=aliases or {},
        compiler_params=pltpu.CompilerParams(vmem_limit_bytes=24 * 2**20),
        cost_estimate=pl.CostEstimate(flops=flops, bytes_accessed=moved, transcendentals=0),
        name=name,
    )(*operands)


def per_device(volume):
    depth, rows, cols = volume.shape
    n_row, n_col = lax.axis_size("row"), lax.axis_size("col")
    table, place_of, zs = weight_table(depth, rows, cols)
    ext = rows + 2 * HALO
    gr = rows + 16
    quarter_rows, quarter = rows // 4, cols // 4
    n_rows = 6 * quarter_rows
    n_side = 1 if n_col == 2 else 2
    pairs, quads = depth // 2, depth // 4
    n2, n4 = EXTRA // 2, EXTRA // 4
    sds = jax.ShapeDtypeStruct
    bf16 = lambda *shape: sds(shape, BF16)

    def scratch_for(count):
        return [
            pltpu.VMEM((count, 2 * ext, cols), BF16),
            pltpu.VMEM((3, count, gr, cols), BF16),
            pltpu.VMEM((count, 6 * gr, cols), BF16),
            pltpu.VMEM((count, n_rows, cols), BF16),
        ]

    layer_flops = 2 * cols * (3 * gr * 2 * ext + 3 * gr * cols + n_rows * 3 * gr + n_rows * quarter)

    dma = pltpu.SemaphoreType.DMA
    s1, s2, vol = call(
        load_kernel,
        [bf16(depth * NEED, cols)] * 2 + [bf16(depth, rows, cols)],
        [volume], [dma((3,))], "load", n_hbm=1,
    )
    inner = [(i, i + 1) for i in range(1, n_row - 1, 2)]
    inner = inner + [(j, i) for i, j in inner]
    r2 = lax.ppermute(s2, "row", inner)
    r1 = lax.ppermute(s1, "row", [(i, i ^ 1) for i in range(n_row)])
    (w,) = call(
        stage_kernel, [bf16(*table.shape)], [jnp.asarray(table)], [], "stage", aliases={0: 0}
    )
    own, zmsg, *xown = call(
        lambda *refs: edges_kernel(n_col, *refs),
        [bf16(pairs, SLOTS, 128), bf16(2 * R * rows + n2 * 16, 128)]
        + [bf16(pairs, HALO, 128)] * n_side,
        [vol], [pltpu.VMEM((pairs, 16, 128), BF16)], "edges",
    )
    swap = [(0, 1), (1, 0)]
    zown = lax.ppermute(zmsg, "gz", swap)

    yud, halo, zcmsg, *messages = call(
        lambda *refs: pack_kernel(place_of, n_col, *refs),
        [bf16(depth, 2 * HALO, cols), bf16(quads, SLOTS, 128), bf16(128 + n4 * 16, 128)]
        + [bf16(pairs + quads, HALO, 128)] * n_side
        + [bf16(n2 + n4, HALO, 128)] * n_side,
        [r1, r2, w] + xown, [pltpu.VMEM((quads, 16, 128), BF16)], "pack",
    )
    zcorner = lax.ppermute(zcmsg, "gz", swap)
    xs, zxs = [], []
    for side in range(n_side):
        step = 1 - 2 * side
        line = swap if n_col == 2 else [
            (i, i + step) for i in range(n_col) if 0 <= i + step < n_col
        ]
        both = [(z * n_col + i, (1 - z) * n_col + j) for z in range(2) for i, j in line]
        xs.append(lax.ppermute(messages[side], "col", line))
        zxs.append(lax.ppermute(messages[n_side + side], ("gz", "col"), both))

    (u1,) = call(
        lambda *refs: first_kernel(place_of, n_row, *refs),
        [sds((FIRST, n_rows, quarter), F32)],
        [vol, yud, w], scratch_for(FIRST), "first", flops=FIRST * layer_flops,
    )
    u2, send = call(
        lambda *refs: near_kernel(place_of, zs, n_row, *refs),
        [sds((EDGE, n_rows, quarter), F32), bf16(n_rows, 2 * quarter)],
        [vol, yud, zown, zcorner, u1, w],
        [pltpu.VMEM((R, ext, cols), BF16)] + scratch_for(EDGE),
        "near", flops=EDGE * layer_flops,
    )
    sums = lax.ppermute(send, "gz", swap)

    def last_body(*refs):
        head, x_refs, zx_refs = refs[0:9], refs[9 : 9 + n_side], refs[9 + n_side : 9 + 2 * n_side]
        last_kernel(
            place_of, zs, n_row, n_col, *head, x_refs, zx_refs, *refs[9 + 2 * n_side :]
        )

    count = depth + 8
    (result,) = call(
        last_body,
        [sds((6, depth // 4, quarter_rows, quarter), F32)],
        [vol, yud, own, halo, zown, zcorner, u1, u2, w] + xs + zxs,
        [
            pltpu.VMEM((count * SLOTS, 128), BF16),
            pltpu.VMEM((count * SLOTS, 128), BF16),
            pltpu.VMEM((count // 8, 6 * gr, 256), BF16),
            pltpu.VMEM((LAST, n_rows, quarter), F32),
        ]
        + scratch_for(LAST),
        "last", flops=(LAST + 3) * layer_flops,
    )
    (out,) = call(add_kernel, [sds(result.shape, F32)], [result, sums], [], "add")
    return out


def solution(mesh):
    return jax.shard_map(
        per_device,
        mesh=mesh,
        in_specs=(P("gz", "row", "col"),),
        out_specs=P(None, "gz", "row", "col"),
        check_vma=False,
    )
```

```python
import jax
import jax.numpy as jnp
import ml_dtypes
import numpy as np
from jax import lax
from jax.experimental import pallas as pl
from jax.experimental.pallas import tpu as pltpu
from jax.sharding import PartitionSpec as P

R = 3
R2 = 8
HALO = 16
NEED = R + R2
EXTRA = 12
SLOTS = 32
NT = (((1,), (1,)), ((), ()))
F32 = jnp.float32
BF16 = jnp.bfloat16

pair_table = ((0, 0), (1, 1), (2, 2), (0, 1), (0, 2), (1, 2))


def gauss_taps(radius):
    offsets = np.arange(-radius, radius + 1).astype(np.float32)
    spread = np.float32(radius / 3.0)
    smooth = np.exp(-offsets * offsets / (np.float32(2.0) * spread * spread))
    smooth = smooth / np.sum(smooth)
    slopes = offsets * smooth
    slopes = slopes / np.sum(offsets * slopes)
    as_f32 = lambda t: t.astype(ml_dtypes.bfloat16).astype(np.float32)
    return as_f32(smooth), as_f32(slopes)


SMOOTH_D, SLOPE_D = gauss_taps(R)
SMOOTH_I, _ = gauss_taps(R2)


def band(taps, sources, targets):
    radius = len(taps) // 2
    gap = np.asarray(sources)[:, None] - np.asarray(targets)[None, :]
    return np.where(np.abs(gap) <= radius, taps[np.clip(gap + radius, 0, 2 * radius)], 0.0)


def weight_table(depth, rows, cols):
    ext = rows + 2 * HALO
    grad_rows = rows + 16
    far = 10**6
    y_in = np.arange(ext) - HALO
    y_in[0:HALO] = far
    y_in[0:NEED] = np.arange(-NEED, 0)
    y_out = np.arange(grad_rows) - R2
    smooth_y = band(SMOOTH_D, y_in, y_out).T
    slope_y = band(SLOPE_D, y_in, y_out).T
    zero = np.zeros_like(smooth_y)
    wy = np.block([[smooth_y, zero], [slope_y, zero], [zero, smooth_y]])
    order = np.concatenate([np.arange(rows) + HALO, np.arange(HALO), rows + HALO + np.arange(HALO)])
    x_all = np.arange(cols)
    slot_in = np.full(SLOTS, far)
    slot_in[0:8] = cols + np.arange(8)
    slot_in[8:14] = np.arange(6)
    slot_in[14:20] = cols - 6 + np.arange(6)
    slot_in[21:32] = np.arange(-11, 0)
    slot_out = np.full(SLOTS, -far)
    slot_out[0:11] = np.arange(-8, 3)
    slot_out[11:19] = cols - 3 + np.arange(8)
    eye8 = np.eye(8)
    inner = np.where((x_all >= R) & (x_all < cols - R), x_all, far)
    quarter = cols // 4
    coarse_edge = np.full(8, 3 * far)
    coarse_edge[0:5] = [0, 1, 2, quarter - 2, quarter - 1]
    xs_edge = band(SMOOTH_I, slot_out, 4 * coarse_edge)
    ys = band(SMOOTH_I, y_out, 4 * np.arange(rows // 4)).T
    zs = band(SMOOTH_I, np.arange(depth), 4 * (np.arange(depth // 4 + 4) - 2))
    place = np.zeros((8, quarter))
    for j in range(5):
        place[j, coarse_edge[j]] = 1.0
    own_z = 4 * np.arange(depth // 4)
    g = [
        np.einsum("zq,jx->zjqx", band(SMOOTH_I, np.arange(depth + 8) + first, own_z), place)
        for first in (0, -8)
    ]
    g = [t.reshape((depth + 8) * 8, len(own_z) * quarter) for t in g]
    packed = np.arange(depth * NEED)
    spread = np.zeros((depth * HALO, depth * NEED))
    spread[packed + packed // NEED * (HALO - NEED), packed] = 1.0
    used = NEED + 8
    packed = np.arange(R * used)
    corner = np.zeros((64, R * 2 * HALO))
    below = (packed % used >= NEED) * (HALO - NEED)
    corner[packed, packed + packed // used * (2 * HALO - used) + below] = 1.0
    groups = [
        {"spread": spread},
        {"corner": corner, "corner_back": corner.T},
        {"wy": wy},
        {
            "wy_strip": np.concatenate([smooth_y, slope_y])[:, order],
            "wy_strip_slope": smooth_y[:, order],
        },
        {"wxd": band(SLOPE_D, x_all, x_all)},
        {"wxs": band(SMOOTH_D, x_all, x_all)},
        {"bdd": np.kron(eye8, band(SLOPE_D, slot_in, slot_out))},
        {"bds": np.kron(eye8, band(SMOOTH_D, slot_in, slot_out))},
        {"ysm": np.kron(np.eye(3), ys)},
        {"xsm": band(SMOOTH_I, inner, 4 * np.arange(quarter)), "bdx": np.kron(eye8, xs_edge)},
        {"g_low": g[0]},
        {"g_high": g[1]},
    ]
    place_of, blocks, at = {}, [], 0
    for group in groups:
        height = max(-(-part.shape[0] // 16) * 16 for part in group.values())
        block = np.zeros((height, 256), np.float32)
        for lane, (name, part) in zip((0, 128), group.items()):
            block[: part.shape[0], lane : lane + part.shape[1]] = part
            place_of[name] = (at, lane) + part.shape
        blocks.append(block)
        at += height
    return np.concatenate(blocks).astype(ml_dtypes.bfloat16), place_of, zs


def z_filter(v, count):
    for z in range(count):
        w = v[z : z + 7]
        smooth = w[3] * float(SMOOTH_D[3])
        slope = None
        for s in (1, 2, 3):
            smooth = smooth + (w[3 + s] + w[3 - s]) * float(SMOOTH_D[3 + s])
            term = (w[3 + s] - w[3 - s]) * float(SLOPE_D[3 + s])
            slope = term if slope is None else slope + term
        yield z, smooth, slope


def getter(place_of, w):
    def get(name, width=None):
        at, lane, height, own_width = place_of[name]
        return w[at : at + height, lane : lane + (width or own_width)]

    return get


def row_mask(get, n_row, rows, gr, quarter_rows):
    row = lax.axis_index("row")
    lane = lax.broadcasted_iota(jnp.int32, (3 * quarter_rows, 3 * gr), 1)
    y_out = lax.rem(lane, gr) - R2
    outside = ((row == 0) & (y_out < 0)) | ((row == n_row - 1) & (y_out >= rows))
    return jnp.where(outside, 0.0, get("ysm").astype(F32)).astype(BF16)


def layers_to_sums(get, ysm, load, count, shape, u_ref, zf, planes, prod, sm):
    rows, cols = shape
    ext = rows + 2 * HALO
    gr = rows + 16
    n_rows = 6 * (rows // 4)
    half_rows = n_rows // 2
    rest = jnp.zeros((8, 128), F32)
    wy = get("wy")

    def z_filters(first, n):
        for tile in range(cols // 128):
            lanes = slice(tile * 128, tile * 128 + 128)
            for at in range(0, ext, 16):
                blocks = load(at, lanes, first, first + n + 2 * R)
                if at == rows + HALO:
                    blocks = [block[0:8] for block in blocks]
                for z, smooth, slope in z_filter(blocks, n):
                    if at == rows + HALO:
                        smooth = jnp.concatenate([smooth, rest], axis=0)
                        slope = jnp.concatenate([slope, rest], axis=0)
                    zf[first + z, at : at + 16, lanes] = smooth.astype(BF16)
                    zf[first + z, ext + at : ext + at + 16, lanes] = slope.astype(BF16)

    def y_filters(first, n):
        for z in range(first, first + n):
            out = jnp.dot(wy, zf[z], preferred_element_type=F32).astype(BF16)
            planes[0, z] = out[0:gr]
            planes[1, z] = out[gr : 2 * gr]
            planes[2, z] = out[2 * gr :]

    def x_filters(first, n):
        grads = []
        for f, name in enumerate(("wxd", "wxs", "wxs")):
            part = planes[f, first : first + n].reshape(n * gr, cols)
            out = jnp.dot(part, get(name), preferred_element_type=F32)
            grads.append(out.astype(BF16).reshape(n, gr, cols))
        for c, (a, b) in enumerate(pair_table):
            prod[first : first + n, c * gr : (c + 1) * gr] = grads[a] * grads[b]

    def y_smoothing(first, n):
        for z in range(first, first + n):
            for half in range(2):
                part = prod[z, half * 3 * gr : (half + 1) * 3 * gr]
                out = jnp.dot(ysm, part, preferred_element_type=F32)
                sm[z, half * half_rows : (half + 1) * half_rows] = out.astype(BF16)

    n_group = -(-count // GROUP)
    ends = [count * i // n_group for i in range(n_group + 1)]
    stages = (z_filters, y_filters, x_filters, y_smoothing)
    for step in range(n_group + len(stages) - 1):
        for k, stage in enumerate(stages):
            i = step - k
            if 0 <= i < n_group:
                stage(ends[i], ends[i + 1] - ends[i])
    out = jnp.dot(
        sm[...].reshape(count * n_rows, cols), get("xsm"), preferred_element_type=F32
    )
    u_ref[...] = out.reshape(count, n_rows, cols // 4)


def block_loader(vol, yud, rows):
    def layer(z, at, lanes):
        if at < HALO:
            return yud[z, at : at + 16, lanes].astype(F32)
        if at < HALO + rows:
            return vol[z, at - HALO : at - HALO + 16, lanes].astype(F32)
        return yud[z, at - rows : at - rows + 16, lanes].astype(F32)

    return layer


def spread_rows(first):
    shape = (16 * NEED, 16 * HALO)
    packed = lax.broadcasted_iota(jnp.int32, shape, 0)
    full = lax.broadcasted_iota(jnp.int32, shape, 1)
    z = lax.shift_right_logical(packed * 373, 12)
    return jnp.where(full == packed + z * (HALO - NEED) + first, 1.0, 0.0).astype(BF16)


def load_kernel(vol, s1, s2, vol_out, sems):
    depth, rows, cols = vol.shape
    odd = lax.rem(lax.axis_index("row"), 2) == 1
    parts = (slice(0, HALO), slice(rows - HALO, rows), slice(HALO, rows - HALO))
    copies = [
        pltpu.make_async_copy(vol.at[:, part, :], vol_out.at[:, part, :], sems.at[i])
        for i, part in enumerate(parts)
    ]
    for copy in copies:
        copy.start()
    first_rows, last_rows = spread_rows(0), spread_rows(HALO - NEED)
    copies[0].wait()
    copies[1].wait()
    to_before = jnp.dot(
        first_rows, vol_out[:, 0:HALO].reshape(depth * HALO, cols), preferred_element_type=F32
    ).astype(BF16)
    to_after = jnp.dot(
        last_rows, vol_out[:, rows - HALO :].reshape(depth * HALO, cols), preferred_element_type=F32
    ).astype(BF16)
    s1[...] = jnp.where(odd, to_before, to_after)
    s2[...] = jnp.where(odd, to_after, to_before)
    copies[2].wait()


def column_select(n_col, cols):
    n_side = 1 if n_col == 2 else 2
    shape = (SLOTS + 16 * n_side, cols)
    row = lax.broadcasted_iota(jnp.int32, shape, 0)
    lane = lax.broadcasted_iota(jnp.int32, shape, 1)
    picked = ((row >= 8) & (row < 14) & (lane == row - 8)) | (
        (row >= 14) & (row < 20) & (lane == row - 20 + cols)
    )
    for side in range(n_side):
        if n_col == 2:
            first = jnp.where(lax.axis_index("col") == 0, cols - HALO, 0)
        else:
            first = (cols - HALO, 0)[side]
        at = row - SLOTS - 16 * side
        picked = picked | ((at >= 0) & (at < 16) & (lane == at + first))
    return jnp.where(picked, 1.0, 0.0).astype(BF16)


def pick_columns(select, source):
    picked = lax.dot_general(select, source, NT, preferred_element_type=F32)
    messages = [picked[at : at + 16].astype(BF16) for at in range(SLOTS, picked.shape[0], 16)]
    return picked[0:SLOTS].astype(BF16), picked[8:24].astype(BF16), messages


def halve(chunk, at, value):
    n = value.shape[0]
    chunk[at : at + n] = value[:, 0:128]
    chunk[at + n : at + 2 * n] = value[:, 128:256]


def joined_halves(chunk, at, n):
    return jnp.concatenate([chunk[at : at + n], chunk[at + n : at + 2 * n]], axis=1)


def edges_kernel(n_col, vol, own, zmsg, *refs):
    depth, rows, cols = vol.shape
    gz = lax.axis_index("gz")
    refs, middles = refs[:-1], refs[-1]
    select = column_select(n_col, cols)
    for b in range(depth // 2):
        source = vol[2 * b : 2 * b + 2].reshape(2 * rows, cols)
        slots, middle, messages = pick_columns(select, source)
        own[b], middles[b] = slots, middle
        for ref, message in zip(refs, messages):
            ref[b] = message
    base = jnp.where(gz == 0, depth - R, 0)
    halve(zmsg, 0, vol[pl.ds(base, R)].reshape(R * rows, cols))
    first = jnp.where(gz == 0, (depth - EXTRA) // 2, 0)
    n = EXTRA // 2
    zmsg[2 * R * rows :] = middles[pl.ds(first, n)].reshape(n * 16, 128)


def pack_kernel(place_of, n_col, r1, r2, w, *refs):
    n_side = 1 if n_col == 2 else 2
    xown, (yud, halo, zcorner) = refs[:n_side], refs[n_side : n_side + 3]
    xmsgs, zxmsgs = refs[n_side + 3 : 2 * n_side + 3], refs[2 * n_side + 3 : 3 * n_side + 3]
    middles = refs[3 * n_side + 3]
    depth, cols = yud.shape[0], yud.shape[2]
    gz = lax.axis_index("gz")
    odd = lax.rem(lax.axis_index("row"), 2) == 1
    get = getter(place_of, w)
    got1, got2 = r1[...], r2[...]
    for at, part in (
        (0, jnp.where(odd, got1, got2)),
        (HALO, jnp.where(odd, got2, got1)),
    ):
        out = jnp.dot(get("spread"), part, preferred_element_type=F32).astype(BF16)
        yud[:, at : at + HALO, :] = out.reshape(depth, HALO, cols)
    select = column_select(n_col, cols)
    pairs, quads = depth // 2, depth // 4
    for b in range(quads):
        source = yud[4 * b : 4 * b + 4].reshape(4 * 2 * HALO, cols)
        slots, middle, messages = pick_columns(select, source)
        halo[b] = slots
        middles[b] = middle
        for ref, message in zip(xmsgs, messages):
            ref[pairs + b] = message
    for ref, part in zip(xmsgs, xown):
        ref[0:pairs] = part[...]
    base = jnp.where(gz == 0, depth - R, 0)
    edge = yud[pl.ds(base, R)].reshape(R * 2 * HALO, cols)
    halve(zcorner, 0, jnp.dot(get("corner"), edge, preferred_element_type=F32).astype(BF16))
    n2, n4 = EXTRA // 2, EXTRA // 4
    first2 = jnp.where(gz == 0, pairs - n2, 0)
    first4 = jnp.where(gz == 0, quads - n4, 0)
    zcorner[128:] = middles[pl.ds(first4, n4)].reshape(n4 * 16, 128)
    for ref, message in zip(zxmsgs, xmsgs):
        ref[0:n2] = message[pl.ds(first2, n2)]
        ref[n2:] = message[pl.ds(pairs + first4, n4)]


def stage_kernel(w, w_out):
    pass


FIRST = 5
GROUP = 4
EDGE = R
LAST = 8


def first_kernel(place_of, n_row, vol, yud, w, u_ref, *scratch):
    depth, rows, cols = vol.shape
    get = getter(place_of, w)
    ysm = row_mask(get, n_row, rows, rows + 16, rows // 4)
    base = jnp.where(lax.axis_index("gz") == 0, depth - EDGE - FIRST - R, 0)
    layer = block_loader(vol, yud, rows)
    load = lambda at, lanes, lo, hi: [layer(base + k, at, lanes) for k in range(lo, hi)]
    layers_to_sums(get, ysm, load, FIRST, (rows, cols), u_ref, *scratch)


def near_kernel(place_of, zs, n_row, vol, yud, zown, zcorner, u1, w, u_ref, send_ref, zext, *scratch):
    depth, rows, cols = vol.shape
    n_zq = zs.shape[1]
    get = getter(place_of, w)
    low = lax.axis_index("gz") == 0
    ysm = row_mask(get, n_row, rows, rows + 16, rows // 4)
    corner = jnp.dot(
        get("corner_back"), joined_halves(zcorner, 0, 64), preferred_element_type=F32
    ).astype(BF16).reshape(R, 2 * HALO, cols)
    zext[:, 0:HALO] = corner[:, 0:HALO]
    zext[:, HALO : HALO + rows] = joined_halves(zown, 0, R * rows).reshape(R, rows, cols)
    zext[:, HALO + rows :] = corner[:, HALO:]
    layer = block_loader(vol, yud, rows)
    start = jnp.where(low, depth - R, 0)
    outer = jnp.where(low, depth - 2 * R, R)

    def load(at, lanes, lo, hi):
        out = []
        for k in range(lo, hi):
            if R <= k < 2 * R:
                out.append(layer(start + k - R, at, lanes))
                continue
            i = k % R
            inner = layer(outer + i, at, lanes)
            beyond = zext[i, at : at + 16, lanes].astype(F32)
            first, second = (inner, beyond) if k < R else (beyond, inner)
            out.append(jnp.where(low, first, second))
        return out

    layers_to_sums(get, ysm, load, EDGE, (rows, cols), u_ref, *scratch)
    sends = []
    for k in range(2):
        total = None
        for i in range(FIRST + EDGE):
            from_low = depth - EDGE - FIRST + i
            from_high = EDGE + i if i < FIRST else i - FIRST
            a = float(zs[from_low, n_zq - 2 + k])
            b = float(zs[from_high, k])
            if a == 0.0 and b == 0.0:
                continue
            term = (u1[i] if i < FIRST else u_ref[i - FIRST]) * jnp.where(low, a, b)
            total = term if total is None else total + term
        sends.append(total)
    send_ref[...] = jnp.concatenate(sends, axis=1).astype(BF16)


def last_layers(place_of, get, ysm, vol, yud, u_ref, *scratch):
    depth, rows, cols = vol.shape
    low = lax.axis_index("gz") == 0
    layer = block_loader(vol, yud, rows)
    base = jnp.where(low, -R, depth - LAST - R)
    before_on = jnp.where(low, 0.0, 1.0)
    after_on = jnp.where(low, 1.0, 0.0)

    def load(at, lanes, lo, hi):
        out = []
        for k in range(lo, hi):
            block = layer(jnp.clip(base + k, 0, depth - 1), at, lanes)
            if k < R:
                block = block * before_on
            elif k >= LAST + R:
                block = block * after_on
            out.append(block)
        return out

    layers_to_sums(get, ysm, load, LAST, (rows, cols), u_ref, *scratch)


def strip_tools(n_col, rows):
    col = lax.axis_index("col")
    slots = lax.broadcasted_iota(jnp.int32, (SLOTS, 128), 0)
    if n_col == 2:
        keep = ((slots < 8) & (col == 0)) | ((slots >= 21) & (col == 1))
    else:
        keep = (slots < 8) | (slots >= 21)

    def join(part, messages, b):
        sides = [messages[-1][b].astype(F32), messages[0][b].astype(F32)]
        return jnp.where(keep, jnp.concatenate(sides, axis=0), part)

    lanes = lax.broadcasted_iota(jnp.int32, (SLOTS, 128), 1)

    def layers_of(pairs, quads):
        out = []
        for z in range(2 * len(pairs)):
            left, right = pairs[z // 2], quads[z // 4]
            if z % 2:
                left = pltpu.roll(left, 64, 1)
            turn = (rows - 32 * (z % 4)) % 128
            if turn:
                right = pltpu.roll(right, turn, 1)
            out.append(jnp.where(lanes < rows, left, right))
        return out

    return join, layers_of


def beyond_kernel(n_col, rows, zown, zcorner, zxs, out):
    join, layers_of = strip_tools(n_col, rows)

    def from_middle(ref, at, b):
        rim = jnp.zeros((8, 128), F32)
        middle = ref[at + 16 * b : at + 16 * (b + 1)].astype(F32)
        return jnp.concatenate([rim, middle, rim], axis=0)

    n2, n4 = EXTRA // 2, EXTRA // 4
    layers = layers_of(
        [join(from_middle(zown, 2 * R * rows, b), zxs, b) for b in range(n2)],
        [join(from_middle(zcorner, 128, b), zxs, n2 + b) for b in range(n4)],
    )
    for k, layer in enumerate(layers):
        out[k] = layer.astype(BF16)


def last_kernel(place_of, zs, n_row, n_col, vol, yud, own, halo, far, u1, u2, w, xs, own_ref,
                hs, hd, pstrip, u3, *scratch):
    depth, rows, cols = vol.shape
    gr = rows + 16
    quarter_rows, quarter = rows // 4, cols // 4
    get = getter(place_of, w)
    gz, col = lax.axis_index("gz"), lax.axis_index("col")
    low = gz == 0
    ysm = row_mask(get, n_row, rows, gr, quarter_rows)
    last_layers(place_of, get, ysm, vol, yud, u3, *scratch)
    join, layers_of = strip_tools(n_col, rows)
    own_layers = layers_of(
        [join(own[b].astype(F32), xs, b) for b in range(depth // 2)],
        [join(halo[b].astype(F32), xs, depth // 2 + b) for b in range(depth // 4)],
    )
    beyond = [far[k].astype(F32) for k in range(EXTRA)]
    count = depth + 8
    zero = [jnp.zeros((SLOTS, 128), F32)] * R
    at_low = zero + own_layers + beyond[0:11]
    at_high = beyond[1:12] + own_layers + zero
    layers = [jnp.where(low, a, b) for a, b in zip(at_low, at_high)]
    for z, smooth, slope in z_filter(layers, count):
        hs[SLOTS * z : SLOTS * (z + 1)] = smooth.astype(BF16)
        hd[SLOTS * z : SLOTS * (z + 1)] = slope.astype(BF16)
    p01 = lax.dot_general(
        get("wy_strip", 128), hs[...], NT, preferred_element_type=F32
    ).astype(BF16)
    p2 = lax.dot_general(
        get("wy_strip_slope", 128), hd[...], NT, preferred_element_type=F32
    ).astype(BF16)
    n = count // 8
    groups = [slice(256 * c, 256 * (c + 1)) for c in range(n)]
    stacks = [
        jnp.concatenate([p[:, g] for g in groups], axis=0) for p in (p01[0:gr], p01[gr:], p2)
    ]
    grads = [
        jnp.dot(stack, get(name), preferred_element_type=F32).astype(BF16).reshape(n, gr, 256)
        for stack, name in zip(stacks, ("bdd", "bds", "bds"))
    ]
    for c, (a, b) in enumerate(pair_table):
        pstrip[:, c * gr : (c + 1) * gr] = grads[a] * grads[b]
    slot = lax.rem(lax.broadcasted_iota(jnp.int32, (3 * quarter_rows, 256), 1), SLOTS)
    outside_x = ((col == 0) & (slot < 8)) | ((col == n_col - 1) & (slot >= 14))
    smoothed = []
    for c in range(n):
        for half in range(2):
            part = pstrip[c, half * 3 * gr : (half + 1) * 3 * gr]
            out = jnp.dot(ysm, part, preferred_element_type=F32)
            smoothed.append(jnp.where(outside_x, 0.0, out).astype(BF16))
    u = jnp.dot(jnp.concatenate(smoothed, axis=0), get("bdx"), preferred_element_type=F32)
    n_rows = 6 * quarter_rows
    u = u.astype(BF16)
    at = jnp.where(low, place_of["g_low"][0], place_of["g_high"][0])
    total = None
    for c in range(n):
        g = w[pl.ds(pl.multiple_of(at + 64 * c, 16), 64), :]
        term = jnp.dot(u[n_rows * c : n_rows * (c + 1)], g, preferred_element_type=F32)
        total = term if total is None else total + term
    sums = [total[:, quarter * q : quarter * (q + 1)] for q in range(depth // 4)]
    for q in range(depth // 4):
        total = sums[q]
        for i in range(depth):
            if i < FIRST:
                u, from_low, from_high = u1[i], depth - EDGE - FIRST + i, EDGE + i
            elif i < FIRST + EDGE:
                k = i - FIRST
                u, from_low, from_high = u2[k], depth - EDGE + k, k
            else:
                k = i - FIRST - EDGE
                u, from_low, from_high = u3[k], k, depth - LAST + k
            a, b = float(zs[from_low, q + 2]), float(zs[from_high, q + 2])
            if a == 0.0 and b == 0.0:
                continue
            total = total + u * jnp.where(low, a, b)
        own_ref[:, q] = total.reshape(6, quarter_rows, quarter)


def add_kernel(own, got, out):
    n_q, quarter = own.shape[1], own.shape[3]
    low = lax.axis_index("gz") == 0
    parts = [
        got[:, k * quarter : (k + 1) * quarter].astype(F32).reshape(own.shape[0], -1, quarter)
        for k in range(2)
    ]
    for q in range(n_q):
        total = own[:, q]
        if q < 2:
            total = total + parts[q] * jnp.where(low, 0.0, 1.0)
        if q >= n_q - 2:
            total = total + parts[q - n_q + 2] * jnp.where(low, 1.0, 0.0)
        out[:, q] = total


def call(body, outs, operands, scratch, name, flops=0, aliases=None, n_hbm=0):
    vmem = pl.BlockSpec(memory_space=pltpu.VMEM)
    hbm = pl.BlockSpec(memory_space=pltpu.HBM)
    operands = [
        pltpu.with_memory_space_constraint(o, pltpu.HBM) if i < n_hbm else o
        for i, o in enumerate(operands)
    ]
    moved = sum(o.size * o.dtype.itemsize for o in list(outs) + list(operands))
    return pl.pallas_call(
        body,
        out_shape=list(outs),
        in_specs=[hbm] * n_hbm + [vmem] * (len(operands) - n_hbm),
        out_specs=[vmem] * len(outs),
        scratch_shapes=scratch,
        input_output_aliases=aliases or {},
        compiler_params=pltpu.CompilerParams(vmem_limit_bytes=24 * 2**20),
        cost_estimate=pl.CostEstimate(flops=flops, bytes_accessed=moved, transcendentals=0),
        name=name,
    )(*operands)


def per_device(volume):
    depth, rows, cols = volume.shape
    n_row, n_col = lax.axis_size("row"), lax.axis_size("col")
    table, place_of, zs = weight_table(depth, rows, cols)
    ext = rows + 2 * HALO
    gr = rows + 16
    quarter_rows, quarter = rows // 4, cols // 4
    n_rows = 6 * quarter_rows
    n_side = 1 if n_col == 2 else 2
    pairs, quads = depth // 2, depth // 4
    n2, n4 = EXTRA // 2, EXTRA // 4
    sds = jax.ShapeDtypeStruct
    bf16 = lambda *shape: sds(shape, BF16)

    def scratch_for(count):
        return [
            pltpu.VMEM((count, 2 * ext, cols), BF16),
            pltpu.VMEM((3, count, gr, cols), BF16),
            pltpu.VMEM((count, 6 * gr, cols), BF16),
            pltpu.VMEM((count, n_rows, cols), BF16),
        ]

    layer_flops = 2 * cols * (3 * gr * 2 * ext + 3 * gr * cols + n_rows * 3 * gr + n_rows * quarter)

    dma = pltpu.SemaphoreType.DMA
    s1, s2, vol = call(
        load_kernel,
        [bf16(depth * NEED, cols)] * 2 + [bf16(depth, rows, cols)],
        [volume], [dma((3,))], "load", n_hbm=1,
    )
    inner = [(i, i + 1) for i in range(1, n_row - 1, 2)]
    inner = inner + [(j, i) for i, j in inner]
    r2 = lax.ppermute(s2, "row", inner)
    r1 = lax.ppermute(s1, "row", [(i, i ^ 1) for i in range(n_row)])
    (w,) = call(
        stage_kernel, [bf16(*table.shape)], [jnp.asarray(table)], [], "stage", aliases={0: 0}
    )
    own, zmsg, *xown = call(
        lambda *refs: edges_kernel(n_col, *refs),
        [bf16(pairs, SLOTS, 128), bf16(2 * R * rows + n2 * 16, 128)]
        + [bf16(pairs, HALO, 128)] * n_side,
        [vol], [pltpu.VMEM((pairs, 16, 128), BF16)], "edges",
    )
    swap = [(0, 1), (1, 0)]
    zown = lax.ppermute(zmsg, "gz", swap)

    yud, halo, zcmsg, *messages = call(
        lambda *refs: pack_kernel(place_of, n_col, *refs),
        [bf16(depth, 2 * HALO, cols), bf16(quads, SLOTS, 128), bf16(128 + n4 * 16, 128)]
        + [bf16(pairs + quads, HALO, 128)] * n_side
        + [bf16(n2 + n4, HALO, 128)] * n_side,
        [r1, r2, w] + xown, [pltpu.VMEM((quads, 16, 128), BF16)], "pack",
    )
    zcorner = lax.ppermute(zcmsg, "gz", swap)
    xs, zxs = [], []
    for side in range(n_side):
        step = 1 - 2 * side
        line = swap if n_col == 2 else [
            (i, i + step) for i in range(n_col) if 0 <= i + step < n_col
        ]
        both = [(z * n_col + i, (1 - z) * n_col + j) for z in range(2) for i, j in line]
        xs.append(lax.ppermute(messages[side], "col", line))
        zxs.append(lax.ppermute(messages[n_side + side], ("gz", "col"), both))

    (u1,) = call(
        lambda *refs: first_kernel(place_of, n_row, *refs),
        [sds((FIRST, n_rows, quarter), F32)],
        [vol, yud, w], scratch_for(FIRST), "first", flops=FIRST * layer_flops,
    )
    u2, send = call(
        lambda *refs: near_kernel(place_of, zs, n_row, *refs),
        [sds((EDGE, n_rows, quarter), F32), bf16(n_rows, 2 * quarter)],
        [vol, yud, zown, zcorner, u1, w],
        [pltpu.VMEM((R, ext, cols), BF16)] + scratch_for(EDGE),
        "near", flops=EDGE * layer_flops,
    )
    sums = lax.ppermute(send, "gz", swap)

    (far,) = call(
        lambda zown, zcorner, *refs: beyond_kernel(
            n_col, rows, zown, zcorner, refs[:n_side], refs[n_side]
        ),
        [bf16(EXTRA, SLOTS, 128)], [zown, zcorner] + zxs, [], "beyond", flops=EDGE * layer_flops,
    )

    def last_body(*refs):
        head, x_refs, tail = refs[0:8], refs[8 : 8 + n_side], refs[8 + n_side :]
        last_kernel(place_of, zs, n_row, n_col, *head, x_refs, *tail)

    count = depth + 8
    (result,) = call(
        last_body,
        [sds((6, depth // 4, quarter_rows, quarter), F32)],
        [vol, yud, own, halo, far, u1, u2, w] + xs,
        [
            pltpu.VMEM((count * SLOTS, 128), BF16),
            pltpu.VMEM((count * SLOTS, 128), BF16),
            pltpu.VMEM((count // 8, 6 * gr, 256), BF16),
            pltpu.VMEM((LAST, n_rows, quarter), F32),
        ]
        + scratch_for(LAST),
        "last", flops=(LAST + 3) * layer_flops,
    )
    (out,) = call(add_kernel, [sds(result.shape, F32)], [result, sums], [], "add")
    return out


def solution(mesh):
    return jax.shard_map(
        per_device,
        mesh=mesh,
        in_specs=(P("gz", "row", "col"),),
        out_specs=P(None, "gz", "row", "col"),
        check_vma=False,
    )
```

```python
import jax
import jax.numpy as jnp
import ml_dtypes
import numpy as np
from jax import lax
from jax.experimental import pallas as pl
from jax.experimental.pallas import tpu as pltpu
from jax.sharding import PartitionSpec as P

R = 3
R2 = 8
HALO = 16
NEED = R + R2
EXTRA = 12
SLOTS = 32
NT = (((1,), (1,)), ((), ()))
F32 = jnp.float32
BF16 = jnp.bfloat16

pair_table = ((0, 0), (1, 1), (2, 2), (0, 1), (0, 2), (1, 2))


def gauss_taps(radius):
    offsets = np.arange(-radius, radius + 1).astype(np.float32)
    spread = np.float32(radius / 3.0)
    smooth = np.exp(-offsets * offsets / (np.float32(2.0) * spread * spread))
    smooth = smooth / np.sum(smooth)
    slopes = offsets * smooth
    slopes = slopes / np.sum(offsets * slopes)
    as_f32 = lambda t: t.astype(ml_dtypes.bfloat16).astype(np.float32)
    return as_f32(smooth), as_f32(slopes)


SMOOTH_D, SLOPE_D = gauss_taps(R)
SMOOTH_I, _ = gauss_taps(R2)


def band(taps, sources, targets):
    radius = len(taps) // 2
    gap = np.asarray(sources)[:, None] - np.asarray(targets)[None, :]
    return np.where(np.abs(gap) <= radius, taps[np.clip(gap + radius, 0, 2 * radius)], 0.0)


def weight_table(depth, rows, cols):
    ext = rows + 2 * HALO
    grad_rows = rows + 16
    far = 10**6
    y_in = np.arange(ext) - HALO
    y_out = np.arange(grad_rows) - R2
    smooth_y = band(SMOOTH_D, y_in, y_out).T
    slope_y = band(SLOPE_D, y_in, y_out).T
    zero = np.zeros_like(smooth_y)
    wy = np.block([[smooth_y, zero], [slope_y, zero], [zero, smooth_y]])
    order = np.concatenate([np.arange(rows), np.arange(HALO) - HALO, rows + np.arange(HALO)]) + HALO
    x_all = np.arange(cols)
    slot_in = np.full(SLOTS, far)
    slot_in[0:8] = cols + np.arange(8)
    slot_in[8:14] = np.arange(6)
    slot_in[14:20] = cols - 6 + np.arange(6)
    slot_in[21:32] = np.arange(-11, 0)
    slot_out = np.full(SLOTS, -far)
    slot_out[0:11] = np.arange(-8, 3)
    slot_out[11:19] = cols - 3 + np.arange(8)
    eye8 = np.eye(8)
    inner = np.where((x_all >= R) & (x_all < cols - R), x_all, far)
    quarter = cols // 4
    coarse_edge = np.full(8, 3 * far)
    coarse_edge[0:5] = [0, 1, 2, quarter - 2, quarter - 1]
    xs_edge = band(SMOOTH_I, slot_out, 4 * coarse_edge)
    ys = band(SMOOTH_I, y_out, 4 * np.arange(rows // 4)).T
    zs = band(SMOOTH_I, np.arange(depth), 4 * (np.arange(depth // 4 + 4) - 2))
    place = np.zeros((8, 128))
    for j in range(5):
        place[j, coarse_edge[j]] = 1.0
    own_z = 4 * np.arange(depth // 4)
    g = [
        np.einsum("zq,jx->zjqx", band(SMOOTH_I, np.arange(depth + 8) + first, own_z), place)
        for first in (0, -8)
    ]
    g = [t.reshape((depth + 8) * 8, len(own_z) * 128) for t in g]
    packed = np.arange(depth * NEED)
    above = np.zeros((depth * HALO, depth * NEED))
    above[packed + packed // NEED * (HALO - NEED) + HALO - NEED, packed] = 1.0
    below = np.zeros((depth * HALO, depth * NEED))
    below[packed + packed // NEED * (HALO - NEED), packed] = 1.0
    used = 2 * R + 13
    packed = np.arange(R * used)
    corner = np.zeros((64, R * 2 * HALO))
    corner[packed, packed + packed // used * (2 * HALO - used) + HALO - NEED] = 1.0
    parts = {
        "above": above,
        "below": below,
        "corner": corner,
        "corner_back": corner.T,
        "wy": wy,
        "wy_strip": np.concatenate([smooth_y, slope_y])[:, order],
        "wy_strip_slope": smooth_y[:, order],
        "wxd": band(SLOPE_D, x_all, x_all),
        "wxs": band(SMOOTH_D, x_all, x_all),
        "bdd": np.kron(eye8, band(SLOPE_D, slot_in, slot_out)),
        "bds": np.kron(eye8, band(SMOOTH_D, slot_in, slot_out)),
        "ysm": np.kron(np.eye(3), ys),
        "xsm": band(SMOOTH_I, inner, 4 * np.arange(quarter)),
        "bdx": np.kron(eye8, xs_edge),
        "g_low0": g[0][:, 0:256],
        "g_low1": g[0][:, 256:512],
        "g_high0": g[1][:, 0:256],
        "g_high1": g[1][:, 256:512],
    }
    place_of, blocks, at = {}, [], 0
    for name, part in parts.items():
        height = -(-part.shape[0] // 16) * 16
        block = np.zeros((height, 256), np.float32)
        block[: part.shape[0], : part.shape[1]] = part
        place_of[name] = (at, part.shape[0], part.shape[1])
        blocks.append(block)
        at += height
    return np.concatenate(blocks).astype(ml_dtypes.bfloat16), place_of, zs


def z_filter(v, count):
    for z in range(count):
        w = v[z : z + 7]
        smooth = w[3] * float(SMOOTH_D[3])
        slope = None
        for s in (1, 2, 3):
            smooth = smooth + (w[3 + s] + w[3 - s]) * float(SMOOTH_D[3 + s])
            term = (w[3 + s] - w[3 - s]) * float(SLOPE_D[3 + s])
            slope = term if slope is None else slope + term
        yield z, smooth, slope


def getter(place_of, w):
    def get(name, width=None):
        at, height, own_width = place_of[name]
        return w[at : at + height, 0 : (width or own_width)]

    return get


def row_mask(get, n_row, rows, gr, quarter_rows):
    row = lax.axis_index("row")
    lane = lax.broadcasted_iota(jnp.int32, (3 * quarter_rows, 3 * gr), 1)
    y_out = lax.rem(lane, gr) - R2
    outside = ((row == 0) & (y_out < 0)) | ((row == n_row - 1) & (y_out >= rows))
    return jnp.where(outside, 0.0, get("ysm").astype(F32)).astype(BF16)


def layers_to_sums(get, ysm, load, count, shape, u_ref, zf, planes, prod, sm):
    rows, cols = shape
    ext = rows + 2 * HALO
    gr = rows + 16
    n_rows = 6 * (rows // 4)
    half_rows = n_rows // 2
    rest = jnp.zeros((8, 128), F32)
    wy = get("wy")

    def z_filters(first, n):
        for tile in range(cols // 128):
            lanes = slice(tile * 128, tile * 128 + 128)
            for at in range(0, ext, 16):
                blocks = load(at, lanes, first, first + n + 2 * R)
                if at == rows + HALO:
                    blocks = [block[0:8] for block in blocks]
                for z, smooth, slope in z_filter(blocks, n):
                    if at == rows + HALO:
                        smooth = jnp.concatenate([smooth, rest], axis=0)
                        slope = jnp.concatenate([slope, rest], axis=0)
                    zf[first + z, at : at + 16, lanes] = smooth.astype(BF16)
                    zf[first + z, ext + at : ext + at + 16, lanes] = slope.astype(BF16)

    def y_filters(first, n):
        for z in range(first, first + n):
            out = jnp.dot(wy, zf[z], preferred_element_type=F32).astype(BF16)
            planes[0, z] = out[0:gr]
            planes[1, z] = out[gr : 2 * gr]
            planes[2, z] = out[2 * gr :]

    def x_filters(first, n):
        grads = []
        for f, name in enumerate(("wxd", "wxs", "wxs")):
            part = planes[f, first : first + n].reshape(n * gr, cols)
            out = jnp.dot(part, get(name), preferred_element_type=F32)
            grads.append(out.astype(BF16).reshape(n, gr, cols))
        for c, (a, b) in enumerate(pair_table):
            prod[first : first + n, c * gr : (c + 1) * gr] = grads[a] * grads[b]

    def y_smoothing(first, n):
        for z in range(first, first + n):
            for half in range(2):
                part = prod[z, half * 3 * gr : (half + 1) * 3 * gr]
                out = jnp.dot(ysm, part, preferred_element_type=F32)
                sm[z, half * half_rows : (half + 1) * half_rows] = out.astype(BF16)

    n_group = -(-count // GROUP)
    ends = [count * i // n_group for i in range(n_group + 1)]
    stages = (z_filters, y_filters, x_filters, y_smoothing)
    for step in range(n_group + len(stages) - 1):
        for k, stage in enumerate(stages):
            i = step - k
            if 0 <= i < n_group:
                stage(ends[i], ends[i + 1] - ends[i])
    out = jnp.dot(
        sm[0:count].reshape(count * n_rows, cols), get("xsm"), preferred_element_type=F32
    )
    u_ref[0:count] = out.reshape(count, n_rows, cols // 4)


def block_loader(vol, yud, rows):
    def layer(z, at, lanes):
        if at < HALO:
            return yud[z, at : at + 16, lanes].astype(F32)
        if at < HALO + rows:
            return vol[z, at - HALO : at - HALO + 16, lanes].astype(F32)
        return yud[z, at - rows : at - rows + 16, lanes].astype(F32)

    return layer


def spread_rows(first):
    shape = (16 * NEED, 16 * HALO)
    packed = lax.broadcasted_iota(jnp.int32, shape, 0)
    full = lax.broadcasted_iota(jnp.int32, shape, 1)
    z = lax.shift_right_logical(packed * 373, 12)
    return jnp.where(full == packed + z * (HALO - NEED) + first, 1.0, 0.0).astype(BF16)


def load_kernel(vol, s1, s2, vol_out, sems):
    depth, rows, cols = vol.shape
    odd = lax.rem(lax.axis_index("row"), 2) == 1
    parts = (slice(0, HALO), slice(rows - HALO, rows), slice(HALO, rows - HALO))
    copies = [
        pltpu.make_async_copy(vol.at[:, part, :], vol_out.at[:, part, :], sems.at[i])
        for i, part in enumerate(parts)
    ]
    for copy in copies:
        copy.start()
    first_rows, last_rows = spread_rows(0), spread_rows(HALO - NEED)
    copies[0].wait()
    copies[1].wait()
    to_before = jnp.dot(
        first_rows, vol_out[:, 0:HALO].reshape(depth * HALO, cols), preferred_element_type=F32
    ).astype(BF16)
    to_after = jnp.dot(
        last_rows, vol_out[:, rows - HALO :].reshape(depth * HALO, cols), preferred_element_type=F32
    ).astype(BF16)
    s1[...] = jnp.where(odd, to_before, to_after)
    s2[...] = jnp.where(odd, to_after, to_before)
    copies[2].wait()


def column_select(n_col, cols):
    n_side = 1 if n_col == 2 else 2
    shape = (SLOTS + 16 * n_side, cols)
    row = lax.broadcasted_iota(jnp.int32, shape, 0)
    lane = lax.broadcasted_iota(jnp.int32, shape, 1)
    picked = ((row >= 8) & (row < 14) & (lane == row - 8)) | (
        (row >= 14) & (row < 20) & (lane == row - 20 + cols)
    )
    for side in range(n_side):
        if n_col == 2:
            first = jnp.where(lax.axis_index("col") == 0, cols - HALO, 0)
        else:
            first = (cols - HALO, 0)[side]
        at = row - SLOTS - 16 * side
        picked = picked | ((at >= 0) & (at < 16) & (lane == at + first))
    return jnp.where(picked, 1.0, 0.0).astype(BF16)


def pick_columns(select, source):
    picked = lax.dot_general(select, source, NT, preferred_element_type=F32)
    messages = [picked[at : at + 16].astype(BF16) for at in range(SLOTS, picked.shape[0], 16)]
    return picked[0:SLOTS].astype(BF16), picked[8:24].astype(BF16), messages


def halve(chunk, at, value):
    n = value.shape[0]
    chunk[at : at + n] = value[:, 0:128]
    chunk[at + n : at + 2 * n] = value[:, 128:256]


def joined_halves(chunk, at, n):
    return jnp.concatenate([chunk[at : at + n], chunk[at + n : at + 2 * n]], axis=1)


def edges_kernel(n_col, vol, own, zmsg, *refs):
    depth, rows, cols = vol.shape
    gz = lax.axis_index("gz")
    refs, middles = refs[:-1], refs[-1]
    select = column_select(n_col, cols)
    for b in range(depth // 2):
        source = vol[2 * b : 2 * b + 2].reshape(2 * rows, cols)
        slots, middle, messages = pick_columns(select, source)
        own[b], middles[b] = slots, middle
        for ref, message in zip(refs, messages):
            ref[b] = message
    base = jnp.where(gz == 0, depth - R, 0)
    halve(zmsg, 0, vol[pl.ds(base, R)].reshape(R * rows, cols))
    first = jnp.where(gz == 0, (depth - EXTRA) // 2, 0)
    n = EXTRA // 2
    zmsg[2 * R * rows :] = middles[pl.ds(first, n)].reshape(n * 16, 128)


def pack_kernel(place_of, n_col, r1, r2, w, *refs):
    n_side = 1 if n_col == 2 else 2
    xown, (yud, halo, zcorner) = refs[:n_side], refs[n_side : n_side + 3]
    xmsgs, zxmsgs = refs[n_side + 3 : 2 * n_side + 3], refs[2 * n_side + 3 : 3 * n_side + 3]
    middles = refs[3 * n_side + 3]
    depth, cols = yud.shape[0], yud.shape[2]
    gz = lax.axis_index("gz")
    odd = lax.rem(lax.axis_index("row"), 2) == 1
    get = getter(place_of, w)
    got1, got2 = r1[...], r2[...]
    for at, name, part in (
        (0, "above", jnp.where(odd, got1, got2)),
        (HALO, "below", jnp.where(odd, got2, got1)),
    ):
        out = jnp.dot(get(name), part, preferred_element_type=F32).astype(BF16)
        yud[:, at : at + HALO, :] = out.reshape(depth, HALO, cols)
    select = column_select(n_col, cols)
    pairs, quads = depth // 2, depth // 4
    for b in range(quads):
        source = yud[4 * b : 4 * b + 4].reshape(4 * 2 * HALO, cols)
        slots, middle, messages = pick_columns(select, source)
        halo[b] = slots
        middles[b] = middle
        for ref, message in zip(xmsgs, messages):
            ref[pairs + b] = message
    for ref, part in zip(xmsgs, xown):
        ref[0:pairs] = part[...]
    base = jnp.where(gz == 0, depth - R, 0)
    edge = yud[pl.ds(base, R)].reshape(R * 2 * HALO, cols)
    halve(zcorner, 0, jnp.dot(get("corner"), edge, preferred_element_type=F32).astype(BF16))
    n2, n4 = EXTRA // 2, EXTRA // 4
    first2 = jnp.where(gz == 0, pairs - n2, 0)
    first4 = jnp.where(gz == 0, quads - n4, 0)
    zcorner[128:] = middles[pl.ds(first4, n4)].reshape(n4 * 16, 128)
    for ref, message in zip(zxmsgs, xmsgs):
        ref[0:n2] = message[pl.ds(first2, n2)]
        ref[n2:] = message[pl.ds(pairs + first4, n4)]


def stage_kernel(w, w_out):
    pass


FIRST = {True: 5, False: 3}
LAST = {True: 8, False: 10}
GROUP = 4
EDGE = R


def by_half(body):
    low = lax.axis_index("gz") == 0
    pl.when(low)(lambda: body(True))
    pl.when(jnp.logical_not(low))(lambda: body(False))


def first_kernel(place_of, n_row, vol, yud, w, u_ref, *scratch):
    depth, rows, cols = vol.shape
    get = getter(place_of, w)
    ysm = row_mask(get, n_row, rows, rows + 16, rows // 4)
    layer = block_loader(vol, yud, rows)

    def body(low):
        count = FIRST[low]
        base = depth - EDGE - count - R if low else 0
        load = lambda at, lanes, lo, hi: [layer(base + k, at, lanes) for k in range(lo, hi)]
        layers_to_sums(get, ysm, load, count, (rows, cols), u_ref, *scratch)

    by_half(body)


def held_layers(depth, low):
    if low:
        near = depth - EDGE
        return range(near - FIRST[low], near), range(near, depth), range(LAST[low])
    last = EDGE + FIRST[low]
    return range(EDGE, last), range(EDGE), range(last, depth)


def weighted(total, refs, held, weights):
    for ref, layers in zip(refs, held):
        for k, z in enumerate(layers):
            if weights[z] != 0.0:
                term = ref[k] * float(weights[z])
                total = term if total is None else total + term
    return total


def near_kernel(place_of, zs, n_row, vol, yud, zown, zcorner, u1, w, u_ref, send_ref, zext, *scratch):
    depth, rows, cols = vol.shape
    n_zq = zs.shape[1]
    get = getter(place_of, w)
    ysm = row_mask(get, n_row, rows, rows + 16, rows // 4)
    corner = jnp.dot(
        get("corner_back"), joined_halves(zcorner, 0, 64), preferred_element_type=F32
    ).astype(BF16).reshape(R, 2 * HALO, cols)
    zext[:, 0:HALO] = corner[:, 0:HALO]
    zext[:, HALO : HALO + rows] = joined_halves(zown, 0, R * rows).reshape(R, rows, cols)
    zext[:, HALO + rows :] = corner[:, HALO:]
    layer = block_loader(vol, yud, rows)

    def body(low):
        start = depth - R if low else 0
        outer = depth - 2 * R if low else R

        def load(at, lanes, lo, hi):
            out = []
            for k in range(lo, hi):
                if R <= k < 2 * R:
                    out.append(layer(start + k - R, at, lanes))
                elif (k < R) == low:
                    out.append(layer(outer + k % R, at, lanes))
                else:
                    out.append(zext[k % R, at : at + 16, lanes].astype(F32))
            return out

        layers_to_sums(get, ysm, load, EDGE, (rows, cols), u_ref, *scratch)
        held = held_layers(depth, low)[0:2]
        first_q = n_zq - 2 if low else 0
        sends = [weighted(None, (u1, u_ref), held, zs[:, first_q + k]) for k in range(2)]
        send_ref[...] = jnp.concatenate(sends, axis=1).astype(BF16)

    by_half(body)


def strip_tools(n_col, rows):
    col = lax.axis_index("col")
    slots = lax.broadcasted_iota(jnp.int32, (SLOTS, 128), 0)
    if n_col == 2:
        keep = ((slots < 8) & (col == 0)) | ((slots >= 21) & (col == 1))
    else:
        keep = (slots < 8) | (slots >= 21)

    def join(part, messages, b):
        sides = [messages[-1][b].astype(F32), messages[0][b].astype(F32)]
        return jnp.where(keep, jnp.concatenate(sides, axis=0), part)

    lanes = lax.broadcasted_iota(jnp.int32, (SLOTS, 128), 1)

    def layers_of(pairs, quads):
        out = []
        for z in range(2 * len(pairs)):
            left, right = pairs[z // 2], quads[z // 4]
            if z % 2:
                left = pltpu.roll(left, 64, 1)
            turn = (rows - 32 * (z % 4)) % 128
            if turn:
                right = pltpu.roll(right, turn, 1)
            out.append(jnp.where(lanes < rows, left, right))
        return out

    return join, layers_of


def beyond_kernel(n_col, rows, zown, zcorner, zxs, out):
    join, layers_of = strip_tools(n_col, rows)

    def from_middle(ref, at, b):
        rim = jnp.zeros((8, 128), F32)
        middle = ref[at + 16 * b : at + 16 * (b + 1)].astype(F32)
        return jnp.concatenate([rim, middle, rim], axis=0)

    n2, n4 = EXTRA // 2, EXTRA // 4
    layers = layers_of(
        [join(from_middle(zown, 2 * R * rows, b), zxs, b) for b in range(n2)],
        [join(from_middle(zcorner, 128, b), zxs, n2 + b) for b in range(n4)],
    )
    for k, layer in enumerate(layers):
        out[k] = layer.astype(BF16)


def last_kernel(place_of, zs, n_row, n_col, vol, yud, own, halo, far, u1, u2, w, xs, own_ref,
                hs, hd, pstrip, u3, *scratch):
    depth, rows, cols = vol.shape
    gr = rows + 16
    quarter_rows, quarter = rows // 4, cols // 4
    get = getter(place_of, w)
    col = lax.axis_index("col")
    ysm = row_mask(get, n_row, rows, gr, quarter_rows)
    join, layers_of = strip_tools(n_col, rows)
    layer = block_loader(vol, yud, rows)
    slot = lax.rem(lax.broadcasted_iota(jnp.int32, (3 * quarter_rows, 256), 1), SLOTS)
    outside_x = ((col == 0) & (slot < 8)) | ((col == n_col - 1) & (slot >= 14))
    n_rows = 6 * quarter_rows
    count = depth + 8
    n = count // 8

    def body(low):
        first = 0 if low else depth - LAST[low]

        def load(at, lanes, lo, hi):
            out = []
            for z in range(first - R + lo, first - R + hi):
                inside = 0 <= z < depth
                out.append(layer(z, at, lanes) if inside else jnp.zeros((16, 128), F32))
            return out

        layers_to_sums(get, ysm, load, LAST[low], (rows, cols), u3, *scratch)
        own_layers = layers_of(
            [join(own[b].astype(F32), xs, b) for b in range(depth // 2)],
            [join(halo[b].astype(F32), xs, depth // 2 + b) for b in range(depth // 4)],
        )
        beyond = [far[k].astype(F32) for k in range(EXTRA)]
        zero = [jnp.zeros((SLOTS, 128), F32)] * R
        if low:
            layers = zero + own_layers + beyond[0:11]
        else:
            layers = beyond[1:12] + own_layers + zero
        for z, smooth, slope in z_filter(layers, count):
            hs[SLOTS * z : SLOTS * (z + 1)] = smooth.astype(BF16)
            hd[SLOTS * z : SLOTS * (z + 1)] = slope.astype(BF16)
        p01 = lax.dot_general(
            get("wy_strip", 128), hs[...], NT, preferred_element_type=F32
        ).astype(BF16)
        p2 = lax.dot_general(
            get("wy_strip_slope", 128), hd[...], NT, preferred_element_type=F32
        ).astype(BF16)
        groups = [slice(256 * c, 256 * (c + 1)) for c in range(n)]
        stacks = [
            jnp.concatenate([p[:, g] for g in groups], axis=0) for p in (p01[0:gr], p01[gr:], p2)
        ]
        grads = [
            jnp.dot(stack, get(name), preferred_element_type=F32).astype(BF16).reshape(n, gr, 256)
            for stack, name in zip(stacks, ("bdd", "bds", "bds"))
        ]
        for c, (a, b) in enumerate(pair_table):
            pstrip[:, c * gr : (c + 1) * gr] = grads[a] * grads[b]
        smoothed = []
        for c in range(n):
            for half in range(2):
                part = pstrip[c, half * 3 * gr : (half + 1) * 3 * gr]
                out = jnp.dot(ysm, part, preferred_element_type=F32)
                smoothed.append(jnp.where(outside_x, 0.0, out).astype(BF16))
        u = jnp.dot(jnp.concatenate(smoothed, axis=0), get("bdx"), preferred_element_type=F32)
        u = u.astype(BF16)
        sums = []
        for name in ("0", "1"):
            at = place_of[("g_low" if low else "g_high") + name][0]
            total = None
            for c in range(n):
                g = w[at + 64 * c : at + 64 * (c + 1), :]
                term = jnp.dot(u[n_rows * c : n_rows * (c + 1)], g, preferred_element_type=F32)
                total = term if total is None else total + term
            sums += [total[:, 0:quarter], total[:, 128 : 128 + quarter]]
        held = held_layers(depth, low)
        for q in range(depth // 4):
            total = weighted(sums[q], (u1, u2, u3), held, zs[:, q + 2])
            own_ref[:, q] = total.reshape(6, quarter_rows, quarter)

    by_half(body)


def add_kernel(own, got, out):
    n_q, quarter = own.shape[1], own.shape[3]
    low = lax.axis_index("gz") == 0
    parts = [
        got[:, k * quarter : (k + 1) * quarter].astype(F32).reshape(own.shape[0], -1, quarter)
        for k in range(2)
    ]
    for q in range(n_q):
        total = own[:, q]
        if q < 2:
            total = total + parts[q] * jnp.where(low, 0.0, 1.0)
        if q >= n_q - 2:
            total = total + parts[q - n_q + 2] * jnp.where(low, 1.0, 0.0)
        out[:, q] = total


def call(body, outs, operands, scratch, name, flops=0, aliases=None, n_hbm=0):
    vmem = pl.BlockSpec(memory_space=pltpu.VMEM)
    hbm = pl.BlockSpec(memory_space=pltpu.HBM)
    operands = [
        pltpu.with_memory_space_constraint(o, pltpu.HBM) if i < n_hbm else o
        for i, o in enumerate(operands)
    ]
    moved = sum(o.size * o.dtype.itemsize for o in list(outs) + list(operands))
    return pl.pallas_call(
        body,
        out_shape=list(outs),
        in_specs=[hbm] * n_hbm + [vmem] * (len(operands) - n_hbm),
        out_specs=[vmem] * len(outs),
        scratch_shapes=scratch,
        input_output_aliases=aliases or {},
        compiler_params=pltpu.CompilerParams(vmem_limit_bytes=24 * 2**20),
        cost_estimate=pl.CostEstimate(flops=flops, bytes_accessed=moved, transcendentals=0),
        name=name,
    )(*operands)


def per_device(volume):
    depth, rows, cols = volume.shape
    n_row, n_col = lax.axis_size("row"), lax.axis_size("col")
    table, place_of, zs = weight_table(depth, rows, cols)
    ext = rows + 2 * HALO
    gr = rows + 16
    quarter_rows, quarter = rows // 4, cols // 4
    n_rows = 6 * quarter_rows
    n_side = 1 if n_col == 2 else 2
    pairs, quads = depth // 2, depth // 4
    n2, n4 = EXTRA // 2, EXTRA // 4
    sds = jax.ShapeDtypeStruct
    bf16 = lambda *shape: sds(shape, BF16)
    most_first, most_last = max(FIRST.values()), max(LAST.values())

    def scratch_for(count):
        return [
            pltpu.VMEM((count, 2 * ext, cols), BF16),
            pltpu.VMEM((3, count, gr, cols), BF16),
            pltpu.VMEM((count, 6 * gr, cols), BF16),
            pltpu.VMEM((count, n_rows, cols), BF16),
        ]

    layer_flops = 2 * cols * (3 * gr * 2 * ext + 3 * gr * cols + n_rows * 3 * gr + n_rows * quarter)

    dma = pltpu.SemaphoreType.DMA
    s1, s2, vol = call(
        load_kernel,
        [bf16(depth * NEED, cols)] * 2 + [bf16(depth, rows, cols)],
        [volume], [dma((3,))], "load", n_hbm=1,
    )
    inner = [(i, i + 1) for i in range(1, n_row - 1, 2)]
    inner = inner + [(j, i) for i, j in inner]
    r2 = lax.ppermute(s2, "row", inner)
    r1 = lax.ppermute(s1, "row", [(i, i ^ 1) for i in range(n_row)])
    (w,) = call(
        stage_kernel, [bf16(*table.shape)], [jnp.asarray(table)], [], "stage", aliases={0: 0}
    )
    own, zmsg, *xown = call(
        lambda *refs: edges_kernel(n_col, *refs),
        [bf16(pairs, SLOTS, 128), bf16(2 * R * rows + n2 * 16, 128)]
        + [bf16(pairs, HALO, 128)] * n_side,
        [vol], [pltpu.VMEM((pairs, 16, 128), BF16)], "edges",
    )
    swap = [(0, 1), (1, 0)]
    zown = lax.ppermute(zmsg, "gz", swap)

    yud, halo, zcmsg, *messages = call(
        lambda *refs: pack_kernel(place_of, n_col, *refs),
        [bf16(depth, 2 * HALO, cols), bf16(quads, SLOTS, 128), bf16(128 + n4 * 16, 128)]
        + [bf16(pairs + quads, HALO, 128)] * n_side
        + [bf16(n2 + n4, HALO, 128)] * n_side,
        [r1, r2, w] + xown, [pltpu.VMEM((quads, 16, 128), BF16)], "pack",
    )
    zcorner = lax.ppermute(zcmsg, "gz", swap)
    xs, zxs = [], []
    for side in range(n_side):
        step = 1 - 2 * side
        line = swap if n_col == 2 else [
            (i, i + step) for i in range(n_col) if 0 <= i + step < n_col
        ]
        both = [(z * n_col + i, (1 - z) * n_col + j) for z in range(2) for i, j in line]
        xs.append(lax.ppermute(messages[side], "col", line))
        zxs.append(lax.ppermute(messages[n_side + side], ("gz", "col"), both))

    (u1,) = call(
        lambda *refs: first_kernel(place_of, n_row, *refs),
        [sds((most_first, n_rows, quarter), F32)],
        [vol, yud, w], scratch_for(most_first), "first", flops=most_first * layer_flops,
    )
    u2, send = call(
        lambda *refs: near_kernel(place_of, zs, n_row, *refs),
        [sds((EDGE, n_rows, quarter), F32), bf16(n_rows, 2 * quarter)],
        [vol, yud, zown, zcorner, u1, w],
        [pltpu.VMEM((R, ext, cols), BF16)] + scratch_for(EDGE),
        "near", flops=EDGE * layer_flops,
    )
    sums = lax.ppermute(send, "gz", swap)

    (far,) = call(
        lambda zown, zcorner, *refs: beyond_kernel(
            n_col, rows, zown, zcorner, refs[:n_side], refs[n_side]
        ),
        [bf16(EXTRA, SLOTS, 128)], [zown, zcorner] + zxs, [], "beyond", flops=EDGE * layer_flops,
    )

    def last_body(*refs):
        head, x_refs, tail = refs[0:8], refs[8 : 8 + n_side], refs[8 + n_side :]
        last_kernel(place_of, zs, n_row, n_col, *head, x_refs, *tail)

    count = depth + 8
    (result,) = call(
        last_body,
        [sds((6, depth // 4, quarter_rows, quarter), F32)],
        [vol, yud, own, halo, far, u1, u2, w] + xs,
        [
            pltpu.VMEM((count * SLOTS, 128), BF16),
            pltpu.VMEM((count * SLOTS, 128), BF16),
            pltpu.VMEM((count // 8, 6 * gr, 256), BF16),
            pltpu.VMEM((most_last, n_rows, quarter), F32),
        ]
        + scratch_for(most_last),
        "last", flops=(most_last + 3) * layer_flops,
    )
    (out,) = call(add_kernel, [sds(result.shape, F32)], [result, sums], [], "add")
    return out


def solution(mesh):
    return jax.shard_map(
        per_device,
        mesh=mesh,
        in_specs=(P("gz", "row", "col"),),
        out_specs=P(None, "gz", "row", "col"),
        check_vma=False,
    )
```

```python
import jax
import jax.numpy as jnp
import ml_dtypes
import numpy as np
from jax import lax
from jax.experimental import pallas as pl
from jax.experimental.pallas import tpu as pltpu
from jax.sharding import PartitionSpec as P

R = 3
R2 = 8
HALO = 16
NEED = R + R2
EXTRA = 12
SLOTS = 32
NT = (((1,), (1,)), ((), ()))
F32 = jnp.float32
BF16 = jnp.bfloat16

pair_table = ((0, 0), (1, 1), (2, 2), (0, 1), (0, 2), (1, 2))


def gauss_taps(radius):
    offsets = np.arange(-radius, radius + 1).astype(np.float32)
    spread = np.float32(radius / 3.0)
    smooth = np.exp(-offsets * offsets / (np.float32(2.0) * spread * spread))
    smooth = smooth / np.sum(smooth)
    slopes = offsets * smooth
    slopes = slopes / np.sum(offsets * slopes)
    as_f32 = lambda t: t.astype(ml_dtypes.bfloat16).astype(np.float32)
    return as_f32(smooth), as_f32(slopes)


SMOOTH_D, SLOPE_D = gauss_taps(R)
SMOOTH_I, _ = gauss_taps(R2)


def band(taps, sources, targets):
    radius = len(taps) // 2
    gap = np.asarray(sources)[:, None] - np.asarray(targets)[None, :]
    return np.where(np.abs(gap) <= radius, taps[np.clip(gap + radius, 0, 2 * radius)], 0.0)


def weight_table(depth, rows, cols):
    ext = rows + 2 * HALO
    grad_rows = rows + 16
    far = 10**6
    y_in = np.arange(ext) - HALO
    y_out = np.arange(grad_rows) - R2
    smooth_y = band(SMOOTH_D, y_in, y_out).T
    slope_y = band(SLOPE_D, y_in, y_out).T
    zero = np.zeros_like(smooth_y)
    wy = np.block([[smooth_y, zero], [slope_y, zero], [zero, smooth_y]])
    order = np.concatenate([np.arange(rows), np.arange(HALO) - HALO, rows + np.arange(HALO)]) + HALO
    x_all = np.arange(cols)
    slot_in = np.full(SLOTS, far)
    slot_in[0:8] = cols + np.arange(8)
    slot_in[8:14] = np.arange(6)
    slot_in[14:20] = cols - 6 + np.arange(6)
    slot_in[21:32] = np.arange(-11, 0)
    slot_out = np.full(SLOTS, -far)
    slot_out[0:11] = np.arange(-8, 3)
    slot_out[11:19] = cols - 3 + np.arange(8)
    eye8 = np.eye(8)
    inner = np.where((x_all >= R) & (x_all < cols - R), x_all, far)
    quarter = cols // 4
    coarse_edge = np.full(8, 3 * far)
    coarse_edge[0:5] = [0, 1, 2, quarter - 2, quarter - 1]
    xs_edge = band(SMOOTH_I, slot_out, 4 * coarse_edge)
    ys = band(SMOOTH_I, y_out, 4 * np.arange(rows // 4)).T
    zs = band(SMOOTH_I, np.arange(depth), 4 * (np.arange(depth // 4 + 4) - 2))
    place = np.zeros((8, 128))
    for j in range(5):
        place[j, coarse_edge[j]] = 1.0
    own_z = 4 * np.arange(depth // 4)
    g = [
        np.einsum("zq,jx->zjqx", band(SMOOTH_I, np.arange(depth + 8) + first, own_z), place)
        for first in (0, -8)
    ]
    g = [t.reshape((depth + 8) * 8, len(own_z) * 128) for t in g]
    packed = np.arange(depth * NEED)
    above = np.zeros((depth * HALO, depth * NEED))
    above[packed + packed // NEED * (HALO - NEED) + HALO - NEED, packed] = 1.0
    below = np.zeros((depth * HALO, depth * NEED))
    below[packed + packed // NEED * (HALO - NEED), packed] = 1.0
    used = 2 * R + 13
    packed = np.arange(R * used)
    corner = np.zeros((64, R * 2 * HALO))
    corner[packed, packed + packed // used * (2 * HALO - used) + HALO - NEED] = 1.0
    parts = {
        "above": above,
        "below": below,
        "corner": corner,
        "corner_back": corner.T,
        "wy": wy,
        "wy_strip": np.concatenate([smooth_y, slope_y])[:, order],
        "wy_strip_slope": smooth_y[:, order],
        "wxd": band(SLOPE_D, x_all, x_all),
        "wxs": band(SMOOTH_D, x_all, x_all),
        "bdd": np.kron(eye8, band(SLOPE_D, slot_in, slot_out)),
        "bds": np.kron(eye8, band(SMOOTH_D, slot_in, slot_out)),
        "ysm": np.kron(np.eye(3), ys),
        "xsm": band(SMOOTH_I, inner, 4 * np.arange(quarter)),
        "bdx": np.kron(eye8, xs_edge),
        "g_low0": g[0][:, 0:256],
        "g_low1": g[0][:, 256:512],
        "g_high0": g[1][:, 0:256],
        "g_high1": g[1][:, 256:512],
    }
    place_of, blocks, at = {}, [], 0
    for name, part in parts.items():
        height = -(-part.shape[0] // 16) * 16
        block = np.zeros((height, 256), np.float32)
        block[: part.shape[0], : part.shape[1]] = part
        place_of[name] = (at, part.shape[0], part.shape[1])
        blocks.append(block)
        at += height
    return np.concatenate(blocks).astype(ml_dtypes.bfloat16), place_of, zs


def z_filter(v, count):
    for z in range(count):
        w = v[z : z + 7]
        smooth = w[3] * float(SMOOTH_D[3])
        slope = None
        for s in (1, 2, 3):
            smooth = smooth + (w[3 + s] + w[3 - s]) * float(SMOOTH_D[3 + s])
            term = (w[3 + s] - w[3 - s]) * float(SLOPE_D[3 + s])
            slope = term if slope is None else slope + term
        yield z, smooth, slope


def getter(place_of, w):
    def get(name, width=None):
        at, height, own_width = place_of[name]
        return w[at : at + height, 0 : (width or own_width)]

    return get


def row_mask(get, n_row, rows, gr, quarter_rows):
    row = lax.axis_index("row")
    lane = lax.broadcasted_iota(jnp.int32, (3 * quarter_rows, 3 * gr), 1)
    y_out = lax.rem(lane, gr) - R2
    outside = ((row == 0) & (y_out < 0)) | ((row == n_row - 1) & (y_out >= rows))
    return jnp.where(outside, 0.0, get("ysm").astype(F32)).astype(BF16)


def layers_to_sums(get, ysm, load, count, shape, u_ref, zf, planes, prod, sm):
    rows, cols = shape
    ext = rows + 2 * HALO
    gr = rows + 16
    n_rows = 6 * (rows // 4)
    half_rows = n_rows // 2
    rest = jnp.zeros((8, 128), F32)
    wy = get("wy")

    def z_filters(first, n):
        for tile in range(cols // 128):
            lanes = slice(tile * 128, tile * 128 + 128)
            for at in range(0, ext, 16):
                blocks = load(at, lanes, first, first + n + 2 * R)
                if at == rows + HALO:
                    blocks = [block[0:8] for block in blocks]
                for z, smooth, slope in z_filter(blocks, n):
                    if at == rows + HALO:
                        smooth = jnp.concatenate([smooth, rest], axis=0)
                        slope = jnp.concatenate([slope, rest], axis=0)
                    zf[first + z, at : at + 16, lanes] = smooth.astype(BF16)
                    zf[first + z, ext + at : ext + at + 16, lanes] = slope.astype(BF16)

    def y_filters(first, n):
        for z in range(first, first + n):
            out = jnp.dot(wy, zf[z], preferred_element_type=F32).astype(BF16)
            planes[0, z] = out[0:gr]
            planes[1, z] = out[gr : 2 * gr]
            planes[2, z] = out[2 * gr :]

    def x_filters(first, n):
        grads = []
        for f, name in enumerate(("wxd", "wxs", "wxs")):
            part = planes[f, first : first + n].reshape(n * gr, cols)
            out = jnp.dot(part, get(name), preferred_element_type=F32)
            grads.append(out.astype(BF16).reshape(n, gr, cols))
        for c, (a, b) in enumerate(pair_table):
            prod[first : first + n, c * gr : (c + 1) * gr] = grads[a] * grads[b]

    def y_smoothing(first, n):
        for z in range(first, first + n):
            for half in range(2):
                part = prod[z, half * 3 * gr : (half + 1) * 3 * gr]
                out = jnp.dot(ysm, part, preferred_element_type=F32)
                sm[z, half * half_rows : (half + 1) * half_rows] = out.astype(BF16)

    n_group = -(-count // GROUP)
    ends = [count * i // n_group for i in range(n_group + 1)]
    stages = (z_filters, y_filters, x_filters, y_smoothing)
    for step in range(n_group + len(stages) - 1):
        for k, stage in enumerate(stages):
            i = step - k
            if 0 <= i < n_group:
                stage(ends[i], ends[i + 1] - ends[i])
    out = jnp.dot(
        sm[0:count].reshape(count * n_rows, cols), get("xsm"), preferred_element_type=F32
    )
    u_ref[0:count] = out.reshape(count, n_rows, cols // 4)


def block_loader(vol, yud, rows):
    def layer(z, at, lanes):
        if at < HALO:
            return yud[z, at : at + 16, lanes].astype(F32)
        if at < HALO + rows:
            return vol[z, at - HALO : at - HALO + 16, lanes].astype(F32)
        return yud[z, at - rows : at - rows + 16, lanes].astype(F32)

    return layer


def spread_rows(first):
    shape = (16 * NEED, 16 * HALO)
    packed = lax.broadcasted_iota(jnp.int32, shape, 0)
    full = lax.broadcasted_iota(jnp.int32, shape, 1)
    z = lax.shift_right_logical(packed * 373, 12)
    return jnp.where(full == packed + z * (HALO - NEED) + first, 1.0, 0.0).astype(BF16)


def load_kernel(vol, s1, s2, vol_out, sems):
    depth, rows, cols = vol.shape
    odd = lax.rem(lax.axis_index("row"), 2) == 1
    parts = (slice(0, HALO), slice(rows - HALO, rows), slice(HALO, rows - HALO))
    copies = [
        pltpu.make_async_copy(vol.at[:, part, :], vol_out.at[:, part, :], sems.at[i])
        for i, part in enumerate(parts)
    ]
    for copy in copies:
        copy.start()
    first_rows, last_rows = spread_rows(0), spread_rows(HALO - NEED)
    copies[0].wait()
    copies[1].wait()
    to_before = jnp.dot(
        first_rows, vol_out[:, 0:HALO].reshape(depth * HALO, cols), preferred_element_type=F32
    ).astype(BF16)
    to_after = jnp.dot(
        last_rows, vol_out[:, rows - HALO :].reshape(depth * HALO, cols), preferred_element_type=F32
    ).astype(BF16)
    s1[...] = jnp.where(odd, to_before, to_after)
    s2[...] = jnp.where(odd, to_after, to_before)
    copies[2].wait()


def column_select(n_col, cols):
    n_side = 1 if n_col == 2 else 2
    shape = (SLOTS + 16 * n_side, cols)
    row = lax.broadcasted_iota(jnp.int32, shape, 0)
    lane = lax.broadcasted_iota(jnp.int32, shape, 1)
    picked = ((row >= 8) & (row < 14) & (lane == row - 8)) | (
        (row >= 14) & (row < 20) & (lane == row - 20 + cols)
    )
    for side in range(n_side):
        if n_col == 2:
            first = jnp.where(lax.axis_index("col") == 0, cols - HALO, 0)
        else:
            first = (cols - HALO, 0)[side]
        at = row - SLOTS - 16 * side
        picked = picked | ((at >= 0) & (at < 16) & (lane == at + first))
    return jnp.where(picked, 1.0, 0.0).astype(BF16)


def pick_columns(select, source):
    picked = lax.dot_general(select, source, NT, preferred_element_type=F32)
    messages = [picked[at : at + 16].astype(BF16) for at in range(SLOTS, picked.shape[0], 16)]
    return picked[0:SLOTS].astype(BF16), picked[8:24].astype(BF16), messages


def halve(chunk, at, value):
    n = value.shape[0]
    chunk[at : at + n] = value[:, 0:128]
    chunk[at + n : at + 2 * n] = value[:, 128:256]


def joined_halves(chunk, at, n):
    return jnp.concatenate([chunk[at : at + n], chunk[at + n : at + 2 * n]], axis=1)


def edges_kernel(n_col, vol, own, zmsg, *refs):
    depth, rows, cols = vol.shape
    gz = lax.axis_index("gz")
    refs, middles = refs[:-1], refs[-1]
    select = column_select(n_col, cols)
    for b in range(depth // 2):
        source = vol[2 * b : 2 * b + 2].reshape(2 * rows, cols)
        slots, middle, messages = pick_columns(select, source)
        own[b], middles[b] = slots, middle
        for ref, message in zip(refs, messages):
            ref[b] = message
    base = jnp.where(gz == 0, depth - R, 0)
    halve(zmsg, 0, vol[pl.ds(base, R)].reshape(R * rows, cols))
    first = jnp.where(gz == 0, (depth - EXTRA) // 2, 0)
    n = EXTRA // 2
    zmsg[2 * R * rows :] = middles[pl.ds(first, n)].reshape(n * 16, 128)


def pack_kernel(place_of, n_col, r1, r2, w, *refs):
    n_side = 1 if n_col == 2 else 2
    xown, (yud, halo, zcorner) = refs[:n_side], refs[n_side : n_side + 3]
    xmsgs, zxmsgs = refs[n_side + 3 : 2 * n_side + 3], refs[2 * n_side + 3 : 3 * n_side + 3]
    middles = refs[3 * n_side + 3]
    depth, cols = yud.shape[0], yud.shape[2]
    gz = lax.axis_index("gz")
    odd = lax.rem(lax.axis_index("row"), 2) == 1
    get = getter(place_of, w)
    got1, got2 = r1[...], r2[...]
    for at, name, part in (
        (0, "above", jnp.where(odd, got1, got2)),
        (HALO, "below", jnp.where(odd, got2, got1)),
    ):
        out = jnp.dot(get(name), part, preferred_element_type=F32).astype(BF16)
        yud[:, at : at + HALO, :] = out.reshape(depth, HALO, cols)
    select = column_select(n_col, cols)
    pairs, quads = depth // 2, depth // 4
    for b in range(quads):
        source = yud[4 * b : 4 * b + 4].reshape(4 * 2 * HALO, cols)
        slots, middle, messages = pick_columns(select, source)
        halo[b] = slots
        middles[b] = middle
        for ref, message in zip(xmsgs, messages):
            ref[pairs + b] = message
    for ref, part in zip(xmsgs, xown):
        ref[0:pairs] = part[...]
    base = jnp.where(gz == 0, depth - R, 0)
    edge = yud[pl.ds(base, R)].reshape(R * 2 * HALO, cols)
    halve(zcorner, 0, jnp.dot(get("corner"), edge, preferred_element_type=F32).astype(BF16))
    n2, n4 = EXTRA // 2, EXTRA // 4
    first2 = jnp.where(gz == 0, pairs - n2, 0)
    first4 = jnp.where(gz == 0, quads - n4, 0)
    zcorner[128:] = middles[pl.ds(first4, n4)].reshape(n4 * 16, 128)
    for ref, message in zip(zxmsgs, xmsgs):
        ref[0:n2] = message[pl.ds(first2, n2)]
        ref[n2:] = message[pl.ds(pairs + first4, n4)]


def stage_kernel(w, w_out):
    pass


FIRST = {True: 5, False: 4}
LAST = {True: 8, False: 9}
GROUP = 4
EDGE = R


def by_half(body):
    low = lax.axis_index("gz") == 0
    pl.when(low)(lambda: body(True))
    pl.when(jnp.logical_not(low))(lambda: body(False))


def first_kernel(place_of, n_row, vol, yud, w, u_ref, *scratch):
    depth, rows, cols = vol.shape
    get = getter(place_of, w)
    ysm = row_mask(get, n_row, rows, rows + 16, rows // 4)
    layer = block_loader(vol, yud, rows)

    def body(low):
        count = FIRST[low]
        base = depth - EDGE - count - R if low else 0
        load = lambda at, lanes, lo, hi: [layer(base + k, at, lanes) for k in range(lo, hi)]
        layers_to_sums(get, ysm, load, count, (rows, cols), u_ref, *scratch)

    by_half(body)


def held_layers(depth, low):
    if low:
        near = depth - EDGE
        return range(near - FIRST[low], near), range(near, depth), range(LAST[low])
    last = EDGE + FIRST[low]
    return range(EDGE, last), range(EDGE), range(last, depth)


def weighted(total, refs, held, weights):
    for ref, layers in zip(refs, held):
        for k, z in enumerate(layers):
            if weights[z] != 0.0:
                term = ref[k] * float(weights[z])
                total = term if total is None else total + term
    return total


def near_kernel(place_of, zs, n_row, vol, yud, zown, zcorner, u1, w, u_ref, send_ref, zext, *scratch):
    depth, rows, cols = vol.shape
    n_zq = zs.shape[1]
    get = getter(place_of, w)
    ysm = row_mask(get, n_row, rows, rows + 16, rows // 4)
    corner = jnp.dot(
        get("corner_back"), joined_halves(zcorner, 0, 64), preferred_element_type=F32
    ).astype(BF16).reshape(R, 2 * HALO, cols)
    zext[:, 0:HALO] = corner[:, 0:HALO]
    zext[:, HALO : HALO + rows] = joined_halves(zown, 0, R * rows).reshape(R, rows, cols)
    zext[:, HALO + rows :] = corner[:, HALO:]
    layer = block_loader(vol, yud, rows)

    def body(low):
        start = depth - R if low else 0
        outer = depth - 2 * R if low else R

        def load(at, lanes, lo, hi):
            out = []
            for k in range(lo, hi):
                if R <= k < 2 * R:
                    out.append(layer(start + k - R, at, lanes))
                elif (k < R) == low:
                    out.append(layer(outer + k % R, at, lanes))
                else:
                    out.append(zext[k % R, at : at + 16, lanes].astype(F32))
            return out

        layers_to_sums(get, ysm, load, EDGE, (rows, cols), u_ref, *scratch)
        held = held_layers(depth, low)[0:2]
        first_q = n_zq - 2 if low else 0
        sends = [weighted(None, (u1, u_ref), held, zs[:, first_q + k]) for k in range(2)]
        send_ref[...] = jnp.concatenate(sends, axis=1).astype(BF16)

    by_half(body)


def strip_tools(n_col, rows):
    col = lax.axis_index("col")
    slots = lax.broadcasted_iota(jnp.int32, (SLOTS, 128), 0)
    if n_col == 2:
        keep = ((slots < 8) & (col == 0)) | ((slots >= 21) & (col == 1))
    else:
        keep = (slots < 8) | (slots >= 21)

    def join(part, messages, b):
        sides = [messages[-1][b].astype(F32), messages[0][b].astype(F32)]
        return jnp.where(keep, jnp.concatenate(sides, axis=0), part)

    lanes = lax.broadcasted_iota(jnp.int32, (SLOTS, 128), 1)

    def layers_of(pairs, quads):
        out = []
        for z in range(2 * len(pairs)):
            left, right = pairs[z // 2], quads[z // 4]
            if z % 2:
                left = pltpu.roll(left, 64, 1)
            turn = (rows - 32 * (z % 4)) % 128
            if turn:
                right = pltpu.roll(right, turn, 1)
            out.append(jnp.where(lanes < rows, left, right))
        return out

    return join, layers_of


def beyond_kernel(n_col, rows, zown, zcorner, zxs, out):
    join, layers_of = strip_tools(n_col, rows)

    def from_middle(ref, at, b):
        rim = jnp.zeros((8, 128), F32)
        middle = ref[at + 16 * b : at + 16 * (b + 1)].astype(F32)
        return jnp.concatenate([rim, middle, rim], axis=0)

    n2, n4 = EXTRA // 2, EXTRA // 4
    layers = layers_of(
        [join(from_middle(zown, 2 * R * rows, b), zxs, b) for b in range(n2)],
        [join(from_middle(zcorner, 128, b), zxs, n2 + b) for b in range(n4)],
    )
    for k, layer in enumerate(layers):
        out[k] = layer.astype(BF16)


def last_kernel(place_of, zs, n_row, n_col, vol, yud, own, halo, far, u1, u2, w, xs, own_ref,
                hs, hd, pstrip, u3, *scratch):
    depth, rows, cols = vol.shape
    gr = rows + 16
    quarter_rows, quarter = rows // 4, cols // 4
    get = getter(place_of, w)
    col = lax.axis_index("col")
    ysm = row_mask(get, n_row, rows, gr, quarter_rows)
    join, layers_of = strip_tools(n_col, rows)
    layer = block_loader(vol, yud, rows)
    slot = lax.rem(lax.broadcasted_iota(jnp.int32, (3 * quarter_rows, 256), 1), SLOTS)
    outside_x = ((col == 0) & (slot < 8)) | ((col == n_col - 1) & (slot >= 14))
    n_rows = 6 * quarter_rows
    count = depth + 8
    n = count // 8

    def body(low):
        first = 0 if low else depth - LAST[low]

        def load(at, lanes, lo, hi):
            out = []
            for z in range(first - R + lo, first - R + hi):
                inside = 0 <= z < depth
                out.append(layer(z, at, lanes) if inside else jnp.zeros((16, 128), F32))
            return out

        layers_to_sums(get, ysm, load, LAST[low], (rows, cols), u3, *scratch)
        own_layers = layers_of(
            [join(own[b].astype(F32), xs, b) for b in range(depth // 2)],
            [join(halo[b].astype(F32), xs, depth // 2 + b) for b in range(depth // 4)],
        )
        beyond = [far[k].astype(F32) for k in range(EXTRA)]
        zero = [jnp.zeros((SLOTS, 128), F32)] * R
        if low:
            layers = zero + own_layers + beyond[0:11]
        else:
            layers = beyond[1:12] + own_layers + zero
        for z, smooth, slope in z_filter(layers, count):
            hs[SLOTS * z : SLOTS * (z + 1)] = smooth.astype(BF16)
            hd[SLOTS * z : SLOTS * (z + 1)] = slope.astype(BF16)
        p01 = lax.dot_general(
            get("wy_strip", 128), hs[...], NT, preferred_element_type=F32
        ).astype(BF16)
        p2 = lax.dot_general(
            get("wy_strip_slope", 128), hd[...], NT, preferred_element_type=F32
        ).astype(BF16)
        groups = [slice(256 * c, 256 * (c + 1)) for c in range(n)]
        stacks = [
            jnp.concatenate([p[:, g] for g in groups], axis=0) for p in (p01[0:gr], p01[gr:], p2)
        ]
        grads = [
            jnp.dot(stack, get(name), preferred_element_type=F32).astype(BF16).reshape(n, gr, 256)
            for stack, name in zip(stacks, ("bdd", "bds", "bds"))
        ]
        for c, (a, b) in enumerate(pair_table):
            pstrip[:, c * gr : (c + 1) * gr] = grads[a] * grads[b]
        smoothed = []
        for c in range(n):
            for half in range(2):
                part = pstrip[c, half * 3 * gr : (half + 1) * 3 * gr]
                out = jnp.dot(ysm, part, preferred_element_type=F32)
                smoothed.append(jnp.where(outside_x, 0.0, out).astype(BF16))
        u = jnp.dot(jnp.concatenate(smoothed, axis=0), get("bdx"), preferred_element_type=F32)
        u = u.astype(BF16)
        sums = []
        for name in ("0", "1"):
            at = place_of[("g_low" if low else "g_high") + name][0]
            total = None
            for c in range(n):
                g = w[at + 64 * c : at + 64 * (c + 1), :]
                term = jnp.dot(u[n_rows * c : n_rows * (c + 1)], g, preferred_element_type=F32)
                total = term if total is None else total + term
            sums += [total[:, 0:quarter], total[:, 128 : 128 + quarter]]
        held = held_layers(depth, low)
        for q in range(depth // 4):
            total = weighted(sums[q], (u1, u2, u3), held, zs[:, q + 2])
            own_ref[:, q] = total.reshape(6, quarter_rows, quarter)

    by_half(body)


def add_kernel(own, got, out):
    n_q, quarter = own.shape[1], own.shape[3]
    low = lax.axis_index("gz") == 0
    parts = [
        got[:, k * quarter : (k + 1) * quarter].astype(F32).reshape(own.shape[0], -1, quarter)
        for k in range(2)
    ]
    for q in range(n_q):
        total = own[:, q]
        if q < 2:
            total = total + parts[q] * jnp.where(low, 0.0, 1.0)
        if q >= n_q - 2:
            total = total + parts[q - n_q + 2] * jnp.where(low, 1.0, 0.0)
        out[:, q] = total


def call(body, outs, operands, scratch, name, flops=0, aliases=None, n_hbm=0):
    vmem = pl.BlockSpec(memory_space=pltpu.VMEM)
    hbm = pl.BlockSpec(memory_space=pltpu.HBM)
    operands = [
        pltpu.with_memory_space_constraint(o, pltpu.HBM) if i < n_hbm else o
        for i, o in enumerate(operands)
    ]
    moved = sum(o.size * o.dtype.itemsize for o in list(outs) + list(operands))
    return pl.pallas_call(
        body,
        out_shape=list(outs),
        in_specs=[hbm] * n_hbm + [vmem] * (len(operands) - n_hbm),
        out_specs=[vmem] * len(outs),
        scratch_shapes=scratch,
        input_output_aliases=aliases or {},
        compiler_params=pltpu.CompilerParams(vmem_limit_bytes=24 * 2**20),
        cost_estimate=pl.CostEstimate(flops=flops, bytes_accessed=moved, transcendentals=0),
        name=name,
    )(*operands)


def per_device(volume):
    depth, rows, cols = volume.shape
    n_row, n_col = lax.axis_size("row"), lax.axis_size("col")
    table, place_of, zs = weight_table(depth, rows, cols)
    ext = rows + 2 * HALO
    gr = rows + 16
    quarter_rows, quarter = rows // 4, cols // 4
    n_rows = 6 * quarter_rows
    n_side = 1 if n_col == 2 else 2
    pairs, quads = depth // 2, depth // 4
    n2, n4 = EXTRA // 2, EXTRA // 4
    sds = jax.ShapeDtypeStruct
    bf16 = lambda *shape: sds(shape, BF16)
    most_first, most_last = max(FIRST.values()), max(LAST.values())

    def scratch_for(count):
        return [
            pltpu.VMEM((count, 2 * ext, cols), BF16),
            pltpu.VMEM((3, count, gr, cols), BF16),
            pltpu.VMEM((count, 6 * gr, cols), BF16),
            pltpu.VMEM((count, n_rows, cols), BF16),
        ]

    layer_flops = 2 * cols * (3 * gr * 2 * ext + 3 * gr * cols + n_rows * 3 * gr + n_rows * quarter)

    dma = pltpu.SemaphoreType.DMA
    s1, s2, vol = call(
        load_kernel,
        [bf16(depth * NEED, cols)] * 2 + [bf16(depth, rows, cols)],
        [volume], [dma((3,))], "load", n_hbm=1,
    )
    inner = [(i, i + 1) for i in range(1, n_row - 1, 2)]
    inner = inner + [(j, i) for i, j in inner]
    r2 = lax.ppermute(s2, "row", inner)
    r1 = lax.ppermute(s1, "row", [(i, i ^ 1) for i in range(n_row)])
    (w,) = call(
        stage_kernel, [bf16(*table.shape)], [jnp.asarray(table)], [], "stage", aliases={0: 0}
    )
    own, zmsg, *xown = call(
        lambda *refs: edges_kernel(n_col, *refs),
        [bf16(pairs, SLOTS, 128), bf16(2 * R * rows + n2 * 16, 128)]
        + [bf16(pairs, HALO, 128)] * n_side,
        [vol], [pltpu.VMEM((pairs, 16, 128), BF16)], "edges",
    )
    swap = [(0, 1), (1, 0)]
    zown = lax.ppermute(zmsg, "gz", swap)

    yud, halo, zcmsg, *messages = call(
        lambda *refs: pack_kernel(place_of, n_col, *refs),
        [bf16(depth, 2 * HALO, cols), bf16(quads, SLOTS, 128), bf16(128 + n4 * 16, 128)]
        + [bf16(pairs + quads, HALO, 128)] * n_side
        + [bf16(n2 + n4, HALO, 128)] * n_side,
        [r1, r2, w] + xown, [pltpu.VMEM((quads, 16, 128), BF16)], "pack",
    )
    zcorner = lax.ppermute(zcmsg, "gz", swap)
    xs, zxs = [], []
    for side in range(n_side):
        step = 1 - 2 * side
        line = swap if n_col == 2 else [
            (i, i + step) for i in range(n_col) if 0 <= i + step < n_col
        ]
        both = [(z * n_col + i, (1 - z) * n_col + j) for z in range(2) for i, j in line]
        xs.append(lax.ppermute(messages[side], "col", line))
        zxs.append(lax.ppermute(messages[n_side + side], ("gz", "col"), both))

    (u1,) = call(
        lambda *refs: first_kernel(place_of, n_row, *refs),
        [sds((most_first, n_rows, quarter), F32)],
        [vol, yud, w], scratch_for(most_first), "first", flops=most_first * layer_flops,
    )
    u2, send = call(
        lambda *refs: near_kernel(place_of, zs, n_row, *refs),
        [sds((EDGE, n_rows, quarter), F32), bf16(n_rows, 2 * quarter)],
        [vol, yud, zown, zcorner, u1, w],
        [pltpu.VMEM((R, ext, cols), BF16)] + scratch_for(EDGE),
        "near", flops=EDGE * layer_flops,
    )
    sums = lax.ppermute(send, "gz", swap)

    (far,) = call(
        lambda zown, zcorner, *refs: beyond_kernel(
            n_col, rows, zown, zcorner, refs[:n_side], refs[n_side]
        ),
        [bf16(EXTRA, SLOTS, 128)], [zown, zcorner] + zxs, [], "beyond", flops=EDGE * layer_flops,
    )

    def last_body(*refs):
        head, x_refs, tail = refs[0:8], refs[8 : 8 + n_side], refs[8 + n_side :]
        last_kernel(place_of, zs, n_row, n_col, *head, x_refs, *tail)

    count = depth + 8
    (result,) = call(
        last_body,
        [sds((6, depth // 4, quarter_rows, quarter), F32)],
        [vol, yud, own, halo, far, u1, u2, w] + xs,
        [
            pltpu.VMEM((count * SLOTS, 128), BF16),
            pltpu.VMEM((count * SLOTS, 128), BF16),
            pltpu.VMEM((count // 8, 6 * gr, 256), BF16),
            pltpu.VMEM((most_last, n_rows, quarter), F32),
        ]
        + scratch_for(most_last),
        "last", flops=(most_last + 3) * layer_flops,
    )
    (out,) = call(add_kernel, [sds(result.shape, F32)], [result, sums], [], "add")
    return out


def solution(mesh):
    return jax.shard_map(
        per_device,
        mesh=mesh,
        in_specs=(P("gz", "row", "col"),),
        out_specs=P(None, "gz", "row", "col"),
        check_vma=False,
    )
```

```python
import jax
import jax.numpy as jnp
import ml_dtypes
import numpy as np
from jax import lax
from jax.experimental import pallas as pl
from jax.experimental.pallas import tpu as pltpu
from jax.sharding import PartitionSpec as P

R = 3
R2 = 8
HALO = 16
NEED = R + R2
EXTRA = 12
SLOTS = 32
NT = (((1,), (1,)), ((), ()))
F32 = jnp.float32
BF16 = jnp.bfloat16

pair_table = ((0, 0), (1, 1), (2, 2), (0, 1), (0, 2), (1, 2))


def gauss_taps(radius):
    offsets = np.arange(-radius, radius + 1).astype(np.float32)
    spread = np.float32(radius / 3.0)
    smooth = np.exp(-offsets * offsets / (np.float32(2.0) * spread * spread))
    smooth = smooth / np.sum(smooth)
    slopes = offsets * smooth
    slopes = slopes / np.sum(offsets * slopes)
    as_f32 = lambda t: t.astype(ml_dtypes.bfloat16).astype(np.float32)
    return as_f32(smooth), as_f32(slopes)


SMOOTH_D, SLOPE_D = gauss_taps(R)
SMOOTH_I, _ = gauss_taps(R2)


def band(taps, sources, targets):
    radius = len(taps) // 2
    gap = np.asarray(sources)[:, None] - np.asarray(targets)[None, :]
    return np.where(np.abs(gap) <= radius, taps[np.clip(gap + radius, 0, 2 * radius)], 0.0)


def weight_table(depth, rows, cols):
    ext = rows + 2 * HALO
    grad_rows = rows + 16
    far = 10**6
    y_in = np.arange(ext) - HALO
    y_out = np.arange(grad_rows) - R2
    smooth_y = band(SMOOTH_D, y_in, y_out).T
    slope_y = band(SLOPE_D, y_in, y_out).T
    zero = np.zeros_like(smooth_y)
    wy = np.block([[smooth_y, zero], [slope_y, zero], [zero, smooth_y]])
    order = np.concatenate([np.arange(rows), np.arange(HALO) - HALO, rows + np.arange(HALO)]) + HALO
    x_all = np.arange(cols)
    slot_in = np.full(SLOTS, far)
    slot_in[0:8] = cols + np.arange(8)
    slot_in[8:14] = np.arange(6)
    slot_in[14:20] = cols - 6 + np.arange(6)
    slot_in[21:32] = np.arange(-11, 0)
    slot_out = np.full(SLOTS, -far)
    slot_out[0:11] = np.arange(-8, 3)
    slot_out[11:19] = cols - 3 + np.arange(8)
    eye8 = np.eye(8)
    inner = np.where((x_all >= R) & (x_all < cols - R), x_all, far)
    quarter = cols // 4
    coarse_edge = np.full(8, 3 * far)
    coarse_edge[0:5] = [0, 1, 2, quarter - 2, quarter - 1]
    xs_edge = band(SMOOTH_I, slot_out, 4 * coarse_edge)
    ys = band(SMOOTH_I, y_out, 4 * np.arange(rows // 4)).T
    zs = band(SMOOTH_I, np.arange(depth), 4 * (np.arange(depth // 4 + 4) - 2))
    place = np.zeros((8, 128))
    for j in range(5):
        place[j, coarse_edge[j]] = 1.0
    own_z = 4 * np.arange(depth // 4)
    g = [
        np.einsum("zq,jx->zjqx", band(SMOOTH_I, np.arange(depth + 8) + first, own_z), place)
        for first in (0, -8)
    ]
    g = [t.reshape((depth + 8) * 8, len(own_z) * 128) for t in g]
    packed = np.arange(depth * NEED)
    above = np.zeros((depth * HALO, depth * NEED))
    above[packed + packed // NEED * (HALO - NEED) + HALO - NEED, packed] = 1.0
    below = np.zeros((depth * HALO, depth * NEED))
    below[packed + packed // NEED * (HALO - NEED), packed] = 1.0
    used = 2 * R + 13
    packed = np.arange(R * used)
    corner = np.zeros((64, R * 2 * HALO))
    corner[packed, packed + packed // used * (2 * HALO - used) + HALO - NEED] = 1.0
    parts = {
        "above": above,
        "below": below,
        "corner": corner,
        "corner_back": corner.T,
        "wy": wy,
        "wy_strip": np.concatenate([smooth_y, slope_y])[:, order],
        "wy_strip_slope": smooth_y[:, order],
        "wxd": band(SLOPE_D, x_all, x_all),
        "wxs": band(SMOOTH_D, x_all, x_all),
        "bdd": np.kron(eye8, band(SLOPE_D, slot_in, slot_out)),
        "bds": np.kron(eye8, band(SMOOTH_D, slot_in, slot_out)),
        "ysm": np.kron(np.eye(3), ys),
        "xsm": band(SMOOTH_I, inner, 4 * np.arange(quarter)),
        "bdx": np.kron(eye8, xs_edge),
        "g_low0": g[0][:, 0:256],
        "g_low1": g[0][:, 256:512],
        "g_high0": g[1][:, 0:256],
        "g_high1": g[1][:, 256:512],
    }
    place_of, blocks, at = {}, [], 0
    for name, part in parts.items():
        height = -(-part.shape[0] // 16) * 16
        block = np.zeros((height, 256), np.float32)
        block[: part.shape[0], : part.shape[1]] = part
        place_of[name] = (at, part.shape[0], part.shape[1])
        blocks.append(block)
        at += height
    return np.concatenate(blocks).astype(ml_dtypes.bfloat16), place_of, zs


def z_filter(v, count):
    for z in range(count):
        w = v[z : z + 7]
        smooth = w[3] * float(SMOOTH_D[3])
        slope = None
        for s in (1, 2, 3):
            smooth = smooth + (w[3 + s] + w[3 - s]) * float(SMOOTH_D[3 + s])
            term = (w[3 + s] - w[3 - s]) * float(SLOPE_D[3 + s])
            slope = term if slope is None else slope + term
        yield z, smooth, slope


def getter(place_of, w):
    def get(name, width=None):
        at, height, own_width = place_of[name]
        return w[at : at + height, 0 : (width or own_width)]

    return get


def row_mask(get, n_row, rows, gr, quarter_rows):
    row = lax.axis_index("row")
    lane = lax.broadcasted_iota(jnp.int32, (3 * quarter_rows, 3 * gr), 1)
    y_out = lax.rem(lane, gr) - R2
    outside = ((row == 0) & (y_out < 0)) | ((row == n_row - 1) & (y_out >= rows))
    return jnp.where(outside, 0.0, get("ysm").astype(F32)).astype(BF16)


def layers_to_sums(get, ysm, load, count, shape, u_ref, zf, planes, prod, sm):
    rows, cols = shape
    ext = rows + 2 * HALO
    gr = rows + 16
    n_rows = 6 * (rows // 4)
    half_rows = n_rows // 2
    rest = jnp.zeros((8, 128), F32)
    wy = get("wy")

    def z_filters(first, n):
        for tile in range(cols // 128):
            lanes = slice(tile * 128, tile * 128 + 128)
            for at in range(0, ext, 16):
                blocks = load(at, lanes, first, first + n + 2 * R)
                if at == rows + HALO:
                    blocks = [block[0:8] for block in blocks]
                for z, smooth, slope in z_filter(blocks, n):
                    if at == rows + HALO:
                        smooth = jnp.concatenate([smooth, rest], axis=0)
                        slope = jnp.concatenate([slope, rest], axis=0)
                    zf[first + z, at : at + 16, lanes] = smooth.astype(BF16)
                    zf[first + z, ext + at : ext + at + 16, lanes] = slope.astype(BF16)

    def y_filters(first, n):
        for z in range(first, first + n):
            out = jnp.dot(wy, zf[z], preferred_element_type=F32).astype(BF16)
            planes[0, z] = out[0:gr]
            planes[1, z] = out[gr : 2 * gr]
            planes[2, z] = out[2 * gr :]

    def x_filters(first, n):
        grads = []
        for f, name in enumerate(("wxd", "wxs", "wxs")):
            part = planes[f, first : first + n].reshape(n * gr, cols)
            out = jnp.dot(part, get(name), preferred_element_type=F32)
            grads.append(out.astype(BF16).reshape(n, gr, cols))
        for c, (a, b) in enumerate(pair_table):
            prod[first : first + n, c * gr : (c + 1) * gr] = grads[a] * grads[b]

    def y_smoothing(first, n):
        for z in range(first, first + n):
            for half in range(2):
                part = prod[z, half * 3 * gr : (half + 1) * 3 * gr]
                out = jnp.dot(ysm, part, preferred_element_type=F32)
                sm[z, half * half_rows : (half + 1) * half_rows] = out.astype(BF16)

    n_group = -(-count // GROUP)
    ends = [count * i // n_group for i in range(n_group + 1)]
    stages = (z_filters, y_filters, x_filters, y_smoothing)
    for step in range(n_group + len(stages) - 1):
        for k, stage in enumerate(stages):
            i = step - k
            if 0 <= i < n_group:
                stage(ends[i], ends[i + 1] - ends[i])
    out = jnp.dot(
        sm[0:count].reshape(count * n_rows, cols), get("xsm"), preferred_element_type=F32
    )
    u_ref[0:count] = out.reshape(count, n_rows, cols // 4)


def block_loader(vol, yud, rows):
    def layer(z, at, lanes):
        if at < HALO:
            return yud[z, at : at + 16, lanes].astype(F32)
        if at < HALO + rows:
            return vol[z, at - HALO : at - HALO + 16, lanes].astype(F32)
        return yud[z, at - rows : at - rows + 16, lanes].astype(F32)

    return layer


def spread_rows(first):
    shape = (16 * NEED, 16 * HALO)
    packed = lax.broadcasted_iota(jnp.int32, shape, 0)
    full = lax.broadcasted_iota(jnp.int32, shape, 1)
    z = lax.shift_right_logical(packed * 373, 12)
    return jnp.where(full == packed + z * (HALO - NEED) + first, 1.0, 0.0).astype(BF16)


def load_kernel(vol, s1, s2, vol_out, sems):
    depth, rows, cols = vol.shape
    odd = lax.rem(lax.axis_index("row"), 2) == 1
    parts = (slice(0, HALO), slice(rows - HALO, rows), slice(HALO, rows - HALO))
    copies = [
        pltpu.make_async_copy(vol.at[:, part, :], vol_out.at[:, part, :], sems.at[i])
        for i, part in enumerate(parts)
    ]
    for copy in copies:
        copy.start()
    first_rows, last_rows = spread_rows(0), spread_rows(HALO - NEED)
    copies[0].wait()
    copies[1].wait()
    to_before = jnp.dot(
        first_rows, vol_out[:, 0:HALO].reshape(depth * HALO, cols), preferred_element_type=F32
    ).astype(BF16)
    to_after = jnp.dot(
        last_rows, vol_out[:, rows - HALO :].reshape(depth * HALO, cols), preferred_element_type=F32
    ).astype(BF16)
    s1[...] = jnp.where(odd, to_before, to_after)
    s2[...] = jnp.where(odd, to_after, to_before)
    copies[2].wait()


def column_select(n_col, cols, odd):
    n_side = 1 if n_col == 2 else 2
    shape = (SLOTS + 16 * n_side, cols)
    row = lax.broadcasted_iota(jnp.int32, shape, 0)
    lane = lax.broadcasted_iota(jnp.int32, shape, 1)
    picked = ((row >= 8) & (row < 14) & (lane == row - 8)) | (
        (row >= 14) & (row < 20) & (lane == row - 20 + cols)
    )
    for side in range(n_side):
        if n_col == 2:
            here = lax.axis_index("col")
            near = jnp.where(here == 0, cols - 8, 0)
            behind = jnp.where(here == 0, cols - NEED, -NEED)
        else:
            near = (cols - 8, 0)[side]
            behind = (cols - NEED, -NEED)[side]
        at = row - SLOTS - 16 * side
        picked = picked | ((at >= 0) & (at < 8) & (lane == at + near))
        at = at - 8 - (1 if odd else 5)
        picked = picked | ((at >= 0) & (at < 3) & (lane == at + behind))
    return jnp.where(picked, 1.0, 0.0).astype(BF16)


def pick_columns(selects, sources, n_side):
    slots, middles = [], []
    near, behind = [[] for _ in range(n_side)], [[] for _ in range(n_side)]
    for b, source in enumerate(sources):
        picked = lax.dot_general(selects[b % 2], source, NT, preferred_element_type=F32)
        slots.append(picked[0:SLOTS].astype(BF16))
        middles.append(picked[8:24].astype(BF16))
        for side in range(n_side):
            at = SLOTS + 16 * side
            near[side].append(picked[at : at + 8])
            part = picked[at + 8 : at + 16]
            if b % 2:
                behind[side][-1] = behind[side][-1] + part
            else:
                behind[side].append(part)
    messages = [
        jnp.concatenate(near[side] + behind[side], axis=0).astype(BF16) for side in range(n_side)
    ]
    return slots, middles, messages


def halve(chunk, at, value):
    n = value.shape[0]
    chunk[at : at + n] = value[:, 0:128]
    chunk[at + n : at + 2 * n] = value[:, 128:256]


def joined_halves(chunk, at, n):
    return jnp.concatenate([chunk[at : at + n], chunk[at + n : at + 2 * n]], axis=1)


def edges_kernel(n_col, vol, own, zmsg, *refs):
    depth, rows, cols = vol.shape
    gz = lax.axis_index("gz")
    refs, middles = refs[:-1], refs[-1]
    selects = [column_select(n_col, cols, odd) for odd in (False, True)]
    sources = [vol[2 * b : 2 * b + 2].reshape(2 * rows, cols) for b in range(depth // 2)]
    slots, middle, messages = pick_columns(selects, sources, len(refs))
    for b in range(depth // 2):
        own[b], middles[b] = slots[b], middle[b]
    for ref, message in zip(refs, messages):
        ref[...] = message
    base = jnp.where(gz == 0, depth - R, 0)
    halve(zmsg, 0, vol[pl.ds(base, R)].reshape(R * rows, cols))
    first = jnp.where(gz == 0, (depth - EXTRA) // 2, 0)
    n = EXTRA // 2
    zmsg[2 * R * rows :] = middles[pl.ds(first, n)].reshape(n * 16, 128)


def pack_kernel(place_of, n_col, r1, r2, w, *refs):
    n_side = 1 if n_col == 2 else 2
    xown, (yud, halo, zcorner) = refs[:n_side], refs[n_side : n_side + 3]
    xmsgs, zxmsgs = refs[n_side + 3 : 2 * n_side + 3], refs[2 * n_side + 3 : 3 * n_side + 3]
    middles = refs[3 * n_side + 3]
    depth, cols = yud.shape[0], yud.shape[2]
    gz = lax.axis_index("gz")
    odd = lax.rem(lax.axis_index("row"), 2) == 1
    get = getter(place_of, w)
    got1, got2 = r1[...], r2[...]
    for at, name, part in (
        (0, "above", jnp.where(odd, got1, got2)),
        (HALO, "below", jnp.where(odd, got2, got1)),
    ):
        out = jnp.dot(get(name), part, preferred_element_type=F32).astype(BF16)
        yud[:, at : at + HALO, :] = out.reshape(depth, HALO, cols)
    selects = [column_select(n_col, cols, odd) for odd in (False, True)]
    pairs, quads = depth // 2, depth // 4
    sources = [yud[4 * b : 4 * b + 4].reshape(4 * 2 * HALO, cols) for b in range(quads)]
    slots, middle, messages = pick_columns(selects, sources, n_side)
    for b in range(quads):
        halo[b], middles[b] = slots[b], middle[b]
    n2, n4 = EXTRA // 2, EXTRA // 4
    low = gz == 0
    first2 = jnp.where(low, pairs - n2, 0)
    first4 = jnp.where(low, quads - n4, 0)
    skip = 8 * (pairs - n2)
    for x_own, message, xmsg, zxmsg in zip(xown, messages, xmsgs, zxmsgs):
        split = x_own.shape[0]
        xmsg[0:split] = x_own[...]
        xmsg[split:] = message
        zxmsg[0 : 8 * n2] = x_own[pl.ds(pl.multiple_of(8 * first2, 16), 8 * n2)]
        zxmsg[8 * n2 : 8 * n2 + message.shape[0]] = message
        at = 8 * n2 + message.shape[0]
        behind = x_own[8 * pairs :]
        sent = 4 * n2
        zxmsg[at : at + sent] = jnp.where(
            low, behind[skip // 2 : skip // 2 + sent], behind[0:sent]
        )
    base = jnp.where(gz == 0, depth - R, 0)
    edge = yud[pl.ds(base, R)].reshape(R * 2 * HALO, cols)
    halve(zcorner, 0, jnp.dot(get("corner"), edge, preferred_element_type=F32).astype(BF16))
    zcorner[128:] = middles[pl.ds(first4, n4)].reshape(n4 * 16, 128)


def stage_kernel(w, w_out):
    pass


FIRST = {True: 5, False: 3}
LAST = {True: 8, False: 10}
GROUP = 4
EDGE = R


def by_half(body):
    low = lax.axis_index("gz") == 0
    pl.when(low)(lambda: body(True))
    pl.when(jnp.logical_not(low))(lambda: body(False))


def first_kernel(place_of, n_row, vol, yud, w, u_ref, *scratch):
    depth, rows, cols = vol.shape
    get = getter(place_of, w)
    ysm = row_mask(get, n_row, rows, rows + 16, rows // 4)
    layer = block_loader(vol, yud, rows)

    def body(low):
        count = FIRST[low]
        base = depth - EDGE - count - R if low else 0
        load = lambda at, lanes, lo, hi: [layer(base + k, at, lanes) for k in range(lo, hi)]
        layers_to_sums(get, ysm, load, count, (rows, cols), u_ref, *scratch)

    by_half(body)


def held_layers(depth, low):
    if low:
        near = depth - EDGE
        return range(near - FIRST[low], near), range(near, depth), range(LAST[low])
    last = EDGE + FIRST[low]
    return range(EDGE, last), range(EDGE), range(last, depth)


def weighted(total, refs, held, weights):
    for ref, layers in zip(refs, held):
        for k, z in enumerate(layers):
            if weights[z] != 0.0:
                term = ref[k] * float(weights[z])
                total = term if total is None else total + term
    return total


def near_kernel(place_of, zs, n_row, vol, yud, zown, zcorner, u1, w, u_ref, send_ref, zext, *scratch):
    depth, rows, cols = vol.shape
    n_zq = zs.shape[1]
    get = getter(place_of, w)
    ysm = row_mask(get, n_row, rows, rows + 16, rows // 4)
    corner = jnp.dot(
        get("corner_back"), joined_halves(zcorner, 0, 64), preferred_element_type=F32
    ).astype(BF16).reshape(R, 2 * HALO, cols)
    zext[:, 0:HALO] = corner[:, 0:HALO]
    zext[:, HALO : HALO + rows] = joined_halves(zown, 0, R * rows).reshape(R, rows, cols)
    zext[:, HALO + rows :] = corner[:, HALO:]
    layer = block_loader(vol, yud, rows)

    def body(low):
        start = depth - R if low else 0
        outer = depth - 2 * R if low else R

        def load(at, lanes, lo, hi):
            out = []
            for k in range(lo, hi):
                if R <= k < 2 * R:
                    out.append(layer(start + k - R, at, lanes))
                elif (k < R) == low:
                    out.append(layer(outer + k % R, at, lanes))
                else:
                    out.append(zext[k % R, at : at + 16, lanes].astype(F32))
            return out

        layers_to_sums(get, ysm, load, EDGE, (rows, cols), u_ref, *scratch)
        held = held_layers(depth, low)[0:2]
        first_q = n_zq - 2 if low else 0
        sends = [weighted(None, (u1, u_ref), held, zs[:, first_q + k]) for k in range(2)]
        send_ref[...] = jnp.concatenate(sends, axis=1).astype(BF16)

    by_half(body)


def strip_tools(n_col, rows):
    col = lax.axis_index("col")
    slots = lax.broadcasted_iota(jnp.int32, (SLOTS, 128), 0)
    if n_col == 2:
        keep = ((slots < 8) & (col == 0)) | ((slots >= 21) & (col == 1))
    else:
        keep = (slots < 8) | (slots >= 21)

    def join(part, messages, at, behind_at, b):
        def eight(message, start, i):
            first = start + 16 * (i // 2)
            return message[first : first + 16].astype(F32)[8 * (i % 2) : 8 * (i % 2) + 8]

        left, right = messages[0], messages[-1]
        behind = eight(left, behind_at, b // 2)
        if b % 2:
            behind = pltpu.roll(behind, 4, 0)
        rows_of = [eight(right, at, b), jnp.zeros((8, 128), F32), behind, eight(left, at, b)]
        return jnp.where(keep, jnp.concatenate(rows_of, axis=0), part)

    lanes = lax.broadcasted_iota(jnp.int32, (SLOTS, 128), 1)

    def layers_of(pairs, quads):
        out = []
        for z in range(2 * len(pairs)):
            left, right = pairs[z // 2], quads[z // 4]
            if z % 2:
                left = pltpu.roll(left, 64, 1)
            turn = (rows - 32 * (z % 4)) % 128
            if turn:
                right = pltpu.roll(right, turn, 1)
            out.append(jnp.where(lanes < rows, left, right))
        return out

    return join, layers_of


def beyond_kernel(n_col, n_quads, rows, zown, zcorner, zxs, out):
    join, layers_of = strip_tools(n_col, rows)

    def from_middle(ref, at, b):
        rim = jnp.zeros((8, 128), F32)
        middle = ref[at + 16 * b : at + 16 * (b + 1)].astype(F32)
        return jnp.concatenate([rim, middle, rim], axis=0)

    n2, n4 = EXTRA // 2, EXTRA // 4
    far_at = 8 * n2
    far_behind = far_at + 8 * n_quads
    behind_at = far_behind + 4 * n_quads

    def body(low):
        first = 0 if low else n_quads - n4
        layers = layers_of(
            [join(from_middle(zown, 2 * R * rows, b), zxs, 0, behind_at, b) for b in range(n2)],
            [
                join(from_middle(zcorner, 128, b), zxs, far_at, far_behind, first + b)
                for b in range(n4)
            ],
        )
        for k, layer in enumerate(layers):
            out[k] = layer.astype(BF16)

    by_half(body)


def last_kernel(place_of, zs, n_row, n_col, vol, yud, own, halo, far, u1, u2, w, xs, own_ref,
                hs, hd, pstrip, u3, *scratch):
    depth, rows, cols = vol.shape
    gr = rows + 16
    quarter_rows, quarter = rows // 4, cols // 4
    get = getter(place_of, w)
    col = lax.axis_index("col")
    ysm = row_mask(get, n_row, rows, gr, quarter_rows)
    join, layers_of = strip_tools(n_col, rows)
    layer = block_loader(vol, yud, rows)
    slot = lax.rem(lax.broadcasted_iota(jnp.int32, (3 * quarter_rows, 256), 1), SLOTS)
    outside_x = ((col == 0) & (slot < 8)) | ((col == n_col - 1) & (slot >= 14))
    n_rows = 6 * quarter_rows
    count = depth + 8
    n = count // 8

    def body(low):
        first = 0 if low else depth - LAST[low]

        def load(at, lanes, lo, hi):
            out = []
            for z in range(first - R + lo, first - R + hi):
                inside = 0 <= z < depth
                out.append(layer(z, at, lanes) if inside else jnp.zeros((16, 128), F32))
            return out

        layers_to_sums(get, ysm, load, LAST[low], (rows, cols), u3, *scratch)
        own_layers = layers_of(
            [join(own[b].astype(F32), xs, 0, 4 * depth, b) for b in range(depth // 2)],
            [
                join(halo[b].astype(F32), xs, 6 * depth, 8 * depth, b)
                for b in range(depth // 4)
            ],
        )
        beyond = [far[k].astype(F32) for k in range(EXTRA)]
        zero = [jnp.zeros((SLOTS, 128), F32)] * R
        if low:
            layers = zero + own_layers + beyond[0:11]
        else:
            layers = beyond[1:12] + own_layers + zero
        for z, smooth, slope in z_filter(layers, count):
            hs[SLOTS * z : SLOTS * (z + 1)] = smooth.astype(BF16)
            hd[SLOTS * z : SLOTS * (z + 1)] = slope.astype(BF16)
        p01 = lax.dot_general(
            get("wy_strip", 128), hs[...], NT, preferred_element_type=F32
        ).astype(BF16)
        p2 = lax.dot_general(
            get("wy_strip_slope", 128), hd[...], NT, preferred_element_type=F32
        ).astype(BF16)
        groups = [slice(256 * c, 256 * (c + 1)) for c in range(n)]
        stacks = [
            jnp.concatenate([p[:, g] for g in groups], axis=0) for p in (p01[0:gr], p01[gr:], p2)
        ]
        grads = [
            jnp.dot(stack, get(name), preferred_element_type=F32).astype(BF16).reshape(n, gr, 256)
            for stack, name in zip(stacks, ("bdd", "bds", "bds"))
        ]
        for c, (a, b) in enumerate(pair_table):
            pstrip[:, c * gr : (c + 1) * gr] = grads[a] * grads[b]
        smoothed = []
        for c in range(n):
            for half in range(2):
                part = pstrip[c, half * 3 * gr : (half + 1) * 3 * gr]
                out = jnp.dot(ysm, part, preferred_element_type=F32)
                smoothed.append(jnp.where(outside_x, 0.0, out).astype(BF16))
        u = jnp.dot(jnp.concatenate(smoothed, axis=0), get("bdx"), preferred_element_type=F32)
        u = u.astype(BF16)
        sums = []
        for name in ("0", "1"):
            at = place_of[("g_low" if low else "g_high") + name][0]
            total = None
            for c in range(n):
                g = w[at + 64 * c : at + 64 * (c + 1), :]
                term = jnp.dot(u[n_rows * c : n_rows * (c + 1)], g, preferred_element_type=F32)
                total = term if total is None else total + term
            sums += [total[:, 0:quarter], total[:, 128 : 128 + quarter]]
        held = held_layers(depth, low)
        for q in range(depth // 4):
            total = weighted(sums[q], (u1, u2, u3), held, zs[:, q + 2])
            own_ref[:, q] = total.reshape(6, quarter_rows, quarter)

    by_half(body)


def add_kernel(own, got, out):
    n_q, quarter = own.shape[1], own.shape[3]
    low = lax.axis_index("gz") == 0
    parts = [
        got[:, k * quarter : (k + 1) * quarter].astype(F32).reshape(own.shape[0], -1, quarter)
        for k in range(2)
    ]
    for q in range(n_q):
        total = own[:, q]
        if q < 2:
            total = total + parts[q] * jnp.where(low, 0.0, 1.0)
        if q >= n_q - 2:
            total = total + parts[q - n_q + 2] * jnp.where(low, 1.0, 0.0)
        out[:, q] = total


def call(body, outs, operands, scratch, name, flops=0, aliases=None, n_hbm=0):
    vmem = pl.BlockSpec(memory_space=pltpu.VMEM)
    hbm = pl.BlockSpec(memory_space=pltpu.HBM)
    operands = [
        pltpu.with_memory_space_constraint(o, pltpu.HBM) if i < n_hbm else o
        for i, o in enumerate(operands)
    ]
    moved = sum(o.size * o.dtype.itemsize for o in list(outs) + list(operands))
    return pl.pallas_call(
        body,
        out_shape=list(outs),
        in_specs=[hbm] * n_hbm + [vmem] * (len(operands) - n_hbm),
        out_specs=[vmem] * len(outs),
        scratch_shapes=scratch,
        input_output_aliases=aliases or {},
        compiler_params=pltpu.CompilerParams(vmem_limit_bytes=24 * 2**20),
        cost_estimate=pl.CostEstimate(flops=flops, bytes_accessed=moved, transcendentals=0),
        name=name,
    )(*operands)


def per_device(volume):
    depth, rows, cols = volume.shape
    n_row, n_col = lax.axis_size("row"), lax.axis_size("col")
    table, place_of, zs = weight_table(depth, rows, cols)
    ext = rows + 2 * HALO
    gr = rows + 16
    quarter_rows, quarter = rows // 4, cols // 4
    n_rows = 6 * quarter_rows
    n_side = 1 if n_col == 2 else 2
    pairs, quads = depth // 2, depth // 4
    n2, n4 = EXTRA // 2, EXTRA // 4
    sds = jax.ShapeDtypeStruct
    bf16 = lambda *shape: sds(shape, BF16)
    most_first, most_last = max(FIRST.values()), max(LAST.values())

    def scratch_for(count):
        return [
            pltpu.VMEM((count, 2 * ext, cols), BF16),
            pltpu.VMEM((3, count, gr, cols), BF16),
            pltpu.VMEM((count, 6 * gr, cols), BF16),
            pltpu.VMEM((count, n_rows, cols), BF16),
        ]

    layer_flops = 2 * cols * (3 * gr * 2 * ext + 3 * gr * cols + n_rows * 3 * gr + n_rows * quarter)

    dma = pltpu.SemaphoreType.DMA
    s1, s2, vol = call(
        load_kernel,
        [bf16(depth * NEED, cols)] * 2 + [bf16(depth, rows, cols)],
        [volume], [dma((3,))], "load", n_hbm=1,
    )
    inner = [(i, i + 1) for i in range(1, n_row - 1, 2)]
    inner = inner + [(j, i) for i, j in inner]
    r2 = lax.ppermute(s2, "row", inner)
    r1 = lax.ppermute(s1, "row", [(i, i ^ 1) for i in range(n_row)])
    (w,) = call(
        stage_kernel, [bf16(*table.shape)], [jnp.asarray(table)], [], "stage", aliases={0: 0}
    )
    own, zmsg, *xown = call(
        lambda *refs: edges_kernel(n_col, *refs),
        [bf16(pairs, SLOTS, 128), bf16(2 * R * rows + n2 * 16, 128)]
        + [bf16(12 * pairs, 128)] * n_side,
        [vol], [pltpu.VMEM((pairs, 16, 128), BF16)], "edges",
    )
    swap = [(0, 1), (1, 0)]
    zown = lax.ppermute(zmsg, "gz", swap)

    yud, halo, zcmsg, *messages = call(
        lambda *refs: pack_kernel(place_of, n_col, *refs),
        [bf16(depth, 2 * HALO, cols), bf16(quads, SLOTS, 128), bf16(128 + n4 * 16, 128)]
        + [bf16(12 * (pairs + quads), 128)] * n_side
        + [bf16(12 * (n2 + quads) + 8, 128)] * n_side,
        [r1, r2, w] + xown, [pltpu.VMEM((quads, 16, 128), BF16)], "pack",
    )
    zcorner = lax.ppermute(zcmsg, "gz", swap)
    xs, zxs = [], []
    for side in range(n_side):
        step = 1 - 2 * side
        line = swap if n_col == 2 else [
            (i, i + step) for i in range(n_col) if 0 <= i + step < n_col
        ]
        both = [(z * n_col + i, (1 - z) * n_col + j) for z in range(2) for i, j in line]
        xs.append(lax.ppermute(messages[side], "col", line))
        zxs.append(lax.ppermute(messages[n_side + side], ("gz", "col"), both))

    (u1,) = call(
        lambda *refs: first_kernel(place_of, n_row, *refs),
        [sds((most_first, n_rows, quarter), F32)],
        [vol, yud, w], scratch_for(most_first), "first", flops=most_first * layer_flops,
    )
    u2, send = call(
        lambda *refs: near_kernel(place_of, zs, n_row, *refs),
        [sds((EDGE, n_rows, quarter), F32), bf16(n_rows, 2 * quarter)],
        [vol, yud, zown, zcorner, u1, w],
        [pltpu.VMEM((R, ext, cols), BF16)] + scratch_for(EDGE),
        "near", flops=EDGE * layer_flops,
    )
    sums = lax.ppermute(send, "gz", swap)

    (far,) = call(
        lambda zown, zcorner, *refs: beyond_kernel(
            n_col, quads, rows, zown, zcorner, refs[:n_side], refs[n_side]
        ),
        [bf16(EXTRA, SLOTS, 128)], [zown, zcorner] + zxs, [], "beyond", flops=layer_flops,
    )

    def last_body(*refs):
        head, x_refs, tail = refs[0:8], refs[8 : 8 + n_side], refs[8 + n_side :]
        last_kernel(place_of, zs, n_row, n_col, *head, x_refs, *tail)

    count = depth + 8
    (result,) = call(
        last_body,
        [sds((6, depth // 4, quarter_rows, quarter), F32)],
        [vol, yud, own, halo, far, u1, u2, w] + xs,
        [
            pltpu.VMEM((count * SLOTS, 128), BF16),
            pltpu.VMEM((count * SLOTS, 128), BF16),
            pltpu.VMEM((count // 8, 6 * gr, 256), BF16),
            pltpu.VMEM((most_last, n_rows, quarter), F32),
        ]
        + scratch_for(most_last),
        "last", flops=(most_last + 3) * layer_flops,
    )
    (out,) = call(add_kernel, [sds(result.shape, F32)], [result, sums], [], "add")
    return out


def solution(mesh):
    return jax.shard_map(
        per_device,
        mesh=mesh,
        in_specs=(P("gz", "row", "col"),),
        out_specs=P(None, "gz", "row", "col"),
        check_vma=False,
    )
```

```python
import jax
import jax.numpy as jnp
import ml_dtypes
import numpy as np
from jax import lax
from jax.experimental import pallas as pl
from jax.experimental.pallas import tpu as pltpu
from jax.sharding import PartitionSpec as P

R = 3
R2 = 8
HALO = 16
NEED = R + R2
EXTRA = 12
SLOTS = 32
NT = (((1,), (1,)), ((), ()))
F32 = jnp.float32
BF16 = jnp.bfloat16

pair_table = ((0, 0), (1, 1), (2, 2), (0, 1), (0, 2), (1, 2))


def gauss_taps(radius):
    offsets = np.arange(-radius, radius + 1).astype(np.float32)
    spread = np.float32(radius / 3.0)
    smooth = np.exp(-offsets * offsets / (np.float32(2.0) * spread * spread))
    smooth = smooth / np.sum(smooth)
    slopes = offsets * smooth
    slopes = slopes / np.sum(offsets * slopes)
    as_f32 = lambda t: t.astype(ml_dtypes.bfloat16).astype(np.float32)
    return as_f32(smooth), as_f32(slopes)


SMOOTH_D, SLOPE_D = gauss_taps(R)
SMOOTH_I, _ = gauss_taps(R2)


def band(taps, sources, targets):
    radius = len(taps) // 2
    gap = np.asarray(sources)[:, None] - np.asarray(targets)[None, :]
    return np.where(np.abs(gap) <= radius, taps[np.clip(gap + radius, 0, 2 * radius)], 0.0)


def weight_table(depth, rows, cols):
    ext = rows + 2 * HALO
    grad_rows = rows + 16
    far = 10**6
    y_in = np.arange(ext) - HALO
    y_out = np.arange(grad_rows) - R2
    smooth_y = band(SMOOTH_D, y_in, y_out).T
    slope_y = band(SLOPE_D, y_in, y_out).T
    zero = np.zeros_like(smooth_y)
    wy = np.block([[smooth_y, zero], [slope_y, zero], [zero, smooth_y]])
    order = np.concatenate([np.arange(rows), np.arange(HALO) - HALO, rows + np.arange(HALO)]) + HALO
    x_all = np.arange(cols)
    slot_in = np.full(SLOTS, far)
    slot_in[0:8] = cols + np.arange(8)
    slot_in[8:14] = np.arange(6)
    slot_in[14:20] = cols - 6 + np.arange(6)
    slot_in[21:32] = np.arange(-11, 0)
    slot_out = np.full(SLOTS, -far)
    slot_out[0:11] = np.arange(-8, 3)
    slot_out[11:19] = cols - 3 + np.arange(8)
    eye8 = np.eye(8)
    inner = np.where((x_all >= R) & (x_all < cols - R), x_all, far)
    quarter = cols // 4
    coarse_edge = np.full(8, 3 * far)
    coarse_edge[0:5] = [0, 1, 2, quarter - 2, quarter - 1]
    xs_edge = band(SMOOTH_I, slot_out, 4 * coarse_edge)
    ys = band(SMOOTH_I, y_out, 4 * np.arange(rows // 4)).T
    zs = band(SMOOTH_I, np.arange(depth), 4 * (np.arange(depth // 4 + 4) - 2))
    place = np.zeros((8, 128))
    for j in range(5):
        place[j, coarse_edge[j]] = 1.0
    own_z = 4 * np.arange(depth // 4)
    g = [
        np.einsum("zq,jx->zjqx", band(SMOOTH_I, np.arange(depth + 8) + first, own_z), place)
        for first in (0, -8)
    ]
    g = [t.reshape((depth + 8) * 8, len(own_z) * 128) for t in g]
    packed = np.arange(depth * NEED)
    above = np.zeros((depth * HALO, depth * NEED))
    above[packed + packed // NEED * (HALO - NEED) + HALO - NEED, packed] = 1.0
    below = np.zeros((depth * HALO, depth * NEED))
    below[packed + packed // NEED * (HALO - NEED), packed] = 1.0
    used = 2 * R + 13
    packed = np.arange(R * used)
    corner = np.zeros((64, R * 2 * HALO))
    corner[packed, packed + packed // used * (2 * HALO - used) + HALO - NEED] = 1.0
    parts = {
        "above": above,
        "below": below,
        "corner": corner,
        "corner_back": corner.T,
        "wy": wy,
        "wy_strip": np.concatenate([smooth_y, slope_y])[:, order],
        "wy_strip_slope": smooth_y[:, order],
        "wxd": band(SLOPE_D, x_all, x_all),
        "wxs": band(SMOOTH_D, x_all, x_all),
        "bdd": np.kron(eye8, band(SLOPE_D, slot_in, slot_out)),
        "bds": np.kron(eye8, band(SMOOTH_D, slot_in, slot_out)),
        "ysm": np.kron(np.eye(3), ys),
        "xsm": band(SMOOTH_I, inner, 4 * np.arange(quarter)),
        "bdx": np.kron(eye8, xs_edge),
        "g_low0": g[0][:, 0:256],
        "g_low1": g[0][:, 256:512],
        "g_high0": g[1][:, 0:256],
        "g_high1": g[1][:, 256:512],
    }
    place_of, blocks, at = {}, [], 0
    for name, part in parts.items():
        height = -(-part.shape[0] // 16) * 16
        block = np.zeros((height, 256), np.float32)
        block[: part.shape[0], : part.shape[1]] = part
        place_of[name] = (at, part.shape[0], part.shape[1])
        blocks.append(block)
        at += height
    return np.concatenate(blocks).astype(ml_dtypes.bfloat16), place_of, zs


def z_filter(v, count):
    for z in range(count):
        w = v[z : z + 7]
        smooth = w[3] * float(SMOOTH_D[3])
        slope = None
        for s in (1, 2, 3):
            smooth = smooth + (w[3 + s] + w[3 - s]) * float(SMOOTH_D[3 + s])
            term = (w[3 + s] - w[3 - s]) * float(SLOPE_D[3 + s])
            slope = term if slope is None else slope + term
        yield z, smooth, slope


def getter(place_of, w):
    def get(name, width=None):
        at, height, own_width = place_of[name]
        return w[at : at + height, 0 : (width or own_width)]

    return get


def row_mask(get, n_row, rows, gr, quarter_rows):
    row = lax.axis_index("row")
    lane = lax.broadcasted_iota(jnp.int32, (3 * quarter_rows, 3 * gr), 1)
    y_out = lax.rem(lane, gr) - R2
    outside = ((row == 0) & (y_out < 0)) | ((row == n_row - 1) & (y_out >= rows))
    return jnp.where(outside, 0.0, get("ysm").astype(F32)).astype(BF16)


def layers_to_sums(get, ysm, load, count, shape, u_ref, zf, planes, prod, sm):
    rows, cols = shape
    ext = rows + 2 * HALO
    gr = rows + 16
    n_rows = 6 * (rows // 4)
    half_rows = n_rows // 2
    rest = jnp.zeros((8, 128), F32)
    wy = get("wy")

    def z_filters(first, n):
        for tile in range(cols // 128):
            lanes = slice(tile * 128, tile * 128 + 128)
            for at in range(0, ext, 16):
                blocks = load(at, lanes, first, first + n + 2 * R)
                if at == rows + HALO:
                    blocks = [block[0:8] for block in blocks]
                for z, smooth, slope in z_filter(blocks, n):
                    if at == rows + HALO:
                        smooth = jnp.concatenate([smooth, rest], axis=0)
                        slope = jnp.concatenate([slope, rest], axis=0)
                    zf[first + z, at : at + 16, lanes] = smooth.astype(BF16)
                    zf[first + z, ext + at : ext + at + 16, lanes] = slope.astype(BF16)

    def y_filters(first, n):
        for z in range(first, first + n):
            out = jnp.dot(wy, zf[z], preferred_element_type=F32).astype(BF16)
            planes[0, z] = out[0:gr]
            planes[1, z] = out[gr : 2 * gr]
            planes[2, z] = out[2 * gr :]

    def x_filters(first, n):
        grads = []
        for f, name in enumerate(("wxd", "wxs", "wxs")):
            part = planes[f, first : first + n].reshape(n * gr, cols)
            out = jnp.dot(part, get(name), preferred_element_type=F32)
            grads.append(out.astype(BF16).reshape(n, gr, cols))
        for c, (a, b) in enumerate(pair_table):
            prod[first : first + n, c * gr : (c + 1) * gr] = grads[a] * grads[b]

    def y_smoothing(first, n):
        for z in range(first, first + n):
            for half in range(2):
                part = prod[z, half * 3 * gr : (half + 1) * 3 * gr]
                out = jnp.dot(ysm, part, preferred_element_type=F32)
                sm[z, half * half_rows : (half + 1) * half_rows] = out.astype(BF16)

    n_group = -(-count // GROUP)
    ends = [count * i // n_group for i in range(n_group + 1)]
    stages = (z_filters, y_filters, x_filters, y_smoothing)
    for step in range(n_group + len(stages) - 1):
        for k, stage in enumerate(stages):
            i = step - k
            if 0 <= i < n_group:
                stage(ends[i], ends[i + 1] - ends[i])
    out = jnp.dot(
        sm[0:count].reshape(count * n_rows, cols), get("xsm"), preferred_element_type=F32
    )
    u_ref[0:count] = out.reshape(count, n_rows, cols // 4)


def block_loader(vol, yud, rows):
    def layer(z, at, lanes):
        if at < HALO:
            return yud[z, at : at + 16, lanes].astype(F32)
        if at < HALO + rows:
            return vol[z, at - HALO : at - HALO + 16, lanes].astype(F32)
        return yud[z, at - rows : at - rows + 16, lanes].astype(F32)

    return layer


def spread_rows(first):
    shape = (16 * NEED, 16 * HALO)
    packed = lax.broadcasted_iota(jnp.int32, shape, 0)
    full = lax.broadcasted_iota(jnp.int32, shape, 1)
    z = lax.shift_right_logical(packed * 373, 12)
    return jnp.where(full == packed + z * (HALO - NEED) + first, 1.0, 0.0).astype(BF16)


def load_kernel(vol, s1, s2, vol_out, sems):
    depth, rows, cols = vol.shape
    odd = lax.rem(lax.axis_index("row"), 2) == 1
    parts = (slice(0, HALO), slice(rows - HALO, rows), slice(HALO, rows - HALO))
    copies = [
        pltpu.make_async_copy(vol.at[:, part, :], vol_out.at[:, part, :], sems.at[i])
        for i, part in enumerate(parts)
    ]
    for copy in copies:
        copy.start()
    first_rows, last_rows = spread_rows(0), spread_rows(HALO - NEED)
    copies[0].wait()
    copies[1].wait()
    to_before = jnp.dot(
        first_rows, vol_out[:, 0:HALO].reshape(depth * HALO, cols), preferred_element_type=F32
    ).astype(BF16)
    to_after = jnp.dot(
        last_rows, vol_out[:, rows - HALO :].reshape(depth * HALO, cols), preferred_element_type=F32
    ).astype(BF16)
    s1[...] = jnp.where(odd, to_before, to_after)
    s2[...] = jnp.where(odd, to_after, to_before)
    copies[2].wait()


def column_select(n_col, cols, odd):
    n_side = 1 if n_col == 2 else 2
    shape = (SLOTS + 16 * n_side, cols)
    row = lax.broadcasted_iota(jnp.int32, shape, 0)
    lane = lax.broadcasted_iota(jnp.int32, shape, 1)
    picked = ((row >= 8) & (row < 14) & (lane == row - 8)) | (
        (row >= 14) & (row < 20) & (lane == row - 20 + cols)
    )
    for side in range(n_side):
        if n_col == 2:
            here = lax.axis_index("col")
            near = jnp.where(here == 0, cols - 8, 0)
            behind = jnp.where(here == 0, cols - NEED, -NEED)
        else:
            near = (cols - 8, 0)[side]
            behind = (cols - NEED, -NEED)[side]
        at = row - SLOTS - 16 * side
        picked = picked | ((at >= 0) & (at < 8) & (lane == at + near))
        at = at - 8 - (1 if odd else 5)
        picked = picked | ((at >= 0) & (at < 3) & (lane == at + behind))
    return jnp.where(picked, 1.0, 0.0).astype(BF16)


def pick_columns(selects, sources, n_side):
    slots, middles = [], []
    near, behind = [[] for _ in range(n_side)], [[] for _ in range(n_side)]
    for b, source in enumerate(sources):
        picked = lax.dot_general(selects[b % 2], source, NT, preferred_element_type=F32)
        slots.append(picked[0:SLOTS].astype(BF16))
        middles.append(picked[8:24].astype(BF16))
        for side in range(n_side):
            at = SLOTS + 16 * side
            near[side].append(picked[at : at + 8])
            part = picked[at + 8 : at + 16]
            if b % 2:
                behind[side][-1] = behind[side][-1] + part
            else:
                behind[side].append(part)
    messages = [
        jnp.concatenate(near[side] + behind[side], axis=0).astype(BF16) for side in range(n_side)
    ]
    return slots, middles, messages


def halve(chunk, at, value):
    n = value.shape[0]
    chunk[at : at + n] = value[:, 0:128]
    chunk[at + n : at + 2 * n] = value[:, 128:256]


def joined_halves(chunk, at, n):
    return jnp.concatenate([chunk[at : at + n], chunk[at + n : at + 2 * n]], axis=1)


def edges_kernel(n_col, vol, own, zmsg, *refs):
    depth, rows, cols = vol.shape
    gz = lax.axis_index("gz")
    refs, middles = refs[:-1], refs[-1]
    selects = [column_select(n_col, cols, odd) for odd in (False, True)]
    sources = [vol[2 * b : 2 * b + 2].reshape(2 * rows, cols) for b in range(depth // 2)]
    slots, middle, messages = pick_columns(selects, sources, len(refs))
    for b in range(depth // 2):
        own[b], middles[b] = slots[b], middle[b]
    for ref, message in zip(refs, messages):
        ref[...] = message
    base = jnp.where(gz == 0, depth - R, 0)
    halve(zmsg, 0, vol[pl.ds(base, R)].reshape(R * rows, cols))
    first = jnp.where(gz == 0, (depth - EXTRA) // 2, 0)
    n = EXTRA // 2
    zmsg[2 * R * rows :] = middles[pl.ds(first, n)].reshape(n * 16, 128)


def pack_kernel(place_of, n_col, r1, r2, w, *refs):
    n_side = 1 if n_col == 2 else 2
    xown, (yud, halo, zcorner) = refs[:n_side], refs[n_side : n_side + 3]
    xmsgs, zxmsgs = refs[n_side + 3 : 2 * n_side + 3], refs[2 * n_side + 3 : 3 * n_side + 3]
    middles = refs[3 * n_side + 3]
    depth, cols = yud.shape[0], yud.shape[2]
    gz = lax.axis_index("gz")
    odd = lax.rem(lax.axis_index("row"), 2) == 1
    get = getter(place_of, w)
    got1, got2 = r1[...], r2[...]
    for at, name, part in (
        (0, "above", jnp.where(odd, got1, got2)),
        (HALO, "below", jnp.where(odd, got2, got1)),
    ):
        out = jnp.dot(get(name), part, preferred_element_type=F32).astype(BF16)
        yud[:, at : at + HALO, :] = out.reshape(depth, HALO, cols)
    selects = [column_select(n_col, cols, odd) for odd in (False, True)]
    pairs, quads = depth // 2, depth // 4
    sources = [yud[4 * b : 4 * b + 4].reshape(4 * 2 * HALO, cols) for b in range(quads)]
    slots, middle, messages = pick_columns(selects, sources, n_side)
    for b in range(quads):
        halo[b], middles[b] = slots[b], middle[b]
    n2, n4 = EXTRA // 2, EXTRA // 4
    low = gz == 0
    first2 = jnp.where(low, pairs - n2, 0)
    first4 = jnp.where(low, quads - n4, 0)
    skip = 8 * (pairs - n2)
    for x_own, message, xmsg, zxmsg in zip(xown, messages, xmsgs, zxmsgs):
        split = x_own.shape[0]
        xmsg[0:split] = x_own[...]
        xmsg[split:] = message
        zxmsg[0 : 8 * n2] = x_own[pl.ds(pl.multiple_of(8 * first2, 16), 8 * n2)]
        zxmsg[8 * n2 : 8 * n2 + message.shape[0]] = message
        at = 8 * n2 + message.shape[0]
        behind = x_own[8 * pairs :]
        sent = 4 * n2
        zxmsg[at : at + sent] = jnp.where(
            low, behind[skip // 2 : skip // 2 + sent], behind[0:sent]
        )
    base = jnp.where(gz == 0, depth - R, 0)
    edge = yud[pl.ds(base, R)].reshape(R * 2 * HALO, cols)
    halve(zcorner, 0, jnp.dot(get("corner"), edge, preferred_element_type=F32).astype(BF16))
    zcorner[128:] = middles[pl.ds(first4, n4)].reshape(n4 * 16, 128)


def stage_kernel(w, w_out):
    pass


FIRST = {True: 5, False: 3}
LAST = {True: 8, False: 10}
GROUP = 2
EDGE = R


def by_half(body):
    low = lax.axis_index("gz") == 0
    pl.when(low)(lambda: body(True))
    pl.when(jnp.logical_not(low))(lambda: body(False))


def first_kernel(place_of, n_row, vol, yud, w, u_ref, *scratch):
    depth, rows, cols = vol.shape
    get = getter(place_of, w)
    ysm = row_mask(get, n_row, rows, rows + 16, rows // 4)
    layer = block_loader(vol, yud, rows)

    def body(low):
        count = FIRST[low]
        base = depth - EDGE - count - R if low else 0
        load = lambda at, lanes, lo, hi: [layer(base + k, at, lanes) for k in range(lo, hi)]
        layers_to_sums(get, ysm, load, count, (rows, cols), u_ref, *scratch)

    by_half(body)


def held_layers(depth, low):
    if low:
        near = depth - EDGE
        return range(near - FIRST[low], near), range(near, depth), range(LAST[low])
    last = EDGE + FIRST[low]
    return range(EDGE, last), range(EDGE), range(last, depth)


def weighted(total, refs, held, weights):
    for ref, layers in zip(refs, held):
        for k, z in enumerate(layers):
            if weights[z] != 0.0:
                term = ref[k] * float(weights[z])
                total = term if total is None else total + term
    return total


def near_kernel(place_of, zs, n_row, vol, yud, zown, zcorner, u1, w, u_ref, send_ref, corner, *scratch):
    depth, rows, cols = vol.shape
    n_zq = zs.shape[1]
    get = getter(place_of, w)
    ysm = row_mask(get, n_row, rows, rows + 16, rows // 4)
    corner[...] = jnp.dot(
        get("corner_back"), joined_halves(zcorner, 0, 64), preferred_element_type=F32
    ).astype(BF16).reshape(R, 2 * HALO, cols)

    def layer_beyond(k, at, lanes):
        if HALO <= at < HALO + rows:
            first = lanes.start // 128 * R * rows + k * rows + at - HALO
            return zown[first : first + 16].astype(F32)
        first = at if at < HALO else at - rows
        return corner[k, first : first + 16, lanes].astype(F32)

    layer = block_loader(vol, yud, rows)

    def body(low):
        start = depth - R if low else 0
        outer = depth - 2 * R if low else R

        def load(at, lanes, lo, hi):
            out = []
            for k in range(lo, hi):
                if R <= k < 2 * R:
                    out.append(layer(start + k - R, at, lanes))
                elif (k < R) == low:
                    out.append(layer(outer + k % R, at, lanes))
                else:
                    out.append(layer_beyond(k % R, at, lanes))
            return out

        layers_to_sums(get, ysm, load, EDGE, (rows, cols), u_ref, *scratch)
        held = held_layers(depth, low)[0:2]
        first_q = n_zq - 2 if low else 0
        sends = [weighted(None, (u1, u_ref), held, zs[:, first_q + k]) for k in range(2)]
        send_ref[...] = jnp.concatenate(sends, axis=1).astype(BF16)

    by_half(body)


def strip_tools(n_col, rows):
    col = lax.axis_index("col")
    slots = lax.broadcasted_iota(jnp.int32, (SLOTS, 128), 0)
    if n_col == 2:
        keep = ((slots < 8) & (col == 0)) | ((slots >= 21) & (col == 1))
    else:
        keep = (slots < 8) | (slots >= 21)

    def join(part, messages, at, behind_at, b):
        def eight(message, start, i):
            first = start + 16 * (i // 2)
            return message[first : first + 16].astype(F32)[8 * (i % 2) : 8 * (i % 2) + 8]

        left, right = messages[0], messages[-1]
        behind = eight(left, behind_at, b // 2)
        if b % 2:
            behind = pltpu.roll(behind, 4, 0)
        rows_of = [eight(right, at, b), jnp.zeros((8, 128), F32), behind, eight(left, at, b)]
        return jnp.where(keep, jnp.concatenate(rows_of, axis=0), part)

    lanes = lax.broadcasted_iota(jnp.int32, (SLOTS, 128), 1)

    def layers_of(pairs, quads):
        out = []
        for z in range(2 * len(pairs)):
            left, right = pairs[z // 2], quads[z // 4]
            if z % 2:
                left = pltpu.roll(left, 64, 1)
            turn = (rows - 32 * (z % 4)) % 128
            if turn:
                right = pltpu.roll(right, turn, 1)
            out.append(jnp.where(lanes < rows, left, right))
        return out

    return join, layers_of


def beyond_kernel(n_col, n_quads, rows, zown, zcorner, zxs, out):
    join, layers_of = strip_tools(n_col, rows)

    def from_middle(ref, at, b):
        rim = jnp.zeros((8, 128), F32)
        middle = ref[at + 16 * b : at + 16 * (b + 1)].astype(F32)
        return jnp.concatenate([rim, middle, rim], axis=0)

    n2, n4 = EXTRA // 2, EXTRA // 4
    far_at = 8 * n2
    far_behind = far_at + 8 * n_quads
    behind_at = far_behind + 4 * n_quads

    def body(low):
        first = 0 if low else n_quads - n4
        layers = layers_of(
            [join(from_middle(zown, 2 * R * rows, b), zxs, 0, behind_at, b) for b in range(n2)],
            [
                join(from_middle(zcorner, 128, b), zxs, far_at, far_behind, first + b)
                for b in range(n4)
            ],
        )
        for k, layer in enumerate(layers):
            out[k] = layer.astype(BF16)

    by_half(body)


def last_kernel(place_of, zs, n_row, n_col, vol, yud, own, halo, far, u1, u2, w, xs, own_ref,
                hs, hd, pstrip, u3, *scratch):
    depth, rows, cols = vol.shape
    gr = rows + 16
    quarter_rows, quarter = rows // 4, cols // 4
    get = getter(place_of, w)
    col = lax.axis_index("col")
    ysm = row_mask(get, n_row, rows, gr, quarter_rows)
    join, layers_of = strip_tools(n_col, rows)
    layer = block_loader(vol, yud, rows)
    slot = lax.rem(lax.broadcasted_iota(jnp.int32, (3 * quarter_rows, 256), 1), SLOTS)
    outside_x = ((col == 0) & (slot < 8)) | ((col == n_col - 1) & (slot >= 14))
    n_rows = 6 * quarter_rows
    count = depth + 8
    n = count // 8

    def body(low):
        first = 0 if low else depth - LAST[low]

        def load(at, lanes, lo, hi):
            out = []
            for z in range(first - R + lo, first - R + hi):
                inside = 0 <= z < depth
                out.append(layer(z, at, lanes) if inside else jnp.zeros((16, 128), F32))
            return out

        layers_to_sums(get, ysm, load, LAST[low], (rows, cols), u3, *scratch)
        own_layers = layers_of(
            [join(own[b].astype(F32), xs, 0, 4 * depth, b) for b in range(depth // 2)],
            [
                join(halo[b].astype(F32), xs, 6 * depth, 8 * depth, b)
                for b in range(depth // 4)
            ],
        )
        beyond = [far[k].astype(F32) for k in range(EXTRA)]
        zero = [jnp.zeros((SLOTS, 128), F32)] * R
        if low:
            layers = zero + own_layers + beyond[0:11]
        else:
            layers = beyond[1:12] + own_layers + zero
        for z, smooth, slope in z_filter(layers, count):
            hs[SLOTS * z : SLOTS * (z + 1)] = smooth.astype(BF16)
            hd[SLOTS * z : SLOTS * (z + 1)] = slope.astype(BF16)
        p01 = lax.dot_general(
            get("wy_strip", 128), hs[...], NT, preferred_element_type=F32
        ).astype(BF16)
        p2 = lax.dot_general(
            get("wy_strip_slope", 128), hd[...], NT, preferred_element_type=F32
        ).astype(BF16)
        groups = [slice(256 * c, 256 * (c + 1)) for c in range(n)]
        stacks = [
            jnp.concatenate([p[:, g] for g in groups], axis=0) for p in (p01[0:gr], p01[gr:], p2)
        ]
        grads = [
            jnp.dot(stack, get(name), preferred_element_type=F32).astype(BF16).reshape(n, gr, 256)
            for stack, name in zip(stacks, ("bdd", "bds", "bds"))
        ]
        for c, (a, b) in enumerate(pair_table):
            pstrip[:, c * gr : (c + 1) * gr] = grads[a] * grads[b]
        smoothed = []
        for c in range(n):
            for half in range(2):
                part = pstrip[c, half * 3 * gr : (half + 1) * 3 * gr]
                out = jnp.dot(ysm, part, preferred_element_type=F32)
                smoothed.append(jnp.where(outside_x, 0.0, out).astype(BF16))
        u = jnp.dot(jnp.concatenate(smoothed, axis=0), get("bdx"), preferred_element_type=F32)
        u = u.astype(BF16)
        sums = []
        for name in ("0", "1"):
            at = place_of[("g_low" if low else "g_high") + name][0]
            total = None
            for c in range(n):
                g = w[at + 64 * c : at + 64 * (c + 1), :]
                term = jnp.dot(u[n_rows * c : n_rows * (c + 1)], g, preferred_element_type=F32)
                total = term if total is None else total + term
            sums += [total[:, 0:quarter], total[:, 128 : 128 + quarter]]
        held = held_layers(depth, low)
        for q in range(depth // 4):
            total = weighted(sums[q], (u1, u2, u3), held, zs[:, q + 2])
            own_ref[:, q] = total.reshape(6, quarter_rows, quarter)

    by_half(body)


def add_kernel(own, got, out):
    n_q, quarter = own.shape[1], own.shape[3]
    low = lax.axis_index("gz") == 0
    parts = [
        got[:, k * quarter : (k + 1) * quarter].astype(F32).reshape(own.shape[0], -1, quarter)
        for k in range(2)
    ]
    for q in range(n_q):
        total = own[:, q]
        if q < 2:
            total = total + parts[q] * jnp.where(low, 0.0, 1.0)
        if q >= n_q - 2:
            total = total + parts[q - n_q + 2] * jnp.where(low, 1.0, 0.0)
        out[:, q] = total


def call(body, outs, operands, scratch, name, flops=0, aliases=None, n_hbm=0):
    vmem = pl.BlockSpec(memory_space=pltpu.VMEM)
    hbm = pl.BlockSpec(memory_space=pltpu.HBM)
    operands = [
        pltpu.with_memory_space_constraint(o, pltpu.HBM) if i < n_hbm else o
        for i, o in enumerate(operands)
    ]
    moved = sum(o.size * o.dtype.itemsize for o in list(outs) + list(operands))
    return pl.pallas_call(
        body,
        out_shape=list(outs),
        in_specs=[hbm] * n_hbm + [vmem] * (len(operands) - n_hbm),
        out_specs=[vmem] * len(outs),
        scratch_shapes=scratch,
        input_output_aliases=aliases or {},
        compiler_params=pltpu.CompilerParams(vmem_limit_bytes=24 * 2**20),
        cost_estimate=pl.CostEstimate(flops=flops, bytes_accessed=moved, transcendentals=0),
        name=name,
    )(*operands)


def per_device(volume):
    depth, rows, cols = volume.shape
    n_row, n_col = lax.axis_size("row"), lax.axis_size("col")
    table, place_of, zs = weight_table(depth, rows, cols)
    ext = rows + 2 * HALO
    gr = rows + 16
    quarter_rows, quarter = rows // 4, cols // 4
    n_rows = 6 * quarter_rows
    n_side = 1 if n_col == 2 else 2
    pairs, quads = depth // 2, depth // 4
    n2, n4 = EXTRA // 2, EXTRA // 4
    sds = jax.ShapeDtypeStruct
    bf16 = lambda *shape: sds(shape, BF16)
    most_first, most_last = max(FIRST.values()), max(LAST.values())

    def scratch_for(count):
        return [
            pltpu.VMEM((count, 2 * ext, cols), BF16),
            pltpu.VMEM((3, count, gr, cols), BF16),
            pltpu.VMEM((count, 6 * gr, cols), BF16),
            pltpu.VMEM((count, n_rows, cols), BF16),
        ]

    layer_flops = 2 * cols * (3 * gr * 2 * ext + 3 * gr * cols + n_rows * 3 * gr + n_rows * quarter)

    dma = pltpu.SemaphoreType.DMA
    s1, s2, vol = call(
        load_kernel,
        [bf16(depth * NEED, cols)] * 2 + [bf16(depth, rows, cols)],
        [volume], [dma((3,))], "load", n_hbm=1,
    )
    inner = [(i, i + 1) for i in range(1, n_row - 1, 2)]
    inner = inner + [(j, i) for i, j in inner]
    r2 = lax.ppermute(s2, "row", inner)
    r1 = lax.ppermute(s1, "row", [(i, i ^ 1) for i in range(n_row)])
    (w,) = call(
        stage_kernel, [bf16(*table.shape)], [jnp.asarray(table)], [], "stage", aliases={0: 0}
    )
    own, zmsg, *xown = call(
        lambda *refs: edges_kernel(n_col, *refs),
        [bf16(pairs, SLOTS, 128), bf16(2 * R * rows + n2 * 16, 128)]
        + [bf16(12 * pairs, 128)] * n_side,
        [vol], [pltpu.VMEM((pairs, 16, 128), BF16)], "edges",
    )
    swap = [(0, 1), (1, 0)]
    zown = lax.ppermute(zmsg, "gz", swap)

    yud, halo, zcmsg, *messages = call(
        lambda *refs: pack_kernel(place_of, n_col, *refs),
        [bf16(depth, 2 * HALO, cols), bf16(quads, SLOTS, 128), bf16(128 + n4 * 16, 128)]
        + [bf16(12 * (pairs + quads), 128)] * n_side
        + [bf16(12 * (n2 + quads) + 8, 128)] * n_side,
        [r1, r2, w] + xown, [pltpu.VMEM((quads, 16, 128), BF16)], "pack",
    )
    zcorner = lax.ppermute(zcmsg, "gz", swap)
    xs, zxs = [], []
    for side in range(n_side):
        step = 1 - 2 * side
        line = swap if n_col == 2 else [
            (i, i + step) for i in range(n_col) if 0 <= i + step < n_col
        ]
        both = [(z * n_col + i, (1 - z) * n_col + j) for z in range(2) for i, j in line]
        xs.append(lax.ppermute(messages[side], "col", line))
        zxs.append(lax.ppermute(messages[n_side + side], ("gz", "col"), both))

    (u1,) = call(
        lambda *refs: first_kernel(place_of, n_row, *refs),
        [sds((most_first, n_rows, quarter), F32)],
        [vol, yud, w], scratch_for(most_first), "first", flops=most_first * layer_flops,
    )
    u2, send = call(
        lambda *refs: near_kernel(place_of, zs, n_row, *refs),
        [sds((EDGE, n_rows, quarter), F32), bf16(n_rows, 2 * quarter)],
        [vol, yud, zown, zcorner, u1, w],
        [pltpu.VMEM((R, 2 * HALO, cols), BF16)] + scratch_for(EDGE),
        "near", flops=EDGE * layer_flops,
    )
    sums = lax.ppermute(send, "gz", swap)

    (far,) = call(
        lambda zown, zcorner, *refs: beyond_kernel(
            n_col, quads, rows, zown, zcorner, refs[:n_side], refs[n_side]
        ),
        [bf16(EXTRA, SLOTS, 128)], [zown, zcorner] + zxs, [], "beyond", flops=layer_flops,
    )

    def last_body(*refs):
        head, x_refs, tail = refs[0:8], refs[8 : 8 + n_side], refs[8 + n_side :]
        last_kernel(place_of, zs, n_row, n_col, *head, x_refs, *tail)

    count = depth + 8
    (result,) = call(
        last_body,
        [sds((6, depth // 4, quarter_rows, quarter), F32)],
        [vol, yud, own, halo, far, u1, u2, w] + xs,
        [
            pltpu.VMEM((count * SLOTS, 128), BF16),
            pltpu.VMEM((count * SLOTS, 128), BF16),
            pltpu.VMEM((count // 8, 6 * gr, 256), BF16),
            pltpu.VMEM((most_last, n_rows, quarter), F32),
        ]
        + scratch_for(most_last),
        "last", flops=(most_last + 3) * layer_flops,
    )
    (out,) = call(add_kernel, [sds(result.shape, F32)], [result, sums], [], "add")
    return out


def solution(mesh):
    return jax.shard_map(
        per_device,
        mesh=mesh,
        in_specs=(P("gz", "row", "col"),),
        out_specs=P(None, "gz", "row", "col"),
        check_vma=False,
    )
```

```python
import jax
import jax.numpy as jnp
import ml_dtypes
import numpy as np
from jax import lax
from jax.experimental import pallas as pl
from jax.experimental.pallas import tpu as pltpu
from jax.sharding import PartitionSpec as P

R = 3
R2 = 8
HALO = 16
NEED = R + R2
EXTRA = 12
SLOTS = 32
NT = (((1,), (1,)), ((), ()))
F32 = jnp.float32
BF16 = jnp.bfloat16

pair_table = ((0, 0), (1, 1), (2, 2), (0, 1), (0, 2), (1, 2))


def gauss_taps(radius):
    offsets = np.arange(-radius, radius + 1).astype(np.float32)
    spread = np.float32(radius / 3.0)
    smooth = np.exp(-offsets * offsets / (np.float32(2.0) * spread * spread))
    smooth = smooth / np.sum(smooth)
    slopes = offsets * smooth
    slopes = slopes / np.sum(offsets * slopes)
    as_f32 = lambda t: t.astype(ml_dtypes.bfloat16).astype(np.float32)
    return as_f32(smooth), as_f32(slopes)


SMOOTH_D, SLOPE_D = gauss_taps(R)
SMOOTH_I, _ = gauss_taps(R2)


def band(taps, sources, targets):
    radius = len(taps) // 2
    gap = np.asarray(sources)[:, None] - np.asarray(targets)[None, :]
    return np.where(np.abs(gap) <= radius, taps[np.clip(gap + radius, 0, 2 * radius)], 0.0)


def weight_table(depth, rows, cols):
    ext = rows + 2 * HALO
    grad_rows = rows + 16
    far = 10**6
    y_in = np.arange(ext) - HALO
    y_out = np.arange(grad_rows) - R2
    smooth_y = band(SMOOTH_D, y_in, y_out).T
    slope_y = band(SLOPE_D, y_in, y_out).T
    zero = np.zeros_like(smooth_y)
    wy = np.block([[smooth_y, zero], [slope_y, zero], [zero, smooth_y]])
    order = np.concatenate([np.arange(rows), np.arange(HALO) - HALO, rows + np.arange(HALO)]) + HALO
    x_all = np.arange(cols)
    slot_in = np.full(SLOTS, far)
    slot_in[0:8] = cols + np.arange(8)
    slot_in[8:14] = np.arange(6)
    slot_in[14:20] = cols - 6 + np.arange(6)
    slot_in[21:32] = np.arange(-11, 0)
    slot_out = np.full(SLOTS, -far)
    slot_out[0:11] = np.arange(-8, 3)
    slot_out[11:19] = cols - 3 + np.arange(8)
    eye8 = np.eye(8)
    inner = np.where((x_all >= R) & (x_all < cols - R), x_all, far)
    quarter = cols // 4
    coarse_edge = np.full(8, 3 * far)
    coarse_edge[0:5] = [0, 1, 2, quarter - 2, quarter - 1]
    xs_edge = band(SMOOTH_I, slot_out, 4 * coarse_edge)
    ys = band(SMOOTH_I, y_out, 4 * np.arange(rows // 4)).T
    zs = band(SMOOTH_I, np.arange(depth), 4 * (np.arange(depth // 4 + 4) - 2))
    place = np.zeros((8, 128))
    for j in range(5):
        place[j, coarse_edge[j]] = 1.0
    own_z = 4 * np.arange(depth // 4)
    g = [
        np.einsum("zq,jx->zjqx", band(SMOOTH_I, np.arange(depth + 8) + first, own_z), place)
        for first in (0, -8)
    ]
    g = [t.reshape((depth + 8) * 8, len(own_z) * 128) for t in g]
    packed = np.arange(depth * NEED)
    above = np.zeros((depth * HALO, depth * NEED))
    above[packed + packed // NEED * (HALO - NEED) + HALO - NEED, packed] = 1.0
    below = np.zeros((depth * HALO, depth * NEED))
    below[packed + packed // NEED * (HALO - NEED), packed] = 1.0
    used = 2 * R + 13
    packed = np.arange(R * used)
    corner = np.zeros((64, R * 2 * HALO))
    corner[packed, packed + packed // used * (2 * HALO - used) + HALO - NEED] = 1.0
    parts = {
        "above": above,
        "below": below,
        "corner": corner,
        "corner_back": corner.T,
        "wy": wy,
        "wy_strip": np.concatenate([smooth_y, slope_y])[:, order],
        "wy_strip_slope": smooth_y[:, order],
        "wxd": band(SLOPE_D, x_all, x_all),
        "wxs": band(SMOOTH_D, x_all, x_all),
        "bdd": np.kron(eye8, band(SLOPE_D, slot_in, slot_out)),
        "bds": np.kron(eye8, band(SMOOTH_D, slot_in, slot_out)),
        "ysm": np.kron(np.eye(3), ys),
        "xsm": band(SMOOTH_I, inner, 4 * np.arange(quarter)),
        "bdx": np.kron(eye8, xs_edge),
        "g_low0": g[0][:, 0:256],
        "g_low1": g[0][:, 256:512],
        "g_high0": g[1][:, 0:256],
        "g_high1": g[1][:, 256:512],
    }
    place_of, blocks, at = {}, [], 0
    for name, part in parts.items():
        height = -(-part.shape[0] // 16) * 16
        block = np.zeros((height, 256), np.float32)
        block[: part.shape[0], : part.shape[1]] = part
        place_of[name] = (at, part.shape[0], part.shape[1])
        blocks.append(block)
        at += height
    return np.concatenate(blocks).astype(ml_dtypes.bfloat16), place_of, zs


def z_filter(v, count):
    for z in range(count):
        w = v[z : z + 7]
        smooth = w[3] * float(SMOOTH_D[3])
        slope = None
        for s in (1, 2, 3):
            smooth = smooth + (w[3 + s] + w[3 - s]) * float(SMOOTH_D[3 + s])
            term = (w[3 + s] - w[3 - s]) * float(SLOPE_D[3 + s])
            slope = term if slope is None else slope + term
        yield z, smooth, slope


def getter(place_of, w):
    def get(name, width=None):
        at, height, own_width = place_of[name]
        return w[at : at + height, 0 : (width or own_width)]

    return get


def row_mask(get, n_row, rows, gr, quarter_rows):
    row = lax.axis_index("row")
    lane = lax.broadcasted_iota(jnp.int32, (3 * quarter_rows, 3 * gr), 1)
    y_out = lax.rem(lane, gr) - R2
    outside = ((row == 0) & (y_out < 0)) | ((row == n_row - 1) & (y_out >= rows))
    return jnp.where(outside, 0.0, get("ysm").astype(F32)).astype(BF16)


def layers_to_sums(get, ysm, load, count, shape, u_ref, zf, planes, prod, sm):
    rows, cols = shape
    ext = rows + 2 * HALO
    gr = rows + 16
    n_rows = 6 * (rows // 4)
    half_rows = n_rows // 2
    rest = jnp.zeros((8, 128), F32)
    wy = get("wy")

    def z_filters(first, n):
        for tile in range(cols // 128):
            lanes = slice(tile * 128, tile * 128 + 128)
            for at in range(0, ext, 16):
                blocks = load(at, lanes, first, first + n + 2 * R)
                if at == rows + HALO:
                    blocks = [block[0:8] for block in blocks]
                for z, smooth, slope in z_filter(blocks, n):
                    if at == rows + HALO:
                        smooth = jnp.concatenate([smooth, rest], axis=0)
                        slope = jnp.concatenate([slope, rest], axis=0)
                    zf[first + z, at : at + 16, lanes] = smooth.astype(BF16)
                    zf[first + z, ext + at : ext + at + 16, lanes] = slope.astype(BF16)

    def y_filters(first, n):
        for z in range(first, first + n):
            out = jnp.dot(wy, zf[z], preferred_element_type=F32).astype(BF16)
            planes[0, z] = out[0:gr]
            planes[1, z] = out[gr : 2 * gr]
            planes[2, z] = out[2 * gr :]

    def x_filters(first, n):
        grads = []
        for f, name in enumerate(("wxd", "wxs", "wxs")):
            part = planes[f, first : first + n].reshape(n * gr, cols)
            out = jnp.dot(part, get(name), preferred_element_type=F32)
            grads.append(out.astype(BF16).reshape(n, gr, cols))
        for c, (a, b) in enumerate(pair_table):
            prod[first : first + n, c * gr : (c + 1) * gr] = grads[a] * grads[b]

    def y_smoothing(first, n):
        for z in range(first, first + n):
            for half in range(2):
                part = prod[z, half * 3 * gr : (half + 1) * 3 * gr]
                out = jnp.dot(ysm, part, preferred_element_type=F32)
                sm[z, half * half_rows : (half + 1) * half_rows] = out.astype(BF16)

    n_group = -(-count // GROUP)
    ends = [count * i // n_group for i in range(n_group + 1)]
    stages = (z_filters, y_filters, x_filters, y_smoothing)
    for step in range(n_group + len(stages) - 1):
        for k, stage in enumerate(stages):
            i = step - k
            if 0 <= i < n_group:
                stage(ends[i], ends[i + 1] - ends[i])
    out = jnp.dot(
        sm[0:count].reshape(count * n_rows, cols), get("xsm"), preferred_element_type=F32
    )
    u_ref[0:count] = out.reshape(count, n_rows, cols // 4)


def block_loader(vol, yud, rows):
    def layer(z, at, lanes):
        if at < HALO:
            return yud[z, at : at + 16, lanes].astype(F32)
        if at < HALO + rows:
            return vol[z, at - HALO : at - HALO + 16, lanes].astype(F32)
        return yud[z, at - rows : at - rows + 16, lanes].astype(F32)

    return layer


def spread_rows(first):
    shape = (16 * NEED, 16 * HALO)
    packed = lax.broadcasted_iota(jnp.int32, shape, 0)
    full = lax.broadcasted_iota(jnp.int32, shape, 1)
    z = lax.shift_right_logical(packed * 373, 12)
    return jnp.where(full == packed + z * (HALO - NEED) + first, 1.0, 0.0).astype(BF16)


def load_kernel(vol, s1, s2, vol_out, sems):
    depth, rows, cols = vol.shape
    odd = lax.rem(lax.axis_index("row"), 2) == 1
    parts = (slice(0, HALO), slice(rows - HALO, rows), slice(HALO, rows - HALO))
    copies = [
        pltpu.make_async_copy(vol.at[:, part, :], vol_out.at[:, part, :], sems.at[i])
        for i, part in enumerate(parts)
    ]
    for copy in copies:
        copy.start()
    first_rows, last_rows = spread_rows(0), spread_rows(HALO - NEED)
    copies[0].wait()
    copies[1].wait()
    to_before = jnp.dot(
        first_rows, vol_out[:, 0:HALO].reshape(depth * HALO, cols), preferred_element_type=F32
    ).astype(BF16)
    to_after = jnp.dot(
        last_rows, vol_out[:, rows - HALO :].reshape(depth * HALO, cols), preferred_element_type=F32
    ).astype(BF16)
    s1[...] = jnp.where(odd, to_before, to_after)
    s2[...] = jnp.where(odd, to_after, to_before)
    copies[2].wait()


def column_select(n_col, cols, odd):
    n_side = 1 if n_col == 2 else 2
    shape = (SLOTS + 16 * n_side, cols)
    row = lax.broadcasted_iota(jnp.int32, shape, 0)
    lane = lax.broadcasted_iota(jnp.int32, shape, 1)
    picked = ((row >= 8) & (row < 14) & (lane == row - 8)) | (
        (row >= 14) & (row < 20) & (lane == row - 20 + cols)
    )
    for side in range(n_side):
        if n_col == 2:
            here = lax.axis_index("col")
            near = jnp.where(here == 0, cols - 8, 0)
            behind = jnp.where(here == 0, cols - NEED, -NEED)
        else:
            near = (cols - 8, 0)[side]
            behind = (cols - NEED, -NEED)[side]
        at = row - SLOTS - 16 * side
        picked = picked | ((at >= 0) & (at < 8) & (lane == at + near))
        at = at - 8 - (1 if odd else 5)
        picked = picked | ((at >= 0) & (at < 3) & (lane == at + behind))
    return jnp.where(picked, 1.0, 0.0).astype(BF16)


def pick_columns(selects, sources, n_side):
    slots, middles = [], []
    near, behind = [[] for _ in range(n_side)], [[] for _ in range(n_side)]
    for b, source in enumerate(sources):
        picked = lax.dot_general(selects[b % 2], source, NT, preferred_element_type=F32)
        slots.append(picked[0:SLOTS].astype(BF16))
        middles.append(picked[8:24].astype(BF16))
        for side in range(n_side):
            at = SLOTS + 16 * side
            near[side].append(picked[at : at + 8])
            part = picked[at + 8 : at + 16]
            if b % 2:
                behind[side][-1] = behind[side][-1] + part
            else:
                behind[side].append(part)
    messages = [
        jnp.concatenate(near[side] + behind[side], axis=0).astype(BF16) for side in range(n_side)
    ]
    return slots, middles, messages


def halve(chunk, at, value):
    n = value.shape[0]
    chunk[at : at + n] = value[:, 0:128]
    chunk[at + n : at + 2 * n] = value[:, 128:256]


def joined_halves(chunk, at, n):
    return jnp.concatenate([chunk[at : at + n], chunk[at + n : at + 2 * n]], axis=1)


def edges_kernel(n_col, vol, own, zmsg, *refs):
    depth, rows, cols = vol.shape
    gz = lax.axis_index("gz")
    refs, middles = refs[:-1], refs[-1]
    selects = [column_select(n_col, cols, odd) for odd in (False, True)]
    sources = [vol[2 * b : 2 * b + 2].reshape(2 * rows, cols) for b in range(depth // 2)]
    slots, middle, messages = pick_columns(selects, sources, len(refs))
    for b in range(depth // 2):
        own[b], middles[b] = slots[b], middle[b]
    for ref, message in zip(refs, messages):
        ref[...] = message
    base = jnp.where(gz == 0, depth - R, 0)
    halve(zmsg, 0, vol[pl.ds(base, R)].reshape(R * rows, cols))
    first = jnp.where(gz == 0, (depth - EXTRA) // 2, 0)
    n = EXTRA // 2
    zmsg[2 * R * rows :] = middles[pl.ds(first, n)].reshape(n * 16, 128)


def pack_kernel(place_of, n_col, r1, r2, w, *refs):
    n_side = 1 if n_col == 2 else 2
    xown, (yud, halo, zcorner) = refs[:n_side], refs[n_side : n_side + 3]
    xmsgs, zxmsgs = refs[n_side + 3 : 2 * n_side + 3], refs[2 * n_side + 3 : 3 * n_side + 3]
    middles = refs[3 * n_side + 3]
    depth, cols = yud.shape[0], yud.shape[2]
    gz = lax.axis_index("gz")
    odd = lax.rem(lax.axis_index("row"), 2) == 1
    get = getter(place_of, w)
    got1, got2 = r1[...], r2[...]
    for at, name, part in (
        (0, "above", jnp.where(odd, got1, got2)),
        (HALO, "below", jnp.where(odd, got2, got1)),
    ):
        out = jnp.dot(get(name), part, preferred_element_type=F32).astype(BF16)
        yud[:, at : at + HALO, :] = out.reshape(depth, HALO, cols)
    selects = [column_select(n_col, cols, odd) for odd in (False, True)]
    pairs, quads = depth // 2, depth // 4
    sources = [yud[4 * b : 4 * b + 4].reshape(4 * 2 * HALO, cols) for b in range(quads)]
    slots, middle, messages = pick_columns(selects, sources, n_side)
    for b in range(quads):
        halo[b], middles[b] = slots[b], middle[b]
    n2, n4 = EXTRA // 2, EXTRA // 4
    low = gz == 0
    first2 = jnp.where(low, pairs - n2, 0)
    first4 = jnp.where(low, quads - n4, 0)
    skip = 8 * (pairs - n2)
    for x_own, message, xmsg, zxmsg in zip(xown, messages, xmsgs, zxmsgs):
        split = x_own.shape[0]
        xmsg[0:split] = x_own[...]
        xmsg[split:] = message
        zxmsg[0 : 8 * n2] = x_own[pl.ds(pl.multiple_of(8 * first2, 16), 8 * n2)]
        zxmsg[8 * n2 : 8 * n2 + message.shape[0]] = message
        at = 8 * n2 + message.shape[0]
        behind = x_own[8 * pairs :]
        sent = 4 * n2
        zxmsg[at : at + sent] = jnp.where(
            low, behind[skip // 2 : skip // 2 + sent], behind[0:sent]
        )
    base = jnp.where(gz == 0, depth - R, 0)
    edge = yud[pl.ds(base, R)].reshape(R * 2 * HALO, cols)
    halve(zcorner, 0, jnp.dot(get("corner"), edge, preferred_element_type=F32).astype(BF16))
    zcorner[128:] = middles[pl.ds(first4, n4)].reshape(n4 * 16, 128)


def stage_kernel(w, w_out):
    pass


FIRST = {True: 6, False: 3}
LAST = {True: 7, False: 10}
GROUP = 3
EDGE = R


def by_half(body):
    low = lax.axis_index("gz") == 0
    pl.when(low)(lambda: body(True))
    pl.when(jnp.logical_not(low))(lambda: body(False))


def first_kernel(place_of, n_row, vol, yud, w, u_ref, *scratch):
    depth, rows, cols = vol.shape
    get = getter(place_of, w)
    ysm = row_mask(get, n_row, rows, rows + 16, rows // 4)
    layer = block_loader(vol, yud, rows)

    def body(low):
        count = FIRST[low]
        base = depth - EDGE - count - R if low else 0
        load = lambda at, lanes, lo, hi: [layer(base + k, at, lanes) for k in range(lo, hi)]
        layers_to_sums(get, ysm, load, count, (rows, cols), u_ref, *scratch)

    by_half(body)


def held_layers(depth, low):
    if low:
        near = depth - EDGE
        return range(near - FIRST[low], near), range(near, depth), range(LAST[low])
    last = EDGE + FIRST[low]
    return range(EDGE, last), range(EDGE), range(last, depth)


def weighted(total, refs, held, weights):
    for ref, layers in zip(refs, held):
        for k, z in enumerate(layers):
            if weights[z] != 0.0:
                term = ref[k] * float(weights[z])
                total = term if total is None else total + term
    return total


def near_kernel(place_of, zs, n_row, vol, yud, zown, zcorner, u1, w, u_ref, send_ref, zext, *scratch):
    depth, rows, cols = vol.shape
    n_zq = zs.shape[1]
    get = getter(place_of, w)
    ysm = row_mask(get, n_row, rows, rows + 16, rows // 4)
    corner = jnp.dot(
        get("corner_back"), joined_halves(zcorner, 0, 64), preferred_element_type=F32
    ).astype(BF16).reshape(R, 2 * HALO, cols)
    zext[:, 0:HALO] = corner[:, 0:HALO]
    zext[:, HALO : HALO + rows] = joined_halves(zown, 0, R * rows).reshape(R, rows, cols)
    zext[:, HALO + rows :] = corner[:, HALO:]
    layer = block_loader(vol, yud, rows)

    def body(low):
        start = depth - R if low else 0
        outer = depth - 2 * R if low else R

        def load(at, lanes, lo, hi):
            out = []
            for k in range(lo, hi):
                if R <= k < 2 * R:
                    out.append(layer(start + k - R, at, lanes))
                elif (k < R) == low:
                    out.append(layer(outer + k % R, at, lanes))
                else:
                    out.append(zext[k % R, at : at + 16, lanes].astype(F32))
            return out

        layers_to_sums(get, ysm, load, EDGE, (rows, cols), u_ref, *scratch)
        held = held_layers(depth, low)[0:2]
        first_q = n_zq - 2 if low else 0
        sends = [weighted(None, (u1, u_ref), held, zs[:, first_q + k]) for k in range(2)]
        send_ref[...] = jnp.concatenate(sends, axis=1).astype(BF16)

    by_half(body)


def strip_tools(n_col, rows):
    col = lax.axis_index("col")
    slots = lax.broadcasted_iota(jnp.int32, (SLOTS, 128), 0)
    if n_col == 2:
        keep = ((slots < 8) & (col == 0)) | ((slots >= 21) & (col == 1))
    else:
        keep = (slots < 8) | (slots >= 21)

    def join(part, messages, at, behind_at, b):
        def eight(message, start, i):
            first = start + 16 * (i // 2)
            return message[first : first + 16].astype(F32)[8 * (i % 2) : 8 * (i % 2) + 8]

        left, right = messages[0], messages[-1]
        behind = eight(left, behind_at, b // 2)
        if b % 2:
            behind = pltpu.roll(behind, 4, 0)
        rows_of = [eight(right, at, b), jnp.zeros((8, 128), F32), behind, eight(left, at, b)]
        return jnp.where(keep, jnp.concatenate(rows_of, axis=0), part)

    lanes = lax.broadcasted_iota(jnp.int32, (SLOTS, 128), 1)

    def layers_of(pairs, quads):
        out = []
        for z in range(2 * len(pairs)):
            left, right = pairs[z // 2], quads[z // 4]
            if z % 2:
                left = pltpu.roll(left, 64, 1)
            turn = (rows - 32 * (z % 4)) % 128
            if turn:
                right = pltpu.roll(right, turn, 1)
            out.append(jnp.where(lanes < rows, left, right))
        return out

    return join, layers_of


def beyond_kernel(n_col, n_quads, rows, zown, zcorner, zxs, out):
    join, layers_of = strip_tools(n_col, rows)

    def from_middle(ref, at, b):
        rim = jnp.zeros((8, 128), F32)
        middle = ref[at + 16 * b : at + 16 * (b + 1)].astype(F32)
        return jnp.concatenate([rim, middle, rim], axis=0)

    n2, n4 = EXTRA // 2, EXTRA // 4
    far_at = 8 * n2
    far_behind = far_at + 8 * n_quads
    behind_at = far_behind + 4 * n_quads

    def body(low):
        first = 0 if low else n_quads - n4
        layers = layers_of(
            [join(from_middle(zown, 2 * R * rows, b), zxs, 0, behind_at, b) for b in range(n2)],
            [
                join(from_middle(zcorner, 128, b), zxs, far_at, far_behind, first + b)
                for b in range(n4)
            ],
        )
        for k, layer in enumerate(layers):
            out[k] = layer.astype(BF16)

    by_half(body)


def last_kernel(place_of, zs, n_row, n_col, vol, yud, own, halo, far, u1, u2, w, xs, own_ref,
                hs, hd, pstrip, u3, *scratch):
    depth, rows, cols = vol.shape
    gr = rows + 16
    quarter_rows, quarter = rows // 4, cols // 4
    get = getter(place_of, w)
    col = lax.axis_index("col")
    ysm = row_mask(get, n_row, rows, gr, quarter_rows)
    join, layers_of = strip_tools(n_col, rows)
    layer = block_loader(vol, yud, rows)
    slot = lax.rem(lax.broadcasted_iota(jnp.int32, (3 * quarter_rows, 256), 1), SLOTS)
    outside_x = ((col == 0) & (slot < 8)) | ((col == n_col - 1) & (slot >= 14))
    n_rows = 6 * quarter_rows
    count = depth + 8
    n = count // 8

    def body(low):
        first = 0 if low else depth - LAST[low]

        def load(at, lanes, lo, hi):
            out = []
            for z in range(first - R + lo, first - R + hi):
                inside = 0 <= z < depth
                out.append(layer(z, at, lanes) if inside else jnp.zeros((16, 128), F32))
            return out

        layers_to_sums(get, ysm, load, LAST[low], (rows, cols), u3, *scratch)
        own_layers = layers_of(
            [join(own[b].astype(F32), xs, 0, 4 * depth, b) for b in range(depth // 2)],
            [
                join(halo[b].astype(F32), xs, 6 * depth, 8 * depth, b)
                for b in range(depth // 4)
            ],
        )
        beyond = [far[k].astype(F32) for k in range(EXTRA)]
        zero = [jnp.zeros((SLOTS, 128), F32)] * R
        if low:
            layers = zero + own_layers + beyond[0:11]
        else:
            layers = beyond[1:12] + own_layers + zero
        for z, smooth, slope in z_filter(layers, count):
            hs[SLOTS * z : SLOTS * (z + 1)] = smooth.astype(BF16)
            hd[SLOTS * z : SLOTS * (z + 1)] = slope.astype(BF16)
        p01 = lax.dot_general(
            get("wy_strip", 128), hs[...], NT, preferred_element_type=F32
        ).astype(BF16)
        p2 = lax.dot_general(
            get("wy_strip_slope", 128), hd[...], NT, preferred_element_type=F32
        ).astype(BF16)
        groups = [slice(256 * c, 256 * (c + 1)) for c in range(n)]
        stacks = [
            jnp.concatenate([p[:, g] for g in groups], axis=0) for p in (p01[0:gr], p01[gr:], p2)
        ]
        grads = [
            jnp.dot(stack, get(name), preferred_element_type=F32).astype(BF16).reshape(n, gr, 256)
            for stack, name in zip(stacks, ("bdd", "bds", "bds"))
        ]
        for c, (a, b) in enumerate(pair_table):
            pstrip[:, c * gr : (c + 1) * gr] = grads[a] * grads[b]
        smoothed = []
        for c in range(n):
            for half in range(2):
                part = pstrip[c, half * 3 * gr : (half + 1) * 3 * gr]
                out = jnp.dot(ysm, part, preferred_element_type=F32)
                smoothed.append(jnp.where(outside_x, 0.0, out).astype(BF16))
        u = jnp.dot(jnp.concatenate(smoothed, axis=0), get("bdx"), preferred_element_type=F32)
        u = u.astype(BF16)
        sums = []
        for name in ("0", "1"):
            at = place_of[("g_low" if low else "g_high") + name][0]
            total = None
            for c in range(n):
                g = w[at + 64 * c : at + 64 * (c + 1), :]
                term = jnp.dot(u[n_rows * c : n_rows * (c + 1)], g, preferred_element_type=F32)
                total = term if total is None else total + term
            sums += [total[:, 0:quarter], total[:, 128 : 128 + quarter]]
        held = held_layers(depth, low)
        for q in range(depth // 4):
            total = weighted(sums[q], (u1, u2, u3), held, zs[:, q + 2])
            own_ref[:, q] = total.reshape(6, quarter_rows, quarter)

    by_half(body)


def add_kernel(own, got, out):
    n_q, quarter = own.shape[1], own.shape[3]
    low = lax.axis_index("gz") == 0
    parts = [
        got[:, k * quarter : (k + 1) * quarter].astype(F32).reshape(own.shape[0], -1, quarter)
        for k in range(2)
    ]
    for q in range(n_q):
        total = own[:, q]
        if q < 2:
            total = total + parts[q] * jnp.where(low, 0.0, 1.0)
        if q >= n_q - 2:
            total = total + parts[q - n_q + 2] * jnp.where(low, 1.0, 0.0)
        out[:, q] = total


def call(body, outs, operands, scratch, name, flops=0, aliases=None, n_hbm=0):
    vmem = pl.BlockSpec(memory_space=pltpu.VMEM)
    hbm = pl.BlockSpec(memory_space=pltpu.HBM)
    operands = [
        pltpu.with_memory_space_constraint(o, pltpu.HBM) if i < n_hbm else o
        for i, o in enumerate(operands)
    ]
    moved = sum(o.size * o.dtype.itemsize for o in list(outs) + list(operands))
    return pl.pallas_call(
        body,
        out_shape=list(outs),
        in_specs=[hbm] * n_hbm + [vmem] * (len(operands) - n_hbm),
        out_specs=[vmem] * len(outs),
        scratch_shapes=scratch,
        input_output_aliases=aliases or {},
        compiler_params=pltpu.CompilerParams(vmem_limit_bytes=24 * 2**20),
        cost_estimate=pl.CostEstimate(flops=flops, bytes_accessed=moved, transcendentals=0),
        name=name,
    )(*operands)


def per_device(volume):
    depth, rows, cols = volume.shape
    n_row, n_col = lax.axis_size("row"), lax.axis_size("col")
    table, place_of, zs = weight_table(depth, rows, cols)
    ext = rows + 2 * HALO
    gr = rows + 16
    quarter_rows, quarter = rows // 4, cols // 4
    n_rows = 6 * quarter_rows
    n_side = 1 if n_col == 2 else 2
    pairs, quads = depth // 2, depth // 4
    n2, n4 = EXTRA // 2, EXTRA // 4
    sds = jax.ShapeDtypeStruct
    bf16 = lambda *shape: sds(shape, BF16)
    most_first, most_last = max(FIRST.values()), max(LAST.values())

    def scratch_for(count):
        return [
            pltpu.VMEM((count, 2 * ext, cols), BF16),
            pltpu.VMEM((3, count, gr, cols), BF16),
            pltpu.VMEM((count, 6 * gr, cols), BF16),
            pltpu.VMEM((count, n_rows, cols), BF16),
        ]

    layer_flops = 2 * cols * (3 * gr * 2 * ext + 3 * gr * cols + n_rows * 3 * gr + n_rows * quarter)

    dma = pltpu.SemaphoreType.DMA
    s1, s2, vol = call(
        load_kernel,
        [bf16(depth * NEED, cols)] * 2 + [bf16(depth, rows, cols)],
        [volume], [dma((3,))], "load", n_hbm=1,
    )
    inner = [(i, i + 1) for i in range(1, n_row - 1, 2)]
    inner = inner + [(j, i) for i, j in inner]
    r2 = lax.ppermute(s2, "row", inner)
    r1 = lax.ppermute(s1, "row", [(i, i ^ 1) for i in range(n_row)])
    (w,) = call(
        stage_kernel, [bf16(*table.shape)], [jnp.asarray(table)], [], "stage", aliases={0: 0}
    )
    own, zmsg, *xown = call(
        lambda *refs: edges_kernel(n_col, *refs),
        [bf16(pairs, SLOTS, 128), bf16(2 * R * rows + n2 * 16, 128)]
        + [bf16(12 * pairs, 128)] * n_side,
        [vol], [pltpu.VMEM((pairs, 16, 128), BF16)], "edges",
    )
    swap = [(0, 1), (1, 0)]
    zown = lax.ppermute(zmsg, "gz", swap)

    yud, halo, zcmsg, *messages = call(
        lambda *refs: pack_kernel(place_of, n_col, *refs),
        [bf16(depth, 2 * HALO, cols), bf16(quads, SLOTS, 128), bf16(128 + n4 * 16, 128)]
        + [bf16(12 * (pairs + quads), 128)] * n_side
        + [bf16(12 * (n2 + quads) + 8, 128)] * n_side,
        [r1, r2, w] + xown, [pltpu.VMEM((quads, 16, 128), BF16)], "pack",
    )
    zcorner = lax.ppermute(zcmsg, "gz", swap)
    xs, zxs = [], []
    for side in range(n_side):
        step = 1 - 2 * side
        line = swap if n_col == 2 else [
            (i, i + step) for i in range(n_col) if 0 <= i + step < n_col
        ]
        both = [(z * n_col + i, (1 - z) * n_col + j) for z in range(2) for i, j in line]
        xs.append(lax.ppermute(messages[side], "col", line))
        zxs.append(lax.ppermute(messages[n_side + side], ("gz", "col"), both))

    (u1,) = call(
        lambda *refs: first_kernel(place_of, n_row, *refs),
        [sds((most_first, n_rows, quarter), F32)],
        [vol, yud, w], scratch_for(most_first), "first", flops=most_first * layer_flops,
    )
    u2, send = call(
        lambda *refs: near_kernel(place_of, zs, n_row, *refs),
        [sds((EDGE, n_rows, quarter), F32), bf16(n_rows, 2 * quarter)],
        [vol, yud, zown, zcorner, u1, w],
        [pltpu.VMEM((R, ext, cols), BF16)] + scratch_for(EDGE),
        "near", flops=EDGE * layer_flops,
    )
    sums = lax.ppermute(send, "gz", swap)

    (far,) = call(
        lambda zown, zcorner, *refs: beyond_kernel(
            n_col, quads, rows, zown, zcorner, refs[:n_side], refs[n_side]
        ),
        [bf16(EXTRA, SLOTS, 128)], [zown, zcorner] + zxs, [], "beyond", flops=layer_flops,
    )

    def last_body(*refs):
        head, x_refs, tail = refs[0:8], refs[8 : 8 + n_side], refs[8 + n_side :]
        last_kernel(place_of, zs, n_row, n_col, *head, x_refs, *tail)

    count = depth + 8
    (result,) = call(
        last_body,
        [sds((6, depth // 4, quarter_rows, quarter), F32)],
        [vol, yud, own, halo, far, u1, u2, w] + xs,
        [
            pltpu.VMEM((count * SLOTS, 128), BF16),
            pltpu.VMEM((count * SLOTS, 128), BF16),
            pltpu.VMEM((count // 8, 6 * gr, 256), BF16),
            pltpu.VMEM((most_last, n_rows, quarter), F32),
        ]
        + scratch_for(most_last),
        "last", flops=(most_last + 3) * layer_flops,
    )
    (out,) = call(add_kernel, [sds(result.shape, F32)], [result, sums], [], "add")
    return out


def solution(mesh):
    return jax.shard_map(
        per_device,
        mesh=mesh,
        in_specs=(P("gz", "row", "col"),),
        out_specs=P(None, "gz", "row", "col"),
        check_vma=False,
    )
```

```python
import jax
import jax.numpy as jnp
import ml_dtypes
import numpy as np
from jax import lax
from jax.experimental import pallas as pl
from jax.experimental.pallas import tpu as pltpu
from jax.sharding import PartitionSpec as P

R = 3
R2 = 8
HALO = 16
NEED = R + R2
EXTRA = 12
SLOTS = 32
NT = (((1,), (1,)), ((), ()))
F32 = jnp.float32
BF16 = jnp.bfloat16

pair_table = ((0, 0), (1, 1), (2, 2), (0, 1), (0, 2), (1, 2))


def gauss_taps(radius):
    offsets = np.arange(-radius, radius + 1).astype(np.float32)
    spread = np.float32(radius / 3.0)
    smooth = np.exp(-offsets * offsets / (np.float32(2.0) * spread * spread))
    smooth = smooth / np.sum(smooth)
    slopes = offsets * smooth
    slopes = slopes / np.sum(offsets * slopes)
    as_f32 = lambda t: t.astype(ml_dtypes.bfloat16).astype(np.float32)
    return as_f32(smooth), as_f32(slopes)


SMOOTH_D, SLOPE_D = gauss_taps(R)
SMOOTH_I, _ = gauss_taps(R2)


def band(taps, sources, targets):
    radius = len(taps) // 2
    gap = np.asarray(sources)[:, None] - np.asarray(targets)[None, :]
    return np.where(np.abs(gap) <= radius, taps[np.clip(gap + radius, 0, 2 * radius)], 0.0)


def weight_table(depth, rows, cols):
    ext = rows + 2 * HALO
    grad_rows = rows + 16
    far = 10**6
    y_in = np.arange(ext) - HALO
    y_out = np.arange(grad_rows) - R2
    smooth_y = band(SMOOTH_D, y_in, y_out).T
    slope_y = band(SLOPE_D, y_in, y_out).T
    zero = np.zeros_like(smooth_y)
    wy = np.block([[smooth_y, zero], [slope_y, zero], [zero, smooth_y]])
    order = np.concatenate([np.arange(rows), np.arange(HALO) - HALO, rows + np.arange(HALO)]) + HALO
    x_all = np.arange(cols)
    slot_in = np.full(SLOTS, far)
    slot_in[0:8] = cols + np.arange(8)
    slot_in[8:14] = np.arange(6)
    slot_in[14:20] = cols - 6 + np.arange(6)
    slot_in[21:32] = np.arange(-11, 0)
    slot_out = np.full(SLOTS, -far)
    slot_out[0:11] = np.arange(-8, 3)
    slot_out[11:19] = cols - 3 + np.arange(8)
    eye8 = np.eye(8)
    inner = np.where((x_all >= R) & (x_all < cols - R), x_all, far)
    quarter = cols // 4
    coarse_edge = np.full(8, 3 * far)
    coarse_edge[0:5] = [0, 1, 2, quarter - 2, quarter - 1]
    xs_edge = band(SMOOTH_I, slot_out, 4 * coarse_edge)
    ys = band(SMOOTH_I, y_out, 4 * np.arange(rows // 4)).T
    zs = band(SMOOTH_I, np.arange(depth), 4 * (np.arange(depth // 4 + 4) - 2))
    place = np.zeros((8, 128))
    for j in range(5):
        place[j, coarse_edge[j]] = 1.0
    own_z = 4 * np.arange(depth // 4)
    g = [
        np.einsum("zq,jx->zjqx", band(SMOOTH_I, np.arange(depth + 8) + first, own_z), place)
        for first in (0, -8)
    ]
    g = [t.reshape((depth + 8) * 8, len(own_z) * 128) for t in g]
    packed = np.arange(depth * NEED)
    above = np.zeros((depth * HALO, depth * NEED))
    above[packed + packed // NEED * (HALO - NEED) + HALO - NEED, packed] = 1.0
    below = np.zeros((depth * HALO, depth * NEED))
    below[packed + packed // NEED * (HALO - NEED), packed] = 1.0
    used = 2 * R + 13
    packed = np.arange(R * used)
    corner = np.zeros((64, R * 2 * HALO))
    corner[packed, packed + packed // used * (2 * HALO - used) + HALO - NEED] = 1.0
    parts = {
        "above": above,
        "below": below,
        "corner": corner,
        "corner_back": corner.T,
        "wy": wy,
        "wy_strip": np.concatenate([smooth_y, slope_y])[:, order],
        "wy_strip_slope": smooth_y[:, order],
        "wxd": band(SLOPE_D, x_all, x_all),
        "wxs": band(SMOOTH_D, x_all, x_all),
        "bdd": np.kron(eye8, band(SLOPE_D, slot_in, slot_out)),
        "bds": np.kron(eye8, band(SMOOTH_D, slot_in, slot_out)),
        "ysm": np.kron(np.eye(3), ys),
        "xsm": band(SMOOTH_I, inner, 4 * np.arange(quarter)),
        "bdx": np.kron(eye8, xs_edge),
        "g_low0": g[0][:, 0:256],
        "g_low1": g[0][:, 256:512],
        "g_high0": g[1][:, 0:256],
        "g_high1": g[1][:, 256:512],
    }
    place_of, blocks, at = {}, [], 0
    for name, part in parts.items():
        height = -(-part.shape[0] // 16) * 16
        block = np.zeros((height, 256), np.float32)
        block[: part.shape[0], : part.shape[1]] = part
        place_of[name] = (at, part.shape[0], part.shape[1])
        blocks.append(block)
        at += height
    return np.concatenate(blocks).astype(ml_dtypes.bfloat16), place_of, zs


def z_filter(v, count):
    for z in range(count):
        w = v[z : z + 7]
        smooth = w[3] * float(SMOOTH_D[3])
        slope = None
        for s in (1, 2, 3):
            smooth = smooth + (w[3 + s] + w[3 - s]) * float(SMOOTH_D[3 + s])
            term = (w[3 + s] - w[3 - s]) * float(SLOPE_D[3 + s])
            slope = term if slope is None else slope + term
        yield z, smooth, slope


def getter(place_of, w):
    def get(name, width=None):
        at, height, own_width = place_of[name]
        return w[at : at + height, 0 : (width or own_width)]

    return get


def row_mask(get, n_row, rows, gr, quarter_rows):
    row = lax.axis_index("row")
    lane = lax.broadcasted_iota(jnp.int32, (3 * quarter_rows, 3 * gr), 1)
    y_out = lax.rem(lane, gr) - R2
    outside = ((row == 0) & (y_out < 0)) | ((row == n_row - 1) & (y_out >= rows))
    return jnp.where(outside, 0.0, get("ysm").astype(F32)).astype(BF16)


def layers_to_sums(get, ysm, load, count, shape, u_ref, zf, planes, prod, sm):
    rows, cols = shape
    ext = rows + 2 * HALO
    gr = rows + 16
    n_rows = 6 * (rows // 4)
    half_rows = n_rows // 2
    rest = jnp.zeros((8, 128), F32)
    wy = get("wy")

    def z_filters(first, n):
        for tile in range(cols // 128):
            lanes = slice(tile * 128, tile * 128 + 128)
            for at in range(0, ext, 16):
                blocks = load(at, lanes, first, first + n + 2 * R)
                if at == rows + HALO:
                    blocks = [block[0:8] for block in blocks]
                for z, smooth, slope in z_filter(blocks, n):
                    if at == rows + HALO:
                        smooth = jnp.concatenate([smooth, rest], axis=0)
                        slope = jnp.concatenate([slope, rest], axis=0)
                    zf[first + z, at : at + 16, lanes] = smooth.astype(BF16)
                    zf[first + z, ext + at : ext + at + 16, lanes] = slope.astype(BF16)

    def y_filters(first, n):
        for z in range(first, first + n):
            out = jnp.dot(wy, zf[z], preferred_element_type=F32).astype(BF16)
            planes[0, z] = out[0:gr]
            planes[1, z] = out[gr : 2 * gr]
            planes[2, z] = out[2 * gr :]

    def x_filters(first, n):
        grads = []
        for f, name in enumerate(("wxd", "wxs", "wxs")):
            part = planes[f, first : first + n].reshape(n * gr, cols)
            out = jnp.dot(part, get(name), preferred_element_type=F32)
            grads.append(out.astype(BF16).reshape(n, gr, cols))
        for c, (a, b) in enumerate(pair_table):
            prod[first : first + n, c * gr : (c + 1) * gr] = grads[a] * grads[b]

    def y_smoothing(first, n):
        for z in range(first, first + n):
            for half in range(2):
                part = prod[z, half * 3 * gr : (half + 1) * 3 * gr]
                out = jnp.dot(ysm, part, preferred_element_type=F32)
                sm[z, half * half_rows : (half + 1) * half_rows] = out.astype(BF16)

    n_group = -(-count // GROUP)
    ends = [count * i // n_group for i in range(n_group + 1)]
    stages = (z_filters, y_filters, x_filters, y_smoothing)
    for step in range(n_group + len(stages) - 1):
        for k, stage in enumerate(stages):
            i = step - k
            if 0 <= i < n_group:
                stage(ends[i], ends[i + 1] - ends[i])
    out = jnp.dot(
        sm[0:count].reshape(count * n_rows, cols), get("xsm"), preferred_element_type=F32
    )
    u_ref[0:count] = out.reshape(count, n_rows, cols // 4)


def block_loader(vol, yud, rows):
    def layer(z, at, lanes):
        if at < HALO:
            return yud[z, at : at + 16, lanes].astype(F32)
        if at < HALO + rows:
            return vol[z, at - HALO : at - HALO + 16, lanes].astype(F32)
        return yud[z, at - rows : at - rows + 16, lanes].astype(F32)

    return layer


def spread_rows(first):
    shape = (16 * NEED, 16 * HALO)
    packed = lax.broadcasted_iota(jnp.int32, shape, 0)
    full = lax.broadcasted_iota(jnp.int32, shape, 1)
    z = lax.shift_right_logical(packed * 373, 12)
    return jnp.where(full == packed + z * (HALO - NEED) + first, 1.0, 0.0).astype(BF16)


def load_kernel(vol, s1, s2, vol_out, sems):
    depth, rows, cols = vol.shape
    odd = lax.rem(lax.axis_index("row"), 2) == 1
    parts = (slice(0, HALO), slice(rows - HALO, rows), slice(HALO, rows - HALO))
    copies = [
        pltpu.make_async_copy(vol.at[:, part, :], vol_out.at[:, part, :], sems.at[i])
        for i, part in enumerate(parts)
    ]
    for copy in copies:
        copy.start()
    first_rows, last_rows = spread_rows(0), spread_rows(HALO - NEED)
    copies[0].wait()
    copies[1].wait()
    to_before = jnp.dot(
        first_rows, vol_out[:, 0:HALO].reshape(depth * HALO, cols), preferred_element_type=F32
    ).astype(BF16)
    to_after = jnp.dot(
        last_rows, vol_out[:, rows - HALO :].reshape(depth * HALO, cols), preferred_element_type=F32
    ).astype(BF16)
    s1[...] = jnp.where(odd, to_before, to_after)
    s2[...] = jnp.where(odd, to_after, to_before)
    copies[2].wait()


def column_select(n_col, cols, odd):
    n_side = 1 if n_col == 2 else 2
    shape = (SLOTS + 16 * n_side, cols)
    row = lax.broadcasted_iota(jnp.int32, shape, 0)
    lane = lax.broadcasted_iota(jnp.int32, shape, 1)
    picked = ((row >= 8) & (row < 14) & (lane == row - 8)) | (
        (row >= 14) & (row < 20) & (lane == row - 20 + cols)
    )
    for side in range(n_side):
        if n_col == 2:
            here = lax.axis_index("col")
            near = jnp.where(here == 0, cols - 8, 0)
            behind = jnp.where(here == 0, cols - NEED, -NEED)
        else:
            near = (cols - 8, 0)[side]
            behind = (cols - NEED, -NEED)[side]
        at = row - SLOTS - 16 * side
        picked = picked | ((at >= 0) & (at < 8) & (lane == at + near))
        at = at - 8 - (1 if odd else 5)
        picked = picked | ((at >= 0) & (at < 3) & (lane == at + behind))
    return jnp.where(picked, 1.0, 0.0).astype(BF16)


def pick_columns(selects, sources, n_side):
    slots, middles = [], []
    near, behind = [[] for _ in range(n_side)], [[] for _ in range(n_side)]
    for b, source in enumerate(sources):
        picked = lax.dot_general(selects[b % 2], source, NT, preferred_element_type=F32)
        slots.append(picked[0:SLOTS].astype(BF16))
        middles.append(picked[8:24].astype(BF16))
        for side in range(n_side):
            at = SLOTS + 16 * side
            near[side].append(picked[at : at + 8])
            part = picked[at + 8 : at + 16]
            if b % 2:
                behind[side][-1] = behind[side][-1] + part
            else:
                behind[side].append(part)
    messages = [
        jnp.concatenate(near[side] + behind[side], axis=0).astype(BF16) for side in range(n_side)
    ]
    return slots, middles, messages


def halve(chunk, at, value):
    n = value.shape[0]
    chunk[at : at + n] = value[:, 0:128]
    chunk[at + n : at + 2 * n] = value[:, 128:256]


def joined_halves(chunk, at, n):
    return jnp.concatenate([chunk[at : at + n], chunk[at + n : at + 2 * n]], axis=1)


def edges_kernel(n_col, vol, own, zmsg, *refs):
    depth, rows, cols = vol.shape
    gz = lax.axis_index("gz")
    refs, middles = refs[:-1], refs[-1]
    selects = [column_select(n_col, cols, odd) for odd in (False, True)]
    sources = [vol[2 * b : 2 * b + 2].reshape(2 * rows, cols) for b in range(depth // 2)]
    slots, middle, messages = pick_columns(selects, sources, len(refs))
    for b in range(depth // 2):
        own[b], middles[b] = slots[b], middle[b]
    for ref, message in zip(refs, messages):
        ref[...] = message
    base = jnp.where(gz == 0, depth - R, 0)
    halve(zmsg, 0, vol[pl.ds(base, R)].reshape(R * rows, cols))
    first = jnp.where(gz == 0, (depth - EXTRA) // 2, 0)
    n = EXTRA // 2
    zmsg[2 * R * rows :] = middles[pl.ds(first, n)].reshape(n * 16, 128)


def pack_kernel(place_of, n_col, r1, r2, w, *refs):
    n_side = 1 if n_col == 2 else 2
    xown, (yud, halo, zcorner) = refs[:n_side], refs[n_side : n_side + 3]
    xmsgs, zxmsgs = refs[n_side + 3 : 2 * n_side + 3], refs[2 * n_side + 3 : 3 * n_side + 3]
    middles = refs[3 * n_side + 3]
    depth, cols = yud.shape[0], yud.shape[2]
    gz = lax.axis_index("gz")
    odd = lax.rem(lax.axis_index("row"), 2) == 1
    get = getter(place_of, w)
    got1, got2 = r1[...], r2[...]
    for at, name, part in (
        (0, "above", jnp.where(odd, got1, got2)),
        (HALO, "below", jnp.where(odd, got2, got1)),
    ):
        out = jnp.dot(get(name), part, preferred_element_type=F32).astype(BF16)
        yud[:, at : at + HALO, :] = out.reshape(depth, HALO, cols)
    selects = [column_select(n_col, cols, odd) for odd in (False, True)]
    pairs, quads = depth // 2, depth // 4
    sources = [yud[4 * b : 4 * b + 4].reshape(4 * 2 * HALO, cols) for b in range(quads)]
    slots, middle, messages = pick_columns(selects, sources, n_side)
    for b in range(quads):
        halo[b], middles[b] = slots[b], middle[b]
    n2, n4 = EXTRA // 2, EXTRA // 4
    low = gz == 0
    first2 = jnp.where(low, pairs - n2, 0)
    first4 = jnp.where(low, quads - n4, 0)
    skip = 8 * (pairs - n2)
    for x_own, message, xmsg, zxmsg in zip(xown, messages, xmsgs, zxmsgs):
        split = x_own.shape[0]
        xmsg[0:split] = x_own[...]
        xmsg[split:] = message
        zxmsg[0 : 8 * n2] = x_own[pl.ds(pl.multiple_of(8 * first2, 16), 8 * n2)]
        zxmsg[8 * n2 : 8 * n2 + message.shape[0]] = message
        at = 8 * n2 + message.shape[0]
        behind = x_own[8 * pairs :]
        sent = 4 * n2
        zxmsg[at : at + sent] = jnp.where(
            low, behind[skip // 2 : skip // 2 + sent], behind[0:sent]
        )
    base = jnp.where(gz == 0, depth - R, 0)
    edge = yud[pl.ds(base, R)].reshape(R * 2 * HALO, cols)
    halve(zcorner, 0, jnp.dot(get("corner"), edge, preferred_element_type=F32).astype(BF16))
    zcorner[128:] = middles[pl.ds(first4, n4)].reshape(n4 * 16, 128)


def stage_kernel(w, w_out):
    pass


FIRST = {True: 5, False: 3}
LAST = {True: 8, False: 10}
GROUP = 4
EDGE = R


def by_half(body):
    low = lax.axis_index("gz") == 0
    pl.when(low)(lambda: body(True))
    pl.when(jnp.logical_not(low))(lambda: body(False))


def first_kernel(place_of, n_row, vol, yud, w, u_ref, *scratch):
    depth, rows, cols = vol.shape
    get = getter(place_of, w)
    ysm = row_mask(get, n_row, rows, rows + 16, rows // 4)
    layer = block_loader(vol, yud, rows)

    def body(low):
        count = FIRST[low]
        base = depth - EDGE - count - R if low else 0
        load = lambda at, lanes, lo, hi: [layer(base + k, at, lanes) for k in range(lo, hi)]
        layers_to_sums(get, ysm, load, count, (rows, cols), u_ref, *scratch)

    by_half(body)


def held_layers(depth, low):
    if low:
        near = depth - EDGE
        return range(near - FIRST[low], near), range(near, depth), range(LAST[low])
    last = EDGE + FIRST[low]
    return range(EDGE, last), range(EDGE), range(last, depth)


def weighted(total, refs, held, weights):
    for ref, layers in zip(refs, held):
        for k, z in enumerate(layers):
            if weights[z] != 0.0:
                term = ref[k] * float(weights[z])
                total = term if total is None else total + term
    return total


def near_kernel(place_of, zs, n_row, vol, yud, zown, zcorner, u1, w, u_ref, send_ref, zext, *scratch):
    depth, rows, cols = vol.shape
    n_zq = zs.shape[1]
    get = getter(place_of, w)
    ysm = row_mask(get, n_row, rows, rows + 16, rows // 4)
    corner = jnp.dot(
        get("corner_back"), joined_halves(zcorner, 0, 64), preferred_element_type=F32
    ).astype(BF16).reshape(R, 2 * HALO, cols)
    zext[:, 0:HALO] = corner[:, 0:HALO]
    zext[:, HALO : HALO + rows] = joined_halves(zown, 0, R * rows).reshape(R, rows, cols)
    zext[:, HALO + rows :] = corner[:, HALO:]
    layer = block_loader(vol, yud, rows)

    def body(low):
        start = depth - R if low else 0
        outer = depth - 2 * R if low else R

        def load(at, lanes, lo, hi):
            out = []
            for k in range(lo, hi):
                if R <= k < 2 * R:
                    out.append(layer(start + k - R, at, lanes))
                elif (k < R) == low:
                    out.append(layer(outer + k % R, at, lanes))
                else:
                    out.append(zext[k % R, at : at + 16, lanes].astype(F32))
            return out

        layers_to_sums(get, ysm, load, EDGE, (rows, cols), u_ref, *scratch)
        held = held_layers(depth, low)[0:2]
        first_q = n_zq - 2 if low else 0
        sends = [weighted(None, (u1, u_ref), held, zs[:, first_q + k]) for k in range(2)]
        send_ref[...] = jnp.concatenate(sends, axis=1).astype(BF16)

    by_half(body)


def strip_tools(n_col, rows):
    col = lax.axis_index("col")
    slots = lax.broadcasted_iota(jnp.int32, (SLOTS, 128), 0)
    if n_col == 2:
        keep = ((slots < 8) & (col == 0)) | ((slots >= 21) & (col == 1))
    else:
        keep = (slots < 8) | (slots >= 21)

    def join(part, messages, at, behind_at, b):
        def eight(message, start, i):
            first = start + 16 * (i // 2)
            return message[first : first + 16].astype(F32)[8 * (i % 2) : 8 * (i % 2) + 8]

        left, right = messages[0], messages[-1]
        behind = eight(left, behind_at, b // 2)
        if b % 2:
            behind = pltpu.roll(behind, 4, 0)
        rows_of = [eight(right, at, b), jnp.zeros((8, 128), F32), behind, eight(left, at, b)]
        return jnp.where(keep, jnp.concatenate(rows_of, axis=0), part)

    lanes = lax.broadcasted_iota(jnp.int32, (SLOTS, 128), 1)

    def layers_of(pairs, quads):
        out = []
        for z in range(2 * len(pairs)):
            left, right = pairs[z // 2], quads[z // 4]
            if z % 2:
                left = pltpu.roll(left, 64, 1)
            turn = (rows - 32 * (z % 4)) % 128
            if turn:
                right = pltpu.roll(right, turn, 1)
            out.append(jnp.where(lanes < rows, left, right))
        return out

    return join, layers_of


def beyond_kernel(n_col, n_quads, rows, zown, zcorner, zxs, out):
    join, layers_of = strip_tools(n_col, rows)

    def from_middle(ref, at, b):
        rim = jnp.zeros((8, 128), F32)
        middle = ref[at + 16 * b : at + 16 * (b + 1)].astype(F32)
        return jnp.concatenate([rim, middle, rim], axis=0)

    n2, n4 = EXTRA // 2, EXTRA // 4
    far_at = 8 * n2
    far_behind = far_at + 8 * n_quads
    behind_at = far_behind + 4 * n_quads

    def body(low):
        first = 0 if low else n_quads - n4
        layers = layers_of(
            [join(from_middle(zown, 2 * R * rows, b), zxs, 0, behind_at, b) for b in range(n2)],
            [
                join(from_middle(zcorner, 128, b), zxs, far_at, far_behind, first + b)
                for b in range(n4)
            ],
        )
        for k, layer in enumerate(layers):
            out[k] = layer.astype(BF16)

    by_half(body)


def last_kernel(place_of, zs, n_row, n_col, vol, yud, own, halo, far, u1, u2, w, xs, own_ref,
                hs, hd, pstrip, u3, *scratch):
    depth, rows, cols = vol.shape
    gr = rows + 16
    quarter_rows, quarter = rows // 4, cols // 4
    get = getter(place_of, w)
    col = lax.axis_index("col")
    ysm = row_mask(get, n_row, rows, gr, quarter_rows)
    join, layers_of = strip_tools(n_col, rows)
    layer = block_loader(vol, yud, rows)
    slot = lax.rem(lax.broadcasted_iota(jnp.int32, (3 * quarter_rows, 256), 1), SLOTS)
    outside_x = ((col == 0) & (slot < 8)) | ((col == n_col - 1) & (slot >= 14))
    n_rows = 6 * quarter_rows
    count = depth + 8
    n = count // 8

    def body(low):
        first = 0 if low else depth - LAST[low]

        def load(at, lanes, lo, hi):
            out = []
            for z in range(first - R + lo, first - R + hi):
                inside = 0 <= z < depth
                out.append(layer(z, at, lanes) if inside else jnp.zeros((16, 128), F32))
            return out

        own_layers = layers_of(
            [join(own[b].astype(F32), xs, 0, 4 * depth, b) for b in range(depth // 2)],
            [
                join(halo[b].astype(F32), xs, 6 * depth, 8 * depth, b)
                for b in range(depth // 4)
            ],
        )
        beyond = [far[k].astype(F32) for k in range(EXTRA)]
        zero = [jnp.zeros((SLOTS, 128), F32)] * R
        if low:
            layers = zero + own_layers + beyond[0:11]
        else:
            layers = beyond[1:12] + own_layers + zero
        for z, smooth, slope in z_filter(layers, count):
            hs[SLOTS * z : SLOTS * (z + 1)] = smooth.astype(BF16)
            hd[SLOTS * z : SLOTS * (z + 1)] = slope.astype(BF16)
        p01 = lax.dot_general(
            get("wy_strip", 128), hs[...], NT, preferred_element_type=F32
        ).astype(BF16)
        p2 = lax.dot_general(
            get("wy_strip_slope", 128), hd[...], NT, preferred_element_type=F32
        ).astype(BF16)
        groups = [slice(256 * c, 256 * (c + 1)) for c in range(n)]
        stacks = [
            jnp.concatenate([p[:, g] for g in groups], axis=0) for p in (p01[0:gr], p01[gr:], p2)
        ]
        grads = [
            jnp.dot(stack, get(name), preferred_element_type=F32).astype(BF16).reshape(n, gr, 256)
            for stack, name in zip(stacks, ("bdd", "bds", "bds"))
        ]
        for c, (a, b) in enumerate(pair_table):
            pstrip[:, c * gr : (c + 1) * gr] = grads[a] * grads[b]
        smoothed = []
        for c in range(n):
            for half in range(2):
                part = pstrip[c, half * 3 * gr : (half + 1) * 3 * gr]
                out = jnp.dot(ysm, part, preferred_element_type=F32)
                smoothed.append(jnp.where(outside_x, 0.0, out).astype(BF16))
        u = jnp.dot(jnp.concatenate(smoothed, axis=0), get("bdx"), preferred_element_type=F32)
        u = u.astype(BF16)
        sums = []
        for name in ("0", "1"):
            at = place_of[("g_low" if low else "g_high") + name][0]
            total = None
            for c in range(n):
                g = w[at + 64 * c : at + 64 * (c + 1), :]
                term = jnp.dot(u[n_rows * c : n_rows * (c + 1)], g, preferred_element_type=F32)
                total = term if total is None else total + term
            sums += [total[:, 0:quarter], total[:, 128 : 128 + quarter]]
        layers_to_sums(get, ysm, load, LAST[low], (rows, cols), u3, *scratch)
        held = held_layers(depth, low)
        for q in range(depth // 4):
            total = weighted(sums[q], (u1, u2, u3), held, zs[:, q + 2])
            own_ref[:, q] = total.reshape(6, quarter_rows, quarter)

    by_half(body)


def add_kernel(own, got, out):
    n_q, quarter = own.shape[1], own.shape[3]
    low = lax.axis_index("gz") == 0
    parts = [
        got[:, k * quarter : (k + 1) * quarter].astype(F32).reshape(own.shape[0], -1, quarter)
        for k in range(2)
    ]
    for q in range(n_q):
        total = own[:, q]
        if q < 2:
            total = total + parts[q] * jnp.where(low, 0.0, 1.0)
        if q >= n_q - 2:
            total = total + parts[q - n_q + 2] * jnp.where(low, 1.0, 0.0)
        out[:, q] = total


def call(body, outs, operands, scratch, name, flops=0, aliases=None, n_hbm=0):
    vmem = pl.BlockSpec(memory_space=pltpu.VMEM)
    hbm = pl.BlockSpec(memory_space=pltpu.HBM)
    operands = [
        pltpu.with_memory_space_constraint(o, pltpu.HBM) if i < n_hbm else o
        for i, o in enumerate(operands)
    ]
    moved = sum(o.size * o.dtype.itemsize for o in list(outs) + list(operands))
    return pl.pallas_call(
        body,
        out_shape=list(outs),
        in_specs=[hbm] * n_hbm + [vmem] * (len(operands) - n_hbm),
        out_specs=[vmem] * len(outs),
        scratch_shapes=scratch,
        input_output_aliases=aliases or {},
        compiler_params=pltpu.CompilerParams(vmem_limit_bytes=24 * 2**20),
        cost_estimate=pl.CostEstimate(flops=flops, bytes_accessed=moved, transcendentals=0),
        name=name,
    )(*operands)


def per_device(volume):
    depth, rows, cols = volume.shape
    n_row, n_col = lax.axis_size("row"), lax.axis_size("col")
    table, place_of, zs = weight_table(depth, rows, cols)
    ext = rows + 2 * HALO
    gr = rows + 16
    quarter_rows, quarter = rows // 4, cols // 4
    n_rows = 6 * quarter_rows
    n_side = 1 if n_col == 2 else 2
    pairs, quads = depth // 2, depth // 4
    n2, n4 = EXTRA // 2, EXTRA // 4
    sds = jax.ShapeDtypeStruct
    bf16 = lambda *shape: sds(shape, BF16)
    most_first, most_last = max(FIRST.values()), max(LAST.values())

    def scratch_for(count):
        return [
            pltpu.VMEM((count, 2 * ext, cols), BF16),
            pltpu.VMEM((3, count, gr, cols), BF16),
            pltpu.VMEM((count, 6 * gr, cols), BF16),
            pltpu.VMEM((count, n_rows, cols), BF16),
        ]

    layer_flops = 2 * cols * (3 * gr * 2 * ext + 3 * gr * cols + n_rows * 3 * gr + n_rows * quarter)

    dma = pltpu.SemaphoreType.DMA
    s1, s2, vol = call(
        load_kernel,
        [bf16(depth * NEED, cols)] * 2 + [bf16(depth, rows, cols)],
        [volume], [dma((3,))], "load", n_hbm=1,
    )
    inner = [(i, i + 1) for i in range(1, n_row - 1, 2)]
    inner = inner + [(j, i) for i, j in inner]
    r2 = lax.ppermute(s2, "row", inner)
    r1 = lax.ppermute(s1, "row", [(i, i ^ 1) for i in range(n_row)])
    (w,) = call(
        stage_kernel, [bf16(*table.shape)], [jnp.asarray(table)], [], "stage", aliases={0: 0}
    )
    own, zmsg, *xown = call(
        lambda *refs: edges_kernel(n_col, *refs),
        [bf16(pairs, SLOTS, 128), bf16(2 * R * rows + n2 * 16, 128)]
        + [bf16(12 * pairs, 128)] * n_side,
        [vol], [pltpu.VMEM((pairs, 16, 128), BF16)], "edges",
    )
    swap = [(0, 1), (1, 0)]
    zown = lax.ppermute(zmsg, "gz", swap)

    yud, halo, zcmsg, *messages = call(
        lambda *refs: pack_kernel(place_of, n_col, *refs),
        [bf16(depth, 2 * HALO, cols), bf16(quads, SLOTS, 128), bf16(128 + n4 * 16, 128)]
        + [bf16(12 * (pairs + quads), 128)] * n_side
        + [bf16(12 * (n2 + quads) + 8, 128)] * n_side,
        [r1, r2, w] + xown, [pltpu.VMEM((quads, 16, 128), BF16)], "pack",
    )
    zcorner = lax.ppermute(zcmsg, "gz", swap)
    xs, zxs = [], []
    for side in range(n_side):
        step = 1 - 2 * side
        line = swap if n_col == 2 else [
            (i, i + step) for i in range(n_col) if 0 <= i + step < n_col
        ]
        both = [(z * n_col + i, (1 - z) * n_col + j) for z in range(2) for i, j in line]
        xs.append(lax.ppermute(messages[side], "col", line))
        zxs.append(lax.ppermute(messages[n_side + side], ("gz", "col"), both))

    (u1,) = call(
        lambda *refs: first_kernel(place_of, n_row, *refs),
        [sds((most_first, n_rows, quarter), F32)],
        [vol, yud, w], scratch_for(most_first), "first", flops=most_first * layer_flops,
    )
    u2, send = call(
        lambda *refs: near_kernel(place_of, zs, n_row, *refs),
        [sds((EDGE, n_rows, quarter), F32), bf16(n_rows, 2 * quarter)],
        [vol, yud, zown, zcorner, u1, w],
        [pltpu.VMEM((R, ext, cols), BF16)] + scratch_for(EDGE),
        "near", flops=EDGE * layer_flops,
    )
    sums = lax.ppermute(send, "gz", swap)

    (far,) = call(
        lambda zown, zcorner, *refs: beyond_kernel(
            n_col, quads, rows, zown, zcorner, refs[:n_side], refs[n_side]
        ),
        [bf16(EXTRA, SLOTS, 128)], [zown, zcorner] + zxs, [], "beyond", flops=layer_flops,
    )

    def last_body(*refs):
        head, x_refs, tail = refs[0:8], refs[8 : 8 + n_side], refs[8 + n_side :]
        last_kernel(place_of, zs, n_row, n_col, *head, x_refs, *tail)

    count = depth + 8
    (result,) = call(
        last_body,
        [sds((6, depth // 4, quarter_rows, quarter), F32)],
        [vol, yud, own, halo, far, u1, u2, w] + xs,
        [
            pltpu.VMEM((count * SLOTS, 128), BF16),
            pltpu.VMEM((count * SLOTS, 128), BF16),
            pltpu.VMEM((count // 8, 6 * gr, 256), BF16),
            pltpu.VMEM((most_last, n_rows, quarter), F32),
        ]
        + scratch_for(most_last),
        "last", flops=(most_last + 3) * layer_flops,
    )
    (out,) = call(add_kernel, [sds(result.shape, F32)], [result, sums], [], "add")
    return out


def solution(mesh):
    return jax.shard_map(
        per_device,
        mesh=mesh,
        in_specs=(P("gz", "row", "col"),),
        out_specs=P(None, "gz", "row", "col"),
        check_vma=False,
    )
```

```python
import jax
import jax.numpy as jnp
import ml_dtypes
import numpy as np
from jax import lax
from jax.experimental import pallas as pl
from jax.experimental.pallas import tpu as pltpu
from jax.sharding import PartitionSpec as P

R = 3
R2 = 8
HALO = 16
NEED = R + R2
EXTRA = 12
SLOTS = 32
NT = (((1,), (1,)), ((), ()))
F32 = jnp.float32
BF16 = jnp.bfloat16

pair_table = ((0, 0), (1, 1), (2, 2), (0, 1), (0, 2), (1, 2))


def gauss_taps(radius):
    offsets = np.arange(-radius, radius + 1).astype(np.float32)
    spread = np.float32(radius / 3.0)
    smooth = np.exp(-offsets * offsets / (np.float32(2.0) * spread * spread))
    smooth = smooth / np.sum(smooth)
    slopes = offsets * smooth
    slopes = slopes / np.sum(offsets * slopes)
    as_f32 = lambda t: t.astype(ml_dtypes.bfloat16).astype(np.float32)
    return as_f32(smooth), as_f32(slopes)


SMOOTH_D, SLOPE_D = gauss_taps(R)
SMOOTH_I, _ = gauss_taps(R2)


def band(taps, sources, targets):
    radius = len(taps) // 2
    gap = np.asarray(sources)[:, None] - np.asarray(targets)[None, :]
    return np.where(np.abs(gap) <= radius, taps[np.clip(gap + radius, 0, 2 * radius)], 0.0)


def weight_table(depth, rows, cols):
    ext = rows + 2 * HALO
    grad_rows = rows + 16
    far = 10**6
    y_in = np.arange(ext) - HALO
    y_out = np.arange(grad_rows) - R2
    smooth_y = band(SMOOTH_D, y_in, y_out).T
    slope_y = band(SLOPE_D, y_in, y_out).T
    zero = np.zeros_like(smooth_y)
    wy = np.block([[smooth_y, zero], [slope_y, zero], [zero, smooth_y]])
    order = np.concatenate([np.arange(rows), np.arange(HALO) - HALO, rows + np.arange(HALO)]) + HALO
    x_all = np.arange(cols)
    slot_in = np.full(SLOTS, far)
    slot_in[0:8] = cols + np.arange(8)
    slot_in[8:14] = np.arange(6)
    slot_in[14:20] = cols - 6 + np.arange(6)
    slot_in[21:32] = np.arange(-11, 0)
    slot_out = np.full(SLOTS, -far)
    slot_out[0:11] = np.arange(-8, 3)
    slot_out[11:19] = cols - 3 + np.arange(8)
    eye8 = np.eye(8)
    inner = np.where((x_all >= R) & (x_all < cols - R), x_all, far)
    quarter = cols // 4
    coarse_edge = np.full(8, 3 * far)
    coarse_edge[0:5] = [0, 1, 2, quarter - 2, quarter - 1]
    xs_edge = band(SMOOTH_I, slot_out, 4 * coarse_edge)
    ys = band(SMOOTH_I, y_out, 4 * np.arange(rows // 4)).T
    zs = band(SMOOTH_I, np.arange(depth), 4 * (np.arange(depth // 4 + 4) - 2))
    place = np.zeros((8, 128))
    for j in range(5):
        place[j, coarse_edge[j]] = 1.0
    own_z = 4 * np.arange(depth // 4)
    g = [
        np.einsum("zq,jx->zjqx", band(SMOOTH_I, np.arange(depth + 8) + first, own_z), place)
        for first in (0, -8)
    ]
    g = [t.reshape((depth + 8) * 8, len(own_z) * 128) for t in g]
    packed = np.arange(depth * NEED)
    above = np.zeros((depth * HALO, depth * NEED))
    above[packed + packed // NEED * (HALO - NEED) + HALO - NEED, packed] = 1.0
    below = np.zeros((depth * HALO, depth * NEED))
    below[packed + packed // NEED * (HALO - NEED), packed] = 1.0
    used = 2 * R + 13
    packed = np.arange(R * used)
    corner = np.zeros((64, R * 2 * HALO))
    corner[packed, packed + packed // used * (2 * HALO - used) + HALO - NEED] = 1.0
    parts = {
        "above": above,
        "below": below,
        "corner": corner,
        "corner_back": corner.T,
        "wy": wy,
        "wy_strip": np.concatenate([smooth_y, slope_y])[:, order],
        "wy_strip_slope": smooth_y[:, order],
        "wxd": band(SLOPE_D, x_all, x_all),
        "wxs": band(SMOOTH_D, x_all, x_all),
        "bdd": np.kron(eye8, band(SLOPE_D, slot_in, slot_out)),
        "bds": np.kron(eye8, band(SMOOTH_D, slot_in, slot_out)),
        "ysm": np.kron(np.eye(3), ys),
        "xsm": band(SMOOTH_I, inner, 4 * np.arange(quarter)),
        "bdx": np.kron(eye8, xs_edge),
        "g_low0": g[0][:, 0:256],
        "g_low1": g[0][:, 256:512],
        "g_high0": g[1][:, 0:256],
        "g_high1": g[1][:, 256:512],
    }
    place_of, blocks, at = {}, [], 0
    for name, part in parts.items():
        height = -(-part.shape[0] // 16) * 16
        block = np.zeros((height, 256), np.float32)
        block[: part.shape[0], : part.shape[1]] = part
        place_of[name] = (at, part.shape[0], part.shape[1])
        blocks.append(block)
        at += height
    return np.concatenate(blocks).astype(ml_dtypes.bfloat16), place_of, zs


def z_filter(v, count):
    for z in range(count):
        w = v[z : z + 7]
        smooth = w[3] * float(SMOOTH_D[3])
        slope = None
        for s in (1, 2, 3):
            smooth = smooth + (w[3 + s] + w[3 - s]) * float(SMOOTH_D[3 + s])
            term = (w[3 + s] - w[3 - s]) * float(SLOPE_D[3 + s])
            slope = term if slope is None else slope + term
        yield z, smooth, slope


def getter(place_of, w):
    def get(name, width=None):
        at, height, own_width = place_of[name]
        return w[at : at + height, 0 : (width or own_width)]

    return get


def row_mask(get, n_row, rows, gr, quarter_rows):
    row = lax.axis_index("row")
    lane = lax.broadcasted_iota(jnp.int32, (3 * quarter_rows, 3 * gr), 1)
    y_out = lax.rem(lane, gr) - R2
    outside = ((row == 0) & (y_out < 0)) | ((row == n_row - 1) & (y_out >= rows))
    return jnp.where(outside, 0.0, get("ysm").astype(F32)).astype(BF16)


def layers_to_sums(get, ysm, load, count, shape, u_ref, zf, planes, prod, sm, between=()):
    rows, cols = shape
    ext = rows + 2 * HALO
    gr = rows + 16
    n_rows = 6 * (rows // 4)
    half_rows = n_rows // 2
    rest = jnp.zeros((8, 128), F32)
    wy = get("wy")

    def z_filters(first, n):
        for tile in range(cols // 128):
            lanes = slice(tile * 128, tile * 128 + 128)
            for at in range(0, ext, 16):
                blocks = load(at, lanes, first, first + n + 2 * R)
                if at == rows + HALO:
                    blocks = [block[0:8] for block in blocks]
                for z, smooth, slope in z_filter(blocks, n):
                    if at == rows + HALO:
                        smooth = jnp.concatenate([smooth, rest], axis=0)
                        slope = jnp.concatenate([slope, rest], axis=0)
                    zf[first + z, at : at + 16, lanes] = smooth.astype(BF16)
                    zf[first + z, ext + at : ext + at + 16, lanes] = slope.astype(BF16)

    def y_filters(first, n):
        for z in range(first, first + n):
            out = jnp.dot(wy, zf[z], preferred_element_type=F32).astype(BF16)
            planes[0, z] = out[0:gr]
            planes[1, z] = out[gr : 2 * gr]
            planes[2, z] = out[2 * gr :]

    def x_filters(first, n):
        grads = []
        for f, name in enumerate(("wxd", "wxs", "wxs")):
            part = planes[f, first : first + n].reshape(n * gr, cols)
            out = jnp.dot(part, get(name), preferred_element_type=F32)
            grads.append(out.astype(BF16).reshape(n, gr, cols))
        for c, (a, b) in enumerate(pair_table):
            prod[first : first + n, c * gr : (c + 1) * gr] = grads[a] * grads[b]

    def y_smoothing(first, n):
        for z in range(first, first + n):
            for half in range(2):
                part = prod[z, half * 3 * gr : (half + 1) * 3 * gr]
                out = jnp.dot(ysm, part, preferred_element_type=F32)
                sm[z, half * half_rows : (half + 1) * half_rows] = out.astype(BF16)

    between = iter(between)
    n_group = -(-count // GROUP)
    ends = [count * i // n_group for i in range(n_group + 1)]
    stages = (z_filters, y_filters, x_filters, y_smoothing)
    for step in range(n_group + len(stages) - 1):
        for k, stage in enumerate(stages):
            i = step - k
            if 0 <= i < n_group:
                stage(ends[i], ends[i + 1] - ends[i])
        next(between, None)
    out = jnp.dot(
        sm[0:count].reshape(count * n_rows, cols), get("xsm"), preferred_element_type=F32
    )
    u_ref[0:count] = out.reshape(count, n_rows, cols // 4)


def block_loader(vol, yud, rows):
    def layer(z, at, lanes):
        if at < HALO:
            return yud[z, at : at + 16, lanes].astype(F32)
        if at < HALO + rows:
            return vol[z, at - HALO : at - HALO + 16, lanes].astype(F32)
        return yud[z, at - rows : at - rows + 16, lanes].astype(F32)

    return layer


def spread_rows(first):
    shape = (16 * NEED, 16 * HALO)
    packed = lax.broadcasted_iota(jnp.int32, shape, 0)
    full = lax.broadcasted_iota(jnp.int32, shape, 1)
    z = lax.shift_right_logical(packed * 373, 12)
    return jnp.where(full == packed + z * (HALO - NEED) + first, 1.0, 0.0).astype(BF16)


def load_kernel(vol, s1, s2, vol_out, sems):
    depth, rows, cols = vol.shape
    odd = lax.rem(lax.axis_index("row"), 2) == 1
    parts = (slice(0, HALO), slice(rows - HALO, rows), slice(HALO, rows - HALO))
    copies = [
        pltpu.make_async_copy(vol.at[:, part, :], vol_out.at[:, part, :], sems.at[i])
        for i, part in enumerate(parts)
    ]
    for copy in copies:
        copy.start()
    first_rows, last_rows = spread_rows(0), spread_rows(HALO - NEED)
    copies[0].wait()
    copies[1].wait()
    to_before = jnp.dot(
        first_rows, vol_out[:, 0:HALO].reshape(depth * HALO, cols), preferred_element_type=F32
    ).astype(BF16)
    to_after = jnp.dot(
        last_rows, vol_out[:, rows - HALO :].reshape(depth * HALO, cols), preferred_element_type=F32
    ).astype(BF16)
    s1[...] = jnp.where(odd, to_before, to_after)
    s2[...] = jnp.where(odd, to_after, to_before)
    copies[2].wait()


def column_select(n_col, cols, odd):
    n_side = 1 if n_col == 2 else 2
    shape = (SLOTS + 16 * n_side, cols)
    row = lax.broadcasted_iota(jnp.int32, shape, 0)
    lane = lax.broadcasted_iota(jnp.int32, shape, 1)
    picked = ((row >= 8) & (row < 14) & (lane == row - 8)) | (
        (row >= 14) & (row < 20) & (lane == row - 20 + cols)
    )
    for side in range(n_side):
        if n_col == 2:
            here = lax.axis_index("col")
            near = jnp.where(here == 0, cols - 8, 0)
            behind = jnp.where(here == 0, cols - NEED, -NEED)
        else:
            near = (cols - 8, 0)[side]
            behind = (cols - NEED, -NEED)[side]
        at = row - SLOTS - 16 * side
        picked = picked | ((at >= 0) & (at < 8) & (lane == at + near))
        at = at - 8 - (1 if odd else 5)
        picked = picked | ((at >= 0) & (at < 3) & (lane == at + behind))
    return jnp.where(picked, 1.0, 0.0).astype(BF16)


def pick_columns(selects, sources, n_side):
    slots, middles = [], []
    near, behind = [[] for _ in range(n_side)], [[] for _ in range(n_side)]
    for b, source in enumerate(sources):
        picked = lax.dot_general(selects[b % 2], source, NT, preferred_element_type=F32)
        slots.append(picked[0:SLOTS].astype(BF16))
        middles.append(picked[8:24].astype(BF16))
        for side in range(n_side):
            at = SLOTS + 16 * side
            near[side].append(picked[at : at + 8])
            part = picked[at + 8 : at + 16]
            if b % 2:
                behind[side][-1] = behind[side][-1] + part
            else:
                behind[side].append(part)
    messages = [
        jnp.concatenate(near[side] + behind[side], axis=0).astype(BF16) for side in range(n_side)
    ]
    return slots, middles, messages


def halve(chunk, at, value):
    n = value.shape[0]
    chunk[at : at + n] = value[:, 0:128]
    chunk[at + n : at + 2 * n] = value[:, 128:256]


def joined_halves(chunk, at, n):
    return jnp.concatenate([chunk[at : at + n], chunk[at + n : at + 2 * n]], axis=1)


def edges_kernel(n_col, vol, own, zmsg, *refs):
    depth, rows, cols = vol.shape
    gz = lax.axis_index("gz")
    refs, middles = refs[:-1], refs[-1]
    selects = [column_select(n_col, cols, odd) for odd in (False, True)]
    sources = [vol[2 * b : 2 * b + 2].reshape(2 * rows, cols) for b in range(depth // 2)]
    slots, middle, messages = pick_columns(selects, sources, len(refs))
    for b in range(depth // 2):
        own[b], middles[b] = slots[b], middle[b]
    for ref, message in zip(refs, messages):
        ref[...] = message
    base = jnp.where(gz == 0, depth - R, 0)
    halve(zmsg, 0, vol[pl.ds(base, R)].reshape(R * rows, cols))
    first = jnp.where(gz == 0, (depth - EXTRA) // 2, 0)
    n = EXTRA // 2
    zmsg[2 * R * rows :] = middles[pl.ds(first, n)].reshape(n * 16, 128)


def pack_kernel(place_of, n_col, r1, r2, w, *refs):
    n_side = 1 if n_col == 2 else 2
    xown, (yud, halo, zcorner) = refs[:n_side], refs[n_side : n_side + 3]
    xmsgs, zxmsgs = refs[n_side + 3 : 2 * n_side + 3], refs[2 * n_side + 3 : 3 * n_side + 3]
    middles = refs[3 * n_side + 3]
    depth, cols = yud.shape[0], yud.shape[2]
    gz = lax.axis_index("gz")
    odd = lax.rem(lax.axis_index("row"), 2) == 1
    get = getter(place_of, w)
    got1, got2 = r1[...], r2[...]
    for at, name, part in (
        (0, "above", jnp.where(odd, got1, got2)),
        (HALO, "below", jnp.where(odd, got2, got1)),
    ):
        out = jnp.dot(get(name), part, preferred_element_type=F32).astype(BF16)
        yud[:, at : at + HALO, :] = out.reshape(depth, HALO, cols)
    selects = [column_select(n_col, cols, odd) for odd in (False, True)]
    pairs, quads = depth // 2, depth // 4
    sources = [yud[4 * b : 4 * b + 4].reshape(4 * 2 * HALO, cols) for b in range(quads)]
    slots, middle, messages = pick_columns(selects, sources, n_side)
    for b in range(quads):
        halo[b], middles[b] = slots[b], middle[b]
    n2, n4 = EXTRA // 2, EXTRA // 4
    low = gz == 0
    first2 = jnp.where(low, pairs - n2, 0)
    first4 = jnp.where(low, quads - n4, 0)
    skip = 8 * (pairs - n2)
    for x_own, message, xmsg, zxmsg in zip(xown, messages, xmsgs, zxmsgs):
        split = x_own.shape[0]
        xmsg[0:split] = x_own[...]
        xmsg[split:] = message
        zxmsg[0 : 8 * n2] = x_own[pl.ds(pl.multiple_of(8 * first2, 16), 8 * n2)]
        zxmsg[8 * n2 : 8 * n2 + message.shape[0]] = message
        at = 8 * n2 + message.shape[0]
        behind = x_own[8 * pairs :]
        sent = 4 * n2
        zxmsg[at : at + sent] = jnp.where(
            low, behind[skip // 2 : skip // 2 + sent], behind[0:sent]
        )
    base = jnp.where(gz == 0, depth - R, 0)
    edge = yud[pl.ds(base, R)].reshape(R * 2 * HALO, cols)
    halve(zcorner, 0, jnp.dot(get("corner"), edge, preferred_element_type=F32).astype(BF16))
    zcorner[128:] = middles[pl.ds(first4, n4)].reshape(n4 * 16, 128)


def stage_kernel(w, w_out):
    pass


FIRST = {True: 5, False: 3}
LAST = {True: 8, False: 10}
GROUP = 4
EDGE = R


def by_half(body):
    low = lax.axis_index("gz") == 0
    pl.when(low)(lambda: body(True))
    pl.when(jnp.logical_not(low))(lambda: body(False))


def first_kernel(place_of, n_row, vol, yud, w, u_ref, *scratch):
    depth, rows, cols = vol.shape
    get = getter(place_of, w)
    ysm = row_mask(get, n_row, rows, rows + 16, rows // 4)
    layer = block_loader(vol, yud, rows)

    def body(low):
        count = FIRST[low]
        base = depth - EDGE - count - R if low else 0
        load = lambda at, lanes, lo, hi: [layer(base + k, at, lanes) for k in range(lo, hi)]
        layers_to_sums(get, ysm, load, count, (rows, cols), u_ref, *scratch)

    by_half(body)


def held_layers(depth, low):
    if low:
        near = depth - EDGE
        return range(near - FIRST[low], near), range(near, depth), range(LAST[low])
    last = EDGE + FIRST[low]
    return range(EDGE, last), range(EDGE), range(last, depth)


def weighted(total, refs, held, weights):
    for ref, layers in zip(refs, held):
        for k, z in enumerate(layers):
            if weights[z] != 0.0:
                term = ref[k] * float(weights[z])
                total = term if total is None else total + term
    return total


def near_kernel(place_of, zs, n_row, vol, yud, zown, zcorner, u1, w, u_ref, send_ref, zext, *scratch):
    depth, rows, cols = vol.shape
    n_zq = zs.shape[1]
    get = getter(place_of, w)
    ysm = row_mask(get, n_row, rows, rows + 16, rows // 4)
    corner = jnp.dot(
        get("corner_back"), joined_halves(zcorner, 0, 64), preferred_element_type=F32
    ).astype(BF16).reshape(R, 2 * HALO, cols)
    zext[:, 0:HALO] = corner[:, 0:HALO]
    zext[:, HALO : HALO + rows] = joined_halves(zown, 0, R * rows).reshape(R, rows, cols)
    zext[:, HALO + rows :] = corner[:, HALO:]
    layer = block_loader(vol, yud, rows)

    def body(low):
        start = depth - R if low else 0
        outer = depth - 2 * R if low else R

        def load(at, lanes, lo, hi):
            out = []
            for k in range(lo, hi):
                if R <= k < 2 * R:
                    out.append(layer(start + k - R, at, lanes))
                elif (k < R) == low:
                    out.append(layer(outer + k % R, at, lanes))
                else:
                    out.append(zext[k % R, at : at + 16, lanes].astype(F32))
            return out

        layers_to_sums(get, ysm, load, EDGE, (rows, cols), u_ref, *scratch)
        held = held_layers(depth, low)[0:2]
        first_q = n_zq - 2 if low else 0
        sends = [weighted(None, (u1, u_ref), held, zs[:, first_q + k]) for k in range(2)]
        send_ref[...] = jnp.concatenate(sends, axis=1).astype(BF16)

    by_half(body)


def strip_tools(n_col, rows):
    col = lax.axis_index("col")
    slots = lax.broadcasted_iota(jnp.int32, (SLOTS, 128), 0)
    if n_col == 2:
        keep = ((slots < 8) & (col == 0)) | ((slots >= 21) & (col == 1))
    else:
        keep = (slots < 8) | (slots >= 21)

    def join(part, messages, at, behind_at, b):
        def eight(message, start, i):
            first = start + 16 * (i // 2)
            return message[first : first + 16].astype(F32)[8 * (i % 2) : 8 * (i % 2) + 8]

        left, right = messages[0], messages[-1]
        behind = eight(left, behind_at, b // 2)
        if b % 2:
            behind = pltpu.roll(behind, 4, 0)
        rows_of = [eight(right, at, b), jnp.zeros((8, 128), F32), behind, eight(left, at, b)]
        return jnp.where(keep, jnp.concatenate(rows_of, axis=0), part)

    lanes = lax.broadcasted_iota(jnp.int32, (SLOTS, 128), 1)

    def layers_of(pairs, quads):
        out = []
        for z in range(2 * len(pairs)):
            left, right = pairs[z // 2], quads[z // 4]
            if z % 2:
                left = pltpu.roll(left, 64, 1)
            turn = (rows - 32 * (z % 4)) % 128
            if turn:
                right = pltpu.roll(right, turn, 1)
            out.append(jnp.where(lanes < rows, left, right))
        return out

    return join, layers_of


def beyond_kernel(n_col, n_quads, rows, zown, zcorner, zxs, out):
    join, layers_of = strip_tools(n_col, rows)

    def from_middle(ref, at, b):
        rim = jnp.zeros((8, 128), F32)
        middle = ref[at + 16 * b : at + 16 * (b + 1)].astype(F32)
        return jnp.concatenate([rim, middle, rim], axis=0)

    n2, n4 = EXTRA // 2, EXTRA // 4
    far_at = 8 * n2
    far_behind = far_at + 8 * n_quads
    behind_at = far_behind + 4 * n_quads

    def body(low):
        first = 0 if low else n_quads - n4
        layers = layers_of(
            [join(from_middle(zown, 2 * R * rows, b), zxs, 0, behind_at, b) for b in range(n2)],
            [
                join(from_middle(zcorner, 128, b), zxs, far_at, far_behind, first + b)
                for b in range(n4)
            ],
        )
        for k, layer in enumerate(layers):
            out[k] = layer.astype(BF16)

    by_half(body)


def last_kernel(place_of, zs, n_row, n_col, vol, yud, own, halo, far, u1, u2, w, xs, own_ref,
                hs, hd, pstrip, u3, *scratch):
    depth, rows, cols = vol.shape
    gr = rows + 16
    quarter_rows, quarter = rows // 4, cols // 4
    get = getter(place_of, w)
    col = lax.axis_index("col")
    ysm = row_mask(get, n_row, rows, gr, quarter_rows)
    join, layers_of = strip_tools(n_col, rows)
    layer = block_loader(vol, yud, rows)
    slot = lax.rem(lax.broadcasted_iota(jnp.int32, (3 * quarter_rows, 256), 1), SLOTS)
    outside_x = ((col == 0) & (slot < 8)) | ((col == n_col - 1) & (slot >= 14))
    n_rows = 6 * quarter_rows
    count = depth + 8
    n = count // 8

    def body(low):
        first = 0 if low else depth - LAST[low]

        def load(at, lanes, lo, hi):
            out = []
            for z in range(first - R + lo, first - R + hi):
                inside = 0 <= z < depth
                out.append(layer(z, at, lanes) if inside else jnp.zeros((16, 128), F32))
            return out

        sums = []

        def strips_by_stage():
            own_layers = layers_of(
                [join(own[b].astype(F32), xs, 0, 4 * depth, b) for b in range(depth // 2)],
                [
                    join(halo[b].astype(F32), xs, 6 * depth, 8 * depth, b)
                    for b in range(depth // 4)
                ],
            )
            beyond = [far[k].astype(F32) for k in range(EXTRA)]
            zero = [jnp.zeros((SLOTS, 128), F32)] * R
            if low:
                layers = zero + own_layers + beyond[0:11]
            else:
                layers = beyond[1:12] + own_layers + zero
            for z, smooth, slope in z_filter(layers, count):
                hs[SLOTS * z : SLOTS * (z + 1)] = smooth.astype(BF16)
                hd[SLOTS * z : SLOTS * (z + 1)] = slope.astype(BF16)
            yield
            p01 = lax.dot_general(
                get("wy_strip", 128), hs[...], NT, preferred_element_type=F32
            ).astype(BF16)
            p2 = lax.dot_general(
                get("wy_strip_slope", 128), hd[...], NT, preferred_element_type=F32
            ).astype(BF16)
            yield
            groups = [slice(256 * c, 256 * (c + 1)) for c in range(n)]
            stacks = [
                jnp.concatenate([p[:, g] for g in groups], axis=0) for p in (p01[0:gr], p01[gr:], p2)
            ]
            grads = [
                jnp.dot(stack, get(name), preferred_element_type=F32).astype(BF16).reshape(n, gr, 256)
                for stack, name in zip(stacks, ("bdd", "bds", "bds"))
            ]
            yield
            for c, (a, b) in enumerate(pair_table):
                pstrip[:, c * gr : (c + 1) * gr] = grads[a] * grads[b]
            yield
            smoothed = []
            for c in range(n):
                for half in range(2):
                    part = pstrip[c, half * 3 * gr : (half + 1) * 3 * gr]
                    out = jnp.dot(ysm, part, preferred_element_type=F32)
                    smoothed.append(jnp.where(outside_x, 0.0, out).astype(BF16))
            yield
            u = jnp.dot(jnp.concatenate(smoothed, axis=0), get("bdx"), preferred_element_type=F32)
            u = u.astype(BF16)
            for name in ("0", "1"):
                at = place_of[("g_low" if low else "g_high") + name][0]
                total = None
                for c in range(n):
                    g = w[at + 64 * c : at + 64 * (c + 1), :]
                    term = jnp.dot(u[n_rows * c : n_rows * (c + 1)], g, preferred_element_type=F32)
                    total = term if total is None else total + term
                sums.extend([total[:, 0:quarter], total[:, 128 : 128 + quarter]])

        stages = strips_by_stage()
        layers_to_sums(
            get, ysm, load, LAST[low], (rows, cols), u3, *scratch, between=stages
        )
        for _ in stages:
            pass
        held = held_layers(depth, low)
        for q in range(depth // 4):
            total = weighted(sums[q], (u1, u2, u3), held, zs[:, q + 2])
            own_ref[:, q] = total.reshape(6, quarter_rows, quarter)

    by_half(body)


def add_kernel(own, got, out):
    n_q, quarter = own.shape[1], own.shape[3]
    low = lax.axis_index("gz") == 0
    parts = [
        got[:, k * quarter : (k + 1) * quarter].astype(F32).reshape(own.shape[0], -1, quarter)
        for k in range(2)
    ]
    for q in range(n_q):
        total = own[:, q]
        if q < 2:
            total = total + parts[q] * jnp.where(low, 0.0, 1.0)
        if q >= n_q - 2:
            total = total + parts[q - n_q + 2] * jnp.where(low, 1.0, 0.0)
        out[:, q] = total


def call(body, outs, operands, scratch, name, flops=0, aliases=None, n_hbm=0):
    vmem = pl.BlockSpec(memory_space=pltpu.VMEM)
    hbm = pl.BlockSpec(memory_space=pltpu.HBM)
    operands = [
        pltpu.with_memory_space_constraint(o, pltpu.HBM) if i < n_hbm else o
        for i, o in enumerate(operands)
    ]
    moved = sum(o.size * o.dtype.itemsize for o in list(outs) + list(operands))
    return pl.pallas_call(
        body,
        out_shape=list(outs),
        in_specs=[hbm] * n_hbm + [vmem] * (len(operands) - n_hbm),
        out_specs=[vmem] * len(outs),
        scratch_shapes=scratch,
        input_output_aliases=aliases or {},
        compiler_params=pltpu.CompilerParams(vmem_limit_bytes=24 * 2**20),
        cost_estimate=pl.CostEstimate(flops=flops, bytes_accessed=moved, transcendentals=0),
        name=name,
    )(*operands)


def per_device(volume):
    depth, rows, cols = volume.shape
    n_row, n_col = lax.axis_size("row"), lax.axis_size("col")
    table, place_of, zs = weight_table(depth, rows, cols)
    ext = rows + 2 * HALO
    gr = rows + 16
    quarter_rows, quarter = rows // 4, cols // 4
    n_rows = 6 * quarter_rows
    n_side = 1 if n_col == 2 else 2
    pairs, quads = depth // 2, depth // 4
    n2, n4 = EXTRA // 2, EXTRA // 4
    sds = jax.ShapeDtypeStruct
    bf16 = lambda *shape: sds(shape, BF16)
    most_first, most_last = max(FIRST.values()), max(LAST.values())

    def scratch_for(count):
        return [
            pltpu.VMEM((count, 2 * ext, cols), BF16),
            pltpu.VMEM((3, count, gr, cols), BF16),
            pltpu.VMEM((count, 6 * gr, cols), BF16),
            pltpu.VMEM((count, n_rows, cols), BF16),
        ]

    layer_flops = 2 * cols * (3 * gr * 2 * ext + 3 * gr * cols + n_rows * 3 * gr + n_rows * quarter)

    dma = pltpu.SemaphoreType.DMA
    s1, s2, vol = call(
        load_kernel,
        [bf16(depth * NEED, cols)] * 2 + [bf16(depth, rows, cols)],
        [volume], [dma((3,))], "load", n_hbm=1,
    )
    inner = [(i, i + 1) for i in range(1, n_row - 1, 2)]
    inner = inner + [(j, i) for i, j in inner]
    r2 = lax.ppermute(s2, "row", inner)
    r1 = lax.ppermute(s1, "row", [(i, i ^ 1) for i in range(n_row)])
    (w,) = call(
        stage_kernel, [bf16(*table.shape)], [jnp.asarray(table)], [], "stage", aliases={0: 0}
    )
    own, zmsg, *xown = call(
        lambda *refs: edges_kernel(n_col, *refs),
        [bf16(pairs, SLOTS, 128), bf16(2 * R * rows + n2 * 16, 128)]
        + [bf16(12 * pairs, 128)] * n_side,
        [vol], [pltpu.VMEM((pairs, 16, 128), BF16)], "edges",
    )
    swap = [(0, 1), (1, 0)]
    zown = lax.ppermute(zmsg, "gz", swap)

    yud, halo, zcmsg, *messages = call(
        lambda *refs: pack_kernel(place_of, n_col, *refs),
        [bf16(depth, 2 * HALO, cols), bf16(quads, SLOTS, 128), bf16(128 + n4 * 16, 128)]
        + [bf16(12 * (pairs + quads), 128)] * n_side
        + [bf16(12 * (n2 + quads) + 8, 128)] * n_side,
        [r1, r2, w] + xown, [pltpu.VMEM((quads, 16, 128), BF16)], "pack",
    )
    zcorner = lax.ppermute(zcmsg, "gz", swap)
    xs, zxs = [], []
    for side in range(n_side):
        step = 1 - 2 * side
        line = swap if n_col == 2 else [
            (i, i + step) for i in range(n_col) if 0 <= i + step < n_col
        ]
        both = [(z * n_col + i, (1 - z) * n_col + j) for z in range(2) for i, j in line]
        xs.append(lax.ppermute(messages[side], "col", line))
        zxs.append(lax.ppermute(messages[n_side + side], ("gz", "col"), both))

    (u1,) = call(
        lambda *refs: first_kernel(place_of, n_row, *refs),
        [sds((most_first, n_rows, quarter), F32)],
        [vol, yud, w], scratch_for(most_first), "first", flops=most_first * layer_flops,
    )
    u2, send = call(
        lambda *refs: near_kernel(place_of, zs, n_row, *refs),
        [sds((EDGE, n_rows, quarter), F32), bf16(n_rows, 2 * quarter)],
        [vol, yud, zown, zcorner, u1, w],
        [pltpu.VMEM((R, ext, cols), BF16)] + scratch_for(EDGE),
        "near", flops=EDGE * layer_flops,
    )
    sums = lax.ppermute(send, "gz", swap)

    (far,) = call(
        lambda zown, zcorner, *refs: beyond_kernel(
            n_col, quads, rows, zown, zcorner, refs[:n_side], refs[n_side]
        ),
        [bf16(EXTRA, SLOTS, 128)], [zown, zcorner] + zxs, [], "beyond", flops=layer_flops,
    )

    def last_body(*refs):
        head, x_refs, tail = refs[0:8], refs[8 : 8 + n_side], refs[8 + n_side :]
        last_kernel(place_of, zs, n_row, n_col, *head, x_refs, *tail)

    count = depth + 8
    (result,) = call(
        last_body,
        [sds((6, depth // 4, quarter_rows, quarter), F32)],
        [vol, yud, own, halo, far, u1, u2, w] + xs,
        [
            pltpu.VMEM((count * SLOTS, 128), BF16),
            pltpu.VMEM((count * SLOTS, 128), BF16),
            pltpu.VMEM((count // 8, 6 * gr, 256), BF16),
            pltpu.VMEM((most_last, n_rows, quarter), F32),
        ]
        + scratch_for(most_last),
        "last", flops=(most_last + 3) * layer_flops,
    )
    (out,) = call(add_kernel, [sds(result.shape, F32)], [result, sums], [], "add")
    return out


def solution(mesh):
    return jax.shard_map(
        per_device,
        mesh=mesh,
        in_specs=(P("gz", "row", "col"),),
        out_specs=P(None, "gz", "row", "col"),
        check_vma=False,
    )
```

```python
import jax
import jax.numpy as jnp
import ml_dtypes
import numpy as np
from jax import lax
from jax.experimental import pallas as pl
from jax.experimental.pallas import tpu as pltpu
from jax.sharding import PartitionSpec as P

R = 3
R2 = 8
HALO = 16
NEED = R + R2
EXTRA = 12
SLOTS = 32
NT = (((1,), (1,)), ((), ()))
F32 = jnp.float32
BF16 = jnp.bfloat16

pair_table = ((0, 0), (1, 1), (2, 2), (0, 1), (0, 2), (1, 2))


def gauss_taps(radius):
    offsets = np.arange(-radius, radius + 1).astype(np.float32)
    spread = np.float32(radius / 3.0)
    smooth = np.exp(-offsets * offsets / (np.float32(2.0) * spread * spread))
    smooth = smooth / np.sum(smooth)
    slopes = offsets * smooth
    slopes = slopes / np.sum(offsets * slopes)
    as_f32 = lambda t: t.astype(ml_dtypes.bfloat16).astype(np.float32)
    return as_f32(smooth), as_f32(slopes)


SMOOTH_D, SLOPE_D = gauss_taps(R)
SMOOTH_I, _ = gauss_taps(R2)


def band(taps, sources, targets):
    radius = len(taps) // 2
    gap = np.asarray(sources)[:, None] - np.asarray(targets)[None, :]
    return np.where(np.abs(gap) <= radius, taps[np.clip(gap + radius, 0, 2 * radius)], 0.0)


def weight_table(depth, rows, cols):
    ext = rows + 2 * HALO
    grad_rows = rows + 16
    far = 10**6
    y_in = np.arange(ext) - HALO
    y_out = np.arange(grad_rows) - R2
    smooth_y = band(SMOOTH_D, y_in, y_out).T
    slope_y = band(SLOPE_D, y_in, y_out).T
    zero = np.zeros_like(smooth_y)
    wy = np.block([[smooth_y, zero], [slope_y, zero], [zero, smooth_y]])
    order = np.concatenate([np.arange(rows), np.arange(HALO) - HALO, rows + np.arange(HALO)]) + HALO
    x_all = np.arange(cols)
    slot_in = np.full(SLOTS, far)
    slot_in[0:8] = cols + np.arange(8)
    slot_in[8:14] = np.arange(6)
    slot_in[14:20] = cols - 6 + np.arange(6)
    slot_in[21:32] = np.arange(-11, 0)
    slot_out = np.full(SLOTS, -far)
    slot_out[0:11] = np.arange(-8, 3)
    slot_out[11:19] = cols - 3 + np.arange(8)
    eye8 = np.eye(8)
    inner = np.where((x_all >= R) & (x_all < cols - R), x_all, far)
    quarter = cols // 4
    coarse_edge = np.full(8, 3 * far)
    coarse_edge[0:5] = [0, 1, 2, quarter - 2, quarter - 1]
    xs_edge = band(SMOOTH_I, slot_out, 4 * coarse_edge)
    ys = band(SMOOTH_I, y_out, 4 * np.arange(rows // 4)).T
    zs = band(SMOOTH_I, np.arange(depth), 4 * (np.arange(depth // 4 + 4) - 2))
    place = np.zeros((8, 128))
    for j in range(5):
        place[j, coarse_edge[j]] = 1.0
    own_z = 4 * np.arange(depth // 4)
    g = [
        np.einsum("zq,jx->zjqx", band(SMOOTH_I, np.arange(depth + 8) + first, own_z), place)
        for first in (0, -8)
    ]
    g = [t.reshape((depth + 8) * 8, len(own_z) * 128) for t in g]
    packed = np.arange(depth * NEED)
    above = np.zeros((depth * HALO, depth * NEED))
    above[packed + packed // NEED * (HALO - NEED) + HALO - NEED, packed] = 1.0
    below = np.zeros((depth * HALO, depth * NEED))
    below[packed + packed // NEED * (HALO - NEED), packed] = 1.0
    used = 2 * R + 13
    packed = np.arange(R * used)
    corner = np.zeros((64, R * 2 * HALO))
    corner[packed, packed + packed // used * (2 * HALO - used) + HALO - NEED] = 1.0
    parts = {
        "above": above,
        "below": below,
        "corner": corner,
        "corner_back": corner.T,
        "wy": wy,
        "wy_strip": np.concatenate([smooth_y, slope_y])[:, order],
        "wy_strip_slope": smooth_y[:, order],
        "wxd": band(SLOPE_D, x_all, x_all),
        "wxs": band(SMOOTH_D, x_all, x_all),
        "bdd": np.kron(eye8, band(SLOPE_D, slot_in, slot_out)),
        "bds": np.kron(eye8, band(SMOOTH_D, slot_in, slot_out)),
        "ysm": np.kron(np.eye(3), ys),
        "xsm": band(SMOOTH_I, inner, 4 * np.arange(quarter)),
        "bdx": np.kron(eye8, xs_edge),
        "g_low0": g[0][:, 0:256],
        "g_low1": g[0][:, 256:512],
        "g_high0": g[1][:, 0:256],
        "g_high1": g[1][:, 256:512],
    }
    place_of, blocks, at = {}, [], 0
    for name, part in parts.items():
        height = -(-part.shape[0] // 16) * 16
        block = np.zeros((height, 256), np.float32)
        block[: part.shape[0], : part.shape[1]] = part
        place_of[name] = (at, part.shape[0], part.shape[1])
        blocks.append(block)
        at += height
    return np.concatenate(blocks).astype(ml_dtypes.bfloat16), place_of, zs


def z_filter(v, count):
    for z in range(count):
        w = v[z : z + 7]
        smooth = w[3] * float(SMOOTH_D[3])
        slope = None
        for s in (1, 2, 3):
            smooth = smooth + (w[3 + s] + w[3 - s]) * float(SMOOTH_D[3 + s])
            term = (w[3 + s] - w[3 - s]) * float(SLOPE_D[3 + s])
            slope = term if slope is None else slope + term
        yield z, smooth, slope


def getter(place_of, w):
    def get(name, width=None):
        at, height, own_width = place_of[name]
        return w[at : at + height, 0 : (width or own_width)]

    return get


def row_mask(get, n_row, rows, gr, quarter_rows):
    row = lax.axis_index("row")
    lane = lax.broadcasted_iota(jnp.int32, (3 * quarter_rows, 3 * gr), 1)
    y_out = lax.rem(lane, gr) - R2
    outside = ((row == 0) & (y_out < 0)) | ((row == n_row - 1) & (y_out >= rows))
    return jnp.where(outside, 0.0, get("ysm").astype(F32)).astype(BF16)


def layers_to_sums(get, ysm, load, count, shape, u_ref, zf, planes, prod, sm):
    rows, cols = shape
    ext = rows + 2 * HALO
    gr = rows + 16
    n_rows = 6 * (rows // 4)
    half_rows = n_rows // 2
    rest = jnp.zeros((8, 128), F32)
    wy = get("wy")

    def z_filters(first, n):
        for tile in range(cols // 128):
            lanes = slice(tile * 128, tile * 128 + 128)
            for at in range(0, ext, 16):
                blocks = load(at, lanes, first, first + n + 2 * R)
                if at == rows + HALO:
                    blocks = [block[0:8] for block in blocks]
                for z, smooth, slope in z_filter(blocks, n):
                    if at == rows + HALO:
                        smooth = jnp.concatenate([smooth, rest], axis=0)
                        slope = jnp.concatenate([slope, rest], axis=0)
                    zf[first + z, at : at + 16, lanes] = smooth.astype(BF16)
                    zf[first + z, ext + at : ext + at + 16, lanes] = slope.astype(BF16)

    def y_filters(first, n):
        for z in range(first, first + n):
            out = jnp.dot(wy, zf[z], preferred_element_type=F32).astype(BF16)
            planes[0, z] = out[0:gr]
            planes[1, z] = out[gr : 2 * gr]
            planes[2, z] = out[2 * gr :]

    def x_filters(first, n):
        grads = []
        for f, name in enumerate(("wxd", "wxs", "wxs")):
            part = planes[f, first : first + n].reshape(n * gr, cols)
            out = jnp.dot(part, get(name), preferred_element_type=F32)
            grads.append(out.astype(BF16).reshape(n, gr, cols))
        for c, (a, b) in enumerate(pair_table):
            prod[first : first + n, c * gr : (c + 1) * gr] = grads[a] * grads[b]

    def y_smoothing(first, n):
        for z in range(first, first + n):
            for half in range(2):
                part = prod[z, half * 3 * gr : (half + 1) * 3 * gr]
                out = jnp.dot(ysm, part, preferred_element_type=F32)
                sm[z, half * half_rows : (half + 1) * half_rows] = out.astype(BF16)

    n_group = -(-count // GROUP)
    ends = [count * i // n_group for i in range(n_group + 1)]
    stages = (z_filters, y_filters, x_filters, y_smoothing)
    for step in range(n_group + len(stages) - 1):
        for k, stage in enumerate(stages):
            i = step - k
            if 0 <= i < n_group:
                stage(ends[i], ends[i + 1] - ends[i])
    out = jnp.dot(
        sm[0:count].reshape(count * n_rows, cols), get("xsm"), preferred_element_type=F32
    )
    u_ref[0:count] = out.reshape(count, n_rows, cols // 4)


def block_loader(vol, yud, rows):
    def layer(z, at, lanes):
        if at < HALO:
            return yud[z, at : at + 16, lanes].astype(F32)
        if at < HALO + rows:
            return vol[z, at - HALO : at - HALO + 16, lanes].astype(F32)
        return yud[z, at - rows : at - rows + 16, lanes].astype(F32)

    return layer


def spread_rows(first):
    shape = (16 * NEED, 16 * HALO)
    packed = lax.broadcasted_iota(jnp.int32, shape, 0)
    full = lax.broadcasted_iota(jnp.int32, shape, 1)
    z = lax.shift_right_logical(packed * 373, 12)
    return jnp.where(full == packed + z * (HALO - NEED) + first, 1.0, 0.0).astype(BF16)


def load_kernel(vol, s1, s2, vol_out, sems):
    depth, rows, cols = vol.shape
    odd = lax.rem(lax.axis_index("row"), 2) == 1
    parts = (slice(0, HALO), slice(rows - HALO, rows), slice(HALO, rows - HALO))
    copies = [
        pltpu.make_async_copy(vol.at[:, part, :], vol_out.at[:, part, :], sems.at[i])
        for i, part in enumerate(parts)
    ]
    for copy in copies:
        copy.start()
    first_rows, last_rows = spread_rows(0), spread_rows(HALO - NEED)
    copies[0].wait()
    copies[1].wait()
    to_before = jnp.dot(
        first_rows, vol_out[:, 0:HALO].reshape(depth * HALO, cols), preferred_element_type=F32
    ).astype(BF16)
    to_after = jnp.dot(
        last_rows, vol_out[:, rows - HALO :].reshape(depth * HALO, cols), preferred_element_type=F32
    ).astype(BF16)
    s1[...] = jnp.where(odd, to_before, to_after)
    s2[...] = jnp.where(odd, to_after, to_before)
    copies[2].wait()


def column_select(n_col, cols, odd):
    n_side = 1 if n_col == 2 else 2
    shape = (SLOTS + 16 * n_side, cols)
    row = lax.broadcasted_iota(jnp.int32, shape, 0)
    lane = lax.broadcasted_iota(jnp.int32, shape, 1)
    picked = ((row >= 8) & (row < 14) & (lane == row - 8)) | (
        (row >= 14) & (row < 20) & (lane == row - 20 + cols)
    )
    for side in range(n_side):
        if n_col == 2:
            here = lax.axis_index("col")
            near = jnp.where(here == 0, cols - 8, 0)
            behind = jnp.where(here == 0, cols - NEED, -NEED)
        else:
            near = (cols - 8, 0)[side]
            behind = (cols - NEED, -NEED)[side]
        at = row - SLOTS - 16 * side
        picked = picked | ((at >= 0) & (at < 8) & (lane == at + near))
        at = at - 8 - (1 if odd else 5)
        picked = picked | ((at >= 0) & (at < 3) & (lane == at + behind))
    return jnp.where(picked, 1.0, 0.0).astype(BF16)


def pick_columns(selects, sources, n_side):
    slots, middles = [], []
    near, behind = [[] for _ in range(n_side)], [[] for _ in range(n_side)]
    for b, source in enumerate(sources):
        picked = lax.dot_general(selects[b % 2], source, NT, preferred_element_type=F32)
        slots.append(picked[0:SLOTS].astype(BF16))
        middles.append(picked[8:24].astype(BF16))
        for side in range(n_side):
            at = SLOTS + 16 * side
            near[side].append(picked[at : at + 8])
            part = picked[at + 8 : at + 16]
            if b % 2:
                behind[side][-1] = behind[side][-1] + part
            else:
                behind[side].append(part)
    messages = [
        jnp.concatenate(near[side] + behind[side], axis=0).astype(BF16) for side in range(n_side)
    ]
    return slots, middles, messages


def halve(chunk, at, value):
    n = value.shape[0]
    chunk[at : at + n] = value[:, 0:128]
    chunk[at + n : at + 2 * n] = value[:, 128:256]


def joined_halves(chunk, at, n):
    return jnp.concatenate([chunk[at : at + n], chunk[at + n : at + 2 * n]], axis=1)


def edges_kernel(n_col, vol, own, zmsg, *refs):
    depth, rows, cols = vol.shape
    gz = lax.axis_index("gz")
    refs, middles = refs[:-1], refs[-1]
    selects = [column_select(n_col, cols, odd) for odd in (False, True)]
    sources = [vol[2 * b : 2 * b + 2].reshape(2 * rows, cols) for b in range(depth // 2)]
    slots, middle, messages = pick_columns(selects, sources, len(refs))
    for b in range(depth // 2):
        own[b], middles[b] = slots[b], middle[b]
    for ref, message in zip(refs, messages):
        ref[...] = message
    base = jnp.where(gz == 0, depth - R, 0)
    halve(zmsg, 0, vol[pl.ds(base, R)].reshape(R * rows, cols))
    first = jnp.where(gz == 0, (depth - EXTRA) // 2, 0)
    n = EXTRA // 2
    zmsg[2 * R * rows :] = middles[pl.ds(first, n)].reshape(n * 16, 128)


def pack_kernel(place_of, n_col, r1, r2, w, *refs):
    n_side = 1 if n_col == 2 else 2
    xown, (yud, halo, zcorner) = refs[:n_side], refs[n_side : n_side + 3]
    xmsgs, zxmsgs = refs[n_side + 3 : 2 * n_side + 3], refs[2 * n_side + 3 : 3 * n_side + 3]
    middles = refs[3 * n_side + 3]
    depth, cols = yud.shape[0], yud.shape[2]
    gz = lax.axis_index("gz")
    odd = lax.rem(lax.axis_index("row"), 2) == 1
    get = getter(place_of, w)
    got1, got2 = r1[...], r2[...]
    for at, name, part in (
        (0, "above", jnp.where(odd, got1, got2)),
        (HALO, "below", jnp.where(odd, got2, got1)),
    ):
        out = jnp.dot(get(name), part, preferred_element_type=F32).astype(BF16)
        yud[:, at : at + HALO, :] = out.reshape(depth, HALO, cols)
    selects = [column_select(n_col, cols, odd) for odd in (False, True)]
    pairs, quads = depth // 2, depth // 4
    sources = [yud[4 * b : 4 * b + 4].reshape(4 * 2 * HALO, cols) for b in range(quads)]
    slots, middle, messages = pick_columns(selects, sources, n_side)
    for b in range(quads):
        halo[b], middles[b] = slots[b], middle[b]
    n2, n4 = EXTRA // 2, EXTRA // 4
    low = gz == 0
    first2 = jnp.where(low, pairs - n2, 0)
    first4 = jnp.where(low, quads - n4, 0)
    skip = 8 * (pairs - n2)
    for x_own, message, xmsg, zxmsg in zip(xown, messages, xmsgs, zxmsgs):
        split = x_own.shape[0]
        xmsg[0:split] = x_own[...]
        xmsg[split:] = message
        zxmsg[0 : 8 * n2] = x_own[pl.ds(pl.multiple_of(8 * first2, 16), 8 * n2)]
        zxmsg[8 * n2 : 8 * n2 + message.shape[0]] = message
        at = 8 * n2 + message.shape[0]
        behind = x_own[8 * pairs :].astype(F32)
        turned = jnp.concatenate([behind[skip // 2 :], behind[0 : skip // 2]], axis=0)
        zxmsg[at : at + 4 * pairs] = jnp.where(low, turned, behind).astype(BF16)
    base = jnp.where(gz == 0, depth - R, 0)
    edge = yud[pl.ds(base, R)].reshape(R * 2 * HALO, cols)
    halve(zcorner, 0, jnp.dot(get("corner"), edge, preferred_element_type=F32).astype(BF16))
    zcorner[128:] = middles[pl.ds(first4, n4)].reshape(n4 * 16, 128)


def stage_kernel(w, w_out):
    pass


FIRST = {True: 5, False: 3}
LAST = {True: 8, False: 10}
GROUP = 4
EDGE = R


def by_half(body):
    low = lax.axis_index("gz") == 0
    pl.when(low)(lambda: body(True))
    pl.when(jnp.logical_not(low))(lambda: body(False))


def first_kernel(place_of, n_row, vol, yud, w, u_ref, *scratch):
    depth, rows, cols = vol.shape
    get = getter(place_of, w)
    ysm = row_mask(get, n_row, rows, rows + 16, rows // 4)
    layer = block_loader(vol, yud, rows)

    def body(low):
        count = FIRST[low]
        base = depth - EDGE - count - R if low else 0
        load = lambda at, lanes, lo, hi: [layer(base + k, at, lanes) for k in range(lo, hi)]
        layers_to_sums(get, ysm, load, count, (rows, cols), u_ref, *scratch)

    by_half(body)


def held_layers(depth, low):
    if low:
        near = depth - EDGE
        return range(near - FIRST[low], near), range(near, depth), range(LAST[low])
    last = EDGE + FIRST[low]
    return range(EDGE, last), range(EDGE), range(last, depth)


def weighted(total, refs, held, weights):
    for ref, layers in zip(refs, held):
        for k, z in enumerate(layers):
            if weights[z] != 0.0:
                term = ref[k] * float(weights[z])
                total = term if total is None else total + term
    return total


def near_kernel(place_of, zs, n_row, vol, yud, zown, zcorner, u1, w, u_ref, send_ref, zext, *scratch):
    depth, rows, cols = vol.shape
    n_zq = zs.shape[1]
    get = getter(place_of, w)
    ysm = row_mask(get, n_row, rows, rows + 16, rows // 4)
    corner = jnp.dot(
        get("corner_back"), joined_halves(zcorner, 0, 64), preferred_element_type=F32
    ).astype(BF16).reshape(R, 2 * HALO, cols)
    zext[:, 0:HALO] = corner[:, 0:HALO]
    zext[:, HALO : HALO + rows] = joined_halves(zown, 0, R * rows).reshape(R, rows, cols)
    zext[:, HALO + rows :] = corner[:, HALO:]
    layer = block_loader(vol, yud, rows)

    def body(low):
        start = depth - R if low else 0
        outer = depth - 2 * R if low else R

        def load(at, lanes, lo, hi):
            out = []
            for k in range(lo, hi):
                if R <= k < 2 * R:
                    out.append(layer(start + k - R, at, lanes))
                elif (k < R) == low:
                    out.append(layer(outer + k % R, at, lanes))
                else:
                    out.append(zext[k % R, at : at + 16, lanes].astype(F32))
            return out

        layers_to_sums(get, ysm, load, EDGE, (rows, cols), u_ref, *scratch)
        held = held_layers(depth, low)[0:2]
        first_q = n_zq - 2 if low else 0
        sends = [weighted(None, (u1, u_ref), held, zs[:, first_q + k]) for k in range(2)]
        send_ref[...] = jnp.concatenate(sends, axis=1).astype(BF16)

    by_half(body)


def strip_tools(n_col, rows):
    col = lax.axis_index("col")
    slots = lax.broadcasted_iota(jnp.int32, (SLOTS, 128), 0)
    if n_col == 2:
        keep = ((slots < 8) & (col == 0)) | ((slots >= 21) & (col == 1))
    else:
        keep = (slots < 8) | (slots >= 21)

    def join(part, messages, at, behind_at, b):
        def eight(message, start, i):
            first = start + 16 * (i // 2)
            return message[first : first + 16].astype(F32)[8 * (i % 2) : 8 * (i % 2) + 8]

        left, right = messages[0], messages[-1]
        behind = eight(left, behind_at, b // 2)
        if b % 2:
            behind = pltpu.roll(behind, 4, 0)
        rows_of = [eight(right, at, b), jnp.zeros((8, 128), F32), behind, eight(left, at, b)]
        return jnp.where(keep, jnp.concatenate(rows_of, axis=0), part)

    lanes = lax.broadcasted_iota(jnp.int32, (SLOTS, 128), 1)

    def layers_of(pairs, quads):
        out = []
        for z in range(2 * len(pairs)):
            left, right = pairs[z // 2], quads[z // 4]
            if z % 2:
                left = pltpu.roll(left, 64, 1)
            turn = (rows - 32 * (z % 4)) % 128
            if turn:
                right = pltpu.roll(right, turn, 1)
            out.append(jnp.where(lanes < rows, left, right))
        return out

    return join, layers_of


def beyond_kernel(n_col, n_quads, rows, zown, zcorner, zxs, out):
    join, layers_of = strip_tools(n_col, rows)

    def from_middle(ref, at, b):
        rim = jnp.zeros((8, 128), F32)
        middle = ref[at + 16 * b : at + 16 * (b + 1)].astype(F32)
        return jnp.concatenate([rim, middle, rim], axis=0)

    n2, n4 = EXTRA // 2, EXTRA // 4
    far_at = 8 * n2
    far_behind = far_at + 8 * n_quads
    behind_at = far_behind + 4 * n_quads

    def body(low):
        first = 0 if low else n_quads - n4
        layers = layers_of(
            [join(from_middle(zown, 2 * R * rows, b), zxs, 0, behind_at, b) for b in range(n2)],
            [
                join(from_middle(zcorner, 128, b), zxs, far_at, far_behind, first + b)
                for b in range(n4)
            ],
        )
        for k, layer in enumerate(layers):
            out[k] = layer.astype(BF16)

    by_half(body)


def last_kernel(place_of, zs, n_row, n_col, vol, yud, own, halo, far, u1, u2, w, xs, own_ref,
                hs, hd, pstrip, u3, *scratch):
    depth, rows, cols = vol.shape
    gr = rows + 16
    quarter_rows, quarter = rows // 4, cols // 4
    get = getter(place_of, w)
    col = lax.axis_index("col")
    ysm = row_mask(get, n_row, rows, gr, quarter_rows)
    join, layers_of = strip_tools(n_col, rows)
    layer = block_loader(vol, yud, rows)
    slot = lax.rem(lax.broadcasted_iota(jnp.int32, (3 * quarter_rows, 256), 1), SLOTS)
    outside_x = ((col == 0) & (slot < 8)) | ((col == n_col - 1) & (slot >= 14))
    n_rows = 6 * quarter_rows
    count = depth + 8
    n = count // 8

    def body(low):
        first = 0 if low else depth - LAST[low]

        def load(at, lanes, lo, hi):
            out = []
            for z in range(first - R + lo, first - R + hi):
                inside = 0 <= z < depth
                out.append(layer(z, at, lanes) if inside else jnp.zeros((16, 128), F32))
            return out

        layers_to_sums(get, ysm, load, LAST[low], (rows, cols), u3, *scratch)
        own_layers = layers_of(
            [join(own[b].astype(F32), xs, 0, 4 * depth, b) for b in range(depth // 2)],
            [
                join(halo[b].astype(F32), xs, 6 * depth, 8 * depth, b)
                for b in range(depth // 4)
            ],
        )
        beyond = [far[k].astype(F32) for k in range(EXTRA)]
        zero = [jnp.zeros((SLOTS, 128), F32)] * R
        if low:
            layers = zero + own_layers + beyond[0:11]
        else:
            layers = beyond[1:12] + own_layers + zero
        for z, smooth, slope in z_filter(layers, count):
            hs[SLOTS * z : SLOTS * (z + 1)] = smooth.astype(BF16)
            hd[SLOTS * z : SLOTS * (z + 1)] = slope.astype(BF16)
        p01 = lax.dot_general(
            get("wy_strip", 128), hs[...], NT, preferred_element_type=F32
        ).astype(BF16)
        p2 = lax.dot_general(
            get("wy_strip_slope", 128), hd[...], NT, preferred_element_type=F32
        ).astype(BF16)
        groups = [slice(256 * c, 256 * (c + 1)) for c in range(n)]
        stacks = [
            jnp.concatenate([p[:, g] for g in groups], axis=0) for p in (p01[0:gr], p01[gr:], p2)
        ]
        grads = [
            jnp.dot(stack, get(name), preferred_element_type=F32).astype(BF16).reshape(n, gr, 256)
            for stack, name in zip(stacks, ("bdd", "bds", "bds"))
        ]
        for c, (a, b) in enumerate(pair_table):
            pstrip[:, c * gr : (c + 1) * gr] = grads[a] * grads[b]
        smoothed = []
        for c in range(n):
            for half in range(2):
                part = pstrip[c, half * 3 * gr : (half + 1) * 3 * gr]
                out = jnp.dot(ysm, part, preferred_element_type=F32)
                smoothed.append(jnp.where(outside_x, 0.0, out).astype(BF16))
        u = jnp.dot(jnp.concatenate(smoothed, axis=0), get("bdx"), preferred_element_type=F32)
        u = u.astype(BF16)
        sums = []
        for name in ("0", "1"):
            at = place_of[("g_low" if low else "g_high") + name][0]
            total = None
            for c in range(n):
                g = w[at + 64 * c : at + 64 * (c + 1), :]
                term = jnp.dot(u[n_rows * c : n_rows * (c + 1)], g, preferred_element_type=F32)
                total = term if total is None else total + term
            sums += [total[:, 0:quarter], total[:, 128 : 128 + quarter]]
        held = held_layers(depth, low)
        for q in range(depth // 4):
            total = weighted(sums[q], (u1, u2, u3), held, zs[:, q + 2])
            own_ref[:, q] = total.reshape(6, quarter_rows, quarter)

    by_half(body)


def add_kernel(own, got, out):
    n_q, quarter = own.shape[1], own.shape[3]
    low = lax.axis_index("gz") == 0
    parts = [
        got[:, k * quarter : (k + 1) * quarter].astype(F32).reshape(own.shape[0], -1, quarter)
        for k in range(2)
    ]
    for q in range(n_q):
        total = own[:, q]
        if q < 2:
            total = total + parts[q] * jnp.where(low, 0.0, 1.0)
        if q >= n_q - 2:
            total = total + parts[q - n_q + 2] * jnp.where(low, 1.0, 0.0)
        out[:, q] = total


def call(body, outs, operands, scratch, name, flops=0, aliases=None, n_hbm=0):
    vmem = pl.BlockSpec(memory_space=pltpu.VMEM)
    hbm = pl.BlockSpec(memory_space=pltpu.HBM)
    operands = [
        pltpu.with_memory_space_constraint(o, pltpu.HBM) if i < n_hbm else o
        for i, o in enumerate(operands)
    ]
    moved = sum(o.size * o.dtype.itemsize for o in list(outs) + list(operands))
    return pl.pallas_call(
        body,
        out_shape=list(outs),
        in_specs=[hbm] * n_hbm + [vmem] * (len(operands) - n_hbm),
        out_specs=[vmem] * len(outs),
        scratch_shapes=scratch,
        input_output_aliases=aliases or {},
        compiler_params=pltpu.CompilerParams(vmem_limit_bytes=24 * 2**20),
        cost_estimate=pl.CostEstimate(flops=flops, bytes_accessed=moved, transcendentals=0),
        name=name,
    )(*operands)


def per_device(volume):
    depth, rows, cols = volume.shape
    n_row, n_col = lax.axis_size("row"), lax.axis_size("col")
    table, place_of, zs = weight_table(depth, rows, cols)
    ext = rows + 2 * HALO
    gr = rows + 16
    quarter_rows, quarter = rows // 4, cols // 4
    n_rows = 6 * quarter_rows
    n_side = 1 if n_col == 2 else 2
    pairs, quads = depth // 2, depth // 4
    n2, n4 = EXTRA // 2, EXTRA // 4
    sds = jax.ShapeDtypeStruct
    bf16 = lambda *shape: sds(shape, BF16)
    most_first, most_last = max(FIRST.values()), max(LAST.values())

    def scratch_for(count):
        return [
            pltpu.VMEM((count, 2 * ext, cols), BF16),
            pltpu.VMEM((3, count, gr, cols), BF16),
            pltpu.VMEM((count, 6 * gr, cols), BF16),
            pltpu.VMEM((count, n_rows, cols), BF16),
        ]

    layer_flops = 2 * cols * (3 * gr * 2 * ext + 3 * gr * cols + n_rows * 3 * gr + n_rows * quarter)

    dma = pltpu.SemaphoreType.DMA
    s1, s2, vol = call(
        load_kernel,
        [bf16(depth * NEED, cols)] * 2 + [bf16(depth, rows, cols)],
        [volume], [dma((3,))], "load", n_hbm=1,
    )
    inner = [(i, i + 1) for i in range(1, n_row - 1, 2)]
    inner = inner + [(j, i) for i, j in inner]
    r2 = lax.ppermute(s2, "row", inner)
    r1 = lax.ppermute(s1, "row", [(i, i ^ 1) for i in range(n_row)])
    (w,) = call(
        stage_kernel, [bf16(*table.shape)], [jnp.asarray(table)], [], "stage", aliases={0: 0}
    )
    own, zmsg, *xown = call(
        lambda *refs: edges_kernel(n_col, *refs),
        [bf16(pairs, SLOTS, 128), bf16(2 * R * rows + n2 * 16, 128)]
        + [bf16(12 * pairs, 128)] * n_side,
        [vol], [pltpu.VMEM((pairs, 16, 128), BF16)], "edges",
    )
    swap = [(0, 1), (1, 0)]
    zown = lax.ppermute(zmsg, "gz", swap)

    yud, halo, zcmsg, *messages = call(
        lambda *refs: pack_kernel(place_of, n_col, *refs),
        [bf16(depth, 2 * HALO, cols), bf16(quads, SLOTS, 128), bf16(128 + n4 * 16, 128)]
        + [bf16(12 * (pairs + quads), 128)] * n_side
        + [bf16(12 * (n2 + quads) + 8, 128)] * n_side,
        [r1, r2, w] + xown, [pltpu.VMEM((quads, 16, 128), BF16)], "pack",
    )
    zcorner = lax.ppermute(zcmsg, "gz", swap)
    xs, zxs = [], []
    for side in range(n_side):
        step = 1 - 2 * side
        line = swap if n_col == 2 else [
            (i, i + step) for i in range(n_col) if 0 <= i + step < n_col
        ]
        both = [(z * n_col + i, (1 - z) * n_col + j) for z in range(2) for i, j in line]
        xs.append(lax.ppermute(messages[side], "col", line))
        zxs.append(lax.ppermute(messages[n_side + side], ("gz", "col"), both))

    (u1,) = call(
        lambda *refs: first_kernel(place_of, n_row, *refs),
        [sds((most_first, n_rows, quarter), F32)],
        [vol, yud, w], scratch_for(most_first), "first", flops=most_first * layer_flops,
    )
    u2, send = call(
        lambda *refs: near_kernel(place_of, zs, n_row, *refs),
        [sds((EDGE, n_rows, quarter), F32), bf16(n_rows, 2 * quarter)],
        [vol, yud, zown, zcorner, u1, w],
        [pltpu.VMEM((R, ext, cols), BF16)] + scratch_for(EDGE),
        "near", flops=EDGE * layer_flops,
    )
    sums = lax.ppermute(send, "gz", swap)

    (far,) = call(
        lambda zown, zcorner, *refs: beyond_kernel(
            n_col, quads, rows, zown, zcorner, refs[:n_side], refs[n_side]
        ),
        [bf16(EXTRA, SLOTS, 128)], [zown, zcorner] + zxs, [], "beyond", flops=layer_flops,
    )

    def last_body(*refs):
        head, x_refs, tail = refs[0:8], refs[8 : 8 + n_side], refs[8 + n_side :]
        last_kernel(place_of, zs, n_row, n_col, *head, x_refs, *tail)

    count = depth + 8
    (result,) = call(
        last_body,
        [sds((6, depth // 4, quarter_rows, quarter), F32)],
        [vol, yud, own, halo, far, u1, u2, w] + xs,
        [
            pltpu.VMEM((count * SLOTS, 128), BF16),
            pltpu.VMEM((count * SLOTS, 128), BF16),
            pltpu.VMEM((count // 8, 6 * gr, 256), BF16),
            pltpu.VMEM((most_last, n_rows, quarter), F32),
        ]
        + scratch_for(most_last),
        "last", flops=(most_last + 3) * layer_flops,
    )
    (out,) = call(add_kernel, [sds(result.shape, F32)], [result, sums], [], "add")
    return out


def solution(mesh):
    return jax.shard_map(
        per_device,
        mesh=mesh,
        in_specs=(P("gz", "row", "col"),),
        out_specs=P(None, "gz", "row", "col"),
        check_vma=False,
    )
```

```python
import jax
import jax.numpy as jnp
import ml_dtypes
import numpy as np
from jax import lax
from jax.experimental import pallas as pl
from jax.experimental.pallas import tpu as pltpu
from jax.sharding import PartitionSpec as P

R = 3
R2 = 8
HALO = 16
NEED = R + R2
EXTRA = 12
SLOTS = 32
NT = (((1,), (1,)), ((), ()))
F32 = jnp.float32
BF16 = jnp.bfloat16

pair_table = ((0, 0), (1, 1), (2, 2), (0, 1), (0, 2), (1, 2))


def gauss_taps(radius):
    offsets = np.arange(-radius, radius + 1).astype(np.float32)
    spread = np.float32(radius / 3.0)
    smooth = np.exp(-offsets * offsets / (np.float32(2.0) * spread * spread))
    smooth = smooth / np.sum(smooth)
    slopes = offsets * smooth
    slopes = slopes / np.sum(offsets * slopes)
    as_f32 = lambda t: t.astype(ml_dtypes.bfloat16).astype(np.float32)
    return as_f32(smooth), as_f32(slopes)


SMOOTH_D, SLOPE_D = gauss_taps(R)
SMOOTH_I, _ = gauss_taps(R2)


def band(taps, sources, targets):
    radius = len(taps) // 2
    gap = np.asarray(sources)[:, None] - np.asarray(targets)[None, :]
    return np.where(np.abs(gap) <= radius, taps[np.clip(gap + radius, 0, 2 * radius)], 0.0)


def weight_table(depth, rows, cols):
    ext = rows + 2 * HALO
    grad_rows = rows + 16
    far = 10**6
    y_in = np.arange(ext) - HALO
    y_out = np.arange(grad_rows) - R2
    smooth_y = band(SMOOTH_D, y_in, y_out).T
    slope_y = band(SLOPE_D, y_in, y_out).T
    zero = np.zeros_like(smooth_y)
    wy = np.block([[smooth_y, zero], [slope_y, zero], [zero, smooth_y]])
    order = np.concatenate([np.arange(rows), np.arange(HALO) - HALO, rows + np.arange(HALO)]) + HALO
    x_all = np.arange(cols)
    slot_in = np.full(SLOTS, far)
    slot_in[0:8] = cols + np.arange(8)
    slot_in[8:14] = np.arange(6)
    slot_in[14:20] = cols - 6 + np.arange(6)
    slot_in[21:32] = np.arange(-11, 0)
    slot_out = np.full(SLOTS, -far)
    slot_out[0:11] = np.arange(-8, 3)
    slot_out[11:19] = cols - 3 + np.arange(8)
    eye8 = np.eye(8)
    inner = np.where((x_all >= R) & (x_all < cols - R), x_all, far)
    quarter = cols // 4
    coarse_edge = np.full(8, 3 * far)
    coarse_edge[0:5] = [0, 1, 2, quarter - 2, quarter - 1]
    xs_edge = band(SMOOTH_I, slot_out, 4 * coarse_edge)
    ys = band(SMOOTH_I, y_out, 4 * np.arange(rows // 4)).T
    zs = band(SMOOTH_I, np.arange(depth), 4 * (np.arange(depth // 4 + 4) - 2))
    place = np.zeros((8, 128))
    for j in range(5):
        place[j, coarse_edge[j]] = 1.0
    own_z = 4 * np.arange(depth // 4)
    g = [
        np.einsum("zq,jx->zjqx", band(SMOOTH_I, np.arange(depth + 8) + first, own_z), place)
        for first in (0, -8)
    ]
    g = [t.reshape((depth + 8) * 8, len(own_z) * 128) for t in g]
    packed = np.arange(depth * NEED)
    above = np.zeros((depth * HALO, depth * NEED))
    above[packed + packed // NEED * (HALO - NEED) + HALO - NEED, packed] = 1.0
    below = np.zeros((depth * HALO, depth * NEED))
    below[packed + packed // NEED * (HALO - NEED), packed] = 1.0
    used = 2 * R + 13
    packed = np.arange(R * used)
    corner = np.zeros((64, R * 2 * HALO))
    corner[packed, packed + packed // used * (2 * HALO - used) + HALO - NEED] = 1.0
    parts = {
        "above": above,
        "below": below,
        "corner": corner,
        "corner_back": corner.T,
        "wy": wy,
        "wy_strip": np.concatenate([smooth_y, slope_y])[:, order],
        "wy_strip_slope": smooth_y[:, order],
        "wxd": band(SLOPE_D, x_all, x_all),
        "wxs": band(SMOOTH_D, x_all, x_all),
        "bdd": np.kron(eye8, band(SLOPE_D, slot_in, slot_out)),
        "bds": np.kron(eye8, band(SMOOTH_D, slot_in, slot_out)),
        "ysm": np.kron(np.eye(3), ys),
        "xsm": band(SMOOTH_I, inner, 4 * np.arange(quarter)),
        "bdx": np.kron(eye8, xs_edge),
        "g_low0": g[0][:, 0:256],
        "g_low1": g[0][:, 256:512],
        "g_high0": g[1][:, 0:256],
        "g_high1": g[1][:, 256:512],
    }
    place_of, blocks, at = {}, [], 0
    for name, part in parts.items():
        height = -(-part.shape[0] // 16) * 16
        block = np.zeros((height, 256), np.float32)
        block[: part.shape[0], : part.shape[1]] = part
        place_of[name] = (at, part.shape[0], part.shape[1])
        blocks.append(block)
        at += height
    return np.concatenate(blocks).astype(ml_dtypes.bfloat16), place_of, zs


def z_filter(v, count):
    for z in range(count):
        w = v[z : z + 7]
        smooth = w[3] * float(SMOOTH_D[3])
        slope = None
        for s in (1, 2, 3):
            smooth = smooth + (w[3 + s] + w[3 - s]) * float(SMOOTH_D[3 + s])
            term = (w[3 + s] - w[3 - s]) * float(SLOPE_D[3 + s])
            slope = term if slope is None else slope + term
        yield z, smooth, slope


def getter(place_of, w):
    def get(name, width=None):
        at, height, own_width = place_of[name]
        return w[at : at + height, 0 : (width or own_width)]

    return get


def row_mask(get, n_row, rows, gr, quarter_rows):
    row = lax.axis_index("row")
    lane = lax.broadcasted_iota(jnp.int32, (3 * quarter_rows, 3 * gr), 1)
    y_out = lax.rem(lane, gr) - R2
    outside = ((row == 0) & (y_out < 0)) | ((row == n_row - 1) & (y_out >= rows))
    return jnp.where(outside, 0.0, get("ysm").astype(F32)).astype(BF16)


def layers_to_sums(get, ysm, load, count, shape, u_ref, zf, planes, prod, sm):
    rows, cols = shape
    ext = rows + 2 * HALO
    gr = rows + 16
    n_rows = 6 * (rows // 4)
    half_rows = n_rows // 2
    rest = jnp.zeros((8, 128), F32)
    wy = get("wy")

    def z_filters(first, n):
        for tile in range(cols // 128):
            lanes = slice(tile * 128, tile * 128 + 128)
            for at in range(0, ext, 16):
                blocks = load(at, lanes, first, first + n + 2 * R)
                if at == rows + HALO:
                    blocks = [block[0:8] for block in blocks]
                for z, smooth, slope in z_filter(blocks, n):
                    if at == rows + HALO:
                        smooth = jnp.concatenate([smooth, rest], axis=0)
                        slope = jnp.concatenate([slope, rest], axis=0)
                    zf[first + z, at : at + 16, lanes] = smooth.astype(BF16)
                    zf[first + z, ext + at : ext + at + 16, lanes] = slope.astype(BF16)

    def y_filters(first, n):
        for z in range(first, first + n):
            out = jnp.dot(wy, zf[z], preferred_element_type=F32).astype(BF16)
            planes[0, z] = out[0:gr]
            planes[1, z] = out[gr : 2 * gr]
            planes[2, z] = out[2 * gr :]

    def x_filters(first, n):
        grads = []
        for f, name in enumerate(("wxd", "wxs", "wxs")):
            part = planes[f, first : first + n].reshape(n * gr, cols)
            out = jnp.dot(part, get(name), preferred_element_type=F32)
            grads.append(out.astype(BF16).reshape(n, gr, cols))
        for c, (a, b) in enumerate(pair_table):
            prod[first : first + n, c * gr : (c + 1) * gr] = grads[a] * grads[b]

    def y_smoothing(first, n):
        for z in range(first, first + n):
            for half in range(2):
                part = prod[z, half * 3 * gr : (half + 1) * 3 * gr]
                out = jnp.dot(ysm, part, preferred_element_type=F32)
                sm[z, half * half_rows : (half + 1) * half_rows] = out.astype(BF16)

    n_group = -(-count // GROUP)
    ends = [count * i // n_group for i in range(n_group + 1)]
    stages = (z_filters, y_filters, x_filters, y_smoothing)
    for step in range(n_group + len(stages) - 1):
        for k, stage in enumerate(stages):
            i = step - k
            if 0 <= i < n_group:
                stage(ends[i], ends[i + 1] - ends[i])
    out = jnp.dot(
        sm[0:count].reshape(count * n_rows, cols), get("xsm"), preferred_element_type=F32
    )
    u_ref[0:count] = out.reshape(count, n_rows, cols // 4)


def block_loader(vol, yud, rows):
    def layer(z, at, lanes):
        if at < HALO:
            return yud[z, at : at + 16, lanes].astype(F32)
        if at < HALO + rows:
            return vol[z, at - HALO : at - HALO + 16, lanes].astype(F32)
        return yud[z, at - rows : at - rows + 16, lanes].astype(F32)

    return layer


def spread_rows(first):
    shape = (16 * NEED, 16 * HALO)
    packed = lax.broadcasted_iota(jnp.int32, shape, 0)
    full = lax.broadcasted_iota(jnp.int32, shape, 1)
    z = lax.shift_right_logical(packed * 373, 12)
    return jnp.where(full == packed + z * (HALO - NEED) + first, 1.0, 0.0).astype(BF16)


def load_kernel(vol, s1, s2, vol_out, sems):
    depth, rows, cols = vol.shape
    odd = lax.rem(lax.axis_index("row"), 2) == 1
    parts = (slice(0, HALO), slice(rows - HALO, rows), slice(HALO, rows - HALO))
    copies = [
        pltpu.make_async_copy(vol.at[:, part, :], vol_out.at[:, part, :], sems.at[i])
        for i, part in enumerate(parts)
    ]
    for copy in copies:
        copy.start()
    first_rows, last_rows = spread_rows(0), spread_rows(HALO - NEED)
    copies[0].wait()
    copies[1].wait()
    to_before = jnp.dot(
        first_rows, vol_out[:, 0:HALO].reshape(depth * HALO, cols), preferred_element_type=F32
    ).astype(BF16)
    to_after = jnp.dot(
        last_rows, vol_out[:, rows - HALO :].reshape(depth * HALO, cols), preferred_element_type=F32
    ).astype(BF16)
    s1[...] = jnp.where(odd, to_before, to_after)
    s2[...] = jnp.where(odd, to_after, to_before)
    copies[2].wait()


def column_select(n_col, cols, odd):
    n_side = 1 if n_col == 2 else 2
    shape = (SLOTS + 16 * n_side, cols)
    row = lax.broadcasted_iota(jnp.int32, shape, 0)
    lane = lax.broadcasted_iota(jnp.int32, shape, 1)
    picked = ((row >= 8) & (row < 14) & (lane == row - 8)) | (
        (row >= 14) & (row < 20) & (lane == row - 20 + cols)
    )
    for side in range(n_side):
        if n_col == 2:
            here = lax.axis_index("col")
            near = jnp.where(here == 0, cols - 8, 0)
            behind = jnp.where(here == 0, cols - NEED, -NEED)
        else:
            near = (cols - 8, 0)[side]
            behind = (cols - NEED, -NEED)[side]
        at = row - SLOTS - 16 * side
        picked = picked | ((at >= 0) & (at < 8) & (lane == at + near))
        at = at - 8 - (1 if odd else 5)
        picked = picked | ((at >= 0) & (at < 3) & (lane == at + behind))
    return jnp.where(picked, 1.0, 0.0).astype(BF16)


def pick_columns(selects, sources, n_side):
    slots, middles = [], []
    near, behind = [[] for _ in range(n_side)], [[] for _ in range(n_side)]
    for b, source in enumerate(sources):
        picked = lax.dot_general(selects[b % 2], source, NT, preferred_element_type=F32)
        slots.append(picked[0:SLOTS].astype(BF16))
        middles.append(picked[8:24].astype(BF16))
        for side in range(n_side):
            at = SLOTS + 16 * side
            near[side].append(picked[at : at + 8])
            part = picked[at + 8 : at + 16]
            if b % 2:
                behind[side][-1] = behind[side][-1] + part
            else:
                behind[side].append(part)
    messages = [
        jnp.concatenate(near[side] + behind[side], axis=0).astype(BF16) for side in range(n_side)
    ]
    return slots, middles, messages


def halve(chunk, at, value):
    n = value.shape[0]
    chunk[at : at + n] = value[:, 0:128]
    chunk[at + n : at + 2 * n] = value[:, 128:256]


def joined_halves(chunk, at, n):
    return jnp.concatenate([chunk[at : at + n], chunk[at + n : at + 2 * n]], axis=1)


def edges_kernel(n_col, vol, own, zmsg, *refs):
    depth, rows, cols = vol.shape
    gz = lax.axis_index("gz")
    refs, middles = refs[:-1], refs[-1]
    selects = [column_select(n_col, cols, odd) for odd in (False, True)]
    sources = [vol[2 * b : 2 * b + 2].reshape(2 * rows, cols) for b in range(depth // 2)]
    slots, middle, messages = pick_columns(selects, sources, len(refs))
    for b in range(depth // 2):
        own[b], middles[b] = slots[b], middle[b]
    for ref, message in zip(refs, messages):
        ref[...] = message
    base = jnp.where(gz == 0, depth - R, 0)
    halve(zmsg, 0, vol[pl.ds(base, R)].reshape(R * rows, cols))
    first = jnp.where(gz == 0, (depth - EXTRA) // 2, 0)
    n = EXTRA // 2
    zmsg[2 * R * rows :] = middles[pl.ds(first, n)].reshape(n * 16, 128)


def pack_kernel(place_of, n_col, r1, r2, w, *refs):
    n_side = 1 if n_col == 2 else 2
    xown, (yud, halo, zcorner) = refs[:n_side], refs[n_side : n_side + 3]
    xmsgs, zxmsgs = refs[n_side + 3 : 2 * n_side + 3], refs[2 * n_side + 3 : 3 * n_side + 3]
    middles = refs[3 * n_side + 3]
    depth, cols = yud.shape[0], yud.shape[2]
    gz = lax.axis_index("gz")
    odd = lax.rem(lax.axis_index("row"), 2) == 1
    get = getter(place_of, w)
    got1, got2 = r1[...], r2[...]
    for at, name, part in (
        (0, "above", jnp.where(odd, got1, got2)),
        (HALO, "below", jnp.where(odd, got2, got1)),
    ):
        out = jnp.dot(get(name), part, preferred_element_type=F32).astype(BF16)
        yud[:, at : at + HALO, :] = out.reshape(depth, HALO, cols)
    selects = [column_select(n_col, cols, odd) for odd in (False, True)]
    pairs, quads = depth // 2, depth // 4
    sources = [yud[4 * b : 4 * b + 4].reshape(4 * 2 * HALO, cols) for b in range(quads)]
    slots, middle, messages = pick_columns(selects, sources, n_side)
    for b in range(quads):
        halo[b], middles[b] = slots[b], middle[b]
    n2, n4 = EXTRA // 2, EXTRA // 4
    low = gz == 0
    first2 = jnp.where(low, pairs - n2, 0)
    first4 = jnp.where(low, quads - n4, 0)
    skip = 8 * (pairs - n2)
    for x_own, message, xmsg, zxmsg in zip(xown, messages, xmsgs, zxmsgs):
        split = x_own.shape[0]
        xmsg[0:split] = x_own[...]
        xmsg[split:] = message
        zxmsg[0 : 8 * n2] = x_own[pl.ds(pl.multiple_of(8 * first2, 16), 8 * n2)]
        zxmsg[8 * n2 : 8 * n2 + message.shape[0]] = message
        at = 8 * n2 + message.shape[0]
        behind = x_own[8 * pairs :].astype(F32)
        turned = jnp.concatenate([behind[skip // 2 :], behind[0 : skip // 2]], axis=0)
        zxmsg[at : at + 4 * pairs] = jnp.where(low, turned, behind).astype(BF16)
    base = jnp.where(gz == 0, depth - R, 0)
    edge = yud[pl.ds(base, R)].reshape(R * 2 * HALO, cols)
    halve(zcorner, 0, jnp.dot(get("corner"), edge, preferred_element_type=F32).astype(BF16))
    zcorner[128:] = middles[pl.ds(first4, n4)].reshape(n4 * 16, 128)


def stage_kernel(w, w_out):
    pass


FIRST = {True: 5, False: 2}
LAST = {True: 8, False: 11}
GROUP = 4
EDGE = R


def by_half(body):
    low = lax.axis_index("gz") == 0
    pl.when(low)(lambda: body(True))
    pl.when(jnp.logical_not(low))(lambda: body(False))


def first_kernel(place_of, n_row, vol, yud, w, u_ref, *scratch):
    depth, rows, cols = vol.shape
    get = getter(place_of, w)
    ysm = row_mask(get, n_row, rows, rows + 16, rows // 4)
    layer = block_loader(vol, yud, rows)

    def body(low):
        count = FIRST[low]
        base = depth - EDGE - count - R if low else 0
        load = lambda at, lanes, lo, hi: [layer(base + k, at, lanes) for k in range(lo, hi)]
        layers_to_sums(get, ysm, load, count, (rows, cols), u_ref, *scratch)

    by_half(body)


def held_layers(depth, low):
    if low:
        near = depth - EDGE
        return range(near - FIRST[low], near), range(near, depth), range(LAST[low])
    last = EDGE + FIRST[low]
    return range(EDGE, last), range(EDGE), range(last, depth)


def weighted(total, refs, held, weights):
    for ref, layers in zip(refs, held):
        for k, z in enumerate(layers):
            if weights[z] != 0.0:
                term = ref[k] * float(weights[z])
                total = term if total is None else total + term
    return total


def near_kernel(place_of, zs, n_row, vol, yud, zown, zcorner, u1, w, u_ref, send_ref, zext, *scratch):
    depth, rows, cols = vol.shape
    n_zq = zs.shape[1]
    get = getter(place_of, w)
    ysm = row_mask(get, n_row, rows, rows + 16, rows // 4)
    corner = jnp.dot(
        get("corner_back"), joined_halves(zcorner, 0, 64), preferred_element_type=F32
    ).astype(BF16).reshape(R, 2 * HALO, cols)
    zext[:, 0:HALO] = corner[:, 0:HALO]
    zext[:, HALO : HALO + rows] = joined_halves(zown, 0, R * rows).reshape(R, rows, cols)
    zext[:, HALO + rows :] = corner[:, HALO:]
    layer = block_loader(vol, yud, rows)

    def body(low):
        start = depth - R if low else 0
        outer = depth - 2 * R if low else R

        def load(at, lanes, lo, hi):
            out = []
            for k in range(lo, hi):
                if R <= k < 2 * R:
                    out.append(layer(start + k - R, at, lanes))
                elif (k < R) == low:
                    out.append(layer(outer + k % R, at, lanes))
                else:
                    out.append(zext[k % R, at : at + 16, lanes].astype(F32))
            return out

        layers_to_sums(get, ysm, load, EDGE, (rows, cols), u_ref, *scratch)
        held = held_layers(depth, low)[0:2]
        first_q = n_zq - 2 if low else 0
        sends = [weighted(None, (u1, u_ref), held, zs[:, first_q + k]) for k in range(2)]
        send_ref[...] = jnp.concatenate(sends, axis=1).astype(BF16)

    by_half(body)


def strip_tools(n_col, rows):
    col = lax.axis_index("col")
    slots = lax.broadcasted_iota(jnp.int32, (SLOTS, 128), 0)
    if n_col == 2:
        keep = ((slots < 8) & (col == 0)) | ((slots >= 21) & (col == 1))
    else:
        keep = (slots < 8) | (slots >= 21)

    def join(part, messages, at, behind_at, b):
        def eight(message, start, i):
            first = start + 16 * (i // 2)
            return message[first : first + 16].astype(F32)[8 * (i % 2) : 8 * (i % 2) + 8]

        left, right = messages[0], messages[-1]
        behind = eight(left, behind_at, b // 2)
        if b % 2:
            behind = pltpu.roll(behind, 4, 0)
        rows_of = [eight(right, at, b), jnp.zeros((8, 128), F32), behind, eight(left, at, b)]
        return jnp.where(keep, jnp.concatenate(rows_of, axis=0), part)

    lanes = lax.broadcasted_iota(jnp.int32, (SLOTS, 128), 1)

    def layers_of(pairs, quads):
        out = []
        for z in range(2 * len(pairs)):
            left, right = pairs[z // 2], quads[z // 4]
            if z % 2:
                left = pltpu.roll(left, 64, 1)
            turn = (rows - 32 * (z % 4)) % 128
            if turn:
                right = pltpu.roll(right, turn, 1)
            out.append(jnp.where(lanes < rows, left, right))
        return out

    return join, layers_of


def beyond_kernel(n_col, n_quads, rows, zown, zcorner, zxs, out):
    join, layers_of = strip_tools(n_col, rows)

    def from_middle(ref, at, b):
        rim = jnp.zeros((8, 128), F32)
        middle = ref[at + 16 * b : at + 16 * (b + 1)].astype(F32)
        return jnp.concatenate([rim, middle, rim], axis=0)

    n2, n4 = EXTRA // 2, EXTRA // 4
    far_at = 8 * n2
    far_behind = far_at + 8 * n_quads
    behind_at = far_behind + 4 * n_quads

    def body(low):
        first = 0 if low else n_quads - n4
        layers = layers_of(
            [join(from_middle(zown, 2 * R * rows, b), zxs, 0, behind_at, b) for b in range(n2)],
            [
                join(from_middle(zcorner, 128, b), zxs, far_at, far_behind, first + b)
                for b in range(n4)
            ],
        )
        for k, layer in enumerate(layers):
            out[k] = layer.astype(BF16)

    by_half(body)


def last_kernel(place_of, zs, n_row, n_col, vol, yud, own, halo, far, u1, u2, w, xs, own_ref,
                hs, hd, pstrip, u3, *scratch):
    depth, rows, cols = vol.shape
    gr = rows + 16
    quarter_rows, quarter = rows // 4, cols // 4
    get = getter(place_of, w)
    col = lax.axis_index("col")
    ysm = row_mask(get, n_row, rows, gr, quarter_rows)
    join, layers_of = strip_tools(n_col, rows)
    layer = block_loader(vol, yud, rows)
    slot = lax.rem(lax.broadcasted_iota(jnp.int32, (3 * quarter_rows, 256), 1), SLOTS)
    outside_x = ((col == 0) & (slot < 8)) | ((col == n_col - 1) & (slot >= 14))
    n_rows = 6 * quarter_rows
    count = depth + 8
    n = count // 8

    def body(low):
        first = 0 if low else depth - LAST[low]

        def load(at, lanes, lo, hi):
            out = []
            for z in range(first - R + lo, first - R + hi):
                inside = 0 <= z < depth
                out.append(layer(z, at, lanes) if inside else jnp.zeros((16, 128), F32))
            return out

        layers_to_sums(get, ysm, load, LAST[low], (rows, cols), u3, *scratch)
        own_layers = layers_of(
            [join(own[b].astype(F32), xs, 0, 4 * depth, b) for b in range(depth // 2)],
            [
                join(halo[b].astype(F32), xs, 6 * depth, 8 * depth, b)
                for b in range(depth // 4)
            ],
        )
        beyond = [far[k].astype(F32) for k in range(EXTRA)]
        zero = [jnp.zeros((SLOTS, 128), F32)] * R
        if low:
            layers = zero + own_layers + beyond[0:11]
        else:
            layers = beyond[1:12] + own_layers + zero
        for z, smooth, slope in z_filter(layers, count):
            hs[SLOTS * z : SLOTS * (z + 1)] = smooth.astype(BF16)
            hd[SLOTS * z : SLOTS * (z + 1)] = slope.astype(BF16)
        p01 = lax.dot_general(
            get("wy_strip", 128), hs[...], NT, preferred_element_type=F32
        ).astype(BF16)
        p2 = lax.dot_general(
            get("wy_strip_slope", 128), hd[...], NT, preferred_element_type=F32
        ).astype(BF16)
        groups = [slice(256 * c, 256 * (c + 1)) for c in range(n)]
        stacks = [
            jnp.concatenate([p[:, g] for g in groups], axis=0) for p in (p01[0:gr], p01[gr:], p2)
        ]
        grads = [
            jnp.dot(stack, get(name), preferred_element_type=F32).astype(BF16).reshape(n, gr, 256)
            for stack, name in zip(stacks, ("bdd", "bds", "bds"))
        ]
        for c, (a, b) in enumerate(pair_table):
            pstrip[:, c * gr : (c + 1) * gr] = grads[a] * grads[b]
        smoothed = []
        for c in range(n):
            for half in range(2):
                part = pstrip[c, half * 3 * gr : (half + 1) * 3 * gr]
                out = jnp.dot(ysm, part, preferred_element_type=F32)
                smoothed.append(jnp.where(outside_x, 0.0, out).astype(BF16))
        u = jnp.dot(jnp.concatenate(smoothed, axis=0), get("bdx"), preferred_element_type=F32)
        u = u.astype(BF16)
        sums = []
        for name in ("0", "1"):
            at = place_of[("g_low" if low else "g_high") + name][0]
            total = None
            for c in range(n):
                g = w[at + 64 * c : at + 64 * (c + 1), :]
                term = jnp.dot(u[n_rows * c : n_rows * (c + 1)], g, preferred_element_type=F32)
                total = term if total is None else total + term
            sums += [total[:, 0:quarter], total[:, 128 : 128 + quarter]]
        held = held_layers(depth, low)
        for q in range(depth // 4):
            total = weighted(sums[q], (u1, u2, u3), held, zs[:, q + 2])
            own_ref[:, q] = total.reshape(6, quarter_rows, quarter)

    by_half(body)


def add_kernel(own, got, out):
    n_q, quarter = own.shape[1], own.shape[3]
    low = lax.axis_index("gz") == 0
    parts = [
        got[:, k * quarter : (k + 1) * quarter].astype(F32).reshape(own.shape[0], -1, quarter)
        for k in range(2)
    ]
    for q in range(n_q):
        total = own[:, q]
        if q < 2:
            total = total + parts[q] * jnp.where(low, 0.0, 1.0)
        if q >= n_q - 2:
            total = total + parts[q - n_q + 2] * jnp.where(low, 1.0, 0.0)
        out[:, q] = total


def call(body, outs, operands, scratch, name, flops=0, aliases=None, n_hbm=0):
    vmem = pl.BlockSpec(memory_space=pltpu.VMEM)
    hbm = pl.BlockSpec(memory_space=pltpu.HBM)
    operands = [
        pltpu.with_memory_space_constraint(o, pltpu.HBM) if i < n_hbm else o
        for i, o in enumerate(operands)
    ]
    moved = sum(o.size * o.dtype.itemsize for o in list(outs) + list(operands))
    return pl.pallas_call(
        body,
        out_shape=list(outs),
        in_specs=[hbm] * n_hbm + [vmem] * (len(operands) - n_hbm),
        out_specs=[vmem] * len(outs),
        scratch_shapes=scratch,
        input_output_aliases=aliases or {},
        compiler_params=pltpu.CompilerParams(vmem_limit_bytes=24 * 2**20),
        cost_estimate=pl.CostEstimate(flops=flops, bytes_accessed=moved, transcendentals=0),
        name=name,
    )(*operands)


def per_device(volume):
    depth, rows, cols = volume.shape
    n_row, n_col = lax.axis_size("row"), lax.axis_size("col")
    table, place_of, zs = weight_table(depth, rows, cols)
    ext = rows + 2 * HALO
    gr = rows + 16
    quarter_rows, quarter = rows // 4, cols // 4
    n_rows = 6 * quarter_rows
    n_side = 1 if n_col == 2 else 2
    pairs, quads = depth // 2, depth // 4
    n2, n4 = EXTRA // 2, EXTRA // 4
    sds = jax.ShapeDtypeStruct
    bf16 = lambda *shape: sds(shape, BF16)
    most_first, most_last = max(FIRST.values()), max(LAST.values())

    def scratch_for(count):
        return [
            pltpu.VMEM((count, 2 * ext, cols), BF16),
            pltpu.VMEM((3, count, gr, cols), BF16),
            pltpu.VMEM((count, 6 * gr, cols), BF16),
            pltpu.VMEM((count, n_rows, cols), BF16),
        ]

    layer_flops = 2 * cols * (3 * gr * 2 * ext + 3 * gr * cols + n_rows * 3 * gr + n_rows * quarter)

    dma = pltpu.SemaphoreType.DMA
    s1, s2, vol = call(
        load_kernel,
        [bf16(depth * NEED, cols)] * 2 + [bf16(depth, rows, cols)],
        [volume], [dma((3,))], "load", n_hbm=1,
    )
    inner = [(i, i + 1) for i in range(1, n_row - 1, 2)]
    inner = inner + [(j, i) for i, j in inner]
    r2 = lax.ppermute(s2, "row", inner)
    r1 = lax.ppermute(s1, "row", [(i, i ^ 1) for i in range(n_row)])
    (w,) = call(
        stage_kernel, [bf16(*table.shape)], [jnp.asarray(table)], [], "stage", aliases={0: 0}
    )
    own, zmsg, *xown = call(
        lambda *refs: edges_kernel(n_col, *refs),
        [bf16(pairs, SLOTS, 128), bf16(2 * R * rows + n2 * 16, 128)]
        + [bf16(12 * pairs, 128)] * n_side,
        [vol], [pltpu.VMEM((pairs, 16, 128), BF16)], "edges",
    )
    swap = [(0, 1), (1, 0)]
    zown = lax.ppermute(zmsg, "gz", swap)

    yud, halo, zcmsg, *messages = call(
        lambda *refs: pack_kernel(place_of, n_col, *refs),
        [bf16(depth, 2 * HALO, cols), bf16(quads, SLOTS, 128), bf16(128 + n4 * 16, 128)]
        + [bf16(12 * (pairs + quads), 128)] * n_side
        + [bf16(12 * (n2 + quads) + 8, 128)] * n_side,
        [r1, r2, w] + xown, [pltpu.VMEM((quads, 16, 128), BF16)], "pack",
    )
    zcorner = lax.ppermute(zcmsg, "gz", swap)
    xs, zxs = [], []
    for side in range(n_side):
        step = 1 - 2 * side
        line = swap if n_col == 2 else [
            (i, i + step) for i in range(n_col) if 0 <= i + step < n_col
        ]
        both = [(z * n_col + i, (1 - z) * n_col + j) for z in range(2) for i, j in line]
        xs.append(lax.ppermute(messages[side], "col", line))
        zxs.append(lax.ppermute(messages[n_side + side], ("gz", "col"), both))

    (u1,) = call(
        lambda *refs: first_kernel(place_of, n_row, *refs),
        [sds((most_first, n_rows, quarter), F32)],
        [vol, yud, w], scratch_for(most_first), "first", flops=most_first * layer_flops,
    )
    u2, send = call(
        lambda *refs: near_kernel(place_of, zs, n_row, *refs),
        [sds((EDGE, n_rows, quarter), F32), bf16(n_rows, 2 * quarter)],
        [vol, yud, zown, zcorner, u1, w],
        [pltpu.VMEM((R, ext, cols), BF16)] + scratch_for(EDGE),
        "near", flops=EDGE * layer_flops,
    )
    sums = lax.ppermute(send, "gz", swap)

    (far,) = call(
        lambda zown, zcorner, *refs: beyond_kernel(
            n_col, quads, rows, zown, zcorner, refs[:n_side], refs[n_side]
        ),
        [bf16(EXTRA, SLOTS, 128)], [zown, zcorner] + zxs, [], "beyond", flops=layer_flops,
    )

    def last_body(*refs):
        head, x_refs, tail = refs[0:8], refs[8 : 8 + n_side], refs[8 + n_side :]
        last_kernel(place_of, zs, n_row, n_col, *head, x_refs, *tail)

    count = depth + 8
    (result,) = call(
        last_body,
        [sds((6, depth // 4, quarter_rows, quarter), F32)],
        [vol, yud, own, halo, far, u1, u2, w] + xs,
        [
            pltpu.VMEM((count * SLOTS, 128), BF16),
            pltpu.VMEM((count * SLOTS, 128), BF16),
            pltpu.VMEM((count // 8, 6 * gr, 256), BF16),
            pltpu.VMEM((most_last, n_rows, quarter), F32),
        ]
        + scratch_for(most_last),
        "last", flops=(most_last + 3) * layer_flops,
    )
    (out,) = call(add_kernel, [sds(result.shape, F32)], [result, sums], [], "add")
    return out


def solution(mesh):
    return jax.shard_map(
        per_device,
        mesh=mesh,
        in_specs=(P("gz", "row", "col"),),
        out_specs=P(None, "gz", "row", "col"),
        check_vma=False,
    )
```
